32 devices in a mesh: groups: 2 (over x), tensor: 16 (over z, y, core).
Axes of the slice: x: 2, y: 2, z: 4, core: 2. Of those that a mesh axis runs over, the one named last changes fastest.
Arguments:
- hidden_in: bfloat16 [2, 192, 16384], P(None, 'groups', 'tensor'), parts along dimension 1, may hold values from -6 to 6
- norm_gain: bfloat16 [16384], P('tensor'), may hold values from 0.099609375 to 1.8984375
- qkv_weight: bfloat16 [16384, 18432], P('tensor'), may hold values from -0.046875 to 0.046875
- out_weight: bfloat16 [16384, 16384], P(None, 'tensor'), may hold values from -0.046875 to 0.046875
- cache_pool: bfloat16 [768, 8, 16, 256], P(('groups', 'tensor')), parts along dimension 0, may hold values from -6 to 6
- cache_scale: bfloat16 [768, 8, 2], P(('groups', 'tensor')), parts along dimension 0, may hold values from 0.3 to 120
- request_length: int32 [32], P('groups'), parts along dimension 0, may hold values from 1 to 2304, as said below
- block_table: int32 [32, 16], P('groups'), parts along dimension 0, may hold values from 0 to 23, as said below
Outputs:
- hidden_out: bfloat16 [2, 192, 16384], P(None, 'groups', 'tensor'), parts along dimension 1
The draws below stay inside these ranges and needn't reach their ends.
There are 2 independent parts, one for each index of `groups`. The reference program is written for one: setup_inputs(seed, part) draws one part's arguments, and reference() takes and returns one part's arrays. A program takes and returns all parts, laid end to end along the dimension named above; an argument that names none is the same for every part. Nothing has to cross between parts.
Inputs may be any that keep to these rules, and one draw needn't show every extreme that they name: `request_length`: a request spans ceil(length / 256) stripes; the stripes of the requests of one owner (requests with equal index mod 2) number at most 16 in all and exactly 16 for some owner; the stripes of all requests number exactly 24; some request reaches the largest length. `block_table`: row r lists, for the stripes of request r in order, the pool slot that every device uses for its block of that stripe; over all requests each slot appears once; entries past a request's stripes are zero.
All inputs are finite; a program needn't handle non-finite values.
Results may differ from the reference program's by a relative error of at most 0.005.
The reference program's roundings to bfloat16 on the way (of `normed`, `joined`, `queries`, `cached`, `weights` and `attention`) count: a program that leaves them out, or rounds other values in their place, can miss the bound.
Values may be sent and summed in bfloat16 or wider, within the bound.
No kernel may reach another device: no remote copies, remote signals or barrier semaphores. Data moves between devices by JAX's collectives and lax.ppermute only.
A program may use at most 192 MiB of HBM per device.

```python
import math
import jax
import jax.numpy as jnp
from jax import lax

D = 16384
QH = 128
KVH = 8
HD = 128
REQS = 16
QR = 6
STEPS = 2
BLK = 16
TOTU = 24
GQ = 16
GW = 2304
OWN = 2
REQUESTS_PER_OWNER = 8
MAX_OWNER_STRIPES = 16
STRIPE = 256
ROWS = 96
N_TENSOR = 16


def request_plan(key):
    keys = jax.random.split(key, 6)
    owner_ids = jnp.arange(OWN, dtype=jnp.int32)
    full_owner = jax.random.randint(keys[0], (), 0, OWN)
    other_owners = owner_ids != full_owner
    weights = jnp.where(other_owners, jax.random.randint(keys[1], (OWN,), 2, 4), 0)
    extra = TOTU - MAX_OWNER_STRIPES - (OWN - 1) * REQUESTS_PER_OWNER
    stripe_shares = extra * weights // jnp.sum(weights)
    remaining_stripes = extra - jnp.sum(stripe_shares)
    stripe_placement = jnp.cumsum(other_owners.astype(jnp.int32)) - 1
    extra_stripe = (other_owners & (stripe_placement < remaining_stripes)).astype(jnp.int32)
    owner_loads = jnp.where(other_owners, REQUESTS_PER_OWNER + stripe_shares + extra_stripe, MAX_OWNER_STRIPES)
    order = jnp.arange(REQS, dtype=jnp.int32)
    request_owner = order % OWN
    same = request_owner[None, :] == request_owner[:, None]
    rank = jnp.sum((same & (order[None, :] < order[:, None])).astype(jnp.int32), 1)
    split_weights = jax.random.randint(keys[3], (REQS,), 1, 9)
    group_weight = jnp.sum(jnp.where(same, split_weights[None, :], 0), 1)
    owner_load = owner_loads[request_owner]
    on_full = request_owner == full_owner
    parts = jnp.where(on_full, 1, 1 + (owner_load - REQUESTS_PER_OWNER) * split_weights // group_weight)
    group_parts = jnp.sum(jnp.where(same, parts[None, :], 0), 1)
    stripes = parts + jnp.where(rank == 0, owner_load - group_parts, 0)
    tail = jax.random.randint(keys[4], (REQS,), 1, STRIPE + 1)
    tail = jnp.where(on_full & (rank == 0), STRIPE, tail)
    request_length = (stripes - 1) * STRIPE + tail
    start = jnp.cumsum(stripes) - stripes
    slot_order = jax.random.permutation(keys[5], TOTU)
    columns = jnp.arange(MAX_OWNER_STRIPES, dtype=jnp.int32)
    position = jnp.minimum(start[:, None] + columns[None, :], TOTU - 1)
    block_table = jnp.where(columns[None, :] < stripes[:, None], slot_order[position], 0)
    return (request_length.astype(jnp.int32), block_table.astype(jnp.int32))


def draw_request_length(key, part):
    shared = request_plan(key)
    return shared[0]


def draw_block_table(key, part):
    shared = request_plan(key)
    return shared[1]


def draw_cache_scale(key, part):
    key = jax.random.fold_in(key, 4)
    first = jax.random.fold_in(key, 0)
    scales = jnp.exp(jax.random.uniform(first, (N_TENSOR * TOTU, KVH, 2), jnp.float32, math.log(0.3), math.log(3.0)))
    return scales.astype(jnp.bfloat16)


def block_scale(stream_key, shape, cuts, smallest, high):
    loudness = 1.0
    for dim, blocks in cuts:
        draws = jax.random.uniform(jax.random.fold_in(jax.random.fold_in(stream_key, 6), dim), (blocks,), jnp.float32, smallest / len(cuts), high / len(cuts))
        loudness = loudness * jnp.repeat(jnp.exp(draws), shape[dim] // blocks).reshape((-1,) + (1,) * (len(shape) - 1 - dim))
    return loudness


def bell_draw(stream_key, shape, deviation, limit, cuts=(), kind=jnp.bfloat16):
    entries = deviation * jax.random.normal(stream_key, shape, jnp.float32)
    if cuts:
        entries = entries * block_scale(stream_key, shape, cuts, -0.22, 0.18)
    return jnp.clip(entries, -limit, limit).astype(kind)


def setup_inputs(seed: int = 0, part: int = 0) -> dict:
    key_list = jax.random.split(jax.random.key(seed), 9)
    part_splits = jax.random.split(jax.random.fold_in(key_list[8], part), 9)
    return {
        "hidden_in": bell_draw(part_splits[0], (STEPS, ROWS, D), 1.0, 6.0, ((2, 16),)),
        "norm_gain": jnp.clip(1.0 + 0.18 * jax.random.normal(key_list[1], (D,), jnp.float32), 0.099609375, 1.8984375).astype(jnp.bfloat16),
        "qkv_weight": bell_draw(key_list[2], (D, KVH * GW), D ** -0.5, 0.046875, ((0, 16),)),
        "out_weight": bell_draw(key_list[3], (QH * HD, D), (QH * HD) ** -0.5, 0.046875, ((1, 16),)),
        "cache_pool": bell_draw(part_splits[4], (N_TENSOR * TOTU, KVH, BLK, 2 * HD), 1.0, 6.0, ((0, 16),)),
        "cache_scale": draw_cache_scale(jax.random.fold_in(jax.random.fold_in(key_list[8], part), 71), part),
        "request_length": draw_request_length(jax.random.fold_in(jax.random.fold_in(key_list[8], part), 71), part),
        "block_table": draw_block_table(jax.random.fold_in(jax.random.fold_in(key_list[8], part), 71), part),
    }


EPSILON = 1e-05
ROPE_BASE = 500000.0
NEG_FILL = -1e+30

def rotate(values, positions):
    half = values.shape[-1] // 2
    freqs = ROPE_BASE ** (-(jnp.arange(half, dtype=jnp.float32) * 2.0 / values.shape[-1]))
    angles = positions.astype(jnp.float32)[..., None] * freqs
    cosine = jnp.cos(angles)
    sine = jnp.sin(angles)
    first = values[..., :half]
    second = values[..., half:]
    return jnp.concatenate([first * cosine - second * sine, second * cosine + first * sine], -1)

def reference(hidden_in, norm_gain, qkv_weight, out_weight, cache_pool, cache_scale, request_length, block_table):
    stripe = N_TENSOR * BLK
    values = hidden_in.astype(jnp.float32)
    mean_square = lax.optimization_barrier(jnp.mean(values * values, -1, keepdims=True))
    normed = (values * lax.rsqrt(mean_square + EPSILON) * norm_gain.astype(jnp.float32)).astype(jnp.bfloat16)
    joined = jnp.dot(normed.reshape(STEPS * ROWS, D), qkv_weight, preferred_element_type=jnp.float32).astype(jnp.bfloat16)
    joined = joined.reshape(STEPS, REQS, QR, KVH, GW)
    scale = HD ** (-0.5)
    token = jnp.arange(MAX_OWNER_STRIPES * stripe, dtype=jnp.int32)
    token_stripe = token // stripe
    token_device = token % stripe // BLK
    token_row = token % BLK
    step_ids = jnp.arange(STEPS, dtype=jnp.int32)
    row_ids = jnp.arange(QR, dtype=jnp.int32)
    key_step = step_ids[None, None, :, None]
    query_step = step_ids[:, None, None, None]
    allowed = (key_step < query_step) | (key_step == query_step) & (row_ids[None, None, None, :] <= row_ids[None, :, None, None])
    mask_new = allowed[:, :, None, None, :, :]

    def one_request(request):
        block = joined[:, request]
        length = request_length[request]
        position = length + QR * step_ids[:, None] + row_ids[None, :]
        queries = rotate(block[..., :GQ * HD].reshape(STEPS, QR, KVH, GQ, HD).astype(jnp.float32), position[:, :, None, None]).astype(jnp.bfloat16)
        new_keys = rotate(block[..., GQ * HD:GQ * HD + HD].astype(jnp.float32), position[:, :, None]).astype(jnp.bfloat16)
        new_values = block[..., GQ * HD + HD:]
        pool_rows = token_device * TOTU + block_table[request][token_stripe]
        cached = cache_pool[pool_rows, :, token_row, :]
        scales = cache_scale[pool_rows].astype(jnp.float32)
        valid = token < length
        query_wide = queries.astype(jnp.float32)
        cache_scores = jnp.einsum('sihgd,thd->sihgt', query_wide, cached[..., :HD].astype(jnp.float32))
        cache_scores = cache_scores * jnp.transpose(scales[:, :, 0])[:, None, :] * scale
        cache_scores = jnp.where(valid, cache_scores, NEG_FILL)
        new_scores = jnp.einsum('sihgd,pjhd->sihgpj', query_wide, new_keys.astype(jnp.float32)) * scale
        new_scores = jnp.where(mask_new, new_scores, NEG_FILL)
        top = jnp.maximum(lax.optimization_barrier(jnp.max(cache_scores, -1)), lax.optimization_barrier(jnp.max(new_scores, (4, 5))))
        cache_expo = jnp.where(valid, jnp.exp(cache_scores - top[..., None]), 0.0)
        new_expo = jnp.where(mask_new, jnp.exp(new_scores - top[..., None, None]), 0.0)
        total = lax.optimization_barrier(jnp.sum(cache_expo, -1)) + lax.optimization_barrier(jnp.sum(new_expo, (4, 5)))
        cache_weights = lax.optimization_barrier((cache_expo * jnp.transpose(scales[:, :, 1])[:, None, :]).astype(jnp.bfloat16))
        new_weights = lax.optimization_barrier(new_expo.astype(jnp.bfloat16))
        summed = jnp.einsum('sihgt,thd->sihgd', cache_weights.astype(jnp.float32), cached[..., HD:].astype(jnp.float32))
        summed = summed + jnp.einsum('sihgpj,pjhd->sihgd', new_weights.astype(jnp.float32), new_values.astype(jnp.float32))
        return (summed / total[..., None]).astype(jnp.bfloat16).reshape(STEPS, QR, QH * HD)
    mapped = lax.map(one_request, jnp.arange(REQS, dtype=jnp.int32))
    attention = jnp.transpose(mapped, (1, 0, 2, 3)).reshape(STEPS * ROWS, QH * HD)
    mixed = jnp.dot(attention, out_weight, preferred_element_type=jnp.float32).reshape(STEPS, ROWS, D)
    return (values + mixed).astype(jnp.bfloat16)
```

```python
import jax
import jax.numpy as jnp
from jax import lax
from jax.experimental import pallas as pl
from jax.experimental.pallas import tpu as pltpu
from jax.sharding import PartitionSpec as P

D = 16384
QH = 128
KVH = 8
HD = 128
QR = 6
STEPS = 2
BLK = 16
GQ = 16
GW = 2304


EPSILON = 1e-05
ROPE_BASE = 500000.0
NEG_FILL = -1e30


def rotate(values, positions):
    half = values.shape[-1] // 2
    freqs = ROPE_BASE ** (-(jnp.arange(half, dtype=jnp.float32) * 2.0 / values.shape[-1]))
    angles = positions.astype(jnp.float32)[..., None] * freqs
    cosine = jnp.cos(angles)
    sine = jnp.sin(angles)
    first = values[..., :half]
    second = values[..., half:]
    return jnp.concatenate([first * cosine - second * sine, second * cosine + first * sine], -1)


def request_layout(request_owner, request_length, block_table, owners, stripe):
    requests = request_owner.shape[0]
    most = block_table.shape[1]
    order = jnp.arange(requests, dtype=jnp.int32)
    stripes = (request_length + stripe - 1) // stripe
    before = (
        (request_owner[None, :] == request_owner[:, None]) & (order[None, :] < order[:, None])
    ).astype(jnp.int32)
    rank = jnp.sum(before, 1)
    offset = jnp.sum(before * stripes[None, :], 1)
    owner_ids = jnp.arange(owners, dtype=jnp.int32)
    mine = request_owner[None, :] == owner_ids[:, None]
    member = mine[:, :, None] & (
        rank[None, :, None] == jnp.arange(requests // owners, dtype=jnp.int32)[None, None, :]
    )
    owner_requests = jnp.sum(member.astype(jnp.int32) * order[None, :, None], 1)
    columns = jnp.arange(most, dtype=jnp.int32)
    within = columns[None, None, :] - offset[None, :, None]
    hit = (mine[:, :, None] & (within >= 0) & (within < stripes[None, :, None])).astype(jnp.int32)
    stripe_request = jnp.sum(hit * order[None, :, None], 1) - (1 - jnp.sum(hit, 1))
    stripe_rank = jnp.sum(hit * within, 1)
    pick = (within[..., None] == columns[None, None, None, :]).astype(jnp.int32)
    slots = jnp.sum(hit[..., None] * pick * block_table[None, :, None, :], (1, 3))
    return (owner_requests, stripe_request, stripe_rank, slots, rank, stripes)


def cache_partial(queries, keys, values, key_scale, value_scale, mask):
    scores = jnp.einsum("srgd,td->srgt", queries, keys, preferred_element_type=jnp.float32)
    scores = jnp.where(mask, scores * key_scale * HD ** (-0.5), NEG_FILL)
    best = jnp.max(scores, -1)
    expo = jnp.where(mask, jnp.exp(scores - best[..., None]), 0.0)
    total = jnp.sum(expo, -1)
    weights = (expo * value_scale).astype(jnp.bfloat16)
    summed = jnp.einsum("srgt,td->srgd", weights, values, preferred_element_type=jnp.float32)
    return (best, total, summed)


def local_general(
    hidden_in,
    norm_gain,
    qkv_weight,
    out_weight,
    cache_pool,
    cache_scale,
    request_length,
    block_table,
):
    devices = lax.axis_size("tensor")
    device = lax.axis_index("tensor")
    owners = devices // KVH
    stripe = devices * BLK
    requests = request_length.shape[0]
    request_owner = jnp.arange(requests, dtype=jnp.int32) % owners
    unit_rows = requests // owners * QR
    most = block_table.shape[1]
    local_width = hidden_in.shape[2]
    my_owner = device // KVH
    owner_requests, stripe_request, stripe_rank, slots, rank, stripes = request_layout(
        request_owner, request_length, block_table, owners, stripe
    )
    step_rows = jnp.arange(QR, dtype=jnp.int32)
    row_order = (owner_requests[:, :, None] * QR + step_rows[None, None, :]).reshape(
        owners * unit_rows
    )
    inverse = ((request_owner * unit_rows + rank * QR)[:, None] + step_rows[None, :]).reshape(
        requests * QR
    )
    row_request = jnp.repeat(owner_requests[my_owner], QR)
    row_length = request_length[row_request]
    row_step = jnp.arange(unit_rows, dtype=jnp.int32) % QR
    same_request = row_request[:, None] == row_request[None, :]
    gain = norm_gain.astype(jnp.float32)
    weight_grouped = qkv_weight.reshape(local_width, KVH, GW)
    sent = cache_pool[jnp.transpose(slots)].reshape(most, devices, BLK, 2 * HD)
    sent_scale = cache_scale[jnp.transpose(slots)].reshape(most, devices, 2)
    landed, landed_scale = (
        lax.all_to_all(sent, "tensor", split_axis=1, concat_axis=1, tiled=True),
        lax.all_to_all(sent_scale, "tensor", split_axis=1, concat_axis=1, tiled=True),
    )
    cache_data = landed.reshape(most * stripe, 2 * HD)
    token_scale = jnp.broadcast_to(
        landed_scale.astype(jnp.float32)[:, :, None, :], (most, devices, BLK, 2)
    ).reshape(most * stripe, 2)
    token = jnp.arange(most * stripe, dtype=jnp.int32)
    token_stripe = token // stripe
    token_request = stripe_request[my_owner][token_stripe]
    token_position = stripe_rank[my_owner][token_stripe] * stripe + token % stripe
    token_length = jnp.where(token_request >= 0, request_length[jnp.maximum(token_request, 0)], 0)
    cache_mask = (
        (token_request[None, :] == row_request[:, None]) & (token_position < token_length)[None, :]
    )[None, :, None, :]
    outputs = []
    keys_seen = []
    values_seen = []
    for step in range(STEPS):
        block = hidden_in[step : step + 1]
        project_count = block.shape[0]
        values = block.astype(jnp.float32)
        sums = lax.psum(jnp.sum(values * values, -1), "tensor")
        normed = (values * lax.rsqrt(sums[..., None] / D + EPSILON) * gain).astype(jnp.bfloat16)
        ordered = jnp.take(normed, row_order, axis=1).reshape(
            project_count, owners, unit_rows, local_width
        )
        term = jnp.einsum(
            "sojd,dhg->ohsjg", ordered, weight_grouped, preferred_element_type=jnp.float32
        )
        term = term.reshape(owners * KVH * project_count * unit_rows, GW)
        mine = lax.psum_scatter(term, "tensor", scatter_dimension=0, tiled=True)
        joined_block = mine.astype(jnp.bfloat16).reshape(project_count, unit_rows, GW)
        prepare_count = joined_block.shape[0]
        steps_here = step + jnp.arange(prepare_count, dtype=jnp.int32)
        position = row_length[None, :] + QR * steps_here[:, None] + row_step[None, :]
        prepare_queries = rotate(
            joined_block[..., : GQ * HD]
            .reshape(prepare_count, unit_rows, GQ, HD)
            .astype(jnp.float32),
            position[:, :, None],
        ).astype(jnp.bfloat16)
        keys = rotate(
            joined_block[..., GQ * HD : GQ * HD + HD].astype(jnp.float32), position
        ).astype(jnp.bfloat16)
        queries, keys, values = (prepare_queries, keys, joined_block[..., GQ * HD + HD :])
        keys_seen.append(keys)
        values_seen.append(values)
        keys_all = jnp.concatenate(keys_seen, 0)
        attend_count = queries.shape[0]
        cache_best, cache_total, cache_summed = cache_partial(
            queries,
            cache_data[:, :HD],
            cache_data[:, HD:],
            token_scale[:, 0],
            token_scale[:, 1],
            cache_mask,
        )
        news = jnp.einsum(
            "srgd,pjd->srgpj", queries, keys_all, preferred_element_type=jnp.float32
        ) * HD ** (-0.5)
        query_step = step + jnp.arange(attend_count, dtype=jnp.int32)[:, None, None, None]
        key_step = jnp.arange(keys_all.shape[0], dtype=jnp.int32)[None, None, :, None]
        allowed = (key_step < query_step) | (key_step == query_step) & (
            row_step[None, None, None, :] <= row_step[None, :, None, None]
        )
        allowed = (allowed & same_request[None, :, None, :])[:, :, None, :, :]
        news = jnp.where(allowed, news, NEG_FILL)
        best = jnp.maximum(cache_best, jnp.max(news, (3, 4)))
        factor = jnp.exp(cache_best - best)
        expo = jnp.where(allowed, jnp.exp(news - best[..., None, None]), 0.0)
        total = cache_total * factor + jnp.sum(expo, (3, 4))
        summed = cache_summed * factor[..., None] + jnp.einsum(
            "srgpj,pjd->srgd",
            expo.astype(jnp.bfloat16),
            jnp.concatenate(values_seen, 0),
            preferred_element_type=jnp.float32,
        )
        attention = (
            (summed / total[..., None])
            .astype(jnp.bfloat16)
            .reshape(attend_count, unit_rows, GQ * HD)
        )
        count = attention.shape[0]
        gathered = lax.all_gather(attention, "tensor", axis=2, tiled=True).reshape(
            count, unit_rows, owners, QH * HD
        )
        mixed = jnp.einsum(
            "sjof,fd->sojd", gathered, out_weight, preferred_element_type=jnp.float32
        )
        mixed = jnp.take(mixed.reshape(count, owners * unit_rows, local_width), inverse, axis=1)
        outputs.append(
            (hidden_in[step : step + count].astype(jnp.float32) + mixed).astype(jnp.bfloat16)
        )
    return jnp.concatenate(outputs, 0)


VMEM_LIMIT = 48 * 1024 * 1024
LEVELS = 32000.0
TILE = 16
MESH_BITS = (1, 2, 4, 8)


def swap(value, bit):
    devices = lax.axis_size("tensor")
    return lax.ppermute(value, "tensor", [(i, i ^ bit) for i in range(devices)])


def encode(block):
    top = jnp.max(jnp.abs(block), 0, keepdims=True)
    power = jnp.ceil(jnp.log2(jnp.maximum(top, 1e-30)))
    codes = jnp.round(block * (jnp.exp2(-power) * LEVELS))
    return codes.astype(jnp.int32).astype(jnp.int16), power


def decode(codes, power):
    return codes.astype(jnp.int32).astype(jnp.float32) * (jnp.exp2(power) * (1.0 / LEVELS))


def pick_row(rows, index):
    ids = lax.broadcasted_iota(jnp.int32, rows.shape, 0)
    return jnp.sum(jnp.where(ids == index, rows, 0.0), 0, keepdims=True)


def store_codes(sent, powers, block, index, steps):
    rows = block.shape[0]
    codes, power = encode(block)
    sent[pl.ds(pl.multiple_of(index * rows, TILE), rows), :] = codes

    @pl.when(index == 0)
    def _():
        powers[...] = jnp.zeros_like(powers)

    powers[pl.ds(index, 1), :] = power

    @pl.when(index == steps - 1)
    def _():
        sent[pl.ds(steps * rows, TILE), :] = powers[...].astype(jnp.int32).astype(jnp.int16)


def project_kernel(core, normed, *refs):
    weights = refs[:-3]
    kept, sent, powers = refs[-3:]
    half = len(weights) // 2
    index = pl.program_id(0)

    def product(blocks):
        terms = [
            jnp.dot(normed[...], w[...], preferred_element_type=jnp.float32) for w in blocks
        ]
        return terms[0] if len(terms) == 1 else jnp.concatenate(terms, 1)

    store_codes(sent, powers, product(weights[half:]), index, KVH)
    kept[0] = product(weights[:half])


def project(core, normed, qkv_weight, chunk, with_pair):
    rows, width = normed.shape
    columns = 2 * HD + (HD if with_pair else 0)
    per_group = GW // (2 * HD)

    def wide(other):
        def place(t, c):
            mine = c[0] if not other else 1 - c[0]
            return (0, t * per_group + mine * (GQ // 4) + chunk)

        return pl.BlockSpec((width, 2 * HD), place)

    def narrow(other):
        def place(t, c):
            mine = c[0] if not other else 1 - c[0]
            return (0, t * (GW // HD) + GQ + mine)

        return pl.BlockSpec((width, HD), place)

    specs = []
    for other in (False, True):
        specs.append(wide(other))
        if with_pair:
            specs.append(narrow(other))
    return pl.pallas_call(
        project_kernel,
        grid_spec=pltpu.PrefetchScalarGridSpec(
            num_scalar_prefetch=1,
            grid=(KVH,),
            in_specs=[pl.BlockSpec((rows, width), lambda t, c: (0, 0))] + specs,
            out_specs=[
                pl.BlockSpec((1, rows, columns), lambda t, c: (t, 0, 0)),
                pl.BlockSpec((KVH * rows + TILE, columns), lambda t, c: (0, 0)),
            ],
            scratch_shapes=[pltpu.VMEM((TILE, columns), jnp.float32)],
        ),
        out_shape=[
            jax.ShapeDtypeStruct((KVH, rows, columns), jnp.float32),
            jax.ShapeDtypeStruct((KVH * rows + TILE, columns), jnp.int16),
        ],
        compiler_params=pltpu.CompilerParams(vmem_limit_bytes=VMEM_LIMIT),
        cost_estimate=pl.CostEstimate(
            flops=2 * rows * width * columns * 2 * KVH,
            bytes_accessed=width * columns * 4 * KVH + rows * columns * 6 * KVH,
            transcendentals=0,
        ),
        name="project",
    )(core, normed, *([qkv_weight] * len(specs)))


def fold_kernel(steps, bit, held, landed, landed_powers, kept, sent, powers):
    index = pl.program_id(0)
    rows = held.shape[1]
    rows_of_powers = landed_powers[...].astype(jnp.int32).astype(jnp.float32)

    def total(side):
        place = pl.multiple_of(side * rows, TILE)
        codes = landed[pl.ds(place, rows), :]
        return held[side] + decode(codes, pick_row(rows_of_powers, 2 * index + side))

    mine = bit[0]
    store_codes(sent, powers, total(1 - mine), index, steps)
    kept[0] = total(mine)


def fold(bit, held, landed):
    blocks, rows, columns = held.shape
    steps = blocks // 2
    return pl.pallas_call(
        lambda *refs: fold_kernel(steps, *refs),
        grid_spec=pltpu.PrefetchScalarGridSpec(
            num_scalar_prefetch=1,
            grid=(steps,),
            in_specs=[
                pl.BlockSpec((2, rows, columns), lambda i, b: (i, 0, 0)),
                pl.BlockSpec((2 * rows, columns), lambda i, b: (i, 0)),
                pl.BlockSpec((TILE, columns), lambda i, b: (blocks * rows // TILE, 0)),
            ],
            out_specs=[
                pl.BlockSpec((1, rows, columns), lambda i, b: (i, 0, 0)),
                pl.BlockSpec((steps * rows + TILE, columns), lambda i, b: (0, 0)),
            ],
            scratch_shapes=[pltpu.VMEM((TILE, columns), jnp.float32)],
        ),
        out_shape=[
            jax.ShapeDtypeStruct((steps, rows, columns), jnp.float32),
            jax.ShapeDtypeStruct((steps * rows + TILE, columns), jnp.int16),
        ],
        compiler_params=pltpu.CompilerParams(vmem_limit_bytes=VMEM_LIMIT),
        cost_estimate=pl.CostEstimate(
            flops=20 * blocks * rows * columns,
            bytes_accessed=blocks * rows * columns * 9,
            transcendentals=0,
        ),
        name="fold",
    )(bit, held, landed, landed)


def finish_kernel(held, landed, joined):
    rows = held.shape[1]
    power = landed[pl.ds(rows, TILE), :].astype(jnp.int32).astype(jnp.float32)[0:1]
    joined[...] = (held[0] + decode(landed[pl.ds(0, rows), :], power)).astype(jnp.bfloat16)


def finish(held, landed):
    _, rows, columns = held.shape
    return pl.pallas_call(
        finish_kernel,
        out_shape=jax.ShapeDtypeStruct((rows, columns), jnp.bfloat16),
        compiler_params=pltpu.CompilerParams(vmem_limit_bytes=VMEM_LIMIT),
        name="finish",
    )(held, landed)


def attend_kernel(
    slot_request,
    queries,
    new_keys,
    new_values,
    own,
    other,
    key_scale,
    value_scale,
    cache_bias,
    new_bias,
    attention,
    slot_best,
    slot_total,
    slot_sum,
    best,
    total,
    summed,
):
    slots = slot_best.shape[0]
    requests, count, _ = queries.shape
    transposed = (((1,), (1,)), ((), ()))
    for request in range(requests):
        scores = (
            lax.dot_general(
                queries[request],
                new_keys[request],
                transposed,
                preferred_element_type=jnp.float32,
            )
            * HD ** (-0.5)
            + new_bias[...]
        )
        top = jnp.max(scores, -1, keepdims=True)
        expo = jnp.exp(scores - top)
        best[request] = jnp.broadcast_to(top, (count, HD))
        total[request] = jnp.broadcast_to(jnp.sum(expo, -1, keepdims=True), (count, HD))
        summed[request] = jnp.dot(
            expo.astype(jnp.bfloat16), new_values[request], preferred_element_type=jnp.float32
        )
    for slot in range(slots):
        request = slot_request[slot]
        query = queries[request]
        raw = [
            part[:, slot * BLK : (slot + 1) * BLK, :].reshape(KVH * BLK, 2 * HD)
            for part in (own, other)
        ]
        scores = jnp.concatenate(
            [
                lax.dot_general(
                    query, kv[:, :HD], transposed, preferred_element_type=jnp.float32
                )
                for kv in raw
            ],
            1,
        )
        scores = scores * key_scale[slot : slot + 1, :] + cache_bias[slot : slot + 1, :]
        top = jnp.max(scores, -1, keepdims=True)
        expo = jnp.exp(scores - top)
        weights = (expo * value_scale[slot : slot + 1, :]).astype(jnp.bfloat16)
        slot_best[slot] = jnp.broadcast_to(top, (count, HD))
        slot_total[slot] = jnp.broadcast_to(jnp.sum(expo, -1, keepdims=True), (count, HD))
        values = jnp.concatenate([kv[:, HD:] for kv in raw], 0)
        slot_sum[slot] = jnp.dot(weights, values, preferred_element_type=jnp.float32)
    for slot in range(slots):
        request = slot_request[slot]
        before = best[request]
        here = slot_best[slot]
        top = jnp.maximum(before, here)
        keep = jnp.exp(before - top)
        add = jnp.exp(here - top)
        best[request] = top
        total[request] = total[request] * keep + slot_total[slot] * add
        summed[request] = summed[request] * keep + slot_sum[slot] * add
    for request in range(requests):
        attention[request] = (summed[request] / total[request]).astype(jnp.bfloat16)


def attend(slot_request, *arrays):
    queries = arrays[0]
    slots = arrays[5].shape[0]
    requests, count, _ = queries.shape
    whole = pl.BlockSpec(memory_space=pltpu.VMEM)
    return pl.pallas_call(
        attend_kernel,
        in_specs=[pl.BlockSpec(memory_space=pltpu.SMEM)] + [whole] * len(arrays),
        out_specs=whole,
        out_shape=jax.ShapeDtypeStruct((requests, count, HD), jnp.bfloat16),
        scratch_shapes=[pltpu.VMEM((slots, count, HD), jnp.float32)] * 3
        + [pltpu.VMEM((requests, count, HD), jnp.float32)] * 3,
        compiler_params=pltpu.CompilerParams(vmem_limit_bytes=VMEM_LIMIT),
        cost_estimate=pl.CostEstimate(
            flops=4 * slots * count * 2 * KVH * BLK * HD,
            bytes_accessed=2 * slots * 2 * KVH * BLK * 2 * HD,
            transcendentals=slots * count * 2 * KVH * BLK,
        ),
        name="attend",
    )(slot_request, *arrays)


def slot_layout(request_length, block_table, slots, stripe):
    requests, most = block_table.shape
    stripes = (request_length + stripe - 1) // stripe
    columns = jnp.arange(most, dtype=jnp.int32)
    held = columns[None, :] < stripes[:, None]
    hit = held[:, :, None] & (
        block_table[:, :, None] == jnp.arange(slots, dtype=jnp.int32)[None, None, :]
    )
    hit = hit.astype(jnp.int32)
    order = jnp.arange(requests, dtype=jnp.int32)
    request = jnp.sum(hit * order[:, None, None], (0, 1))
    rank = jnp.sum(hit * columns[None, :, None], (0, 1))
    length = jnp.sum(hit * request_length[:, None, None], (0, 1))
    return request, rank, length


def handover(cache_pool, cache_scale, chip):
    slots = cache_pool.shape[0]
    scales = jnp.pad(
        jnp.transpose(cache_scale, (1, 2, 0)).reshape(KVH, 1, 2 * slots),
        ((0, 0), (0, TILE - 1), (0, 2 * HD - 2 * slots)),
    )
    landed = []
    for k in range(KVH):
        head = chip ^ k
        blocks = lax.dynamic_index_in_dim(cache_pool, head, 1, keepdims=False)
        rows = jnp.concatenate(
            [
                blocks.reshape(slots * BLK, 2 * HD),
                lax.dynamic_index_in_dim(scales, head, 0, keepdims=False),
            ],
            0,
        )
        landed.append(swap(rows, 2 * k) if k else rows)
    own = jnp.stack(landed)
    return own, swap(own, 1)


def local_pairs(
    hidden_in,
    norm_gain,
    qkv_weight,
    out_weight,
    cache_pool,
    cache_scale,
    request_length,
    block_table,
):
    devices = lax.axis_size("tensor")
    device = lax.axis_index("tensor")
    core = device % 2
    chip = device // 2
    stripe = devices * BLK
    slots = cache_pool.shape[0]
    requests = request_length.shape[0]
    rows = STEPS * requests * QR
    width = hidden_in.shape[2]
    heads = GQ // 2

    hidden = hidden_in.astype(jnp.float32)
    sums = jnp.sum(hidden * hidden, -1)
    for bit in MESH_BITS:
        sums = sums + swap(sums, bit)
    normed = (
        hidden * lax.rsqrt(sums[..., None] / D + EPSILON) * norm_gain.astype(jnp.float32)
    ).astype(jnp.bfloat16)
    normed = normed.reshape(rows, width)

    own, other = handover(cache_pool, cache_scale, chip)

    bits = [jnp.reshape((device >> b) & 1, (1,)).astype(jnp.int32) for b in range(4)]
    chunks = []
    for chunk in range(GQ // 4):
        held, sent = project(bits[0], normed, qkv_weight, chunk, chunk == 0)
        for b in (1, 2, 3):
            held, sent = fold(bits[b], held, swap(sent, MESH_BITS[b - 1]))
        chunks.append(finish(held, swap(sent, MESH_BITS[3])))
    pair = chunks[0][:, 2 * HD :]
    query_columns = jnp.concatenate([chunks[0][:, : 2 * HD]] + chunks[1:], 1)
    pair_other = swap(pair, 1)
    raw_keys = jnp.where(core == 0, pair, pair_other)
    raw_values = jnp.where(core == 0, pair_other, pair)

    step_ids = jnp.arange(STEPS, dtype=jnp.int32)
    row_ids = jnp.arange(QR, dtype=jnp.int32)
    position = (
        request_length[None, :, None] + QR * step_ids[:, None, None] + row_ids[None, None, :]
    )
    queries = rotate(
        query_columns.reshape(STEPS, requests, QR, heads, HD).astype(jnp.float32),
        position[..., None],
    ).astype(jnp.bfloat16)
    queries = jnp.transpose(queries, (1, 0, 2, 3, 4)).reshape(requests, STEPS * QR * heads, HD)
    keys = rotate(
        raw_keys.reshape(STEPS, requests, QR, HD).astype(jnp.float32), position
    ).astype(jnp.bfloat16)

    def by_request(value):
        value = jnp.transpose(value.reshape(STEPS, requests, QR, HD), (1, 0, 2, 3))
        value = value.reshape(requests, STEPS * QR, HD)
        return jnp.pad(value, ((0, 0), (0, TILE - STEPS * QR), (0, 0)))

    slot_request, slot_rank, slot_length = slot_layout(request_length, block_table, slots, stripe)
    source = chip ^ jnp.arange(KVH, dtype=jnp.int32)
    sources = jnp.stack([source * 2 + core, source * 2 + 1 - core])
    offset = sources[:, :, None] * BLK + jnp.arange(BLK, dtype=jnp.int32)[None, None, :]
    token = slot_rank[:, None] * stripe + offset.reshape(1, stripe)
    cache_bias = jnp.where(token < slot_length[:, None], 0.0, NEG_FILL).astype(jnp.float32)
    scales = jnp.stack([own[:, slots * BLK, : 2 * slots], other[:, slots * BLK, : 2 * slots]])
    scales = scales.astype(jnp.float32).reshape(2 * KVH, 2, slots)
    scales = jnp.repeat(jnp.transpose(scales, (1, 2, 0)), BLK, axis=2)
    order = jnp.arange(STEPS * QR * heads, dtype=jnp.int32) // heads
    key_order = jnp.arange(TILE, dtype=jnp.int32)
    new_bias = jnp.where(key_order[None, :] <= order[:, None], 0.0, NEG_FILL).astype(jnp.float32)
    attention = attend(
        slot_request,
        queries,
        by_request(keys),
        by_request(raw_values),
        own,
        other,
        scales[0] * HD ** (-0.5),
        scales[1],
        cache_bias,
        new_bias,
    )
    attention = jnp.transpose(
        attention.reshape(requests, STEPS, QR, heads, HD), (1, 0, 2, 3, 4)
    ).reshape(STEPS, requests * QR, heads * HD)
    outputs = []
    for step in range(STEPS):
        gathered = lax.all_gather(attention[step], "tensor", axis=1, tiled=True)
        mixed = jnp.dot(gathered, out_weight, preferred_element_type=jnp.float32)
        outputs.append((hidden[step] + mixed).astype(jnp.bfloat16))
    return jnp.stack(outputs)


def solution(mesh):
    return jax.shard_map(
        local_pairs if mesh.shape["tensor"] == 2 * KVH else local_general,
        mesh=mesh,
        in_specs=(
            P(None, "groups", "tensor"),
            P("tensor"),
            P("tensor", None),
            P(None, "tensor"),
            P(("groups", "tensor"), None, None, None),
            P(("groups", "tensor"), None, None),
            P("groups"),
            P("groups", None),
        ),
        out_specs=P(None, "groups", "tensor"),
        check_vma=False,
    )
```

```python
import jax
import jax.numpy as jnp
from jax import lax
from jax.experimental import pallas as pl
from jax.experimental.pallas import tpu as pltpu
from jax.sharding import PartitionSpec as P

D = 16384
QH = 128
KVH = 8
HD = 128
QR = 6
STEPS = 2
BLK = 16
GQ = 16
GW = 2304


EPSILON = 1e-05
ROPE_BASE = 500000.0
NEG_FILL = -1e30


def rotate(values, positions):
    half = values.shape[-1] // 2
    freqs = ROPE_BASE ** (-(jnp.arange(half, dtype=jnp.float32) * 2.0 / values.shape[-1]))
    angles = positions.astype(jnp.float32)[..., None] * freqs
    cosine = jnp.cos(angles)
    sine = jnp.sin(angles)
    first = values[..., :half]
    second = values[..., half:]
    return jnp.concatenate([first * cosine - second * sine, second * cosine + first * sine], -1)


def request_layout(request_owner, request_length, block_table, owners, stripe):
    requests = request_owner.shape[0]
    most = block_table.shape[1]
    order = jnp.arange(requests, dtype=jnp.int32)
    stripes = (request_length + stripe - 1) // stripe
    before = (
        (request_owner[None, :] == request_owner[:, None]) & (order[None, :] < order[:, None])
    ).astype(jnp.int32)
    rank = jnp.sum(before, 1)
    offset = jnp.sum(before * stripes[None, :], 1)
    owner_ids = jnp.arange(owners, dtype=jnp.int32)
    mine = request_owner[None, :] == owner_ids[:, None]
    member = mine[:, :, None] & (
        rank[None, :, None] == jnp.arange(requests // owners, dtype=jnp.int32)[None, None, :]
    )
    owner_requests = jnp.sum(member.astype(jnp.int32) * order[None, :, None], 1)
    columns = jnp.arange(most, dtype=jnp.int32)
    within = columns[None, None, :] - offset[None, :, None]
    hit = (mine[:, :, None] & (within >= 0) & (within < stripes[None, :, None])).astype(jnp.int32)
    stripe_request = jnp.sum(hit * order[None, :, None], 1) - (1 - jnp.sum(hit, 1))
    stripe_rank = jnp.sum(hit * within, 1)
    pick = (within[..., None] == columns[None, None, None, :]).astype(jnp.int32)
    slots = jnp.sum(hit[..., None] * pick * block_table[None, :, None, :], (1, 3))
    return (owner_requests, stripe_request, stripe_rank, slots, rank, stripes)


def cache_partial(queries, keys, values, key_scale, value_scale, mask):
    scores = jnp.einsum("srgd,td->srgt", queries, keys, preferred_element_type=jnp.float32)
    scores = jnp.where(mask, scores * key_scale * HD ** (-0.5), NEG_FILL)
    best = jnp.max(scores, -1)
    expo = jnp.where(mask, jnp.exp(scores - best[..., None]), 0.0)
    total = jnp.sum(expo, -1)
    weights = (expo * value_scale).astype(jnp.bfloat16)
    summed = jnp.einsum("srgt,td->srgd", weights, values, preferred_element_type=jnp.float32)
    return (best, total, summed)


def local_general(
    hidden_in,
    norm_gain,
    qkv_weight,
    out_weight,
    cache_pool,
    cache_scale,
    request_length,
    block_table,
):
    devices = lax.axis_size("tensor")
    device = lax.axis_index("tensor")
    owners = devices // KVH
    stripe = devices * BLK
    requests = request_length.shape[0]
    request_owner = jnp.arange(requests, dtype=jnp.int32) % owners
    unit_rows = requests // owners * QR
    most = block_table.shape[1]
    local_width = hidden_in.shape[2]
    my_owner = device // KVH
    owner_requests, stripe_request, stripe_rank, slots, rank, stripes = request_layout(
        request_owner, request_length, block_table, owners, stripe
    )
    step_rows = jnp.arange(QR, dtype=jnp.int32)
    row_order = (owner_requests[:, :, None] * QR + step_rows[None, None, :]).reshape(
        owners * unit_rows
    )
    inverse = ((request_owner * unit_rows + rank * QR)[:, None] + step_rows[None, :]).reshape(
        requests * QR
    )
    row_request = jnp.repeat(owner_requests[my_owner], QR)
    row_length = request_length[row_request]
    row_step = jnp.arange(unit_rows, dtype=jnp.int32) % QR
    same_request = row_request[:, None] == row_request[None, :]
    gain = norm_gain.astype(jnp.float32)
    weight_grouped = qkv_weight.reshape(local_width, KVH, GW)
    sent = cache_pool[jnp.transpose(slots)].reshape(most, devices, BLK, 2 * HD)
    sent_scale = cache_scale[jnp.transpose(slots)].reshape(most, devices, 2)
    landed, landed_scale = (
        lax.all_to_all(sent, "tensor", split_axis=1, concat_axis=1, tiled=True),
        lax.all_to_all(sent_scale, "tensor", split_axis=1, concat_axis=1, tiled=True),
    )
    cache_data = landed.reshape(most * stripe, 2 * HD)
    token_scale = jnp.broadcast_to(
        landed_scale.astype(jnp.float32)[:, :, None, :], (most, devices, BLK, 2)
    ).reshape(most * stripe, 2)
    token = jnp.arange(most * stripe, dtype=jnp.int32)
    token_stripe = token // stripe
    token_request = stripe_request[my_owner][token_stripe]
    token_position = stripe_rank[my_owner][token_stripe] * stripe + token % stripe
    token_length = jnp.where(token_request >= 0, request_length[jnp.maximum(token_request, 0)], 0)
    cache_mask = (
        (token_request[None, :] == row_request[:, None]) & (token_position < token_length)[None, :]
    )[None, :, None, :]
    outputs = []
    keys_seen = []
    values_seen = []
    for step in range(STEPS):
        block = hidden_in[step : step + 1]
        project_count = block.shape[0]
        values = block.astype(jnp.float32)
        sums = lax.psum(jnp.sum(values * values, -1), "tensor")
        normed = (values * lax.rsqrt(sums[..., None] / D + EPSILON) * gain).astype(jnp.bfloat16)
        ordered = jnp.take(normed, row_order, axis=1).reshape(
            project_count, owners, unit_rows, local_width
        )
        term = jnp.einsum(
            "sojd,dhg->ohsjg", ordered, weight_grouped, preferred_element_type=jnp.float32
        )
        term = term.reshape(owners * KVH * project_count * unit_rows, GW)
        mine = lax.psum_scatter(term, "tensor", scatter_dimension=0, tiled=True)
        joined_block = mine.astype(jnp.bfloat16).reshape(project_count, unit_rows, GW)
        prepare_count = joined_block.shape[0]
        steps_here = step + jnp.arange(prepare_count, dtype=jnp.int32)
        position = row_length[None, :] + QR * steps_here[:, None] + row_step[None, :]
        prepare_queries = rotate(
            joined_block[..., : GQ * HD]
            .reshape(prepare_count, unit_rows, GQ, HD)
            .astype(jnp.float32),
            position[:, :, None],
        ).astype(jnp.bfloat16)
        keys = rotate(
            joined_block[..., GQ * HD : GQ * HD + HD].astype(jnp.float32), position
        ).astype(jnp.bfloat16)
        queries, keys, values = (prepare_queries, keys, joined_block[..., GQ * HD + HD :])
        keys_seen.append(keys)
        values_seen.append(values)
        keys_all = jnp.concatenate(keys_seen, 0)
        attend_count = queries.shape[0]
        cache_best, cache_total, cache_summed = cache_partial(
            queries,
            cache_data[:, :HD],
            cache_data[:, HD:],
            token_scale[:, 0],
            token_scale[:, 1],
            cache_mask,
        )
        news = jnp.einsum(
            "srgd,pjd->srgpj", queries, keys_all, preferred_element_type=jnp.float32
        ) * HD ** (-0.5)
        query_step = step + jnp.arange(attend_count, dtype=jnp.int32)[:, None, None, None]
        key_step = jnp.arange(keys_all.shape[0], dtype=jnp.int32)[None, None, :, None]
        allowed = (key_step < query_step) | (key_step == query_step) & (
            row_step[None, None, None, :] <= row_step[None, :, None, None]
        )
        allowed = (allowed & same_request[None, :, None, :])[:, :, None, :, :]
        news = jnp.where(allowed, news, NEG_FILL)
        best = jnp.maximum(cache_best, jnp.max(news, (3, 4)))
        factor = jnp.exp(cache_best - best)
        expo = jnp.where(allowed, jnp.exp(news - best[..., None, None]), 0.0)
        total = cache_total * factor + jnp.sum(expo, (3, 4))
        summed = cache_summed * factor[..., None] + jnp.einsum(
            "srgpj,pjd->srgd",
            expo.astype(jnp.bfloat16),
            jnp.concatenate(values_seen, 0),
            preferred_element_type=jnp.float32,
        )
        attention = (
            (summed / total[..., None])
            .astype(jnp.bfloat16)
            .reshape(attend_count, unit_rows, GQ * HD)
        )
        count = attention.shape[0]
        gathered = lax.all_gather(attention, "tensor", axis=2, tiled=True).reshape(
            count, unit_rows, owners, QH * HD
        )
        mixed = jnp.einsum(
            "sjof,fd->sojd", gathered, out_weight, preferred_element_type=jnp.float32
        )
        mixed = jnp.take(mixed.reshape(count, owners * unit_rows, local_width), inverse, axis=1)
        outputs.append(
            (hidden_in[step : step + count].astype(jnp.float32) + mixed).astype(jnp.bfloat16)
        )
    return jnp.concatenate(outputs, 0)


VMEM_LIMIT = 48 * 1024 * 1024
LOW_BITS = 4
PACKED = 16 // LOW_BITS
LEVELS = 32600.0 * 2**LOW_BITS
POWER_STEPS = 8.0
TILE = 16
MESH_BITS = (1, 2, 4, 8)


def swap(value, bit):
    devices = lax.axis_size("tensor")
    return lax.ppermute(value, "tensor", [(i, i ^ bit) for i in range(devices)])


def coded_rows(rows):
    return rows + rows // PACKED


def encode(block):
    top = jnp.max(jnp.abs(block), 0, keepdims=True)
    power = jnp.ceil(jnp.log2(jnp.maximum(top, 1e-30)) * POWER_STEPS)
    codes = jnp.round(block * (jnp.exp2(power * (-1.0 / POWER_STEPS)) * LEVELS)).astype(jnp.int32)
    low = codes & (2**LOW_BITS - 1)
    part = block.shape[0] // PACKED
    packed = low[:part]
    for i in range(1, PACKED):
        packed = packed + (low[i * part : (i + 1) * part] << (LOW_BITS * i))
    high = (codes >> LOW_BITS).astype(jnp.int16)
    return jnp.concatenate([high, (packed - 32768).astype(jnp.int16)], 0), power


def decode(codes, power):
    rows = codes.shape[0] * PACKED // (PACKED + 1)
    high = codes[:rows].astype(jnp.int32) << LOW_BITS
    packed = codes[rows:].astype(jnp.int32) + 32768
    low = jnp.concatenate(
        [(packed >> (LOW_BITS * i)) & (2**LOW_BITS - 1) for i in range(PACKED)], 0
    )
    scale = jnp.exp2(power * (1.0 / POWER_STEPS)) * (1.0 / LEVELS)
    return (high + low).astype(jnp.float32) * scale


def pick_row(rows, index):
    ids = lax.broadcasted_iota(jnp.int32, rows.shape, 0)
    return jnp.sum(jnp.where(ids == index, rows, 0.0), 0, keepdims=True)


def store_codes(sent, powers, block, index, steps):
    rows = coded_rows(block.shape[0])
    codes, power = encode(block)
    sent[pl.ds(pl.multiple_of(index * rows, TILE), rows), :] = codes

    @pl.when(index == 0)
    def _():
        powers[...] = jnp.zeros_like(powers)

    powers[pl.ds(index, 1), :] = power

    @pl.when(index == steps - 1)
    def _():
        sent[pl.ds(steps * rows, TILE), :] = powers[...].astype(jnp.int32).astype(jnp.int16)


K_PARTS = 4


def project_kernel(core, normed, *refs):
    weights = refs[:-4]
    kept, sent, powers = refs[-3:]
    half = len(weights) // 2
    depth = normed.shape[1] // K_PARTS
    index = pl.program_id(0)

    def product(blocks):
        wide = []
        for first in range(0, len(blocks), K_PARTS):
            total = None
            for part in range(K_PARTS):
                term = jnp.dot(
                    normed[:, part * depth : (part + 1) * depth],
                    blocks[first + part][...],
                    preferred_element_type=jnp.float32,
                )
                total = term if total is None else total + term
            wide.append(total)
        return wide[0] if len(wide) == 1 else jnp.concatenate(wide, 1)

    store_codes(sent, powers, product(weights[half:]), index, KVH)
    kept[0] = product(weights[:half])


def project(core, normed, qkv_weight, chunk, with_pair, after):
    rows, width = normed.shape
    columns = 2 * HD + (HD if with_pair else 0)
    per_group = GW // (2 * HD)
    depth = width // K_PARTS

    def wide(other, part):
        def place(t, c):
            mine = c[0] if not other else 1 - c[0]
            return (part, t * per_group + mine * (GQ // 4) + chunk)

        return pl.BlockSpec((depth, 2 * HD), place)

    def narrow(other, part):
        def place(t, c):
            mine = c[0] if not other else 1 - c[0]
            return (part, t * (GW // HD) + GQ + mine)

        return pl.BlockSpec((depth, HD), place)

    specs = []
    for other in (False, True):
        specs += [wide(other, part) for part in range(K_PARTS)]
        if with_pair:
            specs += [narrow(other, part) for part in range(K_PARTS)]
    sent_rows = KVH * coded_rows(rows) + TILE
    return pl.pallas_call(
        project_kernel,
        grid_spec=pltpu.PrefetchScalarGridSpec(
            num_scalar_prefetch=1,
            grid=(KVH,),
            in_specs=[pl.BlockSpec((rows, width), lambda t, c: (0, 0))]
            + specs
            + [pl.BlockSpec(memory_space=pl.ANY)],
            out_specs=[
                pl.BlockSpec((1, rows, columns), lambda t, c: (t, 0, 0)),
                pl.BlockSpec((sent_rows, columns), lambda t, c: (0, 0)),
            ],
            scratch_shapes=[pltpu.VMEM((TILE, columns), jnp.float32)],
        ),
        out_shape=[
            jax.ShapeDtypeStruct((KVH, rows, columns), jnp.float32),
            jax.ShapeDtypeStruct((sent_rows, columns), jnp.int16),
        ],
        compiler_params=pltpu.CompilerParams(vmem_limit_bytes=VMEM_LIMIT),
        cost_estimate=pl.CostEstimate(
            flops=2 * rows * width * columns * 2 * KVH,
            bytes_accessed=width * columns * 4 * KVH + rows * columns * 6 * KVH,
            transcendentals=0,
        ),
        name="project",
    )(core, normed, *([qkv_weight] * len(specs)), after)


def fold_kernel(steps, bit, held, landed, landed_powers, kept, sent, powers):
    index = pl.program_id(0)
    rows = coded_rows(held.shape[1])
    rows_of_powers = landed_powers[...].astype(jnp.int32).astype(jnp.float32)

    def total(side):
        place = pl.multiple_of(side * rows, TILE)
        codes = landed[pl.ds(place, rows), :]
        return held[side] + decode(codes, pick_row(rows_of_powers, 2 * index + side))

    mine = bit[0]
    store_codes(sent, powers, total(1 - mine), index, steps)
    kept[0] = total(mine)


def fold(bit, held, landed):
    blocks, rows, columns = held.shape
    steps = blocks // 2
    coded = coded_rows(rows)
    return pl.pallas_call(
        lambda *refs: fold_kernel(steps, *refs),
        grid_spec=pltpu.PrefetchScalarGridSpec(
            num_scalar_prefetch=1,
            grid=(steps,),
            in_specs=[
                pl.BlockSpec((2, rows, columns), lambda i, b: (i, 0, 0)),
                pl.BlockSpec((2 * coded, columns), lambda i, b: (i, 0)),
                pl.BlockSpec((TILE, columns), lambda i, b: (blocks * coded // TILE, 0)),
            ],
            out_specs=[
                pl.BlockSpec((1, rows, columns), lambda i, b: (i, 0, 0)),
                pl.BlockSpec((steps * coded + TILE, columns), lambda i, b: (0, 0)),
            ],
            scratch_shapes=[pltpu.VMEM((TILE, columns), jnp.float32)],
        ),
        out_shape=[
            jax.ShapeDtypeStruct((steps, rows, columns), jnp.float32),
            jax.ShapeDtypeStruct((steps * coded + TILE, columns), jnp.int16),
        ],
        compiler_params=pltpu.CompilerParams(vmem_limit_bytes=VMEM_LIMIT),
        cost_estimate=pl.CostEstimate(
            flops=20 * blocks * rows * columns,
            bytes_accessed=blocks * rows * columns * 9,
            transcendentals=0,
        ),
        name="fold",
    )(bit, held, landed, landed)


def finish_kernel(core, held, landed, cosine, sine, after, queries, *pair):
    rows = held.shape[1]
    coded = coded_rows(rows)
    power = landed[pl.ds(coded, TILE), :].astype(jnp.int32).astype(jnp.float32)[0:1]
    total = held[0] + decode(landed[pl.ds(0, coded), :], power)
    joined = total.astype(jnp.bfloat16)
    parts = []
    for head in range(joined.shape[1] // HD):
        raw = joined[:, head * HD : (head + 1) * HD]
        wide = raw.astype(jnp.float32)
        turned = wide * cosine[...] + pltpu.roll(wide, HD // 2, 1) * sine[...]
        parts.append((raw, turned.astype(jnp.bfloat16)))
    queries[...] = jnp.concatenate([parts[0][1], parts[1][1]], 1)
    if pair:
        raw, turned = parts[2]
        pair[0][...] = jnp.where(core[0] == 0, turned.astype(jnp.float32), raw.astype(jnp.float32)).astype(
            jnp.bfloat16
        )


def finish(core, held, landed, cosine, sine, after):
    _, rows, columns = held.shape
    whole = pl.BlockSpec(memory_space=pltpu.VMEM)
    shapes = [jax.ShapeDtypeStruct((rows, 2 * HD), jnp.bfloat16)]
    if columns > 2 * HD:
        shapes.append(jax.ShapeDtypeStruct((rows, HD), jnp.bfloat16))
    return pl.pallas_call(
        finish_kernel,
        in_specs=[pl.BlockSpec(memory_space=pltpu.SMEM)]
        + [whole] * 4
        + [pl.BlockSpec(memory_space=pl.ANY)],
        out_specs=[whole] * len(shapes),
        out_shape=shapes,
        compiler_params=pltpu.CompilerParams(vmem_limit_bytes=VMEM_LIMIT),
        name="finish",
    )(core, held, landed, cosine, sine, after)


def mix_kernel(places, *refs):
    pieces, weights, start, mixed = refs[0:2], refs[2], refs[3], refs[4]
    total = refs[5]
    step = pl.program_id(0)
    depth = weights.shape[0]
    per_piece = pieces[0].shape[1] // depth

    @pl.when(step == 0)
    def _():
        total[...] = start[...].astype(jnp.float32)

    for part in range(2 * per_piece):

        @pl.when(step == part)
        def _():
            first = part % per_piece * depth
            total[...] += jnp.dot(
                pieces[part // per_piece][:, first : first + depth],
                weights[...],
                preferred_element_type=jnp.float32,
            )

    @pl.when(step == 2 * per_piece - 1)
    def _():
        mixed[...] = total[...].astype(mixed.dtype)


def mix(places, pieces, out_weight, start, dtype):
    rows, width = pieces[0].shape
    columns = out_weight.shape[1]
    depth = width // 2
    whole = pl.BlockSpec((rows, width), lambda i, p: (0, 0))
    return pl.pallas_call(
        mix_kernel,
        grid_spec=pltpu.PrefetchScalarGridSpec(
            num_scalar_prefetch=1,
            grid=(4,),
            in_specs=[
                whole,
                whole,
                pl.BlockSpec((depth, columns), lambda i, p: (p[i // 2] * 2 + i % 2, 0)),
                pl.BlockSpec((rows, columns), lambda i, p: (0, 0)),
            ],
            out_specs=pl.BlockSpec((rows, columns), lambda i, p: (0, 0)),
            scratch_shapes=[pltpu.VMEM((rows, columns), jnp.float32)],
        ),
        out_shape=jax.ShapeDtypeStruct((rows, columns), dtype),
        compiler_params=pltpu.CompilerParams(vmem_limit_bytes=VMEM_LIMIT),
        cost_estimate=pl.CostEstimate(
            flops=4 * rows * width * columns,
            bytes_accessed=4 * width * columns + rows * (4 * width + 8 * columns),
            transcendentals=0,
        ),
        name="mix",
    )(places, *pieces, out_weight, start)


def along(value, pairs):
    devices = lax.axis_size("tensor")
    side = devices // 4
    table = [
        (source * side + i, target * side + i) for source, target in pairs for i in range(side)
    ]
    return lax.ppermute(value, "tensor", table)


def gather_and_mix(attention, out_weight, start, device):
    line = device // 4
    inner = (line == 1) | (line == 2)
    near = swap(attention, 4)
    cross = along(attention, [(1, 2), (2, 1)])
    pieces = {0: attention, 1: near}
    across = {0: swap(attention, 2)}
    passed = along(cross, [(1, 0), (2, 3)])
    cross_near = along(near, [(1, 2), (2, 1)])
    across[1] = swap(near, 2)
    pieces[2] = jnp.where(inner, cross_near, passed)
    last = along(cross_near, [(1, 0), (2, 3)])
    across[2] = swap(pieces[2], 2)
    pieces[3] = jnp.where(inner, cross, last)
    across[3] = swap(pieces[3], 2)
    mixed = start
    order = [(0, 0), (1, 0), (0, 2), (1, 2), (2, 0), (2, 2), (3, 0), (3, 2)]
    for number, (k, y) in enumerate(order):
        piece = (across if y else pieces)[k]
        owner = device ^ (4 * k + y)
        places = jnp.stack([owner, owner ^ 1])
        dtype = jnp.bfloat16 if number == len(order) - 1 else jnp.float32
        mixed = mix(places, [piece, swap(piece, 1)], out_weight, mixed, dtype)
    return mixed


def attend_kernel(
    slot_request,
    queries,
    new_keys,
    new_values,
    own,
    other,
    key_scale,
    value_scale,
    cache_bias,
    new_bias,
    attention,
    slot_best,
    slot_total,
    slot_sum,
    best,
    total,
    summed,
):
    slots = slot_best.shape[0]
    requests, count, _ = queries.shape
    transposed = (((1,), (1,)), ((), ()))
    for request in range(requests):
        scores = (
            lax.dot_general(
                queries[request],
                new_keys[request],
                transposed,
                preferred_element_type=jnp.float32,
            )
            * HD ** (-0.5)
            + new_bias[...]
        )
        top = jnp.max(scores, -1, keepdims=True)
        expo = jnp.exp(scores - top)
        best[request] = jnp.broadcast_to(top, (count, HD))
        total[request] = jnp.broadcast_to(jnp.sum(expo, -1, keepdims=True), (count, HD))
        summed[request] = jnp.dot(
            expo.astype(jnp.bfloat16), new_values[request], preferred_element_type=jnp.float32
        )
    for slot in range(slots):
        request = slot_request[slot]
        query = queries[request]
        raw = [
            part[:, slot * BLK : (slot + 1) * BLK, :].reshape(KVH * BLK, 2 * HD)
            for part in (own, other)
        ]
        scores = jnp.concatenate(
            [
                lax.dot_general(
                    query, kv[:, :HD], transposed, preferred_element_type=jnp.float32
                )
                for kv in raw
            ],
            1,
        )
        scores = scores * key_scale[slot : slot + 1, :] + cache_bias[slot : slot + 1, :]
        top = jnp.max(scores, -1, keepdims=True)
        expo = jnp.exp(scores - top)
        weights = (expo * value_scale[slot : slot + 1, :]).astype(jnp.bfloat16)
        slot_best[slot] = jnp.broadcast_to(top, (count, HD))
        slot_total[slot] = jnp.broadcast_to(jnp.sum(expo, -1, keepdims=True), (count, HD))
        values = jnp.concatenate([kv[:, HD:] for kv in raw], 0)
        slot_sum[slot] = jnp.dot(weights, values, preferred_element_type=jnp.float32)
    for slot in range(slots):
        request = slot_request[slot]
        before = best[request]
        here = slot_best[slot]
        top = jnp.maximum(before, here)
        keep = jnp.exp(before - top)
        add = jnp.exp(here - top)
        best[request] = top
        total[request] = total[request] * keep + slot_total[slot] * add
        summed[request] = summed[request] * keep + slot_sum[slot] * add
    for request in range(requests):
        attention[request] = (summed[request] / total[request]).astype(jnp.bfloat16)


def attend(slot_request, *arrays):
    queries = arrays[0]
    slots = arrays[5].shape[0]
    requests, count, _ = queries.shape
    whole = pl.BlockSpec(memory_space=pltpu.VMEM)
    return pl.pallas_call(
        attend_kernel,
        in_specs=[pl.BlockSpec(memory_space=pltpu.SMEM)] + [whole] * len(arrays),
        out_specs=whole,
        out_shape=jax.ShapeDtypeStruct((requests, count, HD), jnp.bfloat16),
        scratch_shapes=[pltpu.VMEM((slots, count, HD), jnp.float32)] * 3
        + [pltpu.VMEM((requests, count, HD), jnp.float32)] * 3,
        compiler_params=pltpu.CompilerParams(vmem_limit_bytes=VMEM_LIMIT),
        cost_estimate=pl.CostEstimate(
            flops=4 * slots * count * 2 * KVH * BLK * HD,
            bytes_accessed=2 * slots * 2 * KVH * BLK * 2 * HD,
            transcendentals=slots * count * 2 * KVH * BLK,
        ),
        name="attend",
    )(slot_request, *arrays)


def slot_layout(request_length, block_table, slots, stripe):
    requests, most = block_table.shape
    stripes = (request_length + stripe - 1) // stripe
    columns = jnp.arange(most, dtype=jnp.int32)
    held = columns[None, :] < stripes[:, None]
    hit = held[:, :, None] & (
        block_table[:, :, None] == jnp.arange(slots, dtype=jnp.int32)[None, None, :]
    )
    hit = hit.astype(jnp.int32)
    order = jnp.arange(requests, dtype=jnp.int32)
    request = jnp.sum(hit * order[:, None, None], (0, 1))
    rank = jnp.sum(hit * columns[None, :, None], (0, 1))
    length = jnp.sum(hit * request_length[:, None, None], (0, 1))
    return request, rank, length


def handover(cache_pool, cache_scale, chip):
    slots = cache_pool.shape[0]
    scales = jnp.pad(
        jnp.transpose(cache_scale, (1, 2, 0)).reshape(KVH, 1, 2 * slots),
        ((0, 0), (0, TILE - 1), (0, 2 * HD - 2 * slots)),
    )
    landed = []
    for k in range(KVH):
        head = chip ^ k
        blocks = lax.dynamic_index_in_dim(cache_pool, head, 1, keepdims=False)
        rows = jnp.concatenate(
            [
                blocks.reshape(slots * BLK, 2 * HD),
                lax.dynamic_index_in_dim(scales, head, 0, keepdims=False),
            ],
            0,
        )
        landed.append(swap(rows, 2 * k) if k else rows)
    own = jnp.stack(landed)
    return own, swap(own, 1)


def local_pairs(
    hidden_in,
    norm_gain,
    qkv_weight,
    out_weight,
    cache_pool,
    cache_scale,
    request_length,
    block_table,
):
    devices = lax.axis_size("tensor")
    device = lax.axis_index("tensor")
    core = device % 2
    chip = device // 2
    stripe = devices * BLK
    slots = cache_pool.shape[0]
    requests = request_length.shape[0]
    rows = STEPS * requests * QR
    width = hidden_in.shape[2]
    heads = GQ // 2

    hidden = hidden_in.astype(jnp.float32)
    sums = jnp.sum(hidden * hidden, -1)
    for bit in MESH_BITS:
        sums = sums + swap(sums, bit)
    normed = (
        hidden * lax.rsqrt(sums[..., None] / D + EPSILON) * norm_gain.astype(jnp.float32)
    ).astype(jnp.bfloat16)
    normed = normed.reshape(rows, width)

    pool, sums = lax.optimization_barrier((cache_pool, sums))
    own, other = handover(pool, cache_scale, chip)

    step_ids = jnp.arange(STEPS, dtype=jnp.int32)
    row_ids = jnp.arange(QR, dtype=jnp.int32)
    position = (
        request_length[None, :, None] + QR * step_ids[:, None, None] + row_ids[None, None, :]
    )
    freqs = ROPE_BASE ** (-(jnp.arange(HD // 2, dtype=jnp.float32) * 2.0 / HD))
    angles = position.reshape(rows, 1).astype(jnp.float32) * freqs
    cosine = jnp.concatenate([jnp.cos(angles)] * 2, 1)
    sine = jnp.concatenate([-jnp.sin(angles), jnp.sin(angles)], 1)

    bits = [jnp.reshape((device >> b) & 1, (1,)).astype(jnp.int32) for b in range(4)]
    count = GQ // 4
    held, sent = [None] * count, [None] * count

    def folded(chunk, b):
        held[chunk], sent[chunk] = fold(bits[b], held[chunk], swap(sent[chunk], MESH_BITS[b - 1]))

    for chunk in range(count):
        after = held[chunk - 2] if chunk >= 2 else normed
        held[chunk], sent[chunk] = project(
            bits[0], normed, qkv_weight, chunk, chunk == 0, after
        )
        if chunk >= 1:
            folded(chunk - 1, 1)
    folded(count - 1, 1)
    query_chunks = []
    after = normed
    for chunk in range(count):
        folded(chunk, 2)
        folded(chunk, 3)
        done = finish(bits[0], held[chunk], swap(sent[chunk], MESH_BITS[3]), cosine, sine, after)
        query_chunks.append(done[0])
        if chunk == 0:
            pair = done[1]
            pair_other = swap(pair, 1)
            after = pair_other
    keys = jnp.where(core == 0, pair, pair_other)
    raw_values = jnp.where(core == 0, pair_other, pair)
    queries = jnp.concatenate(query_chunks, 1).reshape(STEPS, requests, QR, heads, HD)
    queries = jnp.transpose(queries, (1, 0, 2, 3, 4)).reshape(requests, STEPS * QR * heads, HD)

    def by_request(value):
        value = jnp.transpose(value.reshape(STEPS, requests, QR, HD), (1, 0, 2, 3))
        value = value.reshape(requests, STEPS * QR, HD)
        return jnp.pad(value, ((0, 0), (0, TILE - STEPS * QR), (0, 0)))

    slot_request, slot_rank, slot_length = slot_layout(request_length, block_table, slots, stripe)
    source = chip ^ jnp.arange(KVH, dtype=jnp.int32)
    sources = jnp.stack([source * 2 + core, source * 2 + 1 - core])
    offset = sources[:, :, None] * BLK + jnp.arange(BLK, dtype=jnp.int32)[None, None, :]
    token = slot_rank[:, None] * stripe + offset.reshape(1, stripe)
    cache_bias = jnp.where(token < slot_length[:, None], 0.0, NEG_FILL).astype(jnp.float32)
    scales = jnp.stack([own[:, slots * BLK, : 2 * slots], other[:, slots * BLK, : 2 * slots]])
    scales = scales.astype(jnp.float32).reshape(2 * KVH, 2, slots)
    scales = jnp.repeat(jnp.transpose(scales, (1, 2, 0)), BLK, axis=2)
    order = jnp.arange(STEPS * QR * heads, dtype=jnp.int32) // heads
    key_order = jnp.arange(TILE, dtype=jnp.int32)
    new_bias = jnp.where(key_order[None, :] <= order[:, None], 0.0, NEG_FILL).astype(jnp.float32)
    attention = attend(
        slot_request,
        queries,
        by_request(keys),
        by_request(raw_values),
        own,
        other,
        scales[0] * HD ** (-0.5),
        scales[1],
        cache_bias,
        new_bias,
    )
    attention = jnp.transpose(
        attention.reshape(requests, STEPS, QR, heads, HD), (1, 0, 2, 3, 4)
    ).reshape(rows, heads * HD)
    mixed = gather_and_mix(attention, out_weight, hidden_in.reshape(rows, width), device)
    return mixed.reshape(hidden_in.shape)


def solution(mesh):
    return jax.shard_map(
        local_pairs if mesh.shape["tensor"] == 2 * KVH else local_general,
        mesh=mesh,
        in_specs=(
            P(None, "groups", "tensor"),
            P("tensor"),
            P("tensor", None),
            P(None, "tensor"),
            P(("groups", "tensor"), None, None, None),
            P(("groups", "tensor"), None, None),
            P("groups"),
            P("groups", None),
        ),
        out_specs=P(None, "groups", "tensor"),
        check_vma=False,
    )
```

```python
import functools

import jax
import jax.numpy as jnp
from jax import lax
from jax.experimental import pallas as pl
from jax.experimental.pallas import tpu as pltpu
from jax.sharding import PartitionSpec as P

D = 16384
QH = 128
KVH = 8
HD = 128
QR = 6
STEPS = 2
BLK = 16
GQ = 16
GW = 2304


EPSILON = 1e-05
ROPE_BASE = 500000.0
NEG_FILL = -1e30


def rotate(values, positions):
    half = values.shape[-1] // 2
    freqs = ROPE_BASE ** (-(jnp.arange(half, dtype=jnp.float32) * 2.0 / values.shape[-1]))
    angles = positions.astype(jnp.float32)[..., None] * freqs
    cosine = jnp.cos(angles)
    sine = jnp.sin(angles)
    first = values[..., :half]
    second = values[..., half:]
    return jnp.concatenate([first * cosine - second * sine, second * cosine + first * sine], -1)


def request_layout(request_owner, request_length, block_table, owners, stripe):
    requests = request_owner.shape[0]
    most = block_table.shape[1]
    order = jnp.arange(requests, dtype=jnp.int32)
    stripes = (request_length + stripe - 1) // stripe
    before = (
        (request_owner[None, :] == request_owner[:, None]) & (order[None, :] < order[:, None])
    ).astype(jnp.int32)
    rank = jnp.sum(before, 1)
    offset = jnp.sum(before * stripes[None, :], 1)
    owner_ids = jnp.arange(owners, dtype=jnp.int32)
    mine = request_owner[None, :] == owner_ids[:, None]
    member = mine[:, :, None] & (
        rank[None, :, None] == jnp.arange(requests // owners, dtype=jnp.int32)[None, None, :]
    )
    owner_requests = jnp.sum(member.astype(jnp.int32) * order[None, :, None], 1)
    columns = jnp.arange(most, dtype=jnp.int32)
    within = columns[None, None, :] - offset[None, :, None]
    hit = (mine[:, :, None] & (within >= 0) & (within < stripes[None, :, None])).astype(jnp.int32)
    stripe_request = jnp.sum(hit * order[None, :, None], 1) - (1 - jnp.sum(hit, 1))
    stripe_rank = jnp.sum(hit * within, 1)
    pick = (within[..., None] == columns[None, None, None, :]).astype(jnp.int32)
    slots = jnp.sum(hit[..., None] * pick * block_table[None, :, None, :], (1, 3))
    return (owner_requests, stripe_request, stripe_rank, slots, rank, stripes)


def cache_partial(queries, keys, values, key_scale, value_scale, mask):
    scores = jnp.einsum("srgd,td->srgt", queries, keys, preferred_element_type=jnp.float32)
    scores = jnp.where(mask, scores * key_scale * HD ** (-0.5), NEG_FILL)
    best = jnp.max(scores, -1)
    expo = jnp.where(mask, jnp.exp(scores - best[..., None]), 0.0)
    total = jnp.sum(expo, -1)
    weights = (expo * value_scale).astype(jnp.bfloat16)
    summed = jnp.einsum("srgt,td->srgd", weights, values, preferred_element_type=jnp.float32)
    return (best, total, summed)


def local_general(
    hidden_in,
    norm_gain,
    qkv_weight,
    out_weight,
    cache_pool,
    cache_scale,
    request_length,
    block_table,
):
    devices = lax.axis_size("tensor")
    device = lax.axis_index("tensor")
    owners = devices // KVH
    stripe = devices * BLK
    requests = request_length.shape[0]
    request_owner = jnp.arange(requests, dtype=jnp.int32) % owners
    unit_rows = requests // owners * QR
    most = block_table.shape[1]
    local_width = hidden_in.shape[2]
    my_owner = device // KVH
    owner_requests, stripe_request, stripe_rank, slots, rank, stripes = request_layout(
        request_owner, request_length, block_table, owners, stripe
    )
    step_rows = jnp.arange(QR, dtype=jnp.int32)
    row_order = (owner_requests[:, :, None] * QR + step_rows[None, None, :]).reshape(
        owners * unit_rows
    )
    inverse = ((request_owner * unit_rows + rank * QR)[:, None] + step_rows[None, :]).reshape(
        requests * QR
    )
    row_request = jnp.repeat(owner_requests[my_owner], QR)
    row_length = request_length[row_request]
    row_step = jnp.arange(unit_rows, dtype=jnp.int32) % QR
    same_request = row_request[:, None] == row_request[None, :]
    gain = norm_gain.astype(jnp.float32)
    weight_grouped = qkv_weight.reshape(local_width, KVH, GW)
    sent = cache_pool[jnp.transpose(slots)].reshape(most, devices, BLK, 2 * HD)
    sent_scale = cache_scale[jnp.transpose(slots)].reshape(most, devices, 2)
    landed, landed_scale = (
        lax.all_to_all(sent, "tensor", split_axis=1, concat_axis=1, tiled=True),
        lax.all_to_all(sent_scale, "tensor", split_axis=1, concat_axis=1, tiled=True),
    )
    cache_data = landed.reshape(most * stripe, 2 * HD)
    token_scale = jnp.broadcast_to(
        landed_scale.astype(jnp.float32)[:, :, None, :], (most, devices, BLK, 2)
    ).reshape(most * stripe, 2)
    token = jnp.arange(most * stripe, dtype=jnp.int32)
    token_stripe = token // stripe
    token_request = stripe_request[my_owner][token_stripe]
    token_position = stripe_rank[my_owner][token_stripe] * stripe + token % stripe
    token_length = jnp.where(token_request >= 0, request_length[jnp.maximum(token_request, 0)], 0)
    cache_mask = (
        (token_request[None, :] == row_request[:, None]) & (token_position < token_length)[None, :]
    )[None, :, None, :]
    outputs = []
    keys_seen = []
    values_seen = []
    for step in range(STEPS):
        block = hidden_in[step : step + 1]
        project_count = block.shape[0]
        values = block.astype(jnp.float32)
        sums = lax.psum(jnp.sum(values * values, -1), "tensor")
        normed = (values * lax.rsqrt(sums[..., None] / D + EPSILON) * gain).astype(jnp.bfloat16)
        ordered = jnp.take(normed, row_order, axis=1).reshape(
            project_count, owners, unit_rows, local_width
        )
        term = jnp.einsum(
            "sojd,dhg->ohsjg", ordered, weight_grouped, preferred_element_type=jnp.float32
        )
        term = term.reshape(owners * KVH * project_count * unit_rows, GW)
        mine = lax.psum_scatter(term, "tensor", scatter_dimension=0, tiled=True)
        joined_block = mine.astype(jnp.bfloat16).reshape(project_count, unit_rows, GW)
        prepare_count = joined_block.shape[0]
        steps_here = step + jnp.arange(prepare_count, dtype=jnp.int32)
        position = row_length[None, :] + QR * steps_here[:, None] + row_step[None, :]
        prepare_queries = rotate(
            joined_block[..., : GQ * HD]
            .reshape(prepare_count, unit_rows, GQ, HD)
            .astype(jnp.float32),
            position[:, :, None],
        ).astype(jnp.bfloat16)
        keys = rotate(
            joined_block[..., GQ * HD : GQ * HD + HD].astype(jnp.float32), position
        ).astype(jnp.bfloat16)
        queries, keys, values = (prepare_queries, keys, joined_block[..., GQ * HD + HD :])
        keys_seen.append(keys)
        values_seen.append(values)
        keys_all = jnp.concatenate(keys_seen, 0)
        attend_count = queries.shape[0]
        cache_best, cache_total, cache_summed = cache_partial(
            queries,
            cache_data[:, :HD],
            cache_data[:, HD:],
            token_scale[:, 0],
            token_scale[:, 1],
            cache_mask,
        )
        news = jnp.einsum(
            "srgd,pjd->srgpj", queries, keys_all, preferred_element_type=jnp.float32
        ) * HD ** (-0.5)
        query_step = step + jnp.arange(attend_count, dtype=jnp.int32)[:, None, None, None]
        key_step = jnp.arange(keys_all.shape[0], dtype=jnp.int32)[None, None, :, None]
        allowed = (key_step < query_step) | (key_step == query_step) & (
            row_step[None, None, None, :] <= row_step[None, :, None, None]
        )
        allowed = (allowed & same_request[None, :, None, :])[:, :, None, :, :]
        news = jnp.where(allowed, news, NEG_FILL)
        best = jnp.maximum(cache_best, jnp.max(news, (3, 4)))
        factor = jnp.exp(cache_best - best)
        expo = jnp.where(allowed, jnp.exp(news - best[..., None, None]), 0.0)
        total = cache_total * factor + jnp.sum(expo, (3, 4))
        summed = cache_summed * factor[..., None] + jnp.einsum(
            "srgpj,pjd->srgd",
            expo.astype(jnp.bfloat16),
            jnp.concatenate(values_seen, 0),
            preferred_element_type=jnp.float32,
        )
        attention = (
            (summed / total[..., None])
            .astype(jnp.bfloat16)
            .reshape(attend_count, unit_rows, GQ * HD)
        )
        count = attention.shape[0]
        gathered = lax.all_gather(attention, "tensor", axis=2, tiled=True).reshape(
            count, unit_rows, owners, QH * HD
        )
        mixed = jnp.einsum(
            "sjof,fd->sojd", gathered, out_weight, preferred_element_type=jnp.float32
        )
        mixed = jnp.take(mixed.reshape(count, owners * unit_rows, local_width), inverse, axis=1)
        outputs.append(
            (hidden_in[step : step + count].astype(jnp.float32) + mixed).astype(jnp.bfloat16)
        )
    return jnp.concatenate(outputs, 0)


VMEM_LIMIT = 48 * 1024 * 1024
SHORT = pl.CostEstimate(flops=1, bytes_accessed=1, transcendentals=0)
LOW_BITS = 4
PACKED = 16 // LOW_BITS
LEVELS = 32600.0 * 2**LOW_BITS
POWER_STEPS = 8.0
TILE = 16
MESH_BITS = (1, 2, 4, 8)


def swap(value, bit):
    devices = lax.axis_size("tensor")
    return lax.ppermute(value, "tensor", [(i, i ^ bit) for i in range(devices)])


def coded_rows(rows):
    return rows + rows // PACKED


def encode(block):
    top = jnp.max(jnp.abs(block), 0, keepdims=True)
    power = jnp.ceil(jnp.log2(jnp.maximum(top, 1e-30)) * POWER_STEPS)
    codes = jnp.round(block * (jnp.exp2(power * (-1.0 / POWER_STEPS)) * LEVELS)).astype(jnp.int32)
    low = codes & (2**LOW_BITS - 1)
    part = block.shape[0] // PACKED
    packed = low[:part]
    for i in range(1, PACKED):
        packed = packed + (low[i * part : (i + 1) * part] << (LOW_BITS * i))
    high = (codes >> LOW_BITS).astype(jnp.int16)
    return jnp.concatenate([high, (packed - 32768).astype(jnp.int16)], 0), power


def decode(codes, power):
    rows = codes.shape[0] * PACKED // (PACKED + 1)
    high = codes[:rows].astype(jnp.int32) << LOW_BITS
    packed = codes[rows:].astype(jnp.int32) + 32768
    low = jnp.concatenate(
        [(packed >> (LOW_BITS * i)) & (2**LOW_BITS - 1) for i in range(PACKED)], 0
    )
    scale = jnp.exp2(power * (1.0 / POWER_STEPS)) * (1.0 / LEVELS)
    return (high + low).astype(jnp.float32) * scale


def pick_row(rows, index):
    ids = lax.broadcasted_iota(jnp.int32, rows.shape, 0)
    return jnp.sum(jnp.where(ids == index, rows, 0.0), 0, keepdims=True)


def store_codes(sent, powers, block, index, steps):
    rows = coded_rows(block.shape[0])
    codes, power = encode(block)
    sent[pl.ds(pl.multiple_of(index * rows, TILE), rows), :] = codes

    @pl.when(index == 0)
    def _():
        powers[...] = jnp.zeros_like(powers)

    powers[pl.ds(index, 1), :] = power

    @pl.when(index == steps - 1)
    def _():
        sent[pl.ds(steps * rows, TILE), :] = powers[...].astype(jnp.int32).astype(jnp.int16)


def project_kernel(chunk, with_pair, core, normed, weights, *refs):
    kept, sent, powers, wide, arrived = refs[-5:]
    index = pl.program_id(0)

    def copies(group):
        found = []
        for side in range(2):
            owner = core[0] if side == 0 else 1 - core[0]
            first = group * GW + owner * (GQ // 2 * HD) + chunk * (2 * HD)
            spans = [(first, 0, 2 * HD)]
            if with_pair:
                spans.append((group * GW + (GQ + owner) * HD, 2 * HD, HD))
            for number, (start, offset, size) in enumerate(spans):
                found.append(
                    pltpu.make_async_copy(
                        weights.at[:, pl.ds(pl.multiple_of(start, HD), size)],
                        wide.at[group, side, :, pl.ds(offset, size)],
                        arrived.at[group, side, number],
                    )
                )
        return found

    @pl.when(index == 0)
    def _():
        for group in range(KVH):
            for copy in copies(group):
                copy.start()

    for copy in copies(index):
        copy.wait()

    def product(side):
        return jnp.dot(normed[...], wide[index, side], preferred_element_type=jnp.float32)

    store_codes(sent, powers, product(1), index, KVH)
    kept[0] = product(0)


def project(core, normed, qkv_weight, chunk, with_pair, after):
    rows, width = normed.shape
    columns = 2 * HD + (HD if with_pair else 0)
    sent_rows = KVH * coded_rows(rows) + TILE
    return pl.pallas_call(
        functools.partial(project_kernel, chunk, with_pair),
        grid_spec=pltpu.PrefetchScalarGridSpec(
            num_scalar_prefetch=1,
            grid=(KVH,),
            in_specs=[pl.BlockSpec((rows, width), lambda t, c: (0, 0))]
            + [pl.BlockSpec(memory_space=pl.ANY)] * (1 + len(after)),
            out_specs=[
                pl.BlockSpec((1, rows, columns), lambda t, c: (t, 0, 0)),
                pl.BlockSpec((sent_rows, columns), lambda t, c: (0, 0)),
            ],
            scratch_shapes=[
                pltpu.VMEM((TILE, columns), jnp.float32),
                pltpu.VMEM((KVH, 2, width, columns), jnp.bfloat16),
                pltpu.SemaphoreType.DMA((KVH, 2, 2)),
            ],
        ),
        out_shape=[
            jax.ShapeDtypeStruct((KVH, rows, columns), jnp.float32),
            jax.ShapeDtypeStruct((sent_rows, columns), jnp.int16),
        ],
        compiler_params=pltpu.CompilerParams(vmem_limit_bytes=VMEM_LIMIT),
        cost_estimate=SHORT,
        name="project",
    )(core, normed, qkv_weight, *after)


def fold_kernel(steps, bit, held, landed, landed_powers, *refs):
    kept, sent, powers = refs[-3:]
    index = pl.program_id(0)
    rows = coded_rows(held.shape[1])
    rows_of_powers = landed_powers[...].astype(jnp.int32).astype(jnp.float32)

    def total(side):
        place = pl.multiple_of(side * rows, TILE)
        codes = landed[pl.ds(place, rows), :]
        return held[side] + decode(codes, pick_row(rows_of_powers, 2 * index + side))

    mine = bit[0]
    store_codes(sent, powers, total(1 - mine), index, steps)
    kept[0] = total(mine)


def fold(bit, held, landed, after):
    blocks, rows, columns = held.shape
    steps = blocks // 2
    coded = coded_rows(rows)
    return pl.pallas_call(
        functools.partial(fold_kernel, steps),
        grid_spec=pltpu.PrefetchScalarGridSpec(
            num_scalar_prefetch=1,
            grid=(steps,),
            in_specs=[
                pl.BlockSpec((2, rows, columns), lambda i, b: (i, 0, 0)),
                pl.BlockSpec((2 * coded, columns), lambda i, b: (i, 0)),
                pl.BlockSpec((TILE, columns), lambda i, b: (blocks * coded // TILE, 0)),
            ]
            + [pl.BlockSpec(memory_space=pl.ANY)] * len(after),
            out_specs=[
                pl.BlockSpec((1, rows, columns), lambda i, b: (i, 0, 0)),
                pl.BlockSpec((steps * coded + TILE, columns), lambda i, b: (0, 0)),
            ],
            scratch_shapes=[pltpu.VMEM((TILE, columns), jnp.float32)],
        ),
        out_shape=[
            jax.ShapeDtypeStruct((steps, rows, columns), jnp.float32),
            jax.ShapeDtypeStruct((steps * coded + TILE, columns), jnp.int16),
        ],
        compiler_params=pltpu.CompilerParams(vmem_limit_bytes=VMEM_LIMIT),
        cost_estimate=SHORT,
        name="fold",
    )(bit, held, landed, landed, *after)


def finish_kernel(after_count, core, held, landed, cosine, sine, *refs):
    queries, *pair = refs[after_count:]
    rows = held.shape[1]
    coded = coded_rows(rows)
    power = landed[pl.ds(coded, TILE), :].astype(jnp.int32).astype(jnp.float32)[0:1]
    total = held[0] + decode(landed[pl.ds(0, coded), :], power)
    joined = total.astype(jnp.bfloat16)
    parts = []
    for head in range(joined.shape[1] // HD):
        raw = joined[:, head * HD : (head + 1) * HD]
        wide = raw.astype(jnp.float32)
        turned = wide * cosine[...] + pltpu.roll(wide, HD // 2, 1) * sine[...]
        parts.append((raw, turned.astype(jnp.bfloat16)))
    queries[...] = jnp.concatenate([parts[0][1], parts[1][1]], 1)
    if pair:
        raw, turned = parts[2]
        pair[0][...] = jnp.where(core[0] == 0, turned.astype(jnp.float32), raw.astype(jnp.float32)).astype(
            jnp.bfloat16
        )


def finish(core, held, landed, cosine, sine, after):
    _, rows, columns = held.shape
    whole = pl.BlockSpec(memory_space=pltpu.VMEM)
    shapes = [jax.ShapeDtypeStruct((rows, 2 * HD), jnp.bfloat16)]
    if columns > 2 * HD:
        shapes.append(jax.ShapeDtypeStruct((rows, HD), jnp.bfloat16))
    return pl.pallas_call(
        functools.partial(finish_kernel, len(after)),
        in_specs=[pl.BlockSpec(memory_space=pltpu.SMEM)]
        + [whole] * 4
        + [pl.BlockSpec(memory_space=pl.ANY)] * len(after),
        out_specs=[whole] * len(shapes),
        out_shape=shapes,
        compiler_params=pltpu.CompilerParams(vmem_limit_bytes=VMEM_LIMIT),
        cost_estimate=SHORT,
        name="finish",
    )(core, held, landed, cosine, sine, *after)


MIX_STEPS = 8


def mix_kernel(places, first, second, others, weights, start, mixed, total, wide, arrived):
    step = pl.program_id(0)
    depth = wide.shape[1]

    def copy(part):
        row = places[part // 2] * (2 * depth) + part % 2 * depth
        return pltpu.make_async_copy(
            weights.at[pl.ds(pl.multiple_of(row, depth), depth), :],
            wide.at[part],
            arrived.at[part],
        )

    @pl.when(step == 0)
    def _():
        for part in range(MIX_STEPS):
            copy(part).start()
        total[...] = start[...].astype(jnp.float32)

    for part in range(MIX_STEPS):

        @pl.when(step == part)
        def _():
            copy(part).wait()
            piece = (first, second, others.at[0], others.at[1])[part // 2]
            offset = part % 2 * depth
            total[...] += jnp.dot(
                piece[:, offset : offset + depth],
                wide[part],
                preferred_element_type=jnp.float32,
            )

    @pl.when(step == MIX_STEPS - 1)
    def _():
        mixed[...] = total[...].astype(mixed.dtype)


def mix(places, first, second, others, out_weight, start, dtype):
    rows, width = first.shape
    columns = out_weight.shape[1]
    depth = width // 2
    whole = pl.BlockSpec((rows, width), lambda i, p: (0, 0))
    return pl.pallas_call(
        mix_kernel,
        grid_spec=pltpu.PrefetchScalarGridSpec(
            num_scalar_prefetch=1,
            grid=(MIX_STEPS,),
            in_specs=[
                whole,
                whole,
                pl.BlockSpec((2, rows, width), lambda i, p: (0, 0, 0)),
                pl.BlockSpec(memory_space=pl.ANY),
                pl.BlockSpec((rows, columns), lambda i, p: (0, 0)),
            ],
            out_specs=pl.BlockSpec((rows, columns), lambda i, p: (0, 0)),
            scratch_shapes=[
                pltpu.VMEM((rows, columns), jnp.float32),
                pltpu.VMEM((MIX_STEPS, depth, columns), jnp.bfloat16),
                pltpu.SemaphoreType.DMA((MIX_STEPS,)),
            ],
        ),
        out_shape=jax.ShapeDtypeStruct((rows, columns), dtype),
        compiler_params=pltpu.CompilerParams(vmem_limit_bytes=VMEM_LIMIT),
        cost_estimate=SHORT,
        name="mix",
    )(places, first, second, others, out_weight, start)


def along(value, pairs):
    devices = lax.axis_size("tensor")
    side = devices // 4
    table = [
        (source * side + i, target * side + i) for source, target in pairs for i in range(side)
    ]
    return lax.ppermute(value, "tensor", table)


def gather_and_mix(attention, out_weight, start, device):
    line = device // 4
    inner = (line == 1) | (line == 2)
    near = swap(attention, 4)
    cross = along(attention, [(1, 2), (2, 1)])
    across = swap(attention, 2)
    passed = along(cross, [(1, 0), (2, 3)])
    cross_near = along(near, [(1, 2), (2, 1)])
    across_near = swap(near, 2)
    third = jnp.where(inner, cross_near, passed)
    last = along(cross_near, [(1, 0), (2, 3)])
    across_third = swap(third, 2)
    fourth = jnp.where(inner, cross, last)
    across_fourth = swap(fourth, 2)
    groups = [
        (attention, near, 0, 4),
        (across, across_near, 2, 6),
        (third, across_third, 8, 10),
        (fourth, across_fourth, 12, 14),
    ]
    mixed = start
    for number, (one, two, x, y) in enumerate(groups):
        others = swap(jnp.stack([one, two]), 1)
        places = jnp.stack([device ^ x, device ^ y, device ^ x ^ 1, device ^ y ^ 1])
        dtype = jnp.bfloat16 if number == len(groups) - 1 else jnp.float32
        mixed = mix(places, one, two, others, out_weight, mixed, dtype)
    return mixed


def attend_kernel(
    slot_request,
    queries,
    new_keys,
    new_values,
    own_near,
    own_far,
    other_near,
    other_far,
    key_scale,
    value_scale,
    cache_bias,
    new_bias,
    attention,
    slot_best,
    slot_total,
    slot_sum,
    best,
    total,
    summed,
):
    slots = slot_best.shape[0]
    requests, count, _ = queries.shape
    transposed = (((1,), (1,)), ((), ()))
    for request in range(requests):
        scores = (
            lax.dot_general(
                queries[request],
                new_keys[request],
                transposed,
                preferred_element_type=jnp.float32,
            )
            * HD ** (-0.5)
            + new_bias[...]
        )
        top = jnp.max(scores, -1, keepdims=True)
        expo = jnp.exp(scores - top)
        best[request] = jnp.broadcast_to(top, (count, HD))
        total[request] = jnp.broadcast_to(jnp.sum(expo, -1, keepdims=True), (count, HD))
        summed[request] = jnp.dot(
            expo.astype(jnp.bfloat16), new_values[request], preferred_element_type=jnp.float32
        )
    for slot in range(slots):
        request = slot_request[slot]
        query = queries[request]
        raw = [
            part[:, slot * BLK : (slot + 1) * BLK, :].reshape(KVH // 2 * BLK, 2 * HD)
            for part in (own_near, own_far, other_near, other_far)
        ]
        scores = jnp.concatenate(
            [
                lax.dot_general(
                    query, kv[:, :HD], transposed, preferred_element_type=jnp.float32
                )
                for kv in raw
            ],
            1,
        )
        scores = scores * key_scale[slot : slot + 1, :] + cache_bias[slot : slot + 1, :]
        top = jnp.max(scores, -1, keepdims=True)
        expo = jnp.exp(scores - top)
        weights = (expo * value_scale[slot : slot + 1, :]).astype(jnp.bfloat16)
        slot_best[slot] = jnp.broadcast_to(top, (count, HD))
        slot_total[slot] = jnp.broadcast_to(jnp.sum(expo, -1, keepdims=True), (count, HD))
        values = jnp.concatenate([kv[:, HD:] for kv in raw], 0)
        slot_sum[slot] = jnp.dot(weights, values, preferred_element_type=jnp.float32)
    for slot in range(slots):
        request = slot_request[slot]
        before = best[request]
        here = slot_best[slot]
        top = jnp.maximum(before, here)
        keep = jnp.exp(before - top)
        add = jnp.exp(here - top)
        best[request] = top
        total[request] = total[request] * keep + slot_total[slot] * add
        summed[request] = summed[request] * keep + slot_sum[slot] * add
    for request in range(requests):
        attention[request] = (summed[request] / total[request]).astype(jnp.bfloat16)


def attend(slot_request, *arrays):
    queries = arrays[0]
    slots = arrays[7].shape[0]
    requests, count, _ = queries.shape
    whole = pl.BlockSpec(memory_space=pltpu.VMEM)
    return pl.pallas_call(
        attend_kernel,
        in_specs=[pl.BlockSpec(memory_space=pltpu.SMEM)] + [whole] * len(arrays),
        out_specs=whole,
        out_shape=jax.ShapeDtypeStruct((requests, count, HD), jnp.bfloat16),
        scratch_shapes=[pltpu.VMEM((slots, count, HD), jnp.float32)] * 3
        + [pltpu.VMEM((requests, count, HD), jnp.float32)] * 3,
        compiler_params=pltpu.CompilerParams(vmem_limit_bytes=VMEM_LIMIT),
        cost_estimate=SHORT,
        name="attend",
    )(slot_request, *arrays)


def slot_layout(request_length, block_table, slots, stripe):
    requests, most = block_table.shape
    stripes = (request_length + stripe - 1) // stripe
    columns = jnp.arange(most, dtype=jnp.int32)
    held = columns[None, :] < stripes[:, None]
    hit = held[:, :, None] & (
        block_table[:, :, None] == jnp.arange(slots, dtype=jnp.int32)[None, None, :]
    )
    hit = hit.astype(jnp.int32)
    order = jnp.arange(requests, dtype=jnp.int32)
    request = jnp.sum(hit * order[:, None, None], (0, 1))
    rank = jnp.sum(hit * columns[None, :, None], (0, 1))
    length = jnp.sum(hit * request_length[:, None, None], (0, 1))
    return request, rank, length


def arrange_kernel(chip, even, odd, even_scale, odd_scale, after, kept, sent):
    slots = even.shape[0]
    for blocks, scale, target in ((even, even_scale, kept), (odd, odd_scale, sent)):
        target[0, : slots * BLK, :] = blocks[:, 0].reshape(slots * BLK, 2 * HD)
        target[0, slots * BLK :, :] = scale[0]


def arrange(chip, cache_pool, scales, after):
    slots = cache_pool.shape[0]
    pool = [
        pl.BlockSpec(
            (slots, 1, BLK, 2 * HD), lambda i, c, side=side: (0, c[0] ^ (2 * i + side), 0, 0)
        )
        for side in (0, 1)
    ]
    scale = [
        pl.BlockSpec((1, TILE, 2 * HD), lambda i, c, side=side: (c[0] ^ (2 * i + side), 0, 0))
        for side in (0, 1)
    ]
    rows = slots * BLK + TILE
    out = pl.BlockSpec((1, rows, 2 * HD), lambda i, c: (i, 0, 0))
    shape = jax.ShapeDtypeStruct((KVH // 2, rows, 2 * HD), jnp.bfloat16)
    return pl.pallas_call(
        arrange_kernel,
        grid_spec=pltpu.PrefetchScalarGridSpec(
            num_scalar_prefetch=1,
            grid=(KVH // 2,),
            in_specs=pool + scale + [pl.BlockSpec(memory_space=pl.ANY)],
            out_specs=[out, out],
        ),
        out_shape=[shape, shape],
        compiler_params=pltpu.CompilerParams(vmem_limit_bytes=VMEM_LIMIT),
        cost_estimate=SHORT,
        name="arrange",
    )(chip, cache_pool, cache_pool, scales, scales, after)


SPLIT = (((0, 0), (0, 2), (1, 0), (1, 2)), ((0, 1), (0, 3), (1, 1), (1, 3)))


def regroup_kernel(index_of, kept, landed, *refs):
    out_kept, out_sent = refs[-2:]
    for target, (source, index) in enumerate(index_of[0]):
        out_kept[target] = (kept, landed)[source][index]
    for target, (source, index) in enumerate(index_of[1]):
        out_sent[target] = (kept, landed)[source][index]


def regroup(index_of, kept, landed, after):
    whole = pl.BlockSpec(memory_space=pltpu.VMEM)
    shape = jax.ShapeDtypeStruct(kept.shape, kept.dtype)
    return pl.pallas_call(
        functools.partial(regroup_kernel, index_of),
        in_specs=[whole, whole] + [pl.BlockSpec(memory_space=pl.ANY)] * len(after),
        out_specs=[whole, whole],
        out_shape=[shape, shape],
        compiler_params=pltpu.CompilerParams(vmem_limit_bytes=VMEM_LIMIT),
        cost_estimate=SHORT,
        name="regroup",
    )(kept, landed, *after)


def local_pairs(
    hidden_in,
    norm_gain,
    qkv_weight,
    out_weight,
    cache_pool,
    cache_scale,
    request_length,
    block_table,
):
    devices = lax.axis_size("tensor")
    device = lax.axis_index("tensor")
    core = device % 2
    chip = device // 2
    stripe = devices * BLK
    slots = cache_pool.shape[0]
    requests = request_length.shape[0]
    rows = STEPS * requests * QR
    width = hidden_in.shape[2]
    heads = GQ // 2

    hidden = hidden_in.astype(jnp.float32)
    sums = jnp.sum(hidden * hidden, -1)
    for bit in MESH_BITS:
        sums = sums + swap(sums, bit)
        if bit == 2:
            early = sums
    normed = (
        hidden * lax.rsqrt(sums[..., None] / D + EPSILON) * norm_gain.astype(jnp.float32)
    ).astype(jnp.bfloat16)
    normed = normed.reshape(rows, width)
    bits = [jnp.reshape((device >> b) & 1, (1,)).astype(jnp.int32) for b in range(4)]
    scale_rows = jnp.pad(
        jnp.transpose(cache_scale, (1, 2, 0)).reshape(KVH, 1, 2 * slots),
        ((0, 0), (0, TILE - 1), (0, 2 * HD - 2 * slots)),
    )
    chip_scalar = jnp.reshape(chip, (1,)).astype(jnp.int32)
    cache_kept, cache_sent = arrange(chip_scalar, cache_pool, scale_rows, early)
    cache_landed = swap(cache_sent, 2)

    step_ids = jnp.arange(STEPS, dtype=jnp.int32)
    row_ids = jnp.arange(QR, dtype=jnp.int32)
    position = (
        request_length[None, :, None] + QR * step_ids[:, None, None] + row_ids[None, None, :]
    )
    freqs = ROPE_BASE ** (-(jnp.arange(HD // 2, dtype=jnp.float32) * 2.0 / HD))
    angles = position.reshape(rows, 1).astype(jnp.float32) * freqs
    cosine = jnp.concatenate([jnp.cos(angles)] * 2, 1)
    sine = jnp.concatenate([-jnp.sin(angles), jnp.sin(angles)], 1)

    count = GQ // 4
    held, sent = [None] * count, [None] * count

    def folded(chunk, b, *after):
        held[chunk], sent[chunk] = fold(
            bits[b], held[chunk], swap(sent[chunk], MESH_BITS[b - 1]), after
        )

    def projected(chunk, *after):
        held[chunk], sent[chunk] = project(
            bits[0], normed, qkv_weight, chunk, chunk == 0, after
        )

    projected(0, cache_kept)
    projected(1, held[0])
    cache_kept, cache_sent = regroup(SPLIT, cache_kept, cache_landed, (held[1],))
    cache_landed = swap(cache_sent, 4)
    projected(2, cache_kept)
    projected(3, held[2])
    folded(0, 1, held[3])
    folded(1, 1, held[0])
    folded(2, 1, held[1])
    cache_kept, cache_sent = regroup(SPLIT, cache_kept, cache_landed, (held[2],))
    cache_landed = swap(cache_sent, 8)
    kept_other = swap(cache_kept, 1)
    folded(3, 1, cache_kept)
    folded(0, 2, held[3])
    folded(1, 2, held[0])
    folded(0, 3, held[1])
    folded(2, 2, held[0])
    folded(1, 3, held[2])

    def finished(chunk, *after):
        return finish(
            bits[0], held[chunk], swap(sent[chunk], MESH_BITS[3]), cosine, sine, after
        )

    query_chunks = [None] * count
    query_chunks[0], pair = finished(0, held[1])
    pair_other = swap(pair, 1)
    folded(3, 2, query_chunks[0])
    folded(2, 3, held[3])
    (query_chunks[1],) = finished(1, held[2])
    folded(3, 3, query_chunks[1], pair_other)
    (query_chunks[2],) = finished(2, held[3])
    landed_other = swap(cache_landed, 1)
    (query_chunks[3],) = finished(3, query_chunks[2])
    cache_parts = (cache_kept, cache_landed, kept_other, landed_other)
    keys = jnp.where(core == 0, pair, pair_other)
    raw_values = jnp.where(core == 0, pair_other, pair)
    queries = jnp.concatenate(query_chunks, 1).reshape(STEPS, requests, QR, heads, HD)
    queries = jnp.transpose(queries, (1, 0, 2, 3, 4)).reshape(requests, STEPS * QR * heads, HD)

    def by_request(value):
        value = jnp.transpose(value.reshape(STEPS, requests, QR, HD), (1, 0, 2, 3))
        value = value.reshape(requests, STEPS * QR, HD)
        return jnp.pad(value, ((0, 0), (0, TILE - STEPS * QR), (0, 0)))

    slot_request, slot_rank, slot_length = slot_layout(request_length, block_table, slots, stripe)
    source = chip ^ jnp.arange(KVH, dtype=jnp.int32)
    sources = jnp.stack([source * 2 + core, source * 2 + 1 - core])
    offset = sources[:, :, None] * BLK + jnp.arange(BLK, dtype=jnp.int32)[None, None, :]
    token = slot_rank[:, None] * stripe + offset.reshape(1, stripe)
    cache_bias = jnp.where(token < slot_length[:, None], 0.0, NEG_FILL).astype(jnp.float32)
    scales = jnp.concatenate([part[:, slots * BLK, : 2 * slots] for part in cache_parts])
    scales = scales.astype(jnp.float32).reshape(2 * KVH, 2, slots)
    scales = jnp.repeat(jnp.transpose(scales, (1, 2, 0)), BLK, axis=2)
    order = jnp.arange(STEPS * QR * heads, dtype=jnp.int32) // heads
    key_order = jnp.arange(TILE, dtype=jnp.int32)
    new_bias = jnp.where(key_order[None, :] <= order[:, None], 0.0, NEG_FILL).astype(jnp.float32)
    attention = attend(
        slot_request,
        queries,
        by_request(keys),
        by_request(raw_values),
        *cache_parts,
        scales[0] * HD ** (-0.5),
        scales[1],
        cache_bias,
        new_bias,
    )
    attention = jnp.transpose(
        attention.reshape(requests, STEPS, QR, heads, HD), (1, 0, 2, 3, 4)
    ).reshape(rows, heads * HD)
    mixed = gather_and_mix(attention, out_weight, hidden_in.reshape(rows, width), device)
    return mixed.reshape(hidden_in.shape)


def solution(mesh):
    return jax.shard_map(
        local_pairs if mesh.shape["tensor"] == 2 * KVH else local_general,
        mesh=mesh,
        in_specs=(
            P(None, "groups", "tensor"),
            P("tensor"),
            P("tensor", None),
            P(None, "tensor"),
            P(("groups", "tensor"), None, None, None),
            P(("groups", "tensor"), None, None),
            P("groups"),
            P("groups", None),
        ),
        out_specs=P(None, "groups", "tensor"),
        check_vma=False,
    )
```

```python
import functools

import jax
import jax.numpy as jnp
from jax import lax
from jax.experimental import pallas as pl
from jax.experimental.pallas import tpu as pltpu
from jax.sharding import PartitionSpec as P

D = 16384
QH = 128
KVH = 8
HD = 128
QR = 6
STEPS = 2
BLK = 16
GQ = 16
GW = 2304


EPSILON = 1e-05
ROPE_BASE = 500000.0
NEG_FILL = -1e30


def rotate(values, positions):
    half = values.shape[-1] // 2
    freqs = ROPE_BASE ** (-(jnp.arange(half, dtype=jnp.float32) * 2.0 / values.shape[-1]))
    angles = positions.astype(jnp.float32)[..., None] * freqs
    cosine = jnp.cos(angles)
    sine = jnp.sin(angles)
    first = values[..., :half]
    second = values[..., half:]
    return jnp.concatenate([first * cosine - second * sine, second * cosine + first * sine], -1)


def request_layout(request_owner, request_length, block_table, owners, stripe):
    requests = request_owner.shape[0]
    most = block_table.shape[1]
    order = jnp.arange(requests, dtype=jnp.int32)
    stripes = (request_length + stripe - 1) // stripe
    before = (
        (request_owner[None, :] == request_owner[:, None]) & (order[None, :] < order[:, None])
    ).astype(jnp.int32)
    rank = jnp.sum(before, 1)
    offset = jnp.sum(before * stripes[None, :], 1)
    owner_ids = jnp.arange(owners, dtype=jnp.int32)
    mine = request_owner[None, :] == owner_ids[:, None]
    member = mine[:, :, None] & (
        rank[None, :, None] == jnp.arange(requests // owners, dtype=jnp.int32)[None, None, :]
    )
    owner_requests = jnp.sum(member.astype(jnp.int32) * order[None, :, None], 1)
    columns = jnp.arange(most, dtype=jnp.int32)
    within = columns[None, None, :] - offset[None, :, None]
    hit = (mine[:, :, None] & (within >= 0) & (within < stripes[None, :, None])).astype(jnp.int32)
    stripe_request = jnp.sum(hit * order[None, :, None], 1) - (1 - jnp.sum(hit, 1))
    stripe_rank = jnp.sum(hit * within, 1)
    pick = (within[..., None] == columns[None, None, None, :]).astype(jnp.int32)
    slots = jnp.sum(hit[..., None] * pick * block_table[None, :, None, :], (1, 3))
    return (owner_requests, stripe_request, stripe_rank, slots, rank, stripes)


def cache_partial(queries, keys, values, key_scale, value_scale, mask):
    scores = jnp.einsum("srgd,td->srgt", queries, keys, preferred_element_type=jnp.float32)
    scores = jnp.where(mask, scores * key_scale * HD ** (-0.5), NEG_FILL)
    best = jnp.max(scores, -1)
    expo = jnp.where(mask, jnp.exp(scores - best[..., None]), 0.0)
    total = jnp.sum(expo, -1)
    weights = (expo * value_scale).astype(jnp.bfloat16)
    summed = jnp.einsum("srgt,td->srgd", weights, values, preferred_element_type=jnp.float32)
    return (best, total, summed)


def local_general(
    hidden_in,
    norm_gain,
    qkv_weight,
    out_weight,
    cache_pool,
    cache_scale,
    request_length,
    block_table,
):
    devices = lax.axis_size("tensor")
    device = lax.axis_index("tensor")
    owners = devices // KVH
    stripe = devices * BLK
    requests = request_length.shape[0]
    request_owner = jnp.arange(requests, dtype=jnp.int32) % owners
    unit_rows = requests // owners * QR
    most = block_table.shape[1]
    local_width = hidden_in.shape[2]
    my_owner = device // KVH
    owner_requests, stripe_request, stripe_rank, slots, rank, stripes = request_layout(
        request_owner, request_length, block_table, owners, stripe
    )
    step_rows = jnp.arange(QR, dtype=jnp.int32)
    row_order = (owner_requests[:, :, None] * QR + step_rows[None, None, :]).reshape(
        owners * unit_rows
    )
    inverse = ((request_owner * unit_rows + rank * QR)[:, None] + step_rows[None, :]).reshape(
        requests * QR
    )
    row_request = jnp.repeat(owner_requests[my_owner], QR)
    row_length = request_length[row_request]
    row_step = jnp.arange(unit_rows, dtype=jnp.int32) % QR
    same_request = row_request[:, None] == row_request[None, :]
    gain = norm_gain.astype(jnp.float32)
    weight_grouped = qkv_weight.reshape(local_width, KVH, GW)
    sent = cache_pool[jnp.transpose(slots)].reshape(most, devices, BLK, 2 * HD)
    sent_scale = cache_scale[jnp.transpose(slots)].reshape(most, devices, 2)
    landed, landed_scale = (
        lax.all_to_all(sent, "tensor", split_axis=1, concat_axis=1, tiled=True),
        lax.all_to_all(sent_scale, "tensor", split_axis=1, concat_axis=1, tiled=True),
    )
    cache_data = landed.reshape(most * stripe, 2 * HD)
    token_scale = jnp.broadcast_to(
        landed_scale.astype(jnp.float32)[:, :, None, :], (most, devices, BLK, 2)
    ).reshape(most * stripe, 2)
    token = jnp.arange(most * stripe, dtype=jnp.int32)
    token_stripe = token // stripe
    token_request = stripe_request[my_owner][token_stripe]
    token_position = stripe_rank[my_owner][token_stripe] * stripe + token % stripe
    token_length = jnp.where(token_request >= 0, request_length[jnp.maximum(token_request, 0)], 0)
    cache_mask = (
        (token_request[None, :] == row_request[:, None]) & (token_position < token_length)[None, :]
    )[None, :, None, :]
    outputs = []
    keys_seen = []
    values_seen = []
    for step in range(STEPS):
        block = hidden_in[step : step + 1]
        project_count = block.shape[0]
        values = block.astype(jnp.float32)
        sums = lax.psum(jnp.sum(values * values, -1), "tensor")
        normed = (values * lax.rsqrt(sums[..., None] / D + EPSILON) * gain).astype(jnp.bfloat16)
        ordered = jnp.take(normed, row_order, axis=1).reshape(
            project_count, owners, unit_rows, local_width
        )
        term = jnp.einsum(
            "sojd,dhg->ohsjg", ordered, weight_grouped, preferred_element_type=jnp.float32
        )
        term = term.reshape(owners * KVH * project_count * unit_rows, GW)
        mine = lax.psum_scatter(term, "tensor", scatter_dimension=0, tiled=True)
        joined_block = mine.astype(jnp.bfloat16).reshape(project_count, unit_rows, GW)
        prepare_count = joined_block.shape[0]
        steps_here = step + jnp.arange(prepare_count, dtype=jnp.int32)
        position = row_length[None, :] + QR * steps_here[:, None] + row_step[None, :]
        prepare_queries = rotate(
            joined_block[..., : GQ * HD]
            .reshape(prepare_count, unit_rows, GQ, HD)
            .astype(jnp.float32),
            position[:, :, None],
        ).astype(jnp.bfloat16)
        keys = rotate(
            joined_block[..., GQ * HD : GQ * HD + HD].astype(jnp.float32), position
        ).astype(jnp.bfloat16)
        queries, keys, values = (prepare_queries, keys, joined_block[..., GQ * HD + HD :])
        keys_seen.append(keys)
        values_seen.append(values)
        keys_all = jnp.concatenate(keys_seen, 0)
        attend_count = queries.shape[0]
        cache_best, cache_total, cache_summed = cache_partial(
            queries,
            cache_data[:, :HD],
            cache_data[:, HD:],
            token_scale[:, 0],
            token_scale[:, 1],
            cache_mask,
        )
        news = jnp.einsum(
            "srgd,pjd->srgpj", queries, keys_all, preferred_element_type=jnp.float32
        ) * HD ** (-0.5)
        query_step = step + jnp.arange(attend_count, dtype=jnp.int32)[:, None, None, None]
        key_step = jnp.arange(keys_all.shape[0], dtype=jnp.int32)[None, None, :, None]
        allowed = (key_step < query_step) | (key_step == query_step) & (
            row_step[None, None, None, :] <= row_step[None, :, None, None]
        )
        allowed = (allowed & same_request[None, :, None, :])[:, :, None, :, :]
        news = jnp.where(allowed, news, NEG_FILL)
        best = jnp.maximum(cache_best, jnp.max(news, (3, 4)))
        factor = jnp.exp(cache_best - best)
        expo = jnp.where(allowed, jnp.exp(news - best[..., None, None]), 0.0)
        total = cache_total * factor + jnp.sum(expo, (3, 4))
        summed = cache_summed * factor[..., None] + jnp.einsum(
            "srgpj,pjd->srgd",
            expo.astype(jnp.bfloat16),
            jnp.concatenate(values_seen, 0),
            preferred_element_type=jnp.float32,
        )
        attention = (
            (summed / total[..., None])
            .astype(jnp.bfloat16)
            .reshape(attend_count, unit_rows, GQ * HD)
        )
        count = attention.shape[0]
        gathered = lax.all_gather(attention, "tensor", axis=2, tiled=True).reshape(
            count, unit_rows, owners, QH * HD
        )
        mixed = jnp.einsum(
            "sjof,fd->sojd", gathered, out_weight, preferred_element_type=jnp.float32
        )
        mixed = jnp.take(mixed.reshape(count, owners * unit_rows, local_width), inverse, axis=1)
        outputs.append(
            (hidden_in[step : step + count].astype(jnp.float32) + mixed).astype(jnp.bfloat16)
        )
    return jnp.concatenate(outputs, 0)


VMEM_LIMIT = 48 * 1024 * 1024
SHORT = pl.CostEstimate(flops=1, bytes_accessed=1, transcendentals=0)
LOW_BITS = 4
PACKED = 16 // LOW_BITS
LEVELS = 32600.0 * 2**LOW_BITS
POWER_STEPS = 8.0
TILE = 16
MESH_BITS = (1, 2, 4, 8)


def swap(value, bit):
    devices = lax.axis_size("tensor")
    return lax.ppermute(value, "tensor", [(i, i ^ bit) for i in range(devices)])


def no_work(*refs):
    del refs


def together(*arrays):
    anywhere = pl.BlockSpec(memory_space=pl.ANY)
    return pl.pallas_call(
        no_work,
        in_specs=[anywhere] * len(arrays),
        out_specs=[anywhere] * len(arrays),
        out_shape=[jax.ShapeDtypeStruct(a.shape, a.dtype) for a in arrays],
        input_output_aliases={i: i for i in range(len(arrays))},
        cost_estimate=SHORT,
        name="together",
    )(*arrays)


def coded_rows(rows):
    return rows + rows // PACKED


def encode(block):
    top = jnp.max(jnp.abs(block), 0, keepdims=True)
    power = jnp.ceil(jnp.log2(jnp.maximum(top, 1e-30)) * POWER_STEPS)
    codes = jnp.round(block * (jnp.exp2(power * (-1.0 / POWER_STEPS)) * LEVELS)).astype(jnp.int32)
    low = codes & (2**LOW_BITS - 1)
    part = block.shape[0] // PACKED
    packed = low[:part]
    for i in range(1, PACKED):
        packed = packed + (low[i * part : (i + 1) * part] << (LOW_BITS * i))
    high = (codes >> LOW_BITS).astype(jnp.int16)
    return jnp.concatenate([high, (packed - 32768).astype(jnp.int16)], 0), power


def decode(codes, power):
    rows = codes.shape[0] * PACKED // (PACKED + 1)
    high = codes[:rows].astype(jnp.int32) << LOW_BITS
    packed = codes[rows:].astype(jnp.int32) + 32768
    low = jnp.concatenate(
        [(packed >> (LOW_BITS * i)) & (2**LOW_BITS - 1) for i in range(PACKED)], 0
    )
    scale = jnp.exp2(power * (1.0 / POWER_STEPS)) * (1.0 / LEVELS)
    return (high + low).astype(jnp.float32) * scale


def pick_row(rows, index):
    ids = lax.broadcasted_iota(jnp.int32, rows.shape, 0)
    return jnp.sum(jnp.where(ids == index, rows, 0.0), 0, keepdims=True)


def store_codes(sent, powers, block, index, steps):
    rows = coded_rows(block.shape[0])
    codes, power = encode(block)
    sent[pl.ds(pl.multiple_of(index * rows, TILE), rows), :] = codes

    powers[pl.ds(index, 1), :] = power

    @pl.when(index == steps - 1)
    def _():
        sent[pl.ds(steps * rows, TILE), :] = powers[...].astype(jnp.int32).astype(jnp.int16)


def project_kernel(chunk, with_pair, core, normed, weights, *refs):
    kept, sent, powers, wide, arrived = refs[-5:]
    index = pl.program_id(0)
    columns = kept.shape[2]

    def copies(group):
        found = []
        for side in range(2):
            owner = core[0] if side == 0 else 1 - core[0]
            first = group * GW + owner * (GQ // 2 * HD) + chunk * (2 * HD)
            spans = [(first, 0, 2 * HD)]
            if with_pair:
                spans.append((group * GW + (GQ + owner) * HD, 2 * HD, HD))
            for number, (start, offset, size) in enumerate(spans):
                found.append(
                    pltpu.make_async_copy(
                        weights.at[:, pl.ds(pl.multiple_of(start, HD), size)],
                        wide.at[group, :, pl.ds(side * columns + offset, size)],
                        arrived.at[group, side, number],
                    )
                )
        return found

    @pl.when(index == 0)
    def _():
        for group in range(KVH):
            for copy in copies(group):
                copy.start()
        powers[...] = jnp.zeros_like(powers)

    for copy in copies(index):
        copy.wait()

    product = jnp.dot(normed[...], wide[index], preferred_element_type=jnp.float32)
    kept[0] = product[:, :columns]
    store_codes(sent, powers, product[:, columns:], index, KVH)


def project(core, normed, qkv_weight, chunk, with_pair, after):
    rows, width = normed.shape
    columns = 2 * HD + (HD if with_pair else 0)
    sent_rows = KVH * coded_rows(rows) + TILE
    return pl.pallas_call(
        functools.partial(project_kernel, chunk, with_pair),
        grid_spec=pltpu.PrefetchScalarGridSpec(
            num_scalar_prefetch=1,
            grid=(KVH,),
            in_specs=[pl.BlockSpec((rows, width), lambda t, c: (0, 0))]
            + [pl.BlockSpec(memory_space=pl.ANY)] * (1 + len(after)),
            out_specs=[
                pl.BlockSpec((1, rows, columns), lambda t, c: (t, 0, 0)),
                pl.BlockSpec((sent_rows, columns), lambda t, c: (0, 0)),
            ],
            scratch_shapes=[
                pltpu.VMEM((TILE, columns), jnp.float32),
                pltpu.VMEM((KVH, width, 2 * columns), jnp.bfloat16),
                pltpu.SemaphoreType.DMA((KVH, 2, 2)),
            ],
        ),
        out_shape=[
            jax.ShapeDtypeStruct((KVH, rows, columns), jnp.float32),
            jax.ShapeDtypeStruct((sent_rows, columns), jnp.int16),
        ],
        compiler_params=pltpu.CompilerParams(vmem_limit_bytes=VMEM_LIMIT),
        cost_estimate=SHORT,
        name="project",
    )(core, normed, qkv_weight, *after)


def fold_kernel(steps, bit, held, landed, landed_powers, *refs):
    kept, sent, powers = refs[-3:]
    index = pl.program_id(0)
    rows = coded_rows(held.shape[1])
    rows_of_powers = landed_powers[...].astype(jnp.int32).astype(jnp.float32)

    def total(side):
        place = pl.multiple_of(side * rows, TILE)
        codes = landed[pl.ds(place, rows), :]
        return held[side] + decode(codes, pick_row(rows_of_powers, 2 * index + side))

    @pl.when(index == 0)
    def _():
        powers[...] = jnp.zeros_like(powers)

    mine = bit[0]
    kept[0] = total(mine)
    store_codes(sent, powers, total(1 - mine), index, steps)


def fold(bit, held, landed, after):
    blocks, rows, columns = held.shape
    steps = blocks // 2
    coded = coded_rows(rows)
    return pl.pallas_call(
        functools.partial(fold_kernel, steps),
        grid_spec=pltpu.PrefetchScalarGridSpec(
            num_scalar_prefetch=1,
            grid=(steps,),
            in_specs=[
                pl.BlockSpec((2, rows, columns), lambda i, b: (i, 0, 0)),
                pl.BlockSpec((2 * coded, columns), lambda i, b: (i, 0)),
                pl.BlockSpec((TILE, columns), lambda i, b: (blocks * coded // TILE, 0)),
            ]
            + [pl.BlockSpec(memory_space=pl.ANY)] * len(after),
            out_specs=[
                pl.BlockSpec((1, rows, columns), lambda i, b: (i, 0, 0)),
                pl.BlockSpec((steps * coded + TILE, columns), lambda i, b: (0, 0)),
            ],
            scratch_shapes=[pltpu.VMEM((TILE, columns), jnp.float32)],
        ),
        out_shape=[
            jax.ShapeDtypeStruct((steps, rows, columns), jnp.float32),
            jax.ShapeDtypeStruct((steps * coded + TILE, columns), jnp.int16),
        ],
        compiler_params=pltpu.CompilerParams(vmem_limit_bytes=VMEM_LIMIT),
        cost_estimate=SHORT,
        name="fold",
    )(bit, held, landed, landed, *after)


def finish_kernel(after_count, core, held, landed, cosine, sine, *refs):
    queries, *pair = refs[after_count:]
    rows = held.shape[1]
    coded = coded_rows(rows)
    power = landed[pl.ds(coded, TILE), :].astype(jnp.int32).astype(jnp.float32)[0:1]
    total = held[0] + decode(landed[pl.ds(0, coded), :], power)
    joined = total.astype(jnp.bfloat16)
    parts = []
    for head in range(joined.shape[1] // HD):
        raw = joined[:, head * HD : (head + 1) * HD]
        wide = raw.astype(jnp.float32)
        turned = wide * cosine[...] + pltpu.roll(wide, HD // 2, 1) * sine[...]
        parts.append((raw, turned.astype(jnp.bfloat16)))
    queries[...] = jnp.concatenate([parts[0][1], parts[1][1]], 1)
    if pair:
        raw, turned = parts[2]
        pair[0][...] = jnp.where(core[0] == 0, turned.astype(jnp.float32), raw.astype(jnp.float32)).astype(
            jnp.bfloat16
        )


def finish(core, held, landed, cosine, sine, after):
    _, rows, columns = held.shape
    whole = pl.BlockSpec(memory_space=pltpu.VMEM)
    shapes = [jax.ShapeDtypeStruct((rows, 2 * HD), jnp.bfloat16)]
    if columns > 2 * HD:
        shapes.append(jax.ShapeDtypeStruct((rows, HD), jnp.bfloat16))
    return pl.pallas_call(
        functools.partial(finish_kernel, len(after)),
        in_specs=[pl.BlockSpec(memory_space=pltpu.SMEM)]
        + [whole] * 4
        + [pl.BlockSpec(memory_space=pl.ANY)] * len(after),
        out_specs=[whole] * len(shapes),
        out_shape=shapes,
        compiler_params=pltpu.CompilerParams(vmem_limit_bytes=VMEM_LIMIT),
        cost_estimate=SHORT,
        name="finish",
    )(core, held, landed, cosine, sine, *after)


def mix_kernel(count, places, *refs):
    pieces = refs[:count]
    weights, start, mixed, wide, arrived = refs[count:]
    depth = wide.shape[1]
    columns = wide.shape[2] // 2
    flat = []
    for piece in pieces:
        flat += [piece] if len(piece.shape) == 2 else [piece.at[i] for i in range(piece.shape[0])]
    copies = [
        pltpu.make_async_copy(
            weights.at[pl.ds(pl.multiple_of(places[i] * depth, depth), depth), :],
            wide.at[i],
            arrived.at[i],
        )
        for i in range(len(flat))
    ]
    for copy in copies:
        copy.start()
    half = (len(flat) + 1) // 2
    for first, last in ((0, half), (half, len(flat))):
        for copy in copies[first:last]:
            copy.wait()
        source = start if first == 0 else mixed
        for side in range(2):
            span = pl.ds(side * columns, columns)
            total = source[:, span].astype(jnp.float32)
            for i in range(first, last):
                total = total + jnp.dot(
                    flat[i][...], wide[i, :, span], preferred_element_type=jnp.float32
                )
            mixed[:, span] = total.astype(mixed.dtype)


def mix(places, pieces, out_weight, start, dtype):
    columns = out_weight.shape[1]
    rows, width = pieces[0].shape[-2:]
    count = sum(1 if len(p.shape) == 2 else p.shape[0] for p in pieces)
    whole = pl.BlockSpec(memory_space=pltpu.VMEM)
    return pl.pallas_call(
        functools.partial(mix_kernel, len(pieces)),
        in_specs=[pl.BlockSpec(memory_space=pltpu.SMEM)]
        + [whole] * len(pieces)
        + [pl.BlockSpec(memory_space=pl.ANY), whole],
        out_specs=whole,
        scratch_shapes=[
            pltpu.VMEM((count, width, columns), jnp.bfloat16),
            pltpu.SemaphoreType.DMA((count,)),
        ],
        out_shape=jax.ShapeDtypeStruct((rows, columns), dtype),
        compiler_params=pltpu.CompilerParams(vmem_limit_bytes=VMEM_LIMIT),
        cost_estimate=SHORT,
        name="mix",
    )(places, *pieces, out_weight, start)


def along(value, pairs):
    devices = lax.axis_size("tensor")
    side = devices // 4
    table = [
        (source * side + i, target * side + i) for source, target in pairs for i in range(side)
    ]
    return lax.ppermute(value, "tensor", table)


def gather_and_mix(attention, out_weight, start, device):
    line = device // 4
    inner = (line == 1) | (line == 2)

    def add(mixed, pieces, offsets, dtype=jnp.float32):
        places = jnp.stack([device ^ offset for offset in offsets])
        return mix(places, pieces, out_weight, mixed, dtype)

    near = swap(attention, 4)
    cross = along(attention, [(1, 2), (2, 1)])
    across = swap(attention, 2)
    near, cross, across = together(near, cross, across)

    passed = along(cross, [(1, 0), (2, 3)])
    cross_near = along(near, [(1, 2), (2, 1)])
    across_near = swap(near, 2)
    first = swap(jnp.stack([attention, near]), 1)
    passed, cross_near, across_near, first = together(passed, cross_near, across_near, first)

    third = jnp.where(inner, cross_near, passed)
    last = along(cross_near, [(1, 0), (2, 3)])
    across_third = swap(third, 2)
    second = swap(jnp.stack([across, across_near]), 1)
    mixed = add(start, [attention, near, first], (0, 4, 1, 5))
    last, across_third, second, mixed = together(last, across_third, second, mixed)

    fourth = jnp.where(inner, cross, last)
    across_fourth = swap(fourth, 2)
    both = jnp.stack([third, across_third, fourth])
    most = swap(both, 1)
    mixed = add(mixed, [across, across_near, second], (2, 6, 3, 7))
    across_fourth, most, mixed = together(across_fourth, most, mixed)

    final = swap(across_fourth, 1)
    mixed = add(mixed, [both, most], (8, 10, 12, 9, 11, 13))
    return add(mixed, [across_fourth, final], (14, 15), jnp.bfloat16)


def attend_kernel(
    slot_request,
    queries,
    new_keys,
    new_values,
    own_near,
    own_far,
    other_near,
    other_far,
    key_scale,
    value_scale,
    cache_bias,
    new_bias,
    attention,
    slot_best,
    slot_total,
    slot_sum,
    best,
    total,
    summed,
):
    slots = slot_best.shape[0]
    requests, count, _ = queries.shape
    transposed = (((1,), (1,)), ((), ()))
    for request in range(requests):
        scores = (
            lax.dot_general(
                queries[request],
                new_keys[request],
                transposed,
                preferred_element_type=jnp.float32,
            )
            * HD ** (-0.5)
            + new_bias[...]
        )
        top = jnp.max(scores, -1, keepdims=True)
        expo = jnp.exp(scores - top)
        best[request] = jnp.broadcast_to(top, (count, HD))
        total[request] = jnp.broadcast_to(jnp.sum(expo, -1, keepdims=True), (count, HD))
        summed[request] = jnp.dot(
            expo.astype(jnp.bfloat16), new_values[request], preferred_element_type=jnp.float32
        )
    for slot in range(slots):
        request = slot_request[slot]
        query = queries[request]
        raw = [
            part[:, slot * BLK : (slot + 1) * BLK, :].reshape(KVH // 2 * BLK, 2 * HD)
            for part in (own_near, own_far, other_near, other_far)
        ]
        scores = jnp.concatenate(
            [
                lax.dot_general(
                    query, kv[:, :HD], transposed, preferred_element_type=jnp.float32
                )
                for kv in raw
            ],
            1,
        )
        scores = scores * key_scale[slot : slot + 1, :] + cache_bias[slot : slot + 1, :]
        top = jnp.max(scores, -1, keepdims=True)
        expo = jnp.exp(scores - top)
        weights = (expo * value_scale[slot : slot + 1, :]).astype(jnp.bfloat16)
        slot_best[slot] = jnp.broadcast_to(top, (count, HD))
        slot_total[slot] = jnp.broadcast_to(jnp.sum(expo, -1, keepdims=True), (count, HD))
        values = jnp.concatenate([kv[:, HD:] for kv in raw], 0)
        slot_sum[slot] = jnp.dot(weights, values, preferred_element_type=jnp.float32)
    for slot in range(slots):
        request = slot_request[slot]
        before = best[request]
        here = slot_best[slot]
        top = jnp.maximum(before, here)
        keep = jnp.exp(before - top)
        add = jnp.exp(here - top)
        best[request] = top
        total[request] = total[request] * keep + slot_total[slot] * add
        summed[request] = summed[request] * keep + slot_sum[slot] * add
    for request in range(requests):
        attention[request] = (summed[request] / total[request]).astype(jnp.bfloat16)


def attend(slot_request, *arrays):
    queries = arrays[0]
    slots = arrays[7].shape[0]
    requests, count, _ = queries.shape
    whole = pl.BlockSpec(memory_space=pltpu.VMEM)
    return pl.pallas_call(
        attend_kernel,
        in_specs=[pl.BlockSpec(memory_space=pltpu.SMEM)] + [whole] * len(arrays),
        out_specs=whole,
        out_shape=jax.ShapeDtypeStruct((requests, count, HD), jnp.bfloat16),
        scratch_shapes=[pltpu.VMEM((slots, count, HD), jnp.float32)] * 3
        + [pltpu.VMEM((requests, count, HD), jnp.float32)] * 3,
        compiler_params=pltpu.CompilerParams(vmem_limit_bytes=VMEM_LIMIT),
        cost_estimate=SHORT,
        name="attend",
    )(slot_request, *arrays)


def slot_layout(request_length, block_table, slots, stripe):
    requests, most = block_table.shape
    stripes = (request_length + stripe - 1) // stripe
    columns = jnp.arange(most, dtype=jnp.int32)
    held = columns[None, :] < stripes[:, None]
    hit = held[:, :, None] & (
        block_table[:, :, None] == jnp.arange(slots, dtype=jnp.int32)[None, None, :]
    )
    hit = hit.astype(jnp.int32)
    order = jnp.arange(requests, dtype=jnp.int32)
    request = jnp.sum(hit * order[:, None, None], (0, 1))
    rank = jnp.sum(hit * columns[None, :, None], (0, 1))
    length = jnp.sum(hit * request_length[:, None, None], (0, 1))
    return request, rank, length


def arrange_kernel(chip, even, odd, even_scale, odd_scale, after, kept, sent):
    slots = even.shape[0]
    for blocks, scale, target in ((even, even_scale, kept), (odd, odd_scale, sent)):
        target[0, : slots * BLK, :] = blocks[:, 0].reshape(slots * BLK, 2 * HD)
        target[0, slots * BLK :, :] = scale[0]


def arrange(chip, cache_pool, scales, after):
    slots = cache_pool.shape[0]
    pool = [
        pl.BlockSpec(
            (slots, 1, BLK, 2 * HD), lambda i, c, side=side: (0, c[0] ^ (2 * i + side), 0, 0)
        )
        for side in (0, 1)
    ]
    scale = [
        pl.BlockSpec((1, TILE, 2 * HD), lambda i, c, side=side: (c[0] ^ (2 * i + side), 0, 0))
        for side in (0, 1)
    ]
    rows = slots * BLK + TILE
    out = pl.BlockSpec((1, rows, 2 * HD), lambda i, c: (i, 0, 0))
    shape = jax.ShapeDtypeStruct((KVH // 2, rows, 2 * HD), jnp.bfloat16)
    return pl.pallas_call(
        arrange_kernel,
        grid_spec=pltpu.PrefetchScalarGridSpec(
            num_scalar_prefetch=1,
            grid=(KVH // 2,),
            in_specs=pool + scale + [pl.BlockSpec(memory_space=pl.ANY)],
            out_specs=[out, out],
        ),
        out_shape=[shape, shape],
        compiler_params=pltpu.CompilerParams(vmem_limit_bytes=VMEM_LIMIT),
        cost_estimate=SHORT,
        name="arrange",
    )(chip, cache_pool, cache_pool, scales, scales, after)


SPLIT = (((0, 0), (0, 2), (1, 0), (1, 2)), ((0, 1), (0, 3), (1, 1), (1, 3)))


def regroup_kernel(index_of, kept, landed, *refs):
    out_kept, out_sent = refs[-2:]
    for target, (source, index) in enumerate(index_of[0]):
        out_kept[target] = (kept, landed)[source][index]
    for target, (source, index) in enumerate(index_of[1]):
        out_sent[target] = (kept, landed)[source][index]


def regroup(index_of, kept, landed, after):
    whole = pl.BlockSpec(memory_space=pltpu.VMEM)
    shape = jax.ShapeDtypeStruct(kept.shape, kept.dtype)
    return pl.pallas_call(
        functools.partial(regroup_kernel, index_of),
        in_specs=[whole, whole] + [pl.BlockSpec(memory_space=pl.ANY)] * len(after),
        out_specs=[whole, whole],
        out_shape=[shape, shape],
        compiler_params=pltpu.CompilerParams(vmem_limit_bytes=VMEM_LIMIT),
        cost_estimate=SHORT,
        name="regroup",
    )(kept, landed, *after)


def local_pairs(
    hidden_in,
    norm_gain,
    qkv_weight,
    out_weight,
    cache_pool,
    cache_scale,
    request_length,
    block_table,
):
    devices = lax.axis_size("tensor")
    device = lax.axis_index("tensor")
    core = device % 2
    chip = device // 2
    stripe = devices * BLK
    slots = cache_pool.shape[0]
    requests = request_length.shape[0]
    rows = STEPS * requests * QR
    width = hidden_in.shape[2]
    heads = GQ // 2

    hidden = hidden_in.astype(jnp.float32)
    sums = jnp.sum(hidden * hidden, -1)
    for bit in MESH_BITS:
        sums = sums + swap(sums, bit)
        if bit == 2:
            early = sums
    normed = (
        hidden * lax.rsqrt(sums[..., None] / D + EPSILON) * norm_gain.astype(jnp.float32)
    ).astype(jnp.bfloat16)
    normed = normed.reshape(rows, width)
    bits = [jnp.reshape((device >> b) & 1, (1,)).astype(jnp.int32) for b in range(4)]
    scale_rows = jnp.pad(
        jnp.transpose(cache_scale, (1, 2, 0)).reshape(KVH, 1, 2 * slots),
        ((0, 0), (0, TILE - 1), (0, 2 * HD - 2 * slots)),
    )
    chip_scalar = jnp.reshape(chip, (1,)).astype(jnp.int32)
    cache_kept, cache_sent = arrange(chip_scalar, cache_pool, scale_rows, early)
    cache_landed = swap(cache_sent, 2)

    step_ids = jnp.arange(STEPS, dtype=jnp.int32)
    row_ids = jnp.arange(QR, dtype=jnp.int32)
    position = (
        request_length[None, :, None] + QR * step_ids[:, None, None] + row_ids[None, None, :]
    )
    freqs = ROPE_BASE ** (-(jnp.arange(HD // 2, dtype=jnp.float32) * 2.0 / HD))
    angles = position.reshape(rows, 1).astype(jnp.float32) * freqs
    cosine = jnp.concatenate([jnp.cos(angles)] * 2, 1)
    sine = jnp.concatenate([-jnp.sin(angles), jnp.sin(angles)], 1)

    count = GQ // 4
    held, sent = [None] * count, [None] * count

    def folded(chunk, b, *after):
        held[chunk], sent[chunk] = fold(
            bits[b], held[chunk], swap(sent[chunk], MESH_BITS[b - 1]), after
        )

    def projected(chunk, *after):
        held[chunk], sent[chunk] = project(
            bits[0], normed, qkv_weight, chunk, chunk == 0, after
        )

    projected(0, cache_kept)
    projected(1, held[0])
    cache_kept, cache_sent = regroup(SPLIT, cache_kept, cache_landed, (held[1],))
    cache_landed = swap(cache_sent, 4)
    projected(2, cache_kept)
    projected(3, held[2])
    folded(0, 1, held[3])
    folded(1, 1, held[0])
    folded(2, 1, held[1])
    cache_kept, cache_sent = regroup(SPLIT, cache_kept, cache_landed, (held[2],))
    cache_landed = swap(cache_sent, 8)
    kept_other = swap(cache_kept, 1)
    folded(3, 1, cache_kept)
    folded(0, 2, held[3])
    folded(1, 2, held[0])
    folded(0, 3, held[1])
    folded(2, 2, held[0])
    folded(1, 3, held[2])

    def finished(chunk, *after):
        return finish(
            bits[0], held[chunk], swap(sent[chunk], MESH_BITS[3]), cosine, sine, after
        )

    query_chunks = [None] * count
    query_chunks[0], pair = finished(0, held[1])
    pair_other = swap(pair, 1)
    folded(3, 2, query_chunks[0])
    folded(2, 3, held[3])
    (query_chunks[1],) = finished(1, held[2])
    folded(3, 3, query_chunks[1], pair_other)
    (query_chunks[2],) = finished(2, held[3])
    landed_other = swap(cache_landed, 1)
    (query_chunks[3],) = finished(3, query_chunks[2])
    cache_parts = (cache_kept, cache_landed, kept_other, landed_other)
    keys = jnp.where(core == 0, pair, pair_other)
    raw_values = jnp.where(core == 0, pair_other, pair)
    queries = jnp.concatenate(query_chunks, 1).reshape(STEPS, requests, QR, heads, HD)
    queries = jnp.transpose(queries, (1, 0, 2, 3, 4)).reshape(requests, STEPS * QR * heads, HD)

    def by_request(value):
        value = jnp.transpose(value.reshape(STEPS, requests, QR, HD), (1, 0, 2, 3))
        value = value.reshape(requests, STEPS * QR, HD)
        return jnp.pad(value, ((0, 0), (0, TILE - STEPS * QR), (0, 0)))

    slot_request, slot_rank, slot_length = slot_layout(request_length, block_table, slots, stripe)
    source = chip ^ jnp.arange(KVH, dtype=jnp.int32)
    sources = jnp.stack([source * 2 + core, source * 2 + 1 - core])
    offset = sources[:, :, None] * BLK + jnp.arange(BLK, dtype=jnp.int32)[None, None, :]
    token = slot_rank[:, None] * stripe + offset.reshape(1, stripe)
    cache_bias = jnp.where(token < slot_length[:, None], 0.0, NEG_FILL).astype(jnp.float32)
    scales = jnp.concatenate([part[:, slots * BLK, : 2 * slots] for part in cache_parts])
    scales = scales.astype(jnp.float32).reshape(2 * KVH, 2, slots)
    scales = jnp.repeat(jnp.transpose(scales, (1, 2, 0)), BLK, axis=2)
    order = jnp.arange(STEPS * QR * heads, dtype=jnp.int32) // heads
    key_order = jnp.arange(TILE, dtype=jnp.int32)
    new_bias = jnp.where(key_order[None, :] <= order[:, None], 0.0, NEG_FILL).astype(jnp.float32)
    attention = attend(
        slot_request,
        queries,
        by_request(keys),
        by_request(raw_values),
        *cache_parts,
        scales[0] * HD ** (-0.5),
        scales[1],
        cache_bias,
        new_bias,
    )
    attention = jnp.transpose(
        attention.reshape(requests, STEPS, QR, heads, HD), (1, 0, 2, 3, 4)
    ).reshape(rows, heads * HD)
    mixed = gather_and_mix(attention, out_weight, hidden_in.reshape(rows, width), device)
    return mixed.reshape(hidden_in.shape)


def solution(mesh):
    return jax.shard_map(
        local_pairs if mesh.shape["tensor"] == 2 * KVH else local_general,
        mesh=mesh,
        in_specs=(
            P(None, "groups", "tensor"),
            P("tensor"),
            P("tensor", None),
            P(None, "tensor"),
            P(("groups", "tensor"), None, None, None),
            P(("groups", "tensor"), None, None),
            P("groups"),
            P("groups", None),
        ),
        out_specs=P(None, "groups", "tensor"),
        check_vma=False,
    )
```

```python
import functools

import jax
import jax.numpy as jnp
from jax import lax
from jax.experimental import pallas as pl
from jax.experimental.pallas import tpu as pltpu
from jax.sharding import PartitionSpec as P

D = 16384
QH = 128
KVH = 8
HD = 128
QR = 6
STEPS = 2
BLK = 16
GQ = 16
GW = 2304


EPSILON = 1e-05
ROPE_BASE = 500000.0
NEG_FILL = -1e30


def rotate(values, positions):
    half = values.shape[-1] // 2
    freqs = ROPE_BASE ** (-(jnp.arange(half, dtype=jnp.float32) * 2.0 / values.shape[-1]))
    angles = positions.astype(jnp.float32)[..., None] * freqs
    cosine = jnp.cos(angles)
    sine = jnp.sin(angles)
    first = values[..., :half]
    second = values[..., half:]
    return jnp.concatenate([first * cosine - second * sine, second * cosine + first * sine], -1)


def request_layout(request_owner, request_length, block_table, owners, stripe):
    requests = request_owner.shape[0]
    most = block_table.shape[1]
    order = jnp.arange(requests, dtype=jnp.int32)
    stripes = (request_length + stripe - 1) // stripe
    before = (
        (request_owner[None, :] == request_owner[:, None]) & (order[None, :] < order[:, None])
    ).astype(jnp.int32)
    rank = jnp.sum(before, 1)
    offset = jnp.sum(before * stripes[None, :], 1)
    owner_ids = jnp.arange(owners, dtype=jnp.int32)
    mine = request_owner[None, :] == owner_ids[:, None]
    member = mine[:, :, None] & (
        rank[None, :, None] == jnp.arange(requests // owners, dtype=jnp.int32)[None, None, :]
    )
    owner_requests = jnp.sum(member.astype(jnp.int32) * order[None, :, None], 1)
    columns = jnp.arange(most, dtype=jnp.int32)
    within = columns[None, None, :] - offset[None, :, None]
    hit = (mine[:, :, None] & (within >= 0) & (within < stripes[None, :, None])).astype(jnp.int32)
    stripe_request = jnp.sum(hit * order[None, :, None], 1) - (1 - jnp.sum(hit, 1))
    stripe_rank = jnp.sum(hit * within, 1)
    pick = (within[..., None] == columns[None, None, None, :]).astype(jnp.int32)
    slots = jnp.sum(hit[..., None] * pick * block_table[None, :, None, :], (1, 3))
    return (owner_requests, stripe_request, stripe_rank, slots, rank, stripes)


def cache_partial(queries, keys, values, key_scale, value_scale, mask):
    scores = jnp.einsum("srgd,td->srgt", queries, keys, preferred_element_type=jnp.float32)
    scores = jnp.where(mask, scores * key_scale * HD ** (-0.5), NEG_FILL)
    best = jnp.max(scores, -1)
    expo = jnp.where(mask, jnp.exp(scores - best[..., None]), 0.0)
    total = jnp.sum(expo, -1)
    weights = (expo * value_scale).astype(jnp.bfloat16)
    summed = jnp.einsum("srgt,td->srgd", weights, values, preferred_element_type=jnp.float32)
    return (best, total, summed)


def local_general(
    hidden_in,
    norm_gain,
    qkv_weight,
    out_weight,
    cache_pool,
    cache_scale,
    request_length,
    block_table,
):
    devices = lax.axis_size("tensor")
    device = lax.axis_index("tensor")
    owners = devices // KVH
    stripe = devices * BLK
    requests = request_length.shape[0]
    request_owner = jnp.arange(requests, dtype=jnp.int32) % owners
    unit_rows = requests // owners * QR
    most = block_table.shape[1]
    local_width = hidden_in.shape[2]
    my_owner = device // KVH
    owner_requests, stripe_request, stripe_rank, slots, rank, stripes = request_layout(
        request_owner, request_length, block_table, owners, stripe
    )
    step_rows = jnp.arange(QR, dtype=jnp.int32)
    row_order = (owner_requests[:, :, None] * QR + step_rows[None, None, :]).reshape(
        owners * unit_rows
    )
    inverse = ((request_owner * unit_rows + rank * QR)[:, None] + step_rows[None, :]).reshape(
        requests * QR
    )
    row_request = jnp.repeat(owner_requests[my_owner], QR)
    row_length = request_length[row_request]
    row_step = jnp.arange(unit_rows, dtype=jnp.int32) % QR
    same_request = row_request[:, None] == row_request[None, :]
    gain = norm_gain.astype(jnp.float32)
    weight_grouped = qkv_weight.reshape(local_width, KVH, GW)
    sent = cache_pool[jnp.transpose(slots)].reshape(most, devices, BLK, 2 * HD)
    sent_scale = cache_scale[jnp.transpose(slots)].reshape(most, devices, 2)
    landed, landed_scale = (
        lax.all_to_all(sent, "tensor", split_axis=1, concat_axis=1, tiled=True),
        lax.all_to_all(sent_scale, "tensor", split_axis=1, concat_axis=1, tiled=True),
    )
    cache_data = landed.reshape(most * stripe, 2 * HD)
    token_scale = jnp.broadcast_to(
        landed_scale.astype(jnp.float32)[:, :, None, :], (most, devices, BLK, 2)
    ).reshape(most * stripe, 2)
    token = jnp.arange(most * stripe, dtype=jnp.int32)
    token_stripe = token // stripe
    token_request = stripe_request[my_owner][token_stripe]
    token_position = stripe_rank[my_owner][token_stripe] * stripe + token % stripe
    token_length = jnp.where(token_request >= 0, request_length[jnp.maximum(token_request, 0)], 0)
    cache_mask = (
        (token_request[None, :] == row_request[:, None]) & (token_position < token_length)[None, :]
    )[None, :, None, :]
    outputs = []
    keys_seen = []
    values_seen = []
    for step in range(STEPS):
        block = hidden_in[step : step + 1]
        project_count = block.shape[0]
        values = block.astype(jnp.float32)
        sums = lax.psum(jnp.sum(values * values, -1), "tensor")
        normed = (values * lax.rsqrt(sums[..., None] / D + EPSILON) * gain).astype(jnp.bfloat16)
        ordered = jnp.take(normed, row_order, axis=1).reshape(
            project_count, owners, unit_rows, local_width
        )
        term = jnp.einsum(
            "sojd,dhg->ohsjg", ordered, weight_grouped, preferred_element_type=jnp.float32
        )
        term = term.reshape(owners * KVH * project_count * unit_rows, GW)
        mine = lax.psum_scatter(term, "tensor", scatter_dimension=0, tiled=True)
        joined_block = mine.astype(jnp.bfloat16).reshape(project_count, unit_rows, GW)
        prepare_count = joined_block.shape[0]
        steps_here = step + jnp.arange(prepare_count, dtype=jnp.int32)
        position = row_length[None, :] + QR * steps_here[:, None] + row_step[None, :]
        prepare_queries = rotate(
            joined_block[..., : GQ * HD]
            .reshape(prepare_count, unit_rows, GQ, HD)
            .astype(jnp.float32),
            position[:, :, None],
        ).astype(jnp.bfloat16)
        keys = rotate(
            joined_block[..., GQ * HD : GQ * HD + HD].astype(jnp.float32), position
        ).astype(jnp.bfloat16)
        queries, keys, values = (prepare_queries, keys, joined_block[..., GQ * HD + HD :])
        keys_seen.append(keys)
        values_seen.append(values)
        keys_all = jnp.concatenate(keys_seen, 0)
        attend_count = queries.shape[0]
        cache_best, cache_total, cache_summed = cache_partial(
            queries,
            cache_data[:, :HD],
            cache_data[:, HD:],
            token_scale[:, 0],
            token_scale[:, 1],
            cache_mask,
        )
        news = jnp.einsum(
            "srgd,pjd->srgpj", queries, keys_all, preferred_element_type=jnp.float32
        ) * HD ** (-0.5)
        query_step = step + jnp.arange(attend_count, dtype=jnp.int32)[:, None, None, None]
        key_step = jnp.arange(keys_all.shape[0], dtype=jnp.int32)[None, None, :, None]
        allowed = (key_step < query_step) | (key_step == query_step) & (
            row_step[None, None, None, :] <= row_step[None, :, None, None]
        )
        allowed = (allowed & same_request[None, :, None, :])[:, :, None, :, :]
        news = jnp.where(allowed, news, NEG_FILL)
        best = jnp.maximum(cache_best, jnp.max(news, (3, 4)))
        factor = jnp.exp(cache_best - best)
        expo = jnp.where(allowed, jnp.exp(news - best[..., None, None]), 0.0)
        total = cache_total * factor + jnp.sum(expo, (3, 4))
        summed = cache_summed * factor[..., None] + jnp.einsum(
            "srgpj,pjd->srgd",
            expo.astype(jnp.bfloat16),
            jnp.concatenate(values_seen, 0),
            preferred_element_type=jnp.float32,
        )
        attention = (
            (summed / total[..., None])
            .astype(jnp.bfloat16)
            .reshape(attend_count, unit_rows, GQ * HD)
        )
        count = attention.shape[0]
        gathered = lax.all_gather(attention, "tensor", axis=2, tiled=True).reshape(
            count, unit_rows, owners, QH * HD
        )
        mixed = jnp.einsum(
            "sjof,fd->sojd", gathered, out_weight, preferred_element_type=jnp.float32
        )
        mixed = jnp.take(mixed.reshape(count, owners * unit_rows, local_width), inverse, axis=1)
        outputs.append(
            (hidden_in[step : step + count].astype(jnp.float32) + mixed).astype(jnp.bfloat16)
        )
    return jnp.concatenate(outputs, 0)


MIB = 1024 * 1024
SHORT = pl.CostEstimate(flops=1, bytes_accessed=1, transcendentals=0)
LOW_BITS = 4
PACKED = 16 // LOW_BITS
LEVELS = 32600.0 * 2**LOW_BITS
POWER_STEPS = 8.0
TILE = 16
MESH_BITS = (1, 2, 4, 8)


def swap(value, bit):
    devices = lax.axis_size("tensor")
    return lax.ppermute(value, "tensor", [(i, i ^ bit) for i in range(devices)])


def no_work(*refs):
    del refs


def together(*arrays):
    anywhere = pl.BlockSpec(memory_space=pl.ANY)
    return pl.pallas_call(
        no_work,
        in_specs=[anywhere] * len(arrays),
        out_specs=[anywhere] * len(arrays),
        out_shape=[jax.ShapeDtypeStruct(a.shape, a.dtype) for a in arrays],
        input_output_aliases={i: i for i in range(len(arrays))},
        cost_estimate=SHORT,
        name="together",
    )(*arrays)


def coded_rows(rows):
    return rows + rows // PACKED


def encode(block):
    top = jnp.max(jnp.abs(block), 0, keepdims=True)
    power = jnp.ceil(jnp.log2(jnp.maximum(top, 1e-30)) * POWER_STEPS)
    codes = jnp.round(block * (jnp.exp2(power * (-1.0 / POWER_STEPS)) * LEVELS)).astype(jnp.int32)
    low = codes & (2**LOW_BITS - 1)
    part = block.shape[0] // PACKED
    packed = low[:part]
    for i in range(1, PACKED):
        packed = packed + (low[i * part : (i + 1) * part] << (LOW_BITS * i))
    high = (codes >> LOW_BITS).astype(jnp.int16)
    return jnp.concatenate([high, (packed - 32768).astype(jnp.int16)], 0), power


def decode(codes, power):
    rows = codes.shape[0] * PACKED // (PACKED + 1)
    high = codes[:rows].astype(jnp.int32) << LOW_BITS
    packed = codes[rows:].astype(jnp.int32) + 32768
    low = jnp.concatenate(
        [(packed >> (LOW_BITS * i)) & (2**LOW_BITS - 1) for i in range(PACKED)], 0
    )
    scale = jnp.exp2(power * (1.0 / POWER_STEPS)) * (1.0 / LEVELS)
    return (high + low).astype(jnp.float32) * scale


def pick_row(rows, index):
    ids = lax.broadcasted_iota(jnp.int32, rows.shape, 0)
    return jnp.sum(jnp.where(ids == index, rows, 0.0), 0, keepdims=True)


def store_codes(sent, powers, block, index, steps):
    rows = coded_rows(block.shape[0])
    codes, power = encode(block)
    sent[pl.ds(pl.multiple_of(index * rows, TILE), rows), :] = codes

    powers[pl.ds(index, 1), :] = power

    @pl.when(index == steps - 1)
    def _():
        sent[pl.ds(steps * rows, TILE), :] = powers[...].astype(jnp.int32).astype(jnp.int16)


def project_kernel(chunk, with_pair, core, normed, weights, *refs):
    kept, sent, powers, wide, arrived = refs[-5:]
    index = pl.program_id(0)
    columns = kept.shape[2]

    def copies(group):
        found = []
        for side in range(2):
            owner = core[0] if side == 0 else 1 - core[0]
            first = group * GW + owner * (GQ // 2 * HD) + chunk * (2 * HD)
            spans = [(first, 0, 2 * HD)]
            if with_pair:
                spans.append((group * GW + (GQ + owner) * HD, 2 * HD, HD))
            for number, (start, offset, size) in enumerate(spans):
                found.append(
                    pltpu.make_async_copy(
                        weights.at[:, pl.ds(pl.multiple_of(start, HD), size)],
                        wide.at[group, :, pl.ds(side * columns + offset, size)],
                        arrived.at[group, side, number],
                    )
                )
        return found

    @pl.when(index == 0)
    def _():
        for group in range(KVH):
            for copy in copies(group):
                copy.start()
        powers[...] = jnp.zeros_like(powers)

    for copy in copies(index):
        copy.wait()

    product = jnp.dot(normed[...], wide[index], preferred_element_type=jnp.float32)
    kept[0] = product[:, :columns]
    store_codes(sent, powers, product[:, columns:], index, KVH)


def project(core, normed, qkv_weight, chunk, with_pair, after):
    rows, width = normed.shape
    columns = 2 * HD + (HD if with_pair else 0)
    sent_rows = KVH * coded_rows(rows) + TILE
    return pl.pallas_call(
        functools.partial(project_kernel, chunk, with_pair),
        grid_spec=pltpu.PrefetchScalarGridSpec(
            num_scalar_prefetch=1,
            grid=(KVH,),
            in_specs=[pl.BlockSpec((rows, width), lambda t, c: (0, 0))]
            + [pl.BlockSpec(memory_space=pl.ANY)] * (1 + len(after)),
            out_specs=[
                pl.BlockSpec((1, rows, columns), lambda t, c: (t, 0, 0)),
                pl.BlockSpec((sent_rows, columns), lambda t, c: (0, 0)),
            ],
            scratch_shapes=[
                pltpu.VMEM((TILE, columns), jnp.float32),
                pltpu.VMEM((KVH, width, 2 * columns), jnp.bfloat16),
                pltpu.SemaphoreType.DMA((KVH, 2, 2)),
            ],
        ),
        out_shape=[
            jax.ShapeDtypeStruct((KVH, rows, columns), jnp.float32),
            jax.ShapeDtypeStruct((sent_rows, columns), jnp.int16),
        ],
        compiler_params=pltpu.CompilerParams(vmem_limit_bytes=24 * MIB),
        cost_estimate=SHORT,
        name="project",
    )(core, normed, qkv_weight, *after)


def fold_kernel(steps, bit, held, landed, landed_powers, *refs):
    kept, sent, powers = refs[-3:]
    index = pl.program_id(0)
    rows = coded_rows(held.shape[1])
    rows_of_powers = landed_powers[...].astype(jnp.int32).astype(jnp.float32)

    def total(side):
        place = pl.multiple_of(side * rows, TILE)
        codes = landed[pl.ds(place, rows), :]
        return held[side] + decode(codes, pick_row(rows_of_powers, 2 * index + side))

    @pl.when(index == 0)
    def _():
        powers[...] = jnp.zeros_like(powers)

    mine = bit[0]
    kept[0] = total(mine)
    store_codes(sent, powers, total(1 - mine), index, steps)


def fold(bit, held, landed, after):
    blocks, rows, columns = held.shape
    steps = blocks // 2
    coded = coded_rows(rows)
    return pl.pallas_call(
        functools.partial(fold_kernel, steps),
        grid_spec=pltpu.PrefetchScalarGridSpec(
            num_scalar_prefetch=1,
            grid=(steps,),
            in_specs=[
                pl.BlockSpec((2, rows, columns), lambda i, b: (i, 0, 0)),
                pl.BlockSpec((2 * coded, columns), lambda i, b: (i, 0)),
                pl.BlockSpec((TILE, columns), lambda i, b: (blocks * coded // TILE, 0)),
            ]
            + [pl.BlockSpec(memory_space=pl.ANY)] * len(after),
            out_specs=[
                pl.BlockSpec((1, rows, columns), lambda i, b: (i, 0, 0)),
                pl.BlockSpec((steps * coded + TILE, columns), lambda i, b: (0, 0)),
            ],
            scratch_shapes=[pltpu.VMEM((TILE, columns), jnp.float32)],
        ),
        out_shape=[
            jax.ShapeDtypeStruct((steps, rows, columns), jnp.float32),
            jax.ShapeDtypeStruct((steps * coded + TILE, columns), jnp.int16),
        ],
        compiler_params=pltpu.CompilerParams(vmem_limit_bytes=12 * MIB),
        cost_estimate=SHORT,
        name="fold",
    )(bit, held, landed, landed, *after)


def finish_kernel(after_count, core, held, landed, cosine, sine, *refs):
    queries, *pair = refs[after_count:]
    rows = held.shape[1]
    coded = coded_rows(rows)
    power = landed[pl.ds(coded, TILE), :].astype(jnp.int32).astype(jnp.float32)[0:1]
    total = held[0] + decode(landed[pl.ds(0, coded), :], power)
    joined = total.astype(jnp.bfloat16)
    parts = []
    for head in range(joined.shape[1] // HD):
        raw = joined[:, head * HD : (head + 1) * HD]
        wide = raw.astype(jnp.float32)
        turned = wide * cosine[...] + pltpu.roll(wide, HD // 2, 1) * sine[...]
        parts.append((raw, turned.astype(jnp.bfloat16)))
    queries[...] = jnp.concatenate([parts[0][1], parts[1][1]], 1)
    if pair:
        raw, turned = parts[2]
        pair[0][...] = jnp.where(core[0] == 0, turned.astype(jnp.float32), raw.astype(jnp.float32)).astype(
            jnp.bfloat16
        )


def finish(core, held, landed, cosine, sine, after):
    _, rows, columns = held.shape
    whole = pl.BlockSpec(memory_space=pltpu.VMEM)
    shapes = [jax.ShapeDtypeStruct((rows, 2 * HD), jnp.bfloat16)]
    if columns > 2 * HD:
        shapes.append(jax.ShapeDtypeStruct((rows, HD), jnp.bfloat16))
    return pl.pallas_call(
        functools.partial(finish_kernel, len(after)),
        in_specs=[pl.BlockSpec(memory_space=pltpu.SMEM)]
        + [whole] * 4
        + [pl.BlockSpec(memory_space=pl.ANY)] * len(after),
        out_specs=[whole] * len(shapes),
        out_shape=shapes,
        compiler_params=pltpu.CompilerParams(vmem_limit_bytes=6 * MIB),
        cost_estimate=SHORT,
        name="finish",
    )(core, held, landed, cosine, sine, *after)


def mix_kernel(count, places, *refs):
    pieces = refs[:count]
    weights, start, mixed, total, wide, arrived = refs[count:]
    depth = wide.shape[1]
    columns = wide.shape[2] // 2
    flat = []
    for piece in pieces:
        flat += [piece] if len(piece.shape) == 2 else [piece.at[i] for i in range(piece.shape[0])]
    copies = [
        pltpu.make_async_copy(
            weights.at[pl.ds(pl.multiple_of(places[i] * depth, depth), depth), :],
            wide.at[i],
            arrived.at[i],
        )
        for i in range(len(flat))
    ]
    for copy in copies:
        copy.start()
    cuts = [0, 1, 2, 4, len(flat)]
    cuts = sorted(set(min(cut, len(flat)) for cut in cuts))
    for first, last in zip(cuts, cuts[1:]):
        for copy in copies[first:last]:
            copy.wait()
        for side in range(2):
            span = pl.ds(side * columns, columns)
            source = start if first == 0 else total
            value = source[:, span].astype(jnp.float32)
            for i in range(first, last):
                value = value + jnp.dot(
                    flat[i][...], wide[i, :, span], preferred_element_type=jnp.float32
                )
            target = mixed if last == len(flat) else total
            target[:, span] = value.astype(target.dtype)


def mix(places, pieces, out_weight, start, dtype):
    columns = out_weight.shape[1]
    rows, width = pieces[0].shape[-2:]
    count = sum(1 if len(p.shape) == 2 else p.shape[0] for p in pieces)
    whole = pl.BlockSpec(memory_space=pltpu.VMEM)
    return pl.pallas_call(
        functools.partial(mix_kernel, len(pieces)),
        in_specs=[pl.BlockSpec(memory_space=pltpu.SMEM)]
        + [whole] * len(pieces)
        + [pl.BlockSpec(memory_space=pl.ANY), whole],
        out_specs=whole,
        scratch_shapes=[
            pltpu.VMEM((rows, columns), jnp.float32),
            pltpu.VMEM((count, width, columns), jnp.bfloat16),
            pltpu.SemaphoreType.DMA((count,)),
        ],
        out_shape=jax.ShapeDtypeStruct((rows, columns), dtype),
        compiler_params=pltpu.CompilerParams(vmem_limit_bytes=32 * MIB),
        cost_estimate=SHORT,
        name="mix",
    )(places, *pieces, out_weight, start)


def gather_and_mix(attention, out_weight, start, device):
    def add(mixed, pieces, offsets, dtype=jnp.float32):
        places = jnp.stack([device ^ offset for offset in offsets])
        return mix(places, pieces, out_weight, mixed, dtype)

    near = swap(attention, 4)
    across = swap(attention, 2)
    far = swap(attention, 8)
    partner = swap(attention, 1)
    near, across, far, partner = together(near, across, far, partner)

    across_near = swap(near, 2)
    across_far = swap(far, 2)
    farthest = swap(attention, 12)
    first = jnp.stack([near, across, far])
    first_partner = swap(first, 1)
    mixed = add(start, [attention, partner], (0, 1))
    across_near, across_far, farthest, first_partner, mixed = together(
        across_near, across_far, farthest, first_partner, mixed
    )

    last = swap(farthest, 2)
    second = jnp.stack([across_near, across_far, farthest])
    second_partner = swap(second, 1)
    mixed = add(mixed, [first, first_partner], (4, 2, 8, 5, 3, 9))
    last, second_partner, mixed = together(last, second_partner, mixed)

    last_partner = swap(last, 1)
    mixed = add(mixed, [second, second_partner], (6, 10, 12, 7, 11, 13))
    return add(mixed, [last, last_partner], (14, 15), jnp.bfloat16)


def attend_kernel(
    slot_request,
    queries,
    new_keys,
    new_values,
    own_near,
    own_far,
    other_near,
    other_far,
    key_scale,
    value_scale,
    cache_bias,
    new_bias,
    attention,
    slot_best,
    slot_total,
    slot_sum,
    best,
    total,
    summed,
):
    slots = slot_best.shape[0]
    requests, count, _ = queries.shape
    transposed = (((1,), (1,)), ((), ()))
    for request in range(requests):
        scores = (
            lax.dot_general(
                queries[request],
                new_keys[request],
                transposed,
                preferred_element_type=jnp.float32,
            )
            * HD ** (-0.5)
            + new_bias[...]
        )
        top = jnp.max(scores, -1, keepdims=True)
        expo = jnp.exp(scores - top)
        best[request] = jnp.broadcast_to(top, (count, HD))
        total[request] = jnp.broadcast_to(jnp.sum(expo, -1, keepdims=True), (count, HD))
        summed[request] = jnp.dot(
            expo.astype(jnp.bfloat16), new_values[request], preferred_element_type=jnp.float32
        )
    for slot in range(slots):
        request = slot_request[slot]
        query = queries[request]
        raw = [
            part[:, slot * BLK : (slot + 1) * BLK, :].reshape(KVH // 2 * BLK, 2 * HD)
            for part in (own_near, own_far, other_near, other_far)
        ]
        scores = jnp.concatenate(
            [
                lax.dot_general(
                    query, kv[:, :HD], transposed, preferred_element_type=jnp.float32
                )
                for kv in raw
            ],
            1,
        )
        scores = scores * key_scale[slot : slot + 1, :] + cache_bias[slot : slot + 1, :]
        top = jnp.max(scores, -1, keepdims=True)
        expo = jnp.exp(scores - top)
        weights = (expo * value_scale[slot : slot + 1, :]).astype(jnp.bfloat16)
        slot_best[slot] = jnp.broadcast_to(top, (count, HD))
        slot_total[slot] = jnp.broadcast_to(jnp.sum(expo, -1, keepdims=True), (count, HD))
        values = jnp.concatenate([kv[:, HD:] for kv in raw], 0)
        slot_sum[slot] = jnp.dot(weights, values, preferred_element_type=jnp.float32)
    for slot in range(slots):
        request = slot_request[slot]
        before = best[request]
        here = slot_best[slot]
        top = jnp.maximum(before, here)
        keep = jnp.exp(before - top)
        add = jnp.exp(here - top)
        best[request] = top
        total[request] = total[request] * keep + slot_total[slot] * add
        summed[request] = summed[request] * keep + slot_sum[slot] * add
    for request in range(requests):
        attention[request] = (summed[request] / total[request]).astype(jnp.bfloat16)


def attend(slot_request, *arrays):
    queries = arrays[0]
    slots = arrays[7].shape[0]
    requests, count, _ = queries.shape
    whole = pl.BlockSpec(memory_space=pltpu.VMEM)
    return pl.pallas_call(
        attend_kernel,
        in_specs=[pl.BlockSpec(memory_space=pltpu.SMEM)] + [whole] * len(arrays),
        out_specs=whole,
        out_shape=jax.ShapeDtypeStruct((requests, count, HD), jnp.bfloat16),
        scratch_shapes=[pltpu.VMEM((slots, count, HD), jnp.float32)] * 3
        + [pltpu.VMEM((requests, count, HD), jnp.float32)] * 3,
        compiler_params=pltpu.CompilerParams(vmem_limit_bytes=24 * MIB),
        cost_estimate=SHORT,
        name="attend",
    )(slot_request, *arrays)


def slot_layout(request_length, block_table, slots, stripe):
    requests, most = block_table.shape
    stripes = (request_length + stripe - 1) // stripe
    columns = jnp.arange(most, dtype=jnp.int32)
    held = columns[None, :] < stripes[:, None]
    hit = held[:, :, None] & (
        block_table[:, :, None] == jnp.arange(slots, dtype=jnp.int32)[None, None, :]
    )
    hit = hit.astype(jnp.int32)
    order = jnp.arange(requests, dtype=jnp.int32)
    request = jnp.sum(hit * order[:, None, None], (0, 1))
    rank = jnp.sum(hit * columns[None, :, None], (0, 1))
    length = jnp.sum(hit * request_length[:, None, None], (0, 1))
    return request, rank, length


def arrange_kernel(chip, even, odd, even_scale, odd_scale, after, kept, sent):
    slots = even.shape[0]
    for blocks, scale, target in ((even, even_scale, kept), (odd, odd_scale, sent)):
        target[0, : slots * BLK, :] = blocks[:, 0].reshape(slots * BLK, 2 * HD)
        target[0, slots * BLK :, :] = scale[0]


def arrange(chip, cache_pool, scales, after):
    slots = cache_pool.shape[0]
    pool = [
        pl.BlockSpec(
            (slots, 1, BLK, 2 * HD), lambda i, c, side=side: (0, c[0] ^ (2 * i + side), 0, 0)
        )
        for side in (0, 1)
    ]
    scale = [
        pl.BlockSpec((1, TILE, 2 * HD), lambda i, c, side=side: (c[0] ^ (2 * i + side), 0, 0))
        for side in (0, 1)
    ]
    rows = slots * BLK + TILE
    out = pl.BlockSpec((1, rows, 2 * HD), lambda i, c: (i, 0, 0))
    shape = jax.ShapeDtypeStruct((KVH // 2, rows, 2 * HD), jnp.bfloat16)
    return pl.pallas_call(
        arrange_kernel,
        grid_spec=pltpu.PrefetchScalarGridSpec(
            num_scalar_prefetch=1,
            grid=(KVH // 2,),
            in_specs=pool + scale + [pl.BlockSpec(memory_space=pl.ANY)],
            out_specs=[out, out],
        ),
        out_shape=[shape, shape],
        compiler_params=pltpu.CompilerParams(vmem_limit_bytes=6 * MIB),
        cost_estimate=SHORT,
        name="arrange",
    )(chip, cache_pool, cache_pool, scales, scales, after)


HANDOVER_BITS = (1, 2, 4)


def handover_plan():
    kept = [(0, dest) for dest in range(0, KVH, 2)]
    landed = [(1, dest) for dest in range(0, KVH, 2)]
    splits = []
    for bit in HANDOVER_BITS[1:]:
        entries = [(0, i, e) for i, e in enumerate(kept)] + [
            (1, i, e) for i, e in enumerate(landed)
        ]
        stay = [e for e in entries if not e[2][1] & bit]
        leave = [e for e in entries if e[2][1] & bit]
        splits.append(tuple(tuple((side, i) for side, i, _ in part) for part in (stay, leave)))
        kept = [e for _, _, e in stay]
        landed = [(source ^ bit, dest ^ bit) for _, _, (source, dest) in leave]
    return splits, [source for source, _ in kept + landed]


def regroup_kernel(index_of, kept, landed, *refs):
    out_kept, out_sent = refs[-2:]
    for target, (source, index) in enumerate(index_of[0]):
        out_kept[target] = (kept, landed)[source][index]
    for target, (source, index) in enumerate(index_of[1]):
        out_sent[target] = (kept, landed)[source][index]


def regroup(index_of, kept, landed, after):
    whole = pl.BlockSpec(memory_space=pltpu.VMEM)
    shape = jax.ShapeDtypeStruct(kept.shape, kept.dtype)
    return pl.pallas_call(
        functools.partial(regroup_kernel, index_of),
        in_specs=[whole, whole] + [pl.BlockSpec(memory_space=pl.ANY)] * len(after),
        out_specs=[whole, whole],
        out_shape=[shape, shape],
        compiler_params=pltpu.CompilerParams(vmem_limit_bytes=8 * MIB),
        cost_estimate=SHORT,
        name="regroup",
    )(kept, landed, *after)


def local_pairs(
    hidden_in,
    norm_gain,
    qkv_weight,
    out_weight,
    cache_pool,
    cache_scale,
    request_length,
    block_table,
):
    devices = lax.axis_size("tensor")
    device = lax.axis_index("tensor")
    core = device % 2
    chip = device // 2
    stripe = devices * BLK
    slots = cache_pool.shape[0]
    requests = request_length.shape[0]
    rows = STEPS * requests * QR
    width = hidden_in.shape[2]
    heads = GQ // 2

    hidden = hidden_in.astype(jnp.float32)
    sums = jnp.sum(hidden * hidden, -1)
    bits = [jnp.reshape((device >> b) & 1, (1,)).astype(jnp.int32) for b in range(4)]
    scale_rows = jnp.pad(
        jnp.transpose(cache_scale, (1, 2, 0)).reshape(KVH, 1, 2 * slots),
        ((0, 0), (0, TILE - 1), (0, 2 * HD - 2 * slots)),
    )
    chip_scalar = jnp.reshape(chip, (1,)).astype(jnp.int32)
    sums = sums + swap(sums, 2)
    cache_kept, cache_sent = arrange(chip_scalar, cache_pool, scale_rows, sums)
    cache_landed = swap(cache_sent, 2)
    for bit in (1, 4, 8):
        sums = sums + swap(sums, bit)
    sums, cache_landed = together(sums, cache_landed)
    normed = (
        hidden * lax.rsqrt(sums[..., None] / D + EPSILON) * norm_gain.astype(jnp.float32)
    ).astype(jnp.bfloat16)
    normed = normed.reshape(rows, width)

    step_ids = jnp.arange(STEPS, dtype=jnp.int32)
    row_ids = jnp.arange(QR, dtype=jnp.int32)
    position = (
        request_length[None, :, None] + QR * step_ids[:, None, None] + row_ids[None, None, :]
    )
    freqs = ROPE_BASE ** (-(jnp.arange(HD // 2, dtype=jnp.float32) * 2.0 / HD))
    angles = position.reshape(rows, 1).astype(jnp.float32) * freqs
    cosine = jnp.concatenate([jnp.cos(angles)] * 2, 1)
    sine = jnp.concatenate([-jnp.sin(angles), jnp.sin(angles)], 1)

    count = GQ // 4
    held, sent = [None] * count, [None] * count
    splits, sources_of_cache = handover_plan()

    def projected(chunk, *after):
        held[chunk], sent[chunk] = project(
            bits[0], normed, qkv_weight, chunk, chunk == 0, after
        )

    def hop(chunk, b):
        return swap(sent[chunk], MESH_BITS[b])

    def folded(chunk, b, landed, *after):
        held[chunk], sent[chunk] = fold(bits[b], held[chunk], landed, after)

    def finished(chunk, landed, *after):
        return finish(bits[0], held[chunk], landed, cosine, sine, after)

    projected(0, cache_kept)
    core_0 = hop(0, 0)
    projected(1, held[0])
    core_0, sent[1] = together(core_0, sent[1])

    folded(0, 1, core_0)
    core_1, y_0 = hop(1, 0), hop(0, 1)
    cache_kept, cache_sent = regroup(splits[0], cache_kept, cache_landed, (held[0],))
    cache_landed = swap(cache_sent, 4)
    projected(2, held[0], cache_kept)
    projected(3, held[2])
    core_1, y_0, sent[2], sent[3], cache_landed = together(
        core_1, y_0, sent[2], sent[3], cache_landed
    )

    core_2, core_3 = hop(2, 0), hop(3, 0)
    folded(1, 1, core_1)
    y_1 = hop(1, 1)
    folded(0, 2, y_0, held[1])
    near_0 = hop(0, 2)
    cache_kept, cache_sent = regroup(splits[1], cache_kept, cache_landed, (held[0],))
    cache_landed = swap(cache_sent, 8)
    folded(2, 1, core_2, cache_kept)
    folded(3, 1, core_3, held[2])
    y_1, near_0, sent[2], sent[3] = together(y_1, near_0, sent[2], sent[3])

    y_2 = hop(2, 1)
    folded(0, 3, near_0)
    far_0 = hop(0, 3)
    folded(1, 2, y_1)
    near_1 = hop(1, 2)
    y_2, far_0, near_1 = together(y_2, far_0, near_1)

    y_3 = hop(3, 1)
    folded(1, 3, near_1)
    far_1 = hop(1, 3)
    folded(2, 2, y_2)
    near_2 = hop(2, 2)
    query_chunks = [None] * count
    query_chunks[0], pair = finished(0, far_0, cache_kept)
    pair_other = swap(pair, 1)
    kept_other = swap(cache_kept, 1)
    y_3, far_1, near_2, pair_other, kept_other = together(
        y_3, far_1, near_2, pair_other, kept_other
    )

    folded(3, 2, y_3)
    near_3 = hop(3, 2)
    folded(2, 3, near_2)
    far_2 = hop(2, 3)
    (query_chunks[1],) = finished(1, far_1, held[2])
    near_3, far_2, cache_landed = together(near_3, far_2, cache_landed)
    landed_other = swap(cache_landed, 1)

    folded(3, 3, near_3)
    far_3 = hop(3, 3)
    (query_chunks[2],) = finished(2, far_2, held[3])
    (query_chunks[3],) = finished(3, far_3, query_chunks[2])
    cache_parts = (cache_kept, cache_landed, kept_other, landed_other)
    keys = jnp.where(core == 0, pair, pair_other)
    raw_values = jnp.where(core == 0, pair_other, pair)
    queries = jnp.concatenate(query_chunks, 1).reshape(STEPS, requests, QR, heads, HD)
    queries = jnp.transpose(queries, (1, 0, 2, 3, 4)).reshape(requests, STEPS * QR * heads, HD)

    def by_request(value):
        value = jnp.transpose(value.reshape(STEPS, requests, QR, HD), (1, 0, 2, 3))
        value = value.reshape(requests, STEPS * QR, HD)
        return jnp.pad(value, ((0, 0), (0, TILE - STEPS * QR), (0, 0)))

    slot_request, slot_rank, slot_length = slot_layout(request_length, block_table, slots, stripe)
    source = chip ^ jnp.array(sources_of_cache, dtype=jnp.int32)
    sources = jnp.stack([source * 2 + core, source * 2 + 1 - core])
    offset = sources[:, :, None] * BLK + jnp.arange(BLK, dtype=jnp.int32)[None, None, :]
    token = slot_rank[:, None] * stripe + offset.reshape(1, stripe)
    cache_bias = jnp.where(token < slot_length[:, None], 0.0, NEG_FILL).astype(jnp.float32)
    scales = jnp.concatenate([part[:, slots * BLK, : 2 * slots] for part in cache_parts])
    scales = scales.astype(jnp.float32).reshape(2 * KVH, 2, slots)
    scales = jnp.repeat(jnp.transpose(scales, (1, 2, 0)), BLK, axis=2)
    order = jnp.arange(STEPS * QR * heads, dtype=jnp.int32) // heads
    key_order = jnp.arange(TILE, dtype=jnp.int32)
    new_bias = jnp.where(key_order[None, :] <= order[:, None], 0.0, NEG_FILL).astype(jnp.float32)
    attention = attend(
        slot_request,
        queries,
        by_request(keys),
        by_request(raw_values),
        *cache_parts,
        scales[0] * HD ** (-0.5),
        scales[1],
        cache_bias,
        new_bias,
    )
    attention = jnp.transpose(
        attention.reshape(requests, STEPS, QR, heads, HD), (1, 0, 2, 3, 4)
    ).reshape(rows, heads * HD)
    mixed = gather_and_mix(attention, out_weight, hidden_in.reshape(rows, width), device)
    return mixed.reshape(hidden_in.shape)


def solution(mesh):
    return jax.shard_map(
        local_pairs if mesh.shape["tensor"] == 2 * KVH else local_general,
        mesh=mesh,
        in_specs=(
            P(None, "groups", "tensor"),
            P("tensor"),
            P("tensor", None),
            P(None, "tensor"),
            P(("groups", "tensor"), None, None, None),
            P(("groups", "tensor"), None, None),
            P("groups"),
            P("groups", None),
        ),
        out_specs=P(None, "groups", "tensor"),
        check_vma=False,
    )
```

```python
import functools

import jax
import jax.numpy as jnp
from jax import lax
from jax.experimental import pallas as pl
from jax.experimental.pallas import tpu as pltpu
from jax.sharding import PartitionSpec as P

D = 16384
QH = 128
KVH = 8
HD = 128
QR = 6
STEPS = 2
BLK = 16
GQ = 16
GW = 2304


EPSILON = 1e-05
ROPE_BASE = 500000.0
NEG_FILL = -1e30


def rotate(values, positions):
    half = values.shape[-1] // 2
    freqs = ROPE_BASE ** (-(jnp.arange(half, dtype=jnp.float32) * 2.0 / values.shape[-1]))
    angles = positions.astype(jnp.float32)[..., None] * freqs
    cosine = jnp.cos(angles)
    sine = jnp.sin(angles)
    first = values[..., :half]
    second = values[..., half:]
    return jnp.concatenate([first * cosine - second * sine, second * cosine + first * sine], -1)


def request_layout(request_owner, request_length, block_table, owners, stripe):
    requests = request_owner.shape[0]
    most = block_table.shape[1]
    order = jnp.arange(requests, dtype=jnp.int32)
    stripes = (request_length + stripe - 1) // stripe
    before = (
        (request_owner[None, :] == request_owner[:, None]) & (order[None, :] < order[:, None])
    ).astype(jnp.int32)
    rank = jnp.sum(before, 1)
    offset = jnp.sum(before * stripes[None, :], 1)
    owner_ids = jnp.arange(owners, dtype=jnp.int32)
    mine = request_owner[None, :] == owner_ids[:, None]
    member = mine[:, :, None] & (
        rank[None, :, None] == jnp.arange(requests // owners, dtype=jnp.int32)[None, None, :]
    )
    owner_requests = jnp.sum(member.astype(jnp.int32) * order[None, :, None], 1)
    columns = jnp.arange(most, dtype=jnp.int32)
    within = columns[None, None, :] - offset[None, :, None]
    hit = (mine[:, :, None] & (within >= 0) & (within < stripes[None, :, None])).astype(jnp.int32)
    stripe_request = jnp.sum(hit * order[None, :, None], 1) - (1 - jnp.sum(hit, 1))
    stripe_rank = jnp.sum(hit * within, 1)
    pick = (within[..., None] == columns[None, None, None, :]).astype(jnp.int32)
    slots = jnp.sum(hit[..., None] * pick * block_table[None, :, None, :], (1, 3))
    return (owner_requests, stripe_request, stripe_rank, slots, rank, stripes)


def cache_partial(queries, keys, values, key_scale, value_scale, mask):
    scores = jnp.einsum("srgd,td->srgt", queries, keys, preferred_element_type=jnp.float32)
    scores = jnp.where(mask, scores * key_scale * HD ** (-0.5), NEG_FILL)
    best = jnp.max(scores, -1)
    expo = jnp.where(mask, jnp.exp(scores - best[..., None]), 0.0)
    total = jnp.sum(expo, -1)
    weights = (expo * value_scale).astype(jnp.bfloat16)
    summed = jnp.einsum("srgt,td->srgd", weights, values, preferred_element_type=jnp.float32)
    return (best, total, summed)


def local_general(
    hidden_in,
    norm_gain,
    qkv_weight,
    out_weight,
    cache_pool,
    cache_scale,
    request_length,
    block_table,
):
    devices = lax.axis_size("tensor")
    device = lax.axis_index("tensor")
    owners = devices // KVH
    stripe = devices * BLK
    requests = request_length.shape[0]
    request_owner = jnp.arange(requests, dtype=jnp.int32) % owners
    unit_rows = requests // owners * QR
    most = block_table.shape[1]
    local_width = hidden_in.shape[2]
    my_owner = device // KVH
    owner_requests, stripe_request, stripe_rank, slots, rank, stripes = request_layout(
        request_owner, request_length, block_table, owners, stripe
    )
    step_rows = jnp.arange(QR, dtype=jnp.int32)
    row_order = (owner_requests[:, :, None] * QR + step_rows[None, None, :]).reshape(
        owners * unit_rows
    )
    inverse = ((request_owner * unit_rows + rank * QR)[:, None] + step_rows[None, :]).reshape(
        requests * QR
    )
    row_request = jnp.repeat(owner_requests[my_owner], QR)
    row_length = request_length[row_request]
    row_step = jnp.arange(unit_rows, dtype=jnp.int32) % QR
    same_request = row_request[:, None] == row_request[None, :]
    gain = norm_gain.astype(jnp.float32)
    weight_grouped = qkv_weight.reshape(local_width, KVH, GW)
    sent = cache_pool[jnp.transpose(slots)].reshape(most, devices, BLK, 2 * HD)
    sent_scale = cache_scale[jnp.transpose(slots)].reshape(most, devices, 2)
    landed, landed_scale = (
        lax.all_to_all(sent, "tensor", split_axis=1, concat_axis=1, tiled=True),
        lax.all_to_all(sent_scale, "tensor", split_axis=1, concat_axis=1, tiled=True),
    )
    cache_data = landed.reshape(most * stripe, 2 * HD)
    token_scale = jnp.broadcast_to(
        landed_scale.astype(jnp.float32)[:, :, None, :], (most, devices, BLK, 2)
    ).reshape(most * stripe, 2)
    token = jnp.arange(most * stripe, dtype=jnp.int32)
    token_stripe = token // stripe
    token_request = stripe_request[my_owner][token_stripe]
    token_position = stripe_rank[my_owner][token_stripe] * stripe + token % stripe
    token_length = jnp.where(token_request >= 0, request_length[jnp.maximum(token_request, 0)], 0)
    cache_mask = (
        (token_request[None, :] == row_request[:, None]) & (token_position < token_length)[None, :]
    )[None, :, None, :]
    outputs = []
    keys_seen = []
    values_seen = []
    for step in range(STEPS):
        block = hidden_in[step : step + 1]
        project_count = block.shape[0]
        values = block.astype(jnp.float32)
        sums = lax.psum(jnp.sum(values * values, -1), "tensor")
        normed = (values * lax.rsqrt(sums[..., None] / D + EPSILON) * gain).astype(jnp.bfloat16)
        ordered = jnp.take(normed, row_order, axis=1).reshape(
            project_count, owners, unit_rows, local_width
        )
        term = jnp.einsum(
            "sojd,dhg->ohsjg", ordered, weight_grouped, preferred_element_type=jnp.float32
        )
        term = term.reshape(owners * KVH * project_count * unit_rows, GW)
        mine = lax.psum_scatter(term, "tensor", scatter_dimension=0, tiled=True)
        joined_block = mine.astype(jnp.bfloat16).reshape(project_count, unit_rows, GW)
        prepare_count = joined_block.shape[0]
        steps_here = step + jnp.arange(prepare_count, dtype=jnp.int32)
        position = row_length[None, :] + QR * steps_here[:, None] + row_step[None, :]
        prepare_queries = rotate(
            joined_block[..., : GQ * HD]
            .reshape(prepare_count, unit_rows, GQ, HD)
            .astype(jnp.float32),
            position[:, :, None],
        ).astype(jnp.bfloat16)
        keys = rotate(
            joined_block[..., GQ * HD : GQ * HD + HD].astype(jnp.float32), position
        ).astype(jnp.bfloat16)
        queries, keys, values = (prepare_queries, keys, joined_block[..., GQ * HD + HD :])
        keys_seen.append(keys)
        values_seen.append(values)
        keys_all = jnp.concatenate(keys_seen, 0)
        attend_count = queries.shape[0]
        cache_best, cache_total, cache_summed = cache_partial(
            queries,
            cache_data[:, :HD],
            cache_data[:, HD:],
            token_scale[:, 0],
            token_scale[:, 1],
            cache_mask,
        )
        news = jnp.einsum(
            "srgd,pjd->srgpj", queries, keys_all, preferred_element_type=jnp.float32
        ) * HD ** (-0.5)
        query_step = step + jnp.arange(attend_count, dtype=jnp.int32)[:, None, None, None]
        key_step = jnp.arange(keys_all.shape[0], dtype=jnp.int32)[None, None, :, None]
        allowed = (key_step < query_step) | (key_step == query_step) & (
            row_step[None, None, None, :] <= row_step[None, :, None, None]
        )
        allowed = (allowed & same_request[None, :, None, :])[:, :, None, :, :]
        news = jnp.where(allowed, news, NEG_FILL)
        best = jnp.maximum(cache_best, jnp.max(news, (3, 4)))
        factor = jnp.exp(cache_best - best)
        expo = jnp.where(allowed, jnp.exp(news - best[..., None, None]), 0.0)
        total = cache_total * factor + jnp.sum(expo, (3, 4))
        summed = cache_summed * factor[..., None] + jnp.einsum(
            "srgpj,pjd->srgd",
            expo.astype(jnp.bfloat16),
            jnp.concatenate(values_seen, 0),
            preferred_element_type=jnp.float32,
        )
        attention = (
            (summed / total[..., None])
            .astype(jnp.bfloat16)
            .reshape(attend_count, unit_rows, GQ * HD)
        )
        count = attention.shape[0]
        gathered = lax.all_gather(attention, "tensor", axis=2, tiled=True).reshape(
            count, unit_rows, owners, QH * HD
        )
        mixed = jnp.einsum(
            "sjof,fd->sojd", gathered, out_weight, preferred_element_type=jnp.float32
        )
        mixed = jnp.take(mixed.reshape(count, owners * unit_rows, local_width), inverse, axis=1)
        outputs.append(
            (hidden_in[step : step + count].astype(jnp.float32) + mixed).astype(jnp.bfloat16)
        )
    return jnp.concatenate(outputs, 0)


VMEM_LIMIT = 66977792
SHORT = pl.CostEstimate(flops=1, bytes_accessed=1, transcendentals=0)
LOW_BITS = 4
PACKED = 16 // LOW_BITS
LEVELS = 32600.0 * 2**LOW_BITS
POWER_STEPS = 8.0
TILE = 16
MESH_BITS = (1, 2, 4, 8)


def swap(value, bit):
    devices = lax.axis_size("tensor")
    return lax.ppermute(value, "tensor", [(i, i ^ bit) for i in range(devices)])


def in_hbm(*arrays):
    return [pltpu.with_memory_space_constraint(a, pltpu.HBM) for a in arrays]


def no_work(*refs):
    del refs


def together(arrays, after):
    anywhere = pl.BlockSpec(memory_space=pl.ANY)
    return pl.pallas_call(
        no_work,
        in_specs=[anywhere] * (len(arrays) + len(after)),
        out_specs=[anywhere] * len(arrays),
        out_shape=[pltpu.HBM(a.shape, a.dtype) for a in arrays],
        input_output_aliases={i: i for i in range(len(arrays))},
        compiler_params=pltpu.CompilerParams(vmem_limit_bytes=VMEM_LIMIT),
        cost_estimate=SHORT,
        name="together",
    )(*in_hbm(*arrays), *after)


def coded_rows(rows):
    return rows + rows // PACKED


def encode(block):
    top = jnp.max(jnp.abs(block), 0, keepdims=True)
    power = jnp.ceil(jnp.log2(jnp.maximum(top, 1e-30)) * POWER_STEPS)
    codes = jnp.round(block * (jnp.exp2(power * (-1.0 / POWER_STEPS)) * LEVELS)).astype(jnp.int32)
    low = codes & (2**LOW_BITS - 1)
    part = block.shape[0] // PACKED
    packed = low[:part]
    for i in range(1, PACKED):
        packed = packed + (low[i * part : (i + 1) * part] << (LOW_BITS * i))
    high = (codes >> LOW_BITS).astype(jnp.int16)
    return jnp.concatenate([high, (packed - 32768).astype(jnp.int16)], 0), power


def decode(codes, power):
    rows = codes.shape[0] * PACKED // (PACKED + 1)
    high = codes[:rows].astype(jnp.int32) << LOW_BITS
    packed = codes[rows:].astype(jnp.int32) + 32768
    low = jnp.concatenate(
        [(packed >> (LOW_BITS * i)) & (2**LOW_BITS - 1) for i in range(PACKED)], 0
    )
    scale = jnp.exp2(power * (1.0 / POWER_STEPS)) * (1.0 / LEVELS)
    return (high + low).astype(jnp.float32) * scale


def pick_row(rows, index):
    ids = lax.broadcasted_iota(jnp.int32, rows.shape, 0)
    return jnp.sum(jnp.where(ids == index, rows, 0.0), 0, keepdims=True)


def store_codes(sent, powers, block, index, steps):
    rows = coded_rows(block.shape[0])
    codes, power = encode(block)
    sent[pl.ds(pl.multiple_of(index * rows, TILE), rows), :] = codes

    powers[pl.ds(index, 1), :] = power

    @pl.when(index == steps - 1)
    def _():
        sent[pl.ds(steps * rows, TILE), :] = powers[...].astype(jnp.int32).astype(jnp.int16)


def project_kernel(chunk, with_pair, core, normed, weights, *refs):
    kept, sent, powers, wide, arrived = refs[-5:]
    index = pl.program_id(0)
    columns = kept.shape[2]

    def copies(group):
        found = []
        for side in range(2):
            owner = core[0] if side == 0 else 1 - core[0]
            first = group * GW + owner * (GQ // 2 * HD) + chunk * (2 * HD)
            spans = [(first, 0, 2 * HD)]
            if with_pair:
                spans.append((group * GW + (GQ + owner) * HD, 2 * HD, HD))
            for number, (start, offset, size) in enumerate(spans):
                found.append(
                    pltpu.make_async_copy(
                        weights.at[:, pl.ds(pl.multiple_of(start, HD), size)],
                        wide.at[group, :, pl.ds(side * columns + offset, size)],
                        arrived.at[group, side, number],
                    )
                )
        return found

    @pl.when(index == 0)
    def _():
        for group in range(KVH):
            for copy in copies(group):
                copy.start()
        powers[...] = jnp.zeros_like(powers)

    for copy in copies(index):
        copy.wait()

    product = jnp.dot(normed[...], wide[index], preferred_element_type=jnp.float32)
    kept[0] = product[:, :columns]
    store_codes(sent, powers, product[:, columns:], index, KVH)


def project(core, normed, qkv_weight, chunk, with_pair, after):
    rows, width = normed.shape
    columns = 2 * HD + (HD if with_pair else 0)
    sent_rows = KVH * coded_rows(rows) + TILE
    return pl.pallas_call(
        functools.partial(project_kernel, chunk, with_pair),
        grid_spec=pltpu.PrefetchScalarGridSpec(
            num_scalar_prefetch=1,
            grid=(KVH,),
            in_specs=[pl.BlockSpec((rows, width), lambda t, c: (0, 0))]
            + [pl.BlockSpec(memory_space=pl.ANY)] * (1 + len(after)),
            out_specs=[
                pl.BlockSpec((1, rows, columns), lambda t, c: (t, 0, 0)),
                pl.BlockSpec((sent_rows, columns), lambda t, c: (0, 0)),
            ],
            scratch_shapes=[
                pltpu.VMEM((TILE, columns), jnp.float32),
                pltpu.VMEM((KVH, width, 2 * columns), jnp.bfloat16),
                pltpu.SemaphoreType.DMA((KVH, 2, 2)),
            ],
        ),
        out_shape=[
            pltpu.HBM((KVH, rows, columns), jnp.float32),
            pltpu.HBM((sent_rows, columns), jnp.int16),
        ],
        compiler_params=pltpu.CompilerParams(vmem_limit_bytes=VMEM_LIMIT),
        cost_estimate=SHORT,
        name="project",
    )(core, normed, *in_hbm(qkv_weight), *after)


def fold_kernel(steps, bit, held, landed, landed_powers, *refs):
    kept, sent, powers = refs[-3:]
    index = pl.program_id(0)
    rows = coded_rows(held.shape[1])
    rows_of_powers = landed_powers[...].astype(jnp.int32).astype(jnp.float32)

    def total(side):
        place = pl.multiple_of(side * rows, TILE)
        codes = landed[pl.ds(place, rows), :]
        return held[side] + decode(codes, pick_row(rows_of_powers, 2 * index + side))

    @pl.when(index == 0)
    def _():
        powers[...] = jnp.zeros_like(powers)

    mine = bit[0]
    kept[0] = total(mine)
    store_codes(sent, powers, total(1 - mine), index, steps)


def fold(bit, held, landed, after):
    blocks, rows, columns = held.shape
    steps = blocks // 2
    coded = coded_rows(rows)
    return pl.pallas_call(
        functools.partial(fold_kernel, steps),
        grid_spec=pltpu.PrefetchScalarGridSpec(
            num_scalar_prefetch=1,
            grid=(steps,),
            in_specs=[
                pl.BlockSpec((2, rows, columns), lambda i, b: (i, 0, 0)),
                pl.BlockSpec((2 * coded, columns), lambda i, b: (i, 0)),
                pl.BlockSpec((TILE, columns), lambda i, b: (blocks * coded // TILE, 0)),
            ]
            + [pl.BlockSpec(memory_space=pl.ANY)] * len(after),
            out_specs=[
                pl.BlockSpec((1, rows, columns), lambda i, b: (i, 0, 0)),
                pl.BlockSpec((steps * coded + TILE, columns), lambda i, b: (0, 0)),
            ],
            scratch_shapes=[pltpu.VMEM((TILE, columns), jnp.float32)],
        ),
        out_shape=[
            pltpu.HBM((steps, rows, columns), jnp.float32),
            pltpu.HBM((steps * coded + TILE, columns), jnp.int16),
        ],
        compiler_params=pltpu.CompilerParams(vmem_limit_bytes=VMEM_LIMIT),
        cost_estimate=SHORT,
        name="fold",
    )(bit, *in_hbm(held), landed, landed, *after)


def finish_kernel(after_count, core, held, landed, cosine, sine, *refs):
    queries, *pair = refs[after_count:]
    rows = held.shape[1]
    coded = coded_rows(rows)
    power = landed[pl.ds(coded, TILE), :].astype(jnp.int32).astype(jnp.float32)[0:1]
    total = held[0] + decode(landed[pl.ds(0, coded), :], power)
    joined = total.astype(jnp.bfloat16)
    parts = []
    for head in range(joined.shape[1] // HD):
        raw = joined[:, head * HD : (head + 1) * HD]
        wide = raw.astype(jnp.float32)
        turned = wide * cosine[...] + pltpu.roll(wide, HD // 2, 1) * sine[...]
        parts.append((raw, turned.astype(jnp.bfloat16)))
    queries[...] = jnp.concatenate([parts[0][1], parts[1][1]], 1)
    if pair:
        raw, turned = parts[2]
        pair[0][...] = jnp.where(core[0] == 0, turned.astype(jnp.float32), raw.astype(jnp.float32)).astype(
            jnp.bfloat16
        )


def finish(core, held, landed, cosine, sine, after):
    _, rows, columns = held.shape
    whole = pl.BlockSpec(memory_space=pltpu.VMEM)
    shapes = [pltpu.HBM((rows, 2 * HD), jnp.bfloat16)]
    if columns > 2 * HD:
        shapes.append(pltpu.HBM((rows, HD), jnp.bfloat16))
    return pl.pallas_call(
        functools.partial(finish_kernel, len(after)),
        in_specs=[pl.BlockSpec(memory_space=pltpu.SMEM)]
        + [whole] * 4
        + [pl.BlockSpec(memory_space=pl.ANY)] * len(after),
        out_specs=[whole] * len(shapes),
        out_shape=shapes,
        compiler_params=pltpu.CompilerParams(vmem_limit_bytes=VMEM_LIMIT),
        cost_estimate=SHORT,
        name="finish",
    )(core, *in_hbm(held), landed, *in_hbm(cosine, sine), *after)


def mix_kernel(count, places, *refs):
    pieces = refs[:count]
    weights, start, mixed, total, wide, arrived = refs[count:]
    depth = wide.shape[1]
    columns = wide.shape[2] // 2
    flat = []
    for piece in pieces:
        flat += [piece] if len(piece.shape) == 2 else [piece.at[i] for i in range(piece.shape[0])]
    copies = [
        pltpu.make_async_copy(
            weights.at[pl.ds(pl.multiple_of(places[i] * depth, depth), depth), :],
            wide.at[i],
            arrived.at[i],
        )
        for i in range(len(flat))
    ]
    for copy in copies:
        copy.start()
    cuts = [0, 1, 2, 4, len(flat)]
    cuts = sorted(set(min(cut, len(flat)) for cut in cuts))
    for first, last in zip(cuts, cuts[1:]):
        for copy in copies[first:last]:
            copy.wait()
        for side in range(2):
            span = pl.ds(side * columns, columns)
            source = start if first == 0 else total
            value = source[:, span].astype(jnp.float32)
            for i in range(first, last):
                value = value + jnp.dot(
                    flat[i][...], wide[i, :, span], preferred_element_type=jnp.float32
                )
            target = mixed if last == len(flat) else total
            target[:, span] = value.astype(target.dtype)


def mix(places, pieces, out_weight, start, dtype):
    columns = out_weight.shape[1]
    rows, width = pieces[0].shape[-2:]
    count = sum(1 if len(p.shape) == 2 else p.shape[0] for p in pieces)
    whole = pl.BlockSpec(memory_space=pltpu.VMEM)
    return pl.pallas_call(
        functools.partial(mix_kernel, len(pieces)),
        in_specs=[pl.BlockSpec(memory_space=pltpu.SMEM)]
        + [whole] * len(pieces)
        + [pl.BlockSpec(memory_space=pl.ANY), whole],
        out_specs=whole,
        scratch_shapes=[
            pltpu.VMEM((rows, columns), jnp.float32),
            pltpu.VMEM((count, width, columns), jnp.bfloat16),
            pltpu.SemaphoreType.DMA((count,)),
        ],
        out_shape=pltpu.HBM((rows, columns), dtype),
        compiler_params=pltpu.CompilerParams(vmem_limit_bytes=VMEM_LIMIT),
        cost_estimate=SHORT,
        name="mix",
    )(places, *pieces, *in_hbm(out_weight, start))


def pack_kernel(groups, count, *refs):
    flat = []
    for ref in refs[:count]:
        flat += [ref] if len(ref.shape) == 2 else [ref.at[i] for i in range(ref.shape[0])]
    for group, target in zip(groups, refs[-len(groups) :]):
        for place, index in enumerate(group):
            target[place] = flat[index][...]


def pack(pieces, groups, after):
    whole = pl.BlockSpec(memory_space=pltpu.VMEM)
    shape = pieces[0].shape[-2:]
    return pl.pallas_call(
        functools.partial(pack_kernel, groups, len(pieces)),
        in_specs=[whole] * len(pieces) + [pl.BlockSpec(memory_space=pl.ANY)] * len(after),
        out_specs=[whole] * len(groups),
        out_shape=[pltpu.HBM((len(g),) + shape, pieces[0].dtype) for g in groups],
        compiler_params=pltpu.CompilerParams(vmem_limit_bytes=VMEM_LIMIT),
        cost_estimate=SHORT,
        name="pack",
    )(*pieces, *after)


def gather_and_mix(attention, out_weight, start, device):
    def add(mixed, pieces, offsets, dtype=jnp.float32):
        places = jnp.stack([device ^ offset for offset in offsets])
        return mix(places, pieces, out_weight, mixed, dtype)

    near = swap(attention, 4)
    across = swap(attention, 2)
    far = swap(attention, 8)
    partner = swap(attention, 1)
    first, onward = pack([near, across, far], [(0, 1, 2), (0, 2)], [partner])
    (attention,) = together([attention], [onward])

    across_onward = swap(onward, 2)
    farthest = swap(attention, 12)
    first_partner = swap(first, 1)
    mixed = add(start, [attention, partner], (0, 1))
    mixed = add(mixed, [first, first_partner], (4, 2, 8, 5, 3, 9))
    (second,) = pack([across_onward, farthest], [(0, 1, 2)], [mixed])

    last = swap(farthest, 2)
    second_partner = swap(second, 1)
    mixed = add(mixed, [second, second_partner], (6, 10, 12, 7, 11, 13))
    (last,) = together([last], [mixed])

    last_partner = swap(last, 1)
    return add(mixed, [last, last_partner], (14, 15), jnp.bfloat16)


def attend_kernel(
    slot_request,
    queries,
    new_keys,
    new_values,
    own_near,
    own_far,
    other_near,
    other_far,
    key_scale,
    value_scale,
    cache_bias,
    new_bias,
    attention,
    slot_best,
    slot_total,
    slot_sum,
    best,
    total,
    summed,
):
    slots = slot_best.shape[0]
    requests, count, _ = queries.shape
    transposed = (((1,), (1,)), ((), ()))
    for request in range(requests):
        scores = (
            lax.dot_general(
                queries[request],
                new_keys[request],
                transposed,
                preferred_element_type=jnp.float32,
            )
            * HD ** (-0.5)
            + new_bias[...]
        )
        top = jnp.max(scores, -1, keepdims=True)
        expo = jnp.exp(scores - top)
        best[request] = jnp.broadcast_to(top, (count, HD))
        total[request] = jnp.broadcast_to(jnp.sum(expo, -1, keepdims=True), (count, HD))
        summed[request] = jnp.dot(
            expo.astype(jnp.bfloat16), new_values[request], preferred_element_type=jnp.float32
        )
    for slot in range(slots):
        request = slot_request[slot]
        query = queries[request]
        raw = [
            part[:, slot * BLK : (slot + 1) * BLK, :].reshape(KVH // 2 * BLK, 2 * HD)
            for part in (own_near, own_far, other_near, other_far)
        ]
        scores = jnp.concatenate(
            [
                lax.dot_general(
                    query, kv[:, :HD], transposed, preferred_element_type=jnp.float32
                )
                for kv in raw
            ],
            1,
        )
        scores = scores * key_scale[slot : slot + 1, :] + cache_bias[slot : slot + 1, :]
        top = jnp.max(scores, -1, keepdims=True)
        expo = jnp.exp(scores - top)
        weights = (expo * value_scale[slot : slot + 1, :]).astype(jnp.bfloat16)
        slot_best[slot] = jnp.broadcast_to(top, (count, HD))
        slot_total[slot] = jnp.broadcast_to(jnp.sum(expo, -1, keepdims=True), (count, HD))
        values = jnp.concatenate([kv[:, HD:] for kv in raw], 0)
        slot_sum[slot] = jnp.dot(weights, values, preferred_element_type=jnp.float32)
    for slot in range(slots):
        request = slot_request[slot]
        before = best[request]
        here = slot_best[slot]
        top = jnp.maximum(before, here)
        keep = jnp.exp(before - top)
        add = jnp.exp(here - top)
        best[request] = top
        total[request] = total[request] * keep + slot_total[slot] * add
        summed[request] = summed[request] * keep + slot_sum[slot] * add
    for request in range(requests):
        attention[request] = (summed[request] / total[request]).astype(jnp.bfloat16)


def attend(slot_request, *arrays):
    queries = arrays[0]
    slots = arrays[7].shape[0]
    requests, count, _ = queries.shape
    whole = pl.BlockSpec(memory_space=pltpu.VMEM)
    return pl.pallas_call(
        attend_kernel,
        in_specs=[pl.BlockSpec(memory_space=pltpu.SMEM)] + [whole] * len(arrays),
        out_specs=whole,
        out_shape=pltpu.HBM((requests, count, HD), jnp.bfloat16),
        scratch_shapes=[pltpu.VMEM((slots, count, HD), jnp.float32)] * 3
        + [pltpu.VMEM((requests, count, HD), jnp.float32)] * 3,
        compiler_params=pltpu.CompilerParams(vmem_limit_bytes=VMEM_LIMIT),
        cost_estimate=SHORT,
        name="attend",
    )(slot_request, *arrays)


def slot_layout(request_length, block_table, slots, stripe):
    requests, most = block_table.shape
    stripes = (request_length + stripe - 1) // stripe
    columns = jnp.arange(most, dtype=jnp.int32)
    held = columns[None, :] < stripes[:, None]
    hit = held[:, :, None] & (
        block_table[:, :, None] == jnp.arange(slots, dtype=jnp.int32)[None, None, :]
    )
    hit = hit.astype(jnp.int32)
    order = jnp.arange(requests, dtype=jnp.int32)
    request = jnp.sum(hit * order[:, None, None], (0, 1))
    rank = jnp.sum(hit * columns[None, :, None], (0, 1))
    length = jnp.sum(hit * request_length[:, None, None], (0, 1))
    return request, rank, length


def arrange_kernel(chip, even, odd, even_scale, odd_scale, after, kept, sent):
    slots = even.shape[0]
    for blocks, scale, target in ((even, even_scale, kept), (odd, odd_scale, sent)):
        target[0, : slots * BLK, :] = blocks[:, 0].reshape(slots * BLK, 2 * HD)
        target[0, slots * BLK :, :] = scale[0]


def arrange(chip, cache_pool, scales, first, after):
    slots = cache_pool.shape[0]
    pool = [
        pl.BlockSpec(
            (slots, 1, BLK, 2 * HD), lambda i, c, side=side: (0, c[0] ^ (first + 2 * i + side), 0, 0)
        )
        for side in (0, 1)
    ]
    scale = [
        pl.BlockSpec((1, TILE, 2 * HD), lambda i, c, side=side: (c[0] ^ (first + 2 * i + side), 0, 0))
        for side in (0, 1)
    ]
    rows = slots * BLK + TILE
    out = pl.BlockSpec((1, rows, 2 * HD), lambda i, c: (i, 0, 0))
    shape = pltpu.HBM((KVH // 4, rows, 2 * HD), jnp.bfloat16)
    return pl.pallas_call(
        arrange_kernel,
        grid_spec=pltpu.PrefetchScalarGridSpec(
            num_scalar_prefetch=1,
            grid=(KVH // 4,),
            in_specs=pool + scale + [pl.BlockSpec(memory_space=pl.ANY)],
            out_specs=[out, out],
        ),
        out_shape=[shape, shape],
        compiler_params=pltpu.CompilerParams(vmem_limit_bytes=VMEM_LIMIT),
        cost_estimate=SHORT,
        name="arrange",
    )(chip, *in_hbm(cache_pool, cache_pool, scales, scales), after)


def handover_plan():
    arrays = [[(0, 0), (0, 2)], [(0, 4), (0, 6)], [(1, 0), (1, 2)], [(1, 4), (1, 6)]]
    splits = []
    for bit, parts in ((4, 2), (2, 1)):
        entries = [(a, i, e) for a, part in enumerate(arrays) for i, e in enumerate(part)]
        stay = [e for e in entries if not e[2][1] & bit]
        leave = [e for e in entries if e[2][1] & bit]
        size = len(leave) // parts
        groups = [stay] + [leave[i : i + size] for i in range(0, len(leave), size)]
        splits.append([[(a, i) for a, i, _ in group] for group in groups])
        arrays = [[e for _, _, e in stay]]
        arrays += [[(x ^ bit, y ^ bit) for _, _, (x, y) in group] for group in groups[1:]]
    return splits, [source for part in arrays for source, _ in part]


def regroup_kernel(groups, count, *refs):
    sources, targets = refs[:count], refs[-len(groups) :]
    for group, target in zip(groups, targets):
        for place, (array, index) in enumerate(group):
            target[place] = sources[array][index]


def regroup(groups, sources, after):
    whole = pl.BlockSpec(memory_space=pltpu.VMEM)
    rows = sources[0].shape[1:]
    return pl.pallas_call(
        functools.partial(regroup_kernel, groups, len(sources)),
        in_specs=[whole] * len(sources) + [pl.BlockSpec(memory_space=pl.ANY)] * len(after),
        out_specs=[whole] * len(groups),
        out_shape=[pltpu.HBM((len(g),) + rows, sources[0].dtype) for g in groups],
        compiler_params=pltpu.CompilerParams(vmem_limit_bytes=VMEM_LIMIT),
        cost_estimate=SHORT,
        name="regroup",
    )(*sources, *after)


def local_pairs(
    hidden_in,
    norm_gain,
    qkv_weight,
    out_weight,
    cache_pool,
    cache_scale,
    request_length,
    block_table,
):
    devices = lax.axis_size("tensor")
    device = lax.axis_index("tensor")
    core = device % 2
    chip = device // 2
    stripe = devices * BLK
    slots = cache_pool.shape[0]
    requests = request_length.shape[0]
    rows = STEPS * requests * QR
    width = hidden_in.shape[2]
    heads = GQ // 2

    hidden = hidden_in.astype(jnp.float32)
    sums = jnp.sum(hidden * hidden, -1)
    bits = [jnp.reshape((device >> b) & 1, (1,)).astype(jnp.int32) for b in range(4)]
    scale_rows = jnp.pad(
        jnp.transpose(cache_scale, (1, 2, 0)).reshape(KVH, 1, 2 * slots),
        ((0, 0), (0, TILE - 1), (0, 2 * HD - 2 * slots)),
    )
    chip_scalar = jnp.reshape(chip, (1,)).astype(jnp.int32)
    sums = sums + swap(sums, 2)
    kept_a, sent_a = arrange(chip_scalar, cache_pool, scale_rows, 0, sums)
    landed_a = swap(sent_a, 2)
    kept_b, sent_b = arrange(chip_scalar, cache_pool, scale_rows, KVH // 2, sent_a)
    for bit in (1, 4, 8):
        sums = sums + swap(sums, bit)
    (sent_b,) = together([sent_b], [sums, landed_a])
    landed_b = swap(sent_b, 2)
    normed = (
        hidden * lax.rsqrt(sums[..., None] / D + EPSILON) * norm_gain.astype(jnp.float32)
    ).astype(jnp.bfloat16)
    normed = normed.reshape(rows, width)

    step_ids = jnp.arange(STEPS, dtype=jnp.int32)
    row_ids = jnp.arange(QR, dtype=jnp.int32)
    position = (
        request_length[None, :, None] + QR * step_ids[:, None, None] + row_ids[None, None, :]
    )
    freqs = ROPE_BASE ** (-(jnp.arange(HD // 2, dtype=jnp.float32) * 2.0 / HD))
    angles = position.reshape(rows, 1).astype(jnp.float32) * freqs
    cosine = jnp.concatenate([jnp.cos(angles)] * 2, 1)
    sine = jnp.concatenate([-jnp.sin(angles), jnp.sin(angles)], 1)

    count = GQ // 4
    held, sent = [None] * count, [None] * count
    splits, sources_of_cache = handover_plan()

    def projected(chunk, *after):
        held[chunk], sent[chunk] = project(
            bits[0], normed, qkv_weight, chunk, chunk == 0, after
        )

    def hop(chunk, b):
        return swap(sent[chunk], MESH_BITS[b])

    def folded(chunk, b, landed, *after):
        held[chunk], sent[chunk] = fold(bits[b], held[chunk], landed, after)

    def finished(chunk, landed, *after):
        return finish(bits[0], held[chunk], landed, cosine, sine, after)

    projected(0, sent_b)
    core_0 = hop(0, 0)
    projected(1, held[0])
    (sent[1],) = together([sent[1]], [core_0, landed_b])

    folded(0, 1, core_0, sent[1])
    core_1, y_0 = hop(1, 0), hop(0, 1)
    cache_kept, sent_a, sent_b = regroup(
        splits[0], (kept_a, kept_b, landed_a, landed_b), (held[0],)
    )
    landed_a = swap(sent_a, 8)
    projected(2, held[0], cache_kept)
    projected(3, held[2])
    sent[2], sent[3], sent_b = together(
        [sent[2], sent[3], sent_b], [core_1, y_0, landed_a]
    )

    core_2, core_3 = hop(2, 0), hop(3, 0)
    landed_b = swap(sent_b, 8)
    folded(1, 1, core_1, sent[2])
    y_1 = hop(1, 1)
    folded(0, 2, y_0, held[1])
    near_0 = hop(0, 2)
    folded(2, 1, core_2, held[0])
    folded(3, 1, core_3, held[2])
    sent[2], sent[3] = together([sent[2], sent[3]], [y_1, near_0, landed_b])

    y_2 = hop(2, 1)
    folded(0, 3, near_0, sent[2])
    far_0 = hop(0, 3)
    folded(1, 2, y_1, sent[2])
    near_1 = hop(1, 2)
    cache_kept, cache_sent = regroup(splits[1], (cache_kept, landed_a, landed_b), (held[1],))
    cache_landed = swap(cache_sent, 4)
    sent[3], cache_kept = together([sent[3], cache_kept], [y_2, far_0, near_1, cache_landed])

    y_3 = hop(3, 1)
    folded(1, 3, near_1, sent[3])
    far_1 = hop(1, 3)
    folded(2, 2, y_2, sent[3])
    near_2 = hop(2, 2)
    query_chunks = [None] * count
    query_chunks[0], pair = finished(0, far_0, held[2])
    pair_other = swap(pair, 1)
    kept_other = swap(cache_kept, 1)
    landed_other = swap(cache_landed, 1)
    (held[3],) = together([held[3]], [y_3, far_1, near_2, pair_other, kept_other, landed_other])

    folded(3, 2, y_3)
    near_3 = hop(3, 2)
    folded(2, 3, near_2, held[3])
    far_2 = hop(2, 3)
    (query_chunks[1],) = finished(1, far_1, held[2])
    (held[3],) = together([held[3]], [near_3, far_2])

    folded(3, 3, near_3)
    far_3 = hop(3, 3)
    (query_chunks[2],) = finished(2, far_2, held[3])
    (query_chunks[3],) = finished(3, far_3, query_chunks[2])
    cache_parts = (cache_kept, cache_landed, kept_other, landed_other)
    keys = jnp.where(core == 0, pair, pair_other)
    raw_values = jnp.where(core == 0, pair_other, pair)
    queries = jnp.concatenate(query_chunks, 1).reshape(STEPS, requests, QR, heads, HD)
    queries = jnp.transpose(queries, (1, 0, 2, 3, 4)).reshape(requests, STEPS * QR * heads, HD)

    def by_request(value):
        value = jnp.transpose(value.reshape(STEPS, requests, QR, HD), (1, 0, 2, 3))
        value = value.reshape(requests, STEPS * QR, HD)
        return jnp.pad(value, ((0, 0), (0, TILE - STEPS * QR), (0, 0)))

    slot_request, slot_rank, slot_length = slot_layout(request_length, block_table, slots, stripe)
    source = chip ^ jnp.array(sources_of_cache, dtype=jnp.int32)
    sources = jnp.stack([source * 2 + core, source * 2 + 1 - core])
    offset = sources[:, :, None] * BLK + jnp.arange(BLK, dtype=jnp.int32)[None, None, :]
    token = slot_rank[:, None] * stripe + offset.reshape(1, stripe)
    cache_bias = jnp.where(token < slot_length[:, None], 0.0, NEG_FILL).astype(jnp.float32)
    scales = jnp.concatenate([part[:, slots * BLK, : 2 * slots] for part in cache_parts])
    scales = scales.astype(jnp.float32).reshape(2 * KVH, 2, slots)
    scales = jnp.repeat(jnp.transpose(scales, (1, 2, 0)), BLK, axis=2)
    order = jnp.arange(STEPS * QR * heads, dtype=jnp.int32) // heads
    key_order = jnp.arange(TILE, dtype=jnp.int32)
    new_bias = jnp.where(key_order[None, :] <= order[:, None], 0.0, NEG_FILL).astype(jnp.float32)
    attention = attend(
        slot_request,
        queries,
        by_request(keys),
        by_request(raw_values),
        *cache_parts,
        scales[0] * HD ** (-0.5),
        scales[1],
        cache_bias,
        new_bias,
    )
    attention = jnp.transpose(
        attention.reshape(requests, STEPS, QR, heads, HD), (1, 0, 2, 3, 4)
    ).reshape(rows, heads * HD)
    mixed = gather_and_mix(attention, out_weight, hidden_in.reshape(rows, width), device)
    return mixed.reshape(hidden_in.shape)


def solution(mesh):
    return jax.shard_map(
        local_pairs if mesh.shape["tensor"] == 2 * KVH else local_general,
        mesh=mesh,
        in_specs=(
            P(None, "groups", "tensor"),
            P("tensor"),
            P("tensor", None),
            P(None, "tensor"),
            P(("groups", "tensor"), None, None, None),
            P(("groups", "tensor"), None, None),
            P("groups"),
            P("groups", None),
        ),
        out_specs=P(None, "groups", "tensor"),
        check_vma=False,
    )
```

```python
import functools

import jax
import jax.numpy as jnp
from jax import lax
from jax.experimental import pallas as pl
from jax.experimental.pallas import tpu as pltpu
from jax.sharding import PartitionSpec as P

D = 16384
QH = 128
KVH = 8
HD = 128
QR = 6
STEPS = 2
BLK = 16
GQ = 16
GW = 2304


EPSILON = 1e-05
ROPE_BASE = 500000.0
NEG_FILL = -1e30


def rotate(values, positions):
    half = values.shape[-1] // 2
    freqs = ROPE_BASE ** (-(jnp.arange(half, dtype=jnp.float32) * 2.0 / values.shape[-1]))
    angles = positions.astype(jnp.float32)[..., None] * freqs
    cosine = jnp.cos(angles)
    sine = jnp.sin(angles)
    first = values[..., :half]
    second = values[..., half:]
    return jnp.concatenate([first * cosine - second * sine, second * cosine + first * sine], -1)


def request_layout(request_owner, request_length, block_table, owners, stripe):
    requests = request_owner.shape[0]
    most = block_table.shape[1]
    order = jnp.arange(requests, dtype=jnp.int32)
    stripes = (request_length + stripe - 1) // stripe
    before = (
        (request_owner[None, :] == request_owner[:, None]) & (order[None, :] < order[:, None])
    ).astype(jnp.int32)
    rank = jnp.sum(before, 1)
    offset = jnp.sum(before * stripes[None, :], 1)
    owner_ids = jnp.arange(owners, dtype=jnp.int32)
    mine = request_owner[None, :] == owner_ids[:, None]
    member = mine[:, :, None] & (
        rank[None, :, None] == jnp.arange(requests // owners, dtype=jnp.int32)[None, None, :]
    )
    owner_requests = jnp.sum(member.astype(jnp.int32) * order[None, :, None], 1)
    columns = jnp.arange(most, dtype=jnp.int32)
    within = columns[None, None, :] - offset[None, :, None]
    hit = (mine[:, :, None] & (within >= 0) & (within < stripes[None, :, None])).astype(jnp.int32)
    stripe_request = jnp.sum(hit * order[None, :, None], 1) - (1 - jnp.sum(hit, 1))
    stripe_rank = jnp.sum(hit * within, 1)
    pick = (within[..., None] == columns[None, None, None, :]).astype(jnp.int32)
    slots = jnp.sum(hit[..., None] * pick * block_table[None, :, None, :], (1, 3))
    return (owner_requests, stripe_request, stripe_rank, slots, rank, stripes)


def cache_partial(queries, keys, values, key_scale, value_scale, mask):
    scores = jnp.einsum("srgd,td->srgt", queries, keys, preferred_element_type=jnp.float32)
    scores = jnp.where(mask, scores * key_scale * HD ** (-0.5), NEG_FILL)
    best = jnp.max(scores, -1)
    expo = jnp.where(mask, jnp.exp(scores - best[..., None]), 0.0)
    total = jnp.sum(expo, -1)
    weights = (expo * value_scale).astype(jnp.bfloat16)
    summed = jnp.einsum("srgt,td->srgd", weights, values, preferred_element_type=jnp.float32)
    return (best, total, summed)


def local_general(
    hidden_in,
    norm_gain,
    qkv_weight,
    out_weight,
    cache_pool,
    cache_scale,
    request_length,
    block_table,
):
    devices = lax.axis_size("tensor")
    device = lax.axis_index("tensor")
    owners = devices // KVH
    stripe = devices * BLK
    requests = request_length.shape[0]
    request_owner = jnp.arange(requests, dtype=jnp.int32) % owners
    unit_rows = requests // owners * QR
    most = block_table.shape[1]
    local_width = hidden_in.shape[2]
    my_owner = device // KVH
    owner_requests, stripe_request, stripe_rank, slots, rank, stripes = request_layout(
        request_owner, request_length, block_table, owners, stripe
    )
    step_rows = jnp.arange(QR, dtype=jnp.int32)
    row_order = (owner_requests[:, :, None] * QR + step_rows[None, None, :]).reshape(
        owners * unit_rows
    )
    inverse = ((request_owner * unit_rows + rank * QR)[:, None] + step_rows[None, :]).reshape(
        requests * QR
    )
    row_request = jnp.repeat(owner_requests[my_owner], QR)
    row_length = request_length[row_request]
    row_step = jnp.arange(unit_rows, dtype=jnp.int32) % QR
    same_request = row_request[:, None] == row_request[None, :]
    gain = norm_gain.astype(jnp.float32)
    weight_grouped = qkv_weight.reshape(local_width, KVH, GW)
    sent = cache_pool[jnp.transpose(slots)].reshape(most, devices, BLK, 2 * HD)
    sent_scale = cache_scale[jnp.transpose(slots)].reshape(most, devices, 2)
    landed, landed_scale = (
        lax.all_to_all(sent, "tensor", split_axis=1, concat_axis=1, tiled=True),
        lax.all_to_all(sent_scale, "tensor", split_axis=1, concat_axis=1, tiled=True),
    )
    cache_data = landed.reshape(most * stripe, 2 * HD)
    token_scale = jnp.broadcast_to(
        landed_scale.astype(jnp.float32)[:, :, None, :], (most, devices, BLK, 2)
    ).reshape(most * stripe, 2)
    token = jnp.arange(most * stripe, dtype=jnp.int32)
    token_stripe = token // stripe
    token_request = stripe_request[my_owner][token_stripe]
    token_position = stripe_rank[my_owner][token_stripe] * stripe + token % stripe
    token_length = jnp.where(token_request >= 0, request_length[jnp.maximum(token_request, 0)], 0)
    cache_mask = (
        (token_request[None, :] == row_request[:, None]) & (token_position < token_length)[None, :]
    )[None, :, None, :]
    outputs = []
    keys_seen = []
    values_seen = []
    for step in range(STEPS):
        block = hidden_in[step : step + 1]
        project_count = block.shape[0]
        values = block.astype(jnp.float32)
        sums = lax.psum(jnp.sum(values * values, -1), "tensor")
        normed = (values * lax.rsqrt(sums[..., None] / D + EPSILON) * gain).astype(jnp.bfloat16)
        ordered = jnp.take(normed, row_order, axis=1).reshape(
            project_count, owners, unit_rows, local_width
        )
        term = jnp.einsum(
            "sojd,dhg->ohsjg", ordered, weight_grouped, preferred_element_type=jnp.float32
        )
        term = term.reshape(owners * KVH * project_count * unit_rows, GW)
        mine = lax.psum_scatter(term, "tensor", scatter_dimension=0, tiled=True)
        joined_block = mine.astype(jnp.bfloat16).reshape(project_count, unit_rows, GW)
        prepare_count = joined_block.shape[0]
        steps_here = step + jnp.arange(prepare_count, dtype=jnp.int32)
        position = row_length[None, :] + QR * steps_here[:, None] + row_step[None, :]
        prepare_queries = rotate(
            joined_block[..., : GQ * HD]
            .reshape(prepare_count, unit_rows, GQ, HD)
            .astype(jnp.float32),
            position[:, :, None],
        ).astype(jnp.bfloat16)
        keys = rotate(
            joined_block[..., GQ * HD : GQ * HD + HD].astype(jnp.float32), position
        ).astype(jnp.bfloat16)
        queries, keys, values = (prepare_queries, keys, joined_block[..., GQ * HD + HD :])
        keys_seen.append(keys)
        values_seen.append(values)
        keys_all = jnp.concatenate(keys_seen, 0)
        attend_count = queries.shape[0]
        cache_best, cache_total, cache_summed = cache_partial(
            queries,
            cache_data[:, :HD],
            cache_data[:, HD:],
            token_scale[:, 0],
            token_scale[:, 1],
            cache_mask,
        )
        news = jnp.einsum(
            "srgd,pjd->srgpj", queries, keys_all, preferred_element_type=jnp.float32
        ) * HD ** (-0.5)
        query_step = step + jnp.arange(attend_count, dtype=jnp.int32)[:, None, None, None]
        key_step = jnp.arange(keys_all.shape[0], dtype=jnp.int32)[None, None, :, None]
        allowed = (key_step < query_step) | (key_step == query_step) & (
            row_step[None, None, None, :] <= row_step[None, :, None, None]
        )
        allowed = (allowed & same_request[None, :, None, :])[:, :, None, :, :]
        news = jnp.where(allowed, news, NEG_FILL)
        best = jnp.maximum(cache_best, jnp.max(news, (3, 4)))
        factor = jnp.exp(cache_best - best)
        expo = jnp.where(allowed, jnp.exp(news - best[..., None, None]), 0.0)
        total = cache_total * factor + jnp.sum(expo, (3, 4))
        summed = cache_summed * factor[..., None] + jnp.einsum(
            "srgpj,pjd->srgd",
            expo.astype(jnp.bfloat16),
            jnp.concatenate(values_seen, 0),
            preferred_element_type=jnp.float32,
        )
        attention = (
            (summed / total[..., None])
            .astype(jnp.bfloat16)
            .reshape(attend_count, unit_rows, GQ * HD)
        )
        count = attention.shape[0]
        gathered = lax.all_gather(attention, "tensor", axis=2, tiled=True).reshape(
            count, unit_rows, owners, QH * HD
        )
        mixed = jnp.einsum(
            "sjof,fd->sojd", gathered, out_weight, preferred_element_type=jnp.float32
        )
        mixed = jnp.take(mixed.reshape(count, owners * unit_rows, local_width), inverse, axis=1)
        outputs.append(
            (hidden_in[step : step + count].astype(jnp.float32) + mixed).astype(jnp.bfloat16)
        )
    return jnp.concatenate(outputs, 0)


VMEM_LIMIT = 48 * 1024 * 1024
SHORT = pl.CostEstimate(flops=1, bytes_accessed=1, transcendentals=0)
LOW_BITS = 4
PACKED = 16 // LOW_BITS
LEVELS = 32600.0 * 2**LOW_BITS
POWER_STEPS = 8.0
TILE = 16
MESH_BITS = (1, 2, 4, 8)


def swap(value, bit):
    devices = lax.axis_size("tensor")
    return lax.ppermute(value, "tensor", [(i, i ^ bit) for i in range(devices)])


def no_work(*refs):
    del refs


def together(arrays, after):
    anywhere = pl.BlockSpec(memory_space=pl.ANY)
    return pl.pallas_call(
        no_work,
        in_specs=[anywhere] * (len(arrays) + len(after)),
        out_specs=[anywhere] * len(arrays),
        out_shape=[jax.ShapeDtypeStruct(a.shape, a.dtype) for a in arrays],
        input_output_aliases={i: i for i in range(len(arrays))},
        compiler_params=pltpu.CompilerParams(vmem_limit_bytes=VMEM_LIMIT),
        cost_estimate=SHORT,
        name="together",
    )(*arrays, *after)


def coded_rows(rows):
    return rows + rows // PACKED


def encode(block):
    top = jnp.max(jnp.abs(block), 0, keepdims=True)
    power = jnp.ceil(jnp.log2(jnp.maximum(top, 1e-30)) * POWER_STEPS)
    codes = jnp.round(block * (jnp.exp2(power * (-1.0 / POWER_STEPS)) * LEVELS)).astype(jnp.int32)
    low = codes & (2**LOW_BITS - 1)
    part = block.shape[0] // PACKED
    packed = low[:part]
    for i in range(1, PACKED):
        packed = packed + (low[i * part : (i + 1) * part] << (LOW_BITS * i))
    high = (codes >> LOW_BITS).astype(jnp.int16)
    return jnp.concatenate([high, (packed - 32768).astype(jnp.int16)], 0), power


def decode(codes, power):
    rows = codes.shape[0] * PACKED // (PACKED + 1)
    high = codes[:rows].astype(jnp.int32) << LOW_BITS
    packed = codes[rows:].astype(jnp.int32) + 32768
    low = jnp.concatenate(
        [(packed >> (LOW_BITS * i)) & (2**LOW_BITS - 1) for i in range(PACKED)], 0
    )
    scale = jnp.exp2(power * (1.0 / POWER_STEPS)) * (1.0 / LEVELS)
    return (high + low).astype(jnp.float32) * scale


def pick_row(rows, index):
    ids = lax.broadcasted_iota(jnp.int32, rows.shape, 0)
    return jnp.sum(jnp.where(ids == index, rows, 0.0), 0, keepdims=True)


def store_codes(sent, powers, block, index, steps):
    rows = coded_rows(block.shape[0])
    codes, power = encode(block)
    sent[pl.ds(pl.multiple_of(index * rows, TILE), rows), :] = codes

    powers[pl.ds(index, 1), :] = power

    @pl.when(index == steps - 1)
    def _():
        sent[pl.ds(steps * rows, TILE), :] = powers[...].astype(jnp.int32).astype(jnp.int16)


def project_kernel(chunk, with_pair, core, normed, weights, *refs):
    kept, sent, powers, wide, arrived = refs[-5:]
    index = pl.program_id(0)
    columns = kept.shape[2]

    def copies(group):
        found = []
        for side in range(2):
            owner = core[0] if side == 0 else 1 - core[0]
            first = group * GW + owner * (GQ // 2 * HD) + chunk * (2 * HD)
            spans = [(first, 0, 2 * HD)]
            if with_pair:
                spans.append((group * GW + (GQ + owner) * HD, 2 * HD, HD))
            for number, (start, offset, size) in enumerate(spans):
                found.append(
                    pltpu.make_async_copy(
                        weights.at[:, pl.ds(pl.multiple_of(start, HD), size)],
                        wide.at[group, :, pl.ds(side * columns + offset, size)],
                        arrived.at[group, side, number],
                    )
                )
        return found

    @pl.when(index == 0)
    def _():
        for group in range(KVH):
            for copy in copies(group):
                copy.start()
        powers[...] = jnp.zeros_like(powers)

    for copy in copies(index):
        copy.wait()

    product = jnp.dot(normed[...], wide[index], preferred_element_type=jnp.float32)
    kept[0] = product[:, :columns]
    store_codes(sent, powers, product[:, columns:], index, KVH)


def project(core, normed, qkv_weight, chunk, with_pair, after):
    rows, width = normed.shape
    columns = 2 * HD + (HD if with_pair else 0)
    sent_rows = KVH * coded_rows(rows) + TILE
    return pl.pallas_call(
        functools.partial(project_kernel, chunk, with_pair),
        grid_spec=pltpu.PrefetchScalarGridSpec(
            num_scalar_prefetch=1,
            grid=(KVH,),
            in_specs=[pl.BlockSpec((rows, width), lambda t, c: (0, 0))]
            + [pl.BlockSpec(memory_space=pl.ANY)] * (1 + len(after)),
            out_specs=[
                pl.BlockSpec((1, rows, columns), lambda t, c: (t, 0, 0)),
                pl.BlockSpec((sent_rows, columns), lambda t, c: (0, 0)),
            ],
            scratch_shapes=[
                pltpu.VMEM((TILE, columns), jnp.float32),
                pltpu.VMEM((KVH, width, 2 * columns), jnp.bfloat16),
                pltpu.SemaphoreType.DMA((KVH, 2, 2)),
            ],
        ),
        out_shape=[
            jax.ShapeDtypeStruct((KVH, rows, columns), jnp.float32),
            jax.ShapeDtypeStruct((sent_rows, columns), jnp.int16),
        ],
        compiler_params=pltpu.CompilerParams(vmem_limit_bytes=VMEM_LIMIT),
        cost_estimate=SHORT,
        name="project",
    )(core, normed, qkv_weight, *after)


def fold_kernel(steps, bit, held, landed, landed_powers, *refs):
    kept, sent, powers = refs[-3:]
    index = pl.program_id(0)
    rows = coded_rows(held.shape[1])
    rows_of_powers = landed_powers[...].astype(jnp.int32).astype(jnp.float32)

    def total(side):
        place = pl.multiple_of(side * rows, TILE)
        codes = landed[pl.ds(place, rows), :]
        return held[side] + decode(codes, pick_row(rows_of_powers, 2 * index + side))

    @pl.when(index == 0)
    def _():
        powers[...] = jnp.zeros_like(powers)

    mine = bit[0]
    kept[0] = total(mine)
    store_codes(sent, powers, total(1 - mine), index, steps)


def fold(bit, held, landed, after):
    blocks, rows, columns = held.shape
    steps = blocks // 2
    coded = coded_rows(rows)
    return pl.pallas_call(
        functools.partial(fold_kernel, steps),
        grid_spec=pltpu.PrefetchScalarGridSpec(
            num_scalar_prefetch=1,
            grid=(steps,),
            in_specs=[
                pl.BlockSpec((2, rows, columns), lambda i, b: (i, 0, 0)),
                pl.BlockSpec((2 * coded, columns), lambda i, b: (i, 0)),
                pl.BlockSpec((TILE, columns), lambda i, b: (blocks * coded // TILE, 0)),
            ]
            + [pl.BlockSpec(memory_space=pl.ANY)] * len(after),
            out_specs=[
                pl.BlockSpec((1, rows, columns), lambda i, b: (i, 0, 0)),
                pl.BlockSpec((steps * coded + TILE, columns), lambda i, b: (0, 0)),
            ],
            scratch_shapes=[pltpu.VMEM((TILE, columns), jnp.float32)],
        ),
        out_shape=[
            jax.ShapeDtypeStruct((steps, rows, columns), jnp.float32),
            jax.ShapeDtypeStruct((steps * coded + TILE, columns), jnp.int16),
        ],
        compiler_params=pltpu.CompilerParams(vmem_limit_bytes=VMEM_LIMIT),
        cost_estimate=SHORT,
        name="fold",
    )(bit, held, landed, landed, *after)


def finish_kernel(after_count, core, held, landed, cosine, sine, *refs):
    queries, *pair = refs[after_count:]
    rows = held.shape[1]
    coded = coded_rows(rows)
    power = landed[pl.ds(coded, TILE), :].astype(jnp.int32).astype(jnp.float32)[0:1]
    total = held[0] + decode(landed[pl.ds(0, coded), :], power)
    joined = total.astype(jnp.bfloat16)
    parts = []
    for head in range(joined.shape[1] // HD):
        raw = joined[:, head * HD : (head + 1) * HD]
        wide = raw.astype(jnp.float32)
        turned = wide * cosine[...] + pltpu.roll(wide, HD // 2, 1) * sine[...]
        parts.append((raw, turned.astype(jnp.bfloat16)))
    queries[...] = jnp.concatenate([parts[0][1], parts[1][1]], 1)
    if pair:
        raw, turned = parts[2]
        pair[0][...] = jnp.where(core[0] == 0, turned.astype(jnp.float32), raw.astype(jnp.float32)).astype(
            jnp.bfloat16
        )


def finish(core, held, landed, cosine, sine, after):
    _, rows, columns = held.shape
    whole = pl.BlockSpec(memory_space=pltpu.VMEM)
    shapes = [jax.ShapeDtypeStruct((rows, 2 * HD), jnp.bfloat16)]
    if columns > 2 * HD:
        shapes.append(jax.ShapeDtypeStruct((rows, HD), jnp.bfloat16))
    return pl.pallas_call(
        functools.partial(finish_kernel, len(after)),
        in_specs=[pl.BlockSpec(memory_space=pltpu.SMEM)]
        + [whole] * 4
        + [pl.BlockSpec(memory_space=pl.ANY)] * len(after),
        out_specs=[whole] * len(shapes),
        out_shape=shapes,
        compiler_params=pltpu.CompilerParams(vmem_limit_bytes=VMEM_LIMIT),
        cost_estimate=SHORT,
        name="finish",
    )(core, held, landed, cosine, sine, *after)


def mix_kernel(count, places, *refs):
    pieces = refs[:count]
    weights, start, mixed, total, wide, arrived = refs[count:]
    depth = wide.shape[1]
    columns = wide.shape[2] // 2
    flat = []
    for piece in pieces:
        flat += [piece] if len(piece.shape) == 2 else [piece.at[i] for i in range(piece.shape[0])]
    copies = [
        pltpu.make_async_copy(
            weights.at[pl.ds(pl.multiple_of(places[i] * depth, depth), depth), :],
            wide.at[i],
            arrived.at[i],
        )
        for i in range(len(flat))
    ]
    for copy in copies:
        copy.start()
    cuts = [0, 1, 2, 4, len(flat)]
    cuts = sorted(set(min(cut, len(flat)) for cut in cuts))
    for first, last in zip(cuts, cuts[1:]):
        for copy in copies[first:last]:
            copy.wait()
        for side in range(2):
            span = pl.ds(side * columns, columns)
            source = start if first == 0 else total
            value = source[:, span].astype(jnp.float32)
            for i in range(first, last):
                value = value + jnp.dot(
                    flat[i][...], wide[i, :, span], preferred_element_type=jnp.float32
                )
            target = mixed if last == len(flat) else total
            target[:, span] = value.astype(target.dtype)


def mix(places, pieces, out_weight, start, dtype):
    columns = out_weight.shape[1]
    rows, width = pieces[0].shape[-2:]
    count = sum(1 if len(p.shape) == 2 else p.shape[0] for p in pieces)
    whole = pl.BlockSpec(memory_space=pltpu.VMEM)
    return pl.pallas_call(
        functools.partial(mix_kernel, len(pieces)),
        in_specs=[pl.BlockSpec(memory_space=pltpu.SMEM)]
        + [whole] * len(pieces)
        + [pl.BlockSpec(memory_space=pl.ANY), whole],
        out_specs=whole,
        scratch_shapes=[
            pltpu.VMEM((rows, columns), jnp.float32),
            pltpu.VMEM((count, width, columns), jnp.bfloat16),
            pltpu.SemaphoreType.DMA((count,)),
        ],
        out_shape=jax.ShapeDtypeStruct((rows, columns), dtype),
        compiler_params=pltpu.CompilerParams(vmem_limit_bytes=VMEM_LIMIT),
        cost_estimate=SHORT,
        name="mix",
    )(places, *pieces, out_weight, start)


def pack_kernel(groups, count, *refs):
    flat = []
    for ref in refs[:count]:
        flat += [ref] if len(ref.shape) == 2 else [ref.at[i] for i in range(ref.shape[0])]
    for group, target in zip(groups, refs[-len(groups) :]):
        for place, index in enumerate(group):
            target[place] = flat[index][...]


def pack(pieces, groups, after):
    whole = pl.BlockSpec(memory_space=pltpu.VMEM)
    shape = pieces[0].shape[-2:]
    return pl.pallas_call(
        functools.partial(pack_kernel, groups, len(pieces)),
        in_specs=[whole] * len(pieces) + [pl.BlockSpec(memory_space=pl.ANY)] * len(after),
        out_specs=[whole] * len(groups),
        out_shape=[jax.ShapeDtypeStruct((len(g),) + shape, pieces[0].dtype) for g in groups],
        compiler_params=pltpu.CompilerParams(vmem_limit_bytes=VMEM_LIMIT),
        cost_estimate=SHORT,
        name="pack",
    )(*pieces, *after)


def gather_and_mix(attention, out_weight, start, device):
    def add(mixed, pieces, offsets, dtype=jnp.float32):
        places = jnp.stack([device ^ offset for offset in offsets])
        return mix(places, pieces, out_weight, mixed, dtype)

    near = swap(attention, 4)
    across = swap(attention, 2)
    far = swap(attention, 8)
    partner = swap(attention, 1)
    first, onward = pack([near, across, far], [(0, 1, 2), (0, 2)], [partner])
    (attention,) = together([attention], [onward])

    across_onward = swap(onward, 2)
    farthest = swap(attention, 12)
    first_partner = swap(first, 1)
    mixed = add(start, [attention, partner], (0, 1))
    mixed = add(mixed, [first, first_partner], (4, 2, 8, 5, 3, 9))
    (second,) = pack([across_onward, farthest], [(0, 1, 2)], [mixed])

    last = swap(farthest, 2)
    second_partner = swap(second, 1)
    mixed = add(mixed, [second, second_partner], (6, 10, 12, 7, 11, 13))
    (last,) = together([last], [mixed])

    last_partner = swap(last, 1)
    return add(mixed, [last, last_partner], (14, 15), jnp.bfloat16)


def attend_kernel(
    slot_request,
    queries,
    new_keys,
    new_values,
    own,
    other,
    key_scale,
    value_scale,
    cache_bias,
    new_bias,
    attention,
    slot_best,
    slot_total,
    slot_sum,
    best,
    total,
    summed,
):
    slots = slot_best.shape[0]
    requests, count, _ = queries.shape
    transposed = (((1,), (1,)), ((), ()))
    for request in range(requests):
        scores = (
            lax.dot_general(
                queries[request],
                new_keys[request],
                transposed,
                preferred_element_type=jnp.float32,
            )
            * HD ** (-0.5)
            + new_bias[...]
        )
        top = jnp.max(scores, -1, keepdims=True)
        expo = jnp.exp(scores - top)
        best[request] = jnp.broadcast_to(top, (count, HD))
        total[request] = jnp.broadcast_to(jnp.sum(expo, -1, keepdims=True), (count, HD))
        summed[request] = jnp.dot(
            expo.astype(jnp.bfloat16), new_values[request], preferred_element_type=jnp.float32
        )
    for slot in range(slots):
        request = slot_request[slot]
        query = queries[request]
        raw = [
            part[:, slot * BLK : (slot + 1) * BLK, :].reshape(KVH * BLK, 2 * HD)
            for part in (own, other)
        ]
        scores = jnp.concatenate(
            [
                lax.dot_general(
                    query, kv[:, :HD], transposed, preferred_element_type=jnp.float32
                )
                for kv in raw
            ],
            1,
        )
        scores = scores * key_scale[slot : slot + 1, :] + cache_bias[slot : slot + 1, :]
        top = jnp.max(scores, -1, keepdims=True)
        expo = jnp.exp(scores - top)
        weights = (expo * value_scale[slot : slot + 1, :]).astype(jnp.bfloat16)
        slot_best[slot] = jnp.broadcast_to(top, (count, HD))
        slot_total[slot] = jnp.broadcast_to(jnp.sum(expo, -1, keepdims=True), (count, HD))
        values = jnp.concatenate([kv[:, HD:] for kv in raw], 0)
        slot_sum[slot] = jnp.dot(weights, values, preferred_element_type=jnp.float32)
    for slot in range(slots):
        request = slot_request[slot]
        before = best[request]
        here = slot_best[slot]
        top = jnp.maximum(before, here)
        keep = jnp.exp(before - top)
        add = jnp.exp(here - top)
        best[request] = top
        total[request] = total[request] * keep + slot_total[slot] * add
        summed[request] = summed[request] * keep + slot_sum[slot] * add
    for request in range(requests):
        attention[request] = (summed[request] / total[request]).astype(jnp.bfloat16)


def attend(slot_request, *arrays):
    queries = arrays[0]
    slots = arrays[5].shape[0]
    requests, count, _ = queries.shape
    whole = pl.BlockSpec(memory_space=pltpu.VMEM)
    return pl.pallas_call(
        attend_kernel,
        in_specs=[pl.BlockSpec(memory_space=pltpu.SMEM)] + [whole] * len(arrays),
        out_specs=whole,
        out_shape=jax.ShapeDtypeStruct((requests, count, HD), jnp.bfloat16),
        scratch_shapes=[pltpu.VMEM((slots, count, HD), jnp.float32)] * 3
        + [pltpu.VMEM((requests, count, HD), jnp.float32)] * 3,
        compiler_params=pltpu.CompilerParams(vmem_limit_bytes=VMEM_LIMIT),
        cost_estimate=SHORT,
        name="attend",
    )(slot_request, *arrays)


def slot_layout(request_length, block_table, slots, stripe):
    requests, most = block_table.shape
    stripes = (request_length + stripe - 1) // stripe
    columns = jnp.arange(most, dtype=jnp.int32)
    held = columns[None, :] < stripes[:, None]
    hit = held[:, :, None] & (
        block_table[:, :, None] == jnp.arange(slots, dtype=jnp.int32)[None, None, :]
    )
    hit = hit.astype(jnp.int32)
    order = jnp.arange(requests, dtype=jnp.int32)
    request = jnp.sum(hit * order[:, None, None], (0, 1))
    rank = jnp.sum(hit * columns[None, :, None], (0, 1))
    length = jnp.sum(hit * request_length[:, None, None], (0, 1))
    return request, rank, length


def arrange_kernel(chip, pool, scales, after, *sent):
    slots = pool.shape[0]
    for k, target in enumerate(sent):
        head = chip[0] ^ k
        target[: slots * BLK, :] = pool[:, head].reshape(slots * BLK, 2 * HD)
        target[slots * BLK :, :] = scales[head]


def arrange(chip, cache_pool, scales, after):
    rows = cache_pool.shape[0] * BLK + TILE
    whole = pl.BlockSpec(memory_space=pltpu.VMEM)
    return pl.pallas_call(
        arrange_kernel,
        in_specs=[
            pl.BlockSpec(memory_space=pltpu.SMEM),
            whole,
            whole,
            pl.BlockSpec(memory_space=pl.ANY),
        ],
        out_specs=[whole] * KVH,
        out_shape=[jax.ShapeDtypeStruct((rows, 2 * HD), jnp.bfloat16)] * KVH,
        compiler_params=pltpu.CompilerParams(vmem_limit_bytes=VMEM_LIMIT),
        cost_estimate=SHORT,
        name="arrange",
    )(chip, cache_pool, scales, after)


def local_pairs(
    hidden_in,
    norm_gain,
    qkv_weight,
    out_weight,
    cache_pool,
    cache_scale,
    request_length,
    block_table,
):
    devices = lax.axis_size("tensor")
    device = lax.axis_index("tensor")
    core = device % 2
    chip = device // 2
    stripe = devices * BLK
    slots = cache_pool.shape[0]
    requests = request_length.shape[0]
    rows = STEPS * requests * QR
    width = hidden_in.shape[2]
    heads = GQ // 2

    hidden = hidden_in.astype(jnp.float32)
    sums = jnp.sum(hidden * hidden, -1)
    bits = [jnp.reshape((device >> b) & 1, (1,)).astype(jnp.int32) for b in range(4)]
    scale_rows = jnp.pad(
        jnp.transpose(cache_scale, (1, 2, 0)).reshape(KVH, 1, 2 * slots),
        ((0, 0), (0, TILE - 1), (0, 2 * HD - 2 * slots)),
    )
    sums = sums + swap(sums, 2)
    chip_scalar = jnp.reshape(chip, (1,)).astype(jnp.int32)
    cache_pieces = list(arrange(chip_scalar, cache_pool, scale_rows, sums))

    def handed(k):
        cache_pieces[k] = swap(cache_pieces[k], 2 * k)

    for bit in (1, 4, 8):
        sums = sums + swap(sums, bit)
    normed = (
        hidden * lax.rsqrt(sums[..., None] / D + EPSILON) * norm_gain.astype(jnp.float32)
    ).astype(jnp.bfloat16)
    normed = normed.reshape(rows, width)

    step_ids = jnp.arange(STEPS, dtype=jnp.int32)
    row_ids = jnp.arange(QR, dtype=jnp.int32)
    position = (
        request_length[None, :, None] + QR * step_ids[:, None, None] + row_ids[None, None, :]
    )
    freqs = ROPE_BASE ** (-(jnp.arange(HD // 2, dtype=jnp.float32) * 2.0 / HD))
    angles = position.reshape(rows, 1).astype(jnp.float32) * freqs
    cosine = jnp.concatenate([jnp.cos(angles)] * 2, 1)
    sine = jnp.concatenate([-jnp.sin(angles), jnp.sin(angles)], 1)

    count = GQ // 4
    held, sent = [None] * count, [None] * count

    def projected(chunk, *after):
        held[chunk], sent[chunk] = project(
            bits[0], normed, qkv_weight, chunk, chunk == 0, after
        )

    def hop(chunk, b):
        return swap(sent[chunk], MESH_BITS[b])

    def folded(chunk, b, landed, *after):
        held[chunk], sent[chunk] = fold(bits[b], held[chunk], landed, after)

    def finished(chunk, landed, *after):
        return finish(bits[0], held[chunk], landed, cosine, sine, after)

    projected(0, cache_pieces[0])
    core_0 = hop(0, 0)
    for k in (1, 2, 3, 4):
        handed(k)
    projected(1, held[0])
    (sent[1],) = together([sent[1]], [core_0] + cache_pieces[1:5])

    folded(0, 1, core_0, sent[1])
    core_1, y_0 = hop(1, 0), hop(0, 1)
    handed(5)
    handed(6)
    projected(2, held[0])
    projected(3, held[2])
    sent[2], sent[3] = together(
        [sent[2], sent[3]], [core_1, y_0, cache_pieces[5], cache_pieces[6]]
    )

    core_2, core_3 = hop(2, 0), hop(3, 0)
    handed(7)
    folded(1, 1, core_1, sent[2])
    y_1 = hop(1, 1)
    folded(0, 2, y_0, held[1])
    near_0 = hop(0, 2)
    folded(2, 1, core_2, held[0])
    folded(3, 1, core_3, held[2])
    sent[2], sent[3] = together([sent[2], sent[3]], [y_1, near_0, cache_pieces[7]])

    y_2 = hop(2, 1)
    folded(0, 3, near_0, sent[2])
    far_0 = hop(0, 3)
    folded(1, 2, y_1, sent[2])
    near_1 = hop(1, 2)
    (cache_own,) = pack(cache_pieces, [tuple(range(KVH))], [held[1]])
    cache_other = swap(cache_own, 1)
    (sent[3],) = together([sent[3]], [y_2, far_0, near_1])

    y_3 = hop(3, 1)
    folded(1, 3, near_1, sent[3])
    far_1 = hop(1, 3)
    folded(2, 2, y_2, sent[3])
    near_2 = hop(2, 2)
    query_chunks = [None] * count
    query_chunks[0], pair = finished(0, far_0, held[2])
    pair_other = swap(pair, 1)
    (held[3],) = together([held[3]], [y_3, far_1, near_2, pair_other, cache_other])

    folded(3, 2, y_3)
    near_3 = hop(3, 2)
    folded(2, 3, near_2, held[3])
    far_2 = hop(2, 3)
    (query_chunks[1],) = finished(1, far_1, held[2])
    (held[3],) = together([held[3]], [near_3, far_2])

    folded(3, 3, near_3)
    far_3 = hop(3, 3)
    (query_chunks[2],) = finished(2, far_2, held[3])
    (query_chunks[3],) = finished(3, far_3, query_chunks[2])
    cache_parts = (cache_own, cache_other)
    keys = jnp.where(core == 0, pair, pair_other)
    raw_values = jnp.where(core == 0, pair_other, pair)
    queries = jnp.concatenate(query_chunks, 1).reshape(STEPS, requests, QR, heads, HD)
    queries = jnp.transpose(queries, (1, 0, 2, 3, 4)).reshape(requests, STEPS * QR * heads, HD)

    def by_request(value):
        value = jnp.transpose(value.reshape(STEPS, requests, QR, HD), (1, 0, 2, 3))
        value = value.reshape(requests, STEPS * QR, HD)
        return jnp.pad(value, ((0, 0), (0, TILE - STEPS * QR), (0, 0)))

    slot_request, slot_rank, slot_length = slot_layout(request_length, block_table, slots, stripe)
    source = chip ^ jnp.arange(KVH, dtype=jnp.int32)
    sources = jnp.stack([source * 2 + core, source * 2 + 1 - core])
    offset = sources[:, :, None] * BLK + jnp.arange(BLK, dtype=jnp.int32)[None, None, :]
    token = slot_rank[:, None] * stripe + offset.reshape(1, stripe)
    cache_bias = jnp.where(token < slot_length[:, None], 0.0, NEG_FILL).astype(jnp.float32)
    scales = jnp.concatenate([part[:, slots * BLK, : 2 * slots] for part in cache_parts])
    scales = scales.astype(jnp.float32).reshape(2 * KVH, 2, slots)
    scales = jnp.repeat(jnp.transpose(scales, (1, 2, 0)), BLK, axis=2)
    order = jnp.arange(STEPS * QR * heads, dtype=jnp.int32) // heads
    key_order = jnp.arange(TILE, dtype=jnp.int32)
    new_bias = jnp.where(key_order[None, :] <= order[:, None], 0.0, NEG_FILL).astype(jnp.float32)
    attention = attend(
        slot_request,
        queries,
        by_request(keys),
        by_request(raw_values),
        *cache_parts,
        scales[0] * HD ** (-0.5),
        scales[1],
        cache_bias,
        new_bias,
    )
    attention = jnp.transpose(
        attention.reshape(requests, STEPS, QR, heads, HD), (1, 0, 2, 3, 4)
    ).reshape(rows, heads * HD)
    mixed = gather_and_mix(attention, out_weight, hidden_in.reshape(rows, width), device)
    return mixed.reshape(hidden_in.shape)


def solution(mesh):
    return jax.shard_map(
        local_pairs if mesh.shape["tensor"] == 2 * KVH else local_general,
        mesh=mesh,
        in_specs=(
            P(None, "groups", "tensor"),
            P("tensor"),
            P("tensor", None),
            P(None, "tensor"),
            P(("groups", "tensor"), None, None, None),
            P(("groups", "tensor"), None, None),
            P("groups"),
            P("groups", None),
        ),
        out_specs=P(None, "groups", "tensor"),
        check_vma=False,
    )
```

```python
import functools

import jax
import jax.numpy as jnp
from jax import lax
from jax.experimental import pallas as pl
from jax.experimental.pallas import tpu as pltpu
from jax.sharding import PartitionSpec as P

D = 16384
QH = 128
KVH = 8
HD = 128
QR = 6
STEPS = 2
BLK = 16
GQ = 16
GW = 2304


EPSILON = 1e-05
ROPE_BASE = 500000.0
NEG_FILL = -1e30


def rotate(values, positions):
    half = values.shape[-1] // 2
    freqs = ROPE_BASE ** (-(jnp.arange(half, dtype=jnp.float32) * 2.0 / values.shape[-1]))
    angles = positions.astype(jnp.float32)[..., None] * freqs
    cosine = jnp.cos(angles)
    sine = jnp.sin(angles)
    first = values[..., :half]
    second = values[..., half:]
    return jnp.concatenate([first * cosine - second * sine, second * cosine + first * sine], -1)


def request_layout(request_owner, request_length, block_table, owners, stripe):
    requests = request_owner.shape[0]
    most = block_table.shape[1]
    order = jnp.arange(requests, dtype=jnp.int32)
    stripes = (request_length + stripe - 1) // stripe
    before = (
        (request_owner[None, :] == request_owner[:, None]) & (order[None, :] < order[:, None])
    ).astype(jnp.int32)
    rank = jnp.sum(before, 1)
    offset = jnp.sum(before * stripes[None, :], 1)
    owner_ids = jnp.arange(owners, dtype=jnp.int32)
    mine = request_owner[None, :] == owner_ids[:, None]
    member = mine[:, :, None] & (
        rank[None, :, None] == jnp.arange(requests // owners, dtype=jnp.int32)[None, None, :]
    )
    owner_requests = jnp.sum(member.astype(jnp.int32) * order[None, :, None], 1)
    columns = jnp.arange(most, dtype=jnp.int32)
    within = columns[None, None, :] - offset[None, :, None]
    hit = (mine[:, :, None] & (within >= 0) & (within < stripes[None, :, None])).astype(jnp.int32)
    stripe_request = jnp.sum(hit * order[None, :, None], 1) - (1 - jnp.sum(hit, 1))
    stripe_rank = jnp.sum(hit * within, 1)
    pick = (within[..., None] == columns[None, None, None, :]).astype(jnp.int32)
    slots = jnp.sum(hit[..., None] * pick * block_table[None, :, None, :], (1, 3))
    return (owner_requests, stripe_request, stripe_rank, slots, rank, stripes)


def cache_partial(queries, keys, values, key_scale, value_scale, mask):
    scores = jnp.einsum("srgd,td->srgt", queries, keys, preferred_element_type=jnp.float32)
    scores = jnp.where(mask, scores * key_scale * HD ** (-0.5), NEG_FILL)
    best = jnp.max(scores, -1)
    expo = jnp.where(mask, jnp.exp(scores - best[..., None]), 0.0)
    total = jnp.sum(expo, -1)
    weights = (expo * value_scale).astype(jnp.bfloat16)
    summed = jnp.einsum("srgt,td->srgd", weights, values, preferred_element_type=jnp.float32)
    return (best, total, summed)


def local_general(
    hidden_in,
    norm_gain,
    qkv_weight,
    out_weight,
    cache_pool,
    cache_scale,
    request_length,
    block_table,
):
    devices = lax.axis_size("tensor")
    device = lax.axis_index("tensor")
    owners = devices // KVH
    stripe = devices * BLK
    requests = request_length.shape[0]
    request_owner = jnp.arange(requests, dtype=jnp.int32) % owners
    unit_rows = requests // owners * QR
    most = block_table.shape[1]
    local_width = hidden_in.shape[2]
    my_owner = device // KVH
    owner_requests, stripe_request, stripe_rank, slots, rank, stripes = request_layout(
        request_owner, request_length, block_table, owners, stripe
    )
    step_rows = jnp.arange(QR, dtype=jnp.int32)
    row_order = (owner_requests[:, :, None] * QR + step_rows[None, None, :]).reshape(
        owners * unit_rows
    )
    inverse = ((request_owner * unit_rows + rank * QR)[:, None] + step_rows[None, :]).reshape(
        requests * QR
    )
    row_request = jnp.repeat(owner_requests[my_owner], QR)
    row_length = request_length[row_request]
    row_step = jnp.arange(unit_rows, dtype=jnp.int32) % QR
    same_request = row_request[:, None] == row_request[None, :]
    gain = norm_gain.astype(jnp.float32)
    weight_grouped = qkv_weight.reshape(local_width, KVH, GW)
    sent = cache_pool[jnp.transpose(slots)].reshape(most, devices, BLK, 2 * HD)
    sent_scale = cache_scale[jnp.transpose(slots)].reshape(most, devices, 2)
    landed, landed_scale = (
        lax.all_to_all(sent, "tensor", split_axis=1, concat_axis=1, tiled=True),
        lax.all_to_all(sent_scale, "tensor", split_axis=1, concat_axis=1, tiled=True),
    )
    cache_data = landed.reshape(most * stripe, 2 * HD)
    token_scale = jnp.broadcast_to(
        landed_scale.astype(jnp.float32)[:, :, None, :], (most, devices, BLK, 2)
    ).reshape(most * stripe, 2)
    token = jnp.arange(most * stripe, dtype=jnp.int32)
    token_stripe = token // stripe
    token_request = stripe_request[my_owner][token_stripe]
    token_position = stripe_rank[my_owner][token_stripe] * stripe + token % stripe
    token_length = jnp.where(token_request >= 0, request_length[jnp.maximum(token_request, 0)], 0)
    cache_mask = (
        (token_request[None, :] == row_request[:, None]) & (token_position < token_length)[None, :]
    )[None, :, None, :]
    outputs = []
    keys_seen = []
    values_seen = []
    for step in range(STEPS):
        block = hidden_in[step : step + 1]
        project_count = block.shape[0]
        values = block.astype(jnp.float32)
        sums = lax.psum(jnp.sum(values * values, -1), "tensor")
        normed = (values * lax.rsqrt(sums[..., None] / D + EPSILON) * gain).astype(jnp.bfloat16)
        ordered = jnp.take(normed, row_order, axis=1).reshape(
            project_count, owners, unit_rows, local_width
        )
        term = jnp.einsum(
            "sojd,dhg->ohsjg", ordered, weight_grouped, preferred_element_type=jnp.float32
        )
        term = term.reshape(owners * KVH * project_count * unit_rows, GW)
        mine = lax.psum_scatter(term, "tensor", scatter_dimension=0, tiled=True)
        joined_block = mine.astype(jnp.bfloat16).reshape(project_count, unit_rows, GW)
        prepare_count = joined_block.shape[0]
        steps_here = step + jnp.arange(prepare_count, dtype=jnp.int32)
        position = row_length[None, :] + QR * steps_here[:, None] + row_step[None, :]
        prepare_queries = rotate(
            joined_block[..., : GQ * HD]
            .reshape(prepare_count, unit_rows, GQ, HD)
            .astype(jnp.float32),
            position[:, :, None],
        ).astype(jnp.bfloat16)
        keys = rotate(
            joined_block[..., GQ * HD : GQ * HD + HD].astype(jnp.float32), position
        ).astype(jnp.bfloat16)
        queries, keys, values = (prepare_queries, keys, joined_block[..., GQ * HD + HD :])
        keys_seen.append(keys)
        values_seen.append(values)
        keys_all = jnp.concatenate(keys_seen, 0)
        attend_count = queries.shape[0]
        cache_best, cache_total, cache_summed = cache_partial(
            queries,
            cache_data[:, :HD],
            cache_data[:, HD:],
            token_scale[:, 0],
            token_scale[:, 1],
            cache_mask,
        )
        news = jnp.einsum(
            "srgd,pjd->srgpj", queries, keys_all, preferred_element_type=jnp.float32
        ) * HD ** (-0.5)
        query_step = step + jnp.arange(attend_count, dtype=jnp.int32)[:, None, None, None]
        key_step = jnp.arange(keys_all.shape[0], dtype=jnp.int32)[None, None, :, None]
        allowed = (key_step < query_step) | (key_step == query_step) & (
            row_step[None, None, None, :] <= row_step[None, :, None, None]
        )
        allowed = (allowed & same_request[None, :, None, :])[:, :, None, :, :]
        news = jnp.where(allowed, news, NEG_FILL)
        best = jnp.maximum(cache_best, jnp.max(news, (3, 4)))
        factor = jnp.exp(cache_best - best)
        expo = jnp.where(allowed, jnp.exp(news - best[..., None, None]), 0.0)
        total = cache_total * factor + jnp.sum(expo, (3, 4))
        summed = cache_summed * factor[..., None] + jnp.einsum(
            "srgpj,pjd->srgd",
            expo.astype(jnp.bfloat16),
            jnp.concatenate(values_seen, 0),
            preferred_element_type=jnp.float32,
        )
        attention = (
            (summed / total[..., None])
            .astype(jnp.bfloat16)
            .reshape(attend_count, unit_rows, GQ * HD)
        )
        count = attention.shape[0]
        gathered = lax.all_gather(attention, "tensor", axis=2, tiled=True).reshape(
            count, unit_rows, owners, QH * HD
        )
        mixed = jnp.einsum(
            "sjof,fd->sojd", gathered, out_weight, preferred_element_type=jnp.float32
        )
        mixed = jnp.take(mixed.reshape(count, owners * unit_rows, local_width), inverse, axis=1)
        outputs.append(
            (hidden_in[step : step + count].astype(jnp.float32) + mixed).astype(jnp.bfloat16)
        )
    return jnp.concatenate(outputs, 0)


VMEM_LIMIT = 48 * 1024 * 1024
SHORT = pl.CostEstimate(flops=1, bytes_accessed=1, transcendentals=0)
LOW_BITS = 4
PACKED = 16 // LOW_BITS
LEVELS = 32600.0 * 2**LOW_BITS
POWER_STEPS = 8.0
TILE = 16
MESH_BITS = (1, 2, 4, 8)


def swap(value, bit):
    devices = lax.axis_size("tensor")
    return lax.ppermute(value, "tensor", [(i, i ^ bit) for i in range(devices)])


def no_work(*refs):
    del refs


def together(arrays, after):
    anywhere = pl.BlockSpec(memory_space=pl.ANY)
    return pl.pallas_call(
        no_work,
        in_specs=[anywhere] * (len(arrays) + len(after)),
        out_specs=[anywhere] * len(arrays),
        out_shape=[jax.ShapeDtypeStruct(a.shape, a.dtype) for a in arrays],
        input_output_aliases={i: i for i in range(len(arrays))},
        compiler_params=pltpu.CompilerParams(vmem_limit_bytes=VMEM_LIMIT),
        cost_estimate=SHORT,
        name="together",
    )(*arrays, *after)


def coded_rows(rows):
    return rows + rows // PACKED


def encode(block):
    top = jnp.max(jnp.abs(block), 0, keepdims=True)
    power = jnp.ceil(jnp.log2(jnp.maximum(top, 1e-30)) * POWER_STEPS)
    codes = jnp.round(block * (jnp.exp2(power * (-1.0 / POWER_STEPS)) * LEVELS)).astype(jnp.int32)
    low = codes & (2**LOW_BITS - 1)
    part = block.shape[0] // PACKED
    packed = low[:part]
    for i in range(1, PACKED):
        packed = packed + (low[i * part : (i + 1) * part] << (LOW_BITS * i))
    high = (codes >> LOW_BITS).astype(jnp.int16)
    return jnp.concatenate([high, (packed - 32768).astype(jnp.int16)], 0), power


def decode(codes, power):
    rows = codes.shape[0] * PACKED // (PACKED + 1)
    high = codes[:rows].astype(jnp.int32) << LOW_BITS
    packed = codes[rows:].astype(jnp.int32) + 32768
    low = jnp.concatenate(
        [(packed >> (LOW_BITS * i)) & (2**LOW_BITS - 1) for i in range(PACKED)], 0
    )
    scale = jnp.exp2(power * (1.0 / POWER_STEPS)) * (1.0 / LEVELS)
    return (high + low).astype(jnp.float32) * scale


def pick_row(rows, index):
    ids = lax.broadcasted_iota(jnp.int32, rows.shape, 0)
    return jnp.sum(jnp.where(ids == index, rows, 0.0), 0, keepdims=True)


def store_codes(sent, powers, block, index, steps):
    rows = coded_rows(block.shape[0])
    codes, power = encode(block)
    sent[pl.ds(pl.multiple_of(index * rows, TILE), rows), :] = codes

    powers[pl.ds(index, 1), :] = power

    @pl.when(index == steps - 1)
    def _():
        sent[pl.ds(steps * rows, TILE), :] = powers[...].astype(jnp.int32).astype(jnp.int16)


SLABS = 4
PART_HEADS = GQ // 4


def project_kernel(core, normed, weights, *refs):
    outs, scratch = refs[-8:-4], refs[-4:]
    kept, sent = outs[:2], outs[2:]
    powers, slabs, arrived = scratch[:2], scratch[2], scratch[3]
    index = pl.program_id(0)
    mine = GQ // 2 * HD
    half = mine + HD

    def copies(group):
        slot = group % SLABS
        found = []
        for side in range(2):
            owner = core[0] if side == 0 else 1 - core[0]
            spans = (
                (group * GW + owner * mine, 0, mine),
                (group * GW + (GQ + owner) * HD, mine, HD),
            )
            for number, (start, offset, size) in enumerate(spans):
                found.append(
                    pltpu.make_async_copy(
                        weights.at[:, pl.ds(pl.multiple_of(start, HD), size)],
                        slabs.at[slot, :, pl.ds(side * half + offset, size)],
                        arrived.at[slot, side, number],
                    )
                )
        return found

    @pl.when(index == 0)
    def _():
        for group in range(SLABS):
            for copy in copies(group):
                copy.start()
        for ref in powers:
            ref[...] = jnp.zeros_like(ref)

    for copy in copies(index):
        copy.wait()

    slot = index % SLABS
    part = PART_HEADS * HD
    spans = (((0, part), (mine, HD)), ((part, part),))
    for side in range(2):
        for number in range(2):
            offset = 0
            found = []
            for first, size in spans[number]:
                for start in range(0, size, 2 * HD):
                    wide = min(2 * HD, size - start)
                    product = jnp.dot(
                        normed[...],
                        slabs[slot, :, side * half + first + start : side * half + first + start + wide],
                        preferred_element_type=jnp.float32,
                    )
                    at = slice(offset, offset + wide)
                    if side == 0:
                        kept[number][0, :, at] = product
                    else:
                        rows = coded_rows(product.shape[0])
                        codes, power = encode(product)
                        sent[number][pl.ds(pl.multiple_of(index * rows, TILE), rows), at] = codes
                        found.append(power)
                    offset += wide
            if found:
                powers[number][pl.ds(index, 1), :] = jnp.concatenate(found, 1)

    @pl.when(index + SLABS < KVH)
    def _():
        for copy in copies(index + SLABS):
            copy.start()

    @pl.when(index == KVH - 1)
    def _():
        for target, ref in zip(sent, powers):
            target[pl.ds(target.shape[0] - TILE, TILE), :] = (
                ref[...].astype(jnp.int32).astype(jnp.int16)
            )


def project(core, normed, qkv_weight, after):
    rows, width = normed.shape
    columns = (PART_HEADS * HD + HD, PART_HEADS * HD)
    sent_rows = KVH * coded_rows(rows) + TILE
    return pl.pallas_call(
        project_kernel,
        grid_spec=pltpu.PrefetchScalarGridSpec(
            num_scalar_prefetch=1,
            grid=(KVH,),
            in_specs=[pl.BlockSpec((rows, width), lambda t, c: (0, 0))]
            + [pl.BlockSpec(memory_space=pl.ANY)] * (1 + len(after)),
            out_specs=[pl.BlockSpec((1, rows, n), lambda t, c: (t, 0, 0)) for n in columns]
            + [pl.BlockSpec((sent_rows, n), lambda t, c: (0, 0)) for n in columns],
            scratch_shapes=[pltpu.VMEM((TILE, n), jnp.float32) for n in columns]
            + [
                pltpu.VMEM((SLABS, width, GW), jnp.bfloat16),
                pltpu.SemaphoreType.DMA((SLABS, 2, 2)),
            ],
        ),
        out_shape=[jax.ShapeDtypeStruct((KVH, rows, n), jnp.float32) for n in columns]
        + [jax.ShapeDtypeStruct((sent_rows, n), jnp.int16) for n in columns],
        compiler_params=pltpu.CompilerParams(vmem_limit_bytes=VMEM_LIMIT),
        cost_estimate=SHORT,
        name="project",
    )(core, normed, qkv_weight, *after)


def fold_kernel(steps, low, bit, held, held_out, landed, landed_out, landed_powers, *refs):
    kept, sent, powers = refs[-3:]
    index = pl.program_id(0)
    rows_of_powers = landed_powers[...].astype(jnp.int32).astype(jnp.float32)
    first = index // low * (2 * low) + index % low

    def total(side, block, codes):
        power = pick_row(rows_of_powers, first + side * low)
        return block[0] + decode(codes[...], power)

    @pl.when(index == 0)
    def _():
        powers[...] = jnp.zeros_like(powers)

    kept[0] = total(bit[0], held, landed)
    store_codes(sent, powers, total(1 - bit[0], held_out, landed_out), index, steps)


def fold(bit, held, landed, low, after):
    blocks, rows, columns = held.shape
    steps = blocks // 2
    coded = coded_rows(rows)

    def block(i, b, out):
        side = 1 - b[0] if out else b[0]
        return i // low * (2 * low) + side * low + i % low

    return pl.pallas_call(
        functools.partial(fold_kernel, steps, low),
        grid_spec=pltpu.PrefetchScalarGridSpec(
            num_scalar_prefetch=1,
            grid=(steps,),
            in_specs=[
                pl.BlockSpec((1, rows, columns), lambda i, b: (block(i, b, False), 0, 0)),
                pl.BlockSpec((1, rows, columns), lambda i, b: (block(i, b, True), 0, 0)),
                pl.BlockSpec((coded, columns), lambda i, b: (block(i, b, False), 0)),
                pl.BlockSpec((coded, columns), lambda i, b: (block(i, b, True), 0)),
                pl.BlockSpec((TILE, columns), lambda i, b: (blocks * coded // TILE, 0)),
            ]
            + [pl.BlockSpec(memory_space=pl.ANY)] * len(after),
            out_specs=[
                pl.BlockSpec((1, rows, columns), lambda i, b: (i, 0, 0)),
                pl.BlockSpec((steps * coded + TILE, columns), lambda i, b: (0, 0)),
            ],
            scratch_shapes=[pltpu.VMEM((TILE, columns), jnp.float32)],
        ),
        out_shape=[
            jax.ShapeDtypeStruct((steps, rows, columns), jnp.float32),
            jax.ShapeDtypeStruct((steps * coded + TILE, columns), jnp.int16),
        ],
        compiler_params=pltpu.CompilerParams(vmem_limit_bytes=VMEM_LIMIT),
        cost_estimate=SHORT,
        name="fold",
    )(bit, held, held, landed, landed, landed, *after)


def finish_kernel(after_count, core, held, landed, cosine, sine, *refs):
    queries, *pair = refs[after_count:]
    coded = coded_rows(held.shape[1])
    power = landed[pl.ds(coded, TILE), :].astype(jnp.int32).astype(jnp.float32)[0:1]
    total = held[0] + decode(landed[pl.ds(0, coded), :], power)
    joined = total.astype(jnp.bfloat16)
    for head in range(joined.shape[1] // HD):
        raw = joined[:, head * HD : (head + 1) * HD].astype(jnp.float32)
        turned = raw * cosine[...] + pltpu.roll(raw, HD // 2, 1) * sine[...]
        if head < PART_HEADS:
            queries[:, head * HD : (head + 1) * HD] = turned.astype(jnp.bfloat16)
        else:
            pair[0][...] = jnp.where(core[0] == 0, turned, raw).astype(jnp.bfloat16)


def finish(core, held, landed, cosine, sine, after):
    _, rows, columns = held.shape
    whole = pl.BlockSpec(memory_space=pltpu.VMEM)
    shapes = [jax.ShapeDtypeStruct((rows, PART_HEADS * HD), jnp.bfloat16)]
    if columns > PART_HEADS * HD:
        shapes.append(jax.ShapeDtypeStruct((rows, HD), jnp.bfloat16))
    return pl.pallas_call(
        functools.partial(finish_kernel, len(after)),
        in_specs=[pl.BlockSpec(memory_space=pltpu.SMEM)]
        + [whole] * 4
        + [pl.BlockSpec(memory_space=pl.ANY)] * len(after),
        out_specs=[whole] * len(shapes),
        out_shape=shapes,
        compiler_params=pltpu.CompilerParams(vmem_limit_bytes=VMEM_LIMIT),
        cost_estimate=SHORT,
        name="finish",
    )(core, held, landed, cosine, sine, *after)


def mix_kernel(count, places, *refs):
    pieces = refs[:count]
    weights, start, mixed, total, wide, arrived = refs[count:]
    depth = wide.shape[1]
    columns = wide.shape[2] // 2
    flat = []
    for piece in pieces:
        flat += [piece] if len(piece.shape) == 2 else [piece.at[i] for i in range(piece.shape[0])]
    copies = [
        pltpu.make_async_copy(
            weights.at[pl.ds(pl.multiple_of(places[i] * depth, depth), depth), :],
            wide.at[i],
            arrived.at[i],
        )
        for i in range(len(flat))
    ]
    for copy in copies:
        copy.start()
    cuts = [0, 1, 2, 4, len(flat)]
    cuts = sorted(set(min(cut, len(flat)) for cut in cuts))
    for first, last in zip(cuts, cuts[1:]):
        for copy in copies[first:last]:
            copy.wait()
        for side in range(2):
            span = pl.ds(side * columns, columns)
            source = start if first == 0 else total
            value = source[:, span].astype(jnp.float32)
            for i in range(first, last):
                value = value + jnp.dot(
                    flat[i][...], wide[i, :, span], preferred_element_type=jnp.float32
                )
            target = mixed if last == len(flat) else total
            target[:, span] = value.astype(target.dtype)


def mix(places, pieces, out_weight, start, dtype):
    columns = out_weight.shape[1]
    rows, width = pieces[0].shape[-2:]
    count = sum(1 if len(p.shape) == 2 else p.shape[0] for p in pieces)
    whole = pl.BlockSpec(memory_space=pltpu.VMEM)
    return pl.pallas_call(
        functools.partial(mix_kernel, len(pieces)),
        in_specs=[pl.BlockSpec(memory_space=pltpu.SMEM)]
        + [whole] * len(pieces)
        + [pl.BlockSpec(memory_space=pl.ANY), whole],
        out_specs=whole,
        scratch_shapes=[
            pltpu.VMEM((rows, columns), jnp.float32),
            pltpu.VMEM((count, width, columns), jnp.bfloat16),
            pltpu.SemaphoreType.DMA((count,)),
        ],
        out_shape=jax.ShapeDtypeStruct((rows, columns), dtype),
        compiler_params=pltpu.CompilerParams(vmem_limit_bytes=VMEM_LIMIT),
        cost_estimate=SHORT,
        name="mix",
    )(places, *pieces, out_weight, start)


def pack_kernel(groups, count, *refs):
    flat = []
    for ref in refs[:count]:
        flat += [ref] if len(ref.shape) == 2 else [ref.at[i] for i in range(ref.shape[0])]
    for group, target in zip(groups, refs[-len(groups) :]):
        for place, index in enumerate(group):
            target[place] = flat[index][...]


def pack(pieces, groups, after):
    whole = pl.BlockSpec(memory_space=pltpu.VMEM)
    shape = pieces[0].shape[-2:]
    return pl.pallas_call(
        functools.partial(pack_kernel, groups, len(pieces)),
        in_specs=[whole] * len(pieces) + [pl.BlockSpec(memory_space=pl.ANY)] * len(after),
        out_specs=[whole] * len(groups),
        out_shape=[jax.ShapeDtypeStruct((len(g),) + shape, pieces[0].dtype) for g in groups],
        compiler_params=pltpu.CompilerParams(vmem_limit_bytes=VMEM_LIMIT),
        cost_estimate=SHORT,
        name="pack",
    )(*pieces, *after)


def gather_and_mix(attention, out_weight, start, device):
    def add(mixed, pieces, offsets, dtype=jnp.float32):
        places = jnp.stack([device ^ offset for offset in offsets])
        return mix(places, pieces, out_weight, mixed, dtype)

    near = swap(attention, 4)
    across = swap(attention, 2)
    far = swap(attention, 8)
    partner = swap(attention, 1)
    first, onward = pack([near, across, far], [(0, 1, 2), (0, 2)], [partner])
    (attention,) = together([attention], [onward])

    across_onward = swap(onward, 2)
    farthest = swap(attention, 12)
    first_partner = swap(first, 1)
    mixed = add(start, [attention, partner], (0, 1))
    mixed = add(mixed, [first, first_partner], (4, 2, 8, 5, 3, 9))
    (second,) = pack([across_onward, farthest], [(0, 1, 2)], [mixed])

    last = swap(farthest, 2)
    second_partner = swap(second, 1)
    mixed = add(mixed, [second, second_partner], (6, 10, 12, 7, 11, 13))
    (last,) = together([last], [mixed])

    last_partner = swap(last, 1)
    return add(mixed, [last, last_partner], (14, 15), jnp.bfloat16)


def attend_kernel(
    slot_request,
    queries,
    new_keys,
    new_values,
    own,
    other,
    key_scale,
    value_scale,
    cache_bias,
    new_bias,
    attention,
    slot_best,
    slot_total,
    slot_sum,
    best,
    total,
    summed,
):
    slots = slot_best.shape[0]
    requests, count, _ = queries.shape
    transposed = (((1,), (1,)), ((), ()))
    for request in range(requests):
        scores = (
            lax.dot_general(
                queries[request],
                new_keys[request],
                transposed,
                preferred_element_type=jnp.float32,
            )
            * HD ** (-0.5)
            + new_bias[...]
        )
        top = jnp.max(scores, -1, keepdims=True)
        expo = jnp.exp(scores - top)
        best[request] = jnp.broadcast_to(top, (count, HD))
        total[request] = jnp.broadcast_to(jnp.sum(expo, -1, keepdims=True), (count, HD))
        summed[request] = jnp.dot(
            expo.astype(jnp.bfloat16), new_values[request], preferred_element_type=jnp.float32
        )
    for slot in range(slots):
        request = slot_request[slot]
        query = queries[request]
        raw = [
            part[:, slot * BLK : (slot + 1) * BLK, :].reshape(KVH * BLK, 2 * HD)
            for part in (own, other)
        ]
        scores = jnp.concatenate(
            [
                lax.dot_general(
                    query, kv[:, :HD], transposed, preferred_element_type=jnp.float32
                )
                for kv in raw
            ],
            1,
        )
        scores = scores * key_scale[slot : slot + 1, :] + cache_bias[slot : slot + 1, :]
        top = jnp.max(scores, -1, keepdims=True)
        expo = jnp.exp(scores - top)
        weights = (expo * value_scale[slot : slot + 1, :]).astype(jnp.bfloat16)
        slot_best[slot] = jnp.broadcast_to(top, (count, HD))
        slot_total[slot] = jnp.broadcast_to(jnp.sum(expo, -1, keepdims=True), (count, HD))
        values = jnp.concatenate([kv[:, HD:] for kv in raw], 0)
        slot_sum[slot] = jnp.dot(weights, values, preferred_element_type=jnp.float32)
    for slot in range(slots):
        request = slot_request[slot]
        before = best[request]
        here = slot_best[slot]
        top = jnp.maximum(before, here)
        keep = jnp.exp(before - top)
        add = jnp.exp(here - top)
        best[request] = top
        total[request] = total[request] * keep + slot_total[slot] * add
        summed[request] = summed[request] * keep + slot_sum[slot] * add
    for request in range(requests):
        attention[request] = (summed[request] / total[request]).astype(jnp.bfloat16)


def attend(slot_request, *arrays):
    queries = arrays[0]
    slots = arrays[5].shape[0]
    requests, count, _ = queries.shape
    whole = pl.BlockSpec(memory_space=pltpu.VMEM)
    return pl.pallas_call(
        attend_kernel,
        in_specs=[pl.BlockSpec(memory_space=pltpu.SMEM)] + [whole] * len(arrays),
        out_specs=whole,
        out_shape=jax.ShapeDtypeStruct((requests, count, HD), jnp.bfloat16),
        scratch_shapes=[pltpu.VMEM((slots, count, HD), jnp.float32)] * 3
        + [pltpu.VMEM((requests, count, HD), jnp.float32)] * 3,
        compiler_params=pltpu.CompilerParams(vmem_limit_bytes=VMEM_LIMIT),
        cost_estimate=SHORT,
        name="attend",
    )(slot_request, *arrays)


def slot_layout(request_length, block_table, slots, stripe):
    requests, most = block_table.shape
    stripes = (request_length + stripe - 1) // stripe
    columns = jnp.arange(most, dtype=jnp.int32)
    held = columns[None, :] < stripes[:, None]
    hit = held[:, :, None] & (
        block_table[:, :, None] == jnp.arange(slots, dtype=jnp.int32)[None, None, :]
    )
    hit = hit.astype(jnp.int32)
    order = jnp.arange(requests, dtype=jnp.int32)
    request = jnp.sum(hit * order[:, None, None], (0, 1))
    rank = jnp.sum(hit * columns[None, :, None], (0, 1))
    length = jnp.sum(hit * request_length[:, None, None], (0, 1))
    return request, rank, length


def arrange_kernel(chip, pool, scales, after, *sent):
    slots = pool.shape[0]
    for k, target in enumerate(sent):
        head = chip[0] ^ k
        target[: slots * BLK, :] = pool[:, head].reshape(slots * BLK, 2 * HD)
        target[slots * BLK :, :] = scales[head]


def arrange(chip, cache_pool, scales, after):
    rows = cache_pool.shape[0] * BLK + TILE
    whole = pl.BlockSpec(memory_space=pltpu.VMEM)
    return pl.pallas_call(
        arrange_kernel,
        in_specs=[
            pl.BlockSpec(memory_space=pltpu.SMEM),
            whole,
            whole,
            pl.BlockSpec(memory_space=pl.ANY),
        ],
        out_specs=[whole] * KVH,
        out_shape=[jax.ShapeDtypeStruct((rows, 2 * HD), jnp.bfloat16)] * KVH,
        compiler_params=pltpu.CompilerParams(vmem_limit_bytes=VMEM_LIMIT),
        cost_estimate=SHORT,
        name="arrange",
    )(chip, cache_pool, scales, after)


def local_pairs(
    hidden_in,
    norm_gain,
    qkv_weight,
    out_weight,
    cache_pool,
    cache_scale,
    request_length,
    block_table,
):
    devices = lax.axis_size("tensor")
    device = lax.axis_index("tensor")
    core = device % 2
    chip = device // 2
    stripe = devices * BLK
    slots = cache_pool.shape[0]
    requests = request_length.shape[0]
    rows = STEPS * requests * QR
    width = hidden_in.shape[2]
    heads = GQ // 2

    hidden = hidden_in.astype(jnp.float32)
    sums = jnp.sum(hidden * hidden, -1)
    bits = [jnp.reshape((device >> b) & 1, (1,)).astype(jnp.int32) for b in range(4)]
    scale_rows = jnp.pad(
        jnp.transpose(cache_scale, (1, 2, 0)).reshape(KVH, 1, 2 * slots),
        ((0, 0), (0, TILE - 1), (0, 2 * HD - 2 * slots)),
    )
    sums = sums + swap(sums, 2)
    chip_scalar = jnp.reshape(chip, (1,)).astype(jnp.int32)
    cache_pieces = list(arrange(chip_scalar, cache_pool, scale_rows, sums))

    def handed(k):
        cache_pieces[k] = swap(cache_pieces[k], 2 * k)

    for bit in (1, 4, 8):
        sums = sums + swap(sums, bit)
    normed = (
        hidden * lax.rsqrt(sums[..., None] / D + EPSILON) * norm_gain.astype(jnp.float32)
    ).astype(jnp.bfloat16)
    normed = normed.reshape(rows, width)

    step_ids = jnp.arange(STEPS, dtype=jnp.int32)
    row_ids = jnp.arange(QR, dtype=jnp.int32)
    position = (
        request_length[None, :, None] + QR * step_ids[:, None, None] + row_ids[None, None, :]
    )
    freqs = ROPE_BASE ** (-(jnp.arange(HD // 2, dtype=jnp.float32) * 2.0 / HD))
    angles = position.reshape(rows, 1).astype(jnp.float32) * freqs
    cosine = jnp.concatenate([jnp.cos(angles)] * 2, 1)
    sine = jnp.concatenate([-jnp.sin(angles), jnp.sin(angles)], 1)

    def folded(part, b, landed, low, *after):
        return fold(bits[b], part, landed, low, after)

    def finished(part, landed, *after):
        return finish(bits[0], part, landed, cosine, sine, after)

    for k in range(3, KVH):
        handed(k)
    held_a, held_b, sent_a, sent_b = project(bits[0], normed, qkv_weight, cache_pieces[:1])
    sent_a, sent_b, cache_pieces[1], cache_pieces[2] = together(
        [sent_a, sent_b] + cache_pieces[1:3], cache_pieces[3:]
    )
    core_a, core_b = swap(sent_a, 1), swap(sent_b, 1)
    for k in (1, 2):
        handed(k)
    held_a, sent_a = folded(held_a, 1, core_a, 1)
    line_a = swap(sent_a, 2)
    held_b, sent_b = folded(held_b, 2, core_b, 2, held_a)
    line_b = swap(sent_b, 4)
    (cache_own,) = pack(cache_pieces, [tuple(range(KVH))], [held_b])
    cache_other = swap(cache_own, 1)
    held_b, sent_b = folded(held_b, 1, line_b, 1, cache_own)
    line_b = swap(sent_b, 2)
    held_a, sent_a = folded(held_a, 2, line_a, 1, held_b)
    line_a = swap(sent_a, 4)
    held_b, sent_b = folded(held_b, 3, line_b, 1, held_a)
    line_b = swap(sent_b, 8)
    held_a, sent_a = folded(held_a, 3, line_a, 1, held_b)
    line_a = swap(sent_a, 8)
    (query_b,) = finished(held_b, line_b, held_a)
    query_a, pair = finished(held_a, line_a, query_b)
    pair_other = swap(pair, 1)
    query_chunks = [query_a, query_b]
    cache_parts = (cache_own, cache_other)
    keys = jnp.where(core == 0, pair, pair_other)
    raw_values = jnp.where(core == 0, pair_other, pair)
    queries = jnp.concatenate(query_chunks, 1).reshape(STEPS, requests, QR, heads, HD)
    queries = jnp.transpose(queries, (1, 0, 2, 3, 4)).reshape(requests, STEPS * QR * heads, HD)

    def by_request(value):
        value = jnp.transpose(value.reshape(STEPS, requests, QR, HD), (1, 0, 2, 3))
        value = value.reshape(requests, STEPS * QR, HD)
        return jnp.pad(value, ((0, 0), (0, TILE - STEPS * QR), (0, 0)))

    slot_request, slot_rank, slot_length = slot_layout(request_length, block_table, slots, stripe)
    source = chip ^ jnp.arange(KVH, dtype=jnp.int32)
    sources = jnp.stack([source * 2 + core, source * 2 + 1 - core])
    offset = sources[:, :, None] * BLK + jnp.arange(BLK, dtype=jnp.int32)[None, None, :]
    token = slot_rank[:, None] * stripe + offset.reshape(1, stripe)
    cache_bias = jnp.where(token < slot_length[:, None], 0.0, NEG_FILL).astype(jnp.float32)
    scales = jnp.concatenate([part[:, slots * BLK, : 2 * slots] for part in cache_parts])
    scales = scales.astype(jnp.float32).reshape(2 * KVH, 2, slots)
    scales = jnp.repeat(jnp.transpose(scales, (1, 2, 0)), BLK, axis=2)
    order = jnp.arange(STEPS * QR * heads, dtype=jnp.int32) // heads
    key_order = jnp.arange(TILE, dtype=jnp.int32)
    new_bias = jnp.where(key_order[None, :] <= order[:, None], 0.0, NEG_FILL).astype(jnp.float32)
    attention = attend(
        slot_request,
        queries,
        by_request(keys),
        by_request(raw_values),
        *cache_parts,
        scales[0] * HD ** (-0.5),
        scales[1],
        cache_bias,
        new_bias,
    )
    attention = jnp.transpose(
        attention.reshape(requests, STEPS, QR, heads, HD), (1, 0, 2, 3, 4)
    ).reshape(rows, heads * HD)
    mixed = gather_and_mix(attention, out_weight, hidden_in.reshape(rows, width), device)
    return mixed.reshape(hidden_in.shape)


def solution(mesh):
    return jax.shard_map(
        local_pairs if mesh.shape["tensor"] == 2 * KVH else local_general,
        mesh=mesh,
        in_specs=(
            P(None, "groups", "tensor"),
            P("tensor"),
            P("tensor", None),
            P(None, "tensor"),
            P(("groups", "tensor"), None, None, None),
            P(("groups", "tensor"), None, None),
            P("groups"),
            P("groups", None),
        ),
        out_specs=P(None, "groups", "tensor"),
        check_vma=False,
    )
```

```python
import functools

import jax
import jax.numpy as jnp
from jax import lax
from jax.experimental import pallas as pl
from jax.experimental.pallas import tpu as pltpu
from jax.sharding import PartitionSpec as P

D = 16384
QH = 128
KVH = 8
HD = 128
QR = 6
STEPS = 2
BLK = 16
GQ = 16
GW = 2304


EPSILON = 1e-05
ROPE_BASE = 500000.0
NEG_FILL = -1e30


def rotate(values, positions):
    half = values.shape[-1] // 2
    freqs = ROPE_BASE ** (-(jnp.arange(half, dtype=jnp.float32) * 2.0 / values.shape[-1]))
    angles = positions.astype(jnp.float32)[..., None] * freqs
    cosine = jnp.cos(angles)
    sine = jnp.sin(angles)
    first = values[..., :half]
    second = values[..., half:]
    return jnp.concatenate([first * cosine - second * sine, second * cosine + first * sine], -1)


def request_layout(request_owner, request_length, block_table, owners, stripe):
    requests = request_owner.shape[0]
    most = block_table.shape[1]
    order = jnp.arange(requests, dtype=jnp.int32)
    stripes = (request_length + stripe - 1) // stripe
    before = (
        (request_owner[None, :] == request_owner[:, None]) & (order[None, :] < order[:, None])
    ).astype(jnp.int32)
    rank = jnp.sum(before, 1)
    offset = jnp.sum(before * stripes[None, :], 1)
    owner_ids = jnp.arange(owners, dtype=jnp.int32)
    mine = request_owner[None, :] == owner_ids[:, None]
    member = mine[:, :, None] & (
        rank[None, :, None] == jnp.arange(requests // owners, dtype=jnp.int32)[None, None, :]
    )
    owner_requests = jnp.sum(member.astype(jnp.int32) * order[None, :, None], 1)
    columns = jnp.arange(most, dtype=jnp.int32)
    within = columns[None, None, :] - offset[None, :, None]
    hit = (mine[:, :, None] & (within >= 0) & (within < stripes[None, :, None])).astype(jnp.int32)
    stripe_request = jnp.sum(hit * order[None, :, None], 1) - (1 - jnp.sum(hit, 1))
    stripe_rank = jnp.sum(hit * within, 1)
    pick = (within[..., None] == columns[None, None, None, :]).astype(jnp.int32)
    slots = jnp.sum(hit[..., None] * pick * block_table[None, :, None, :], (1, 3))
    return (owner_requests, stripe_request, stripe_rank, slots, rank, stripes)


def cache_partial(queries, keys, values, key_scale, value_scale, mask):
    scores = jnp.einsum("srgd,td->srgt", queries, keys, preferred_element_type=jnp.float32)
    scores = jnp.where(mask, scores * key_scale * HD ** (-0.5), NEG_FILL)
    best = jnp.max(scores, -1)
    expo = jnp.where(mask, jnp.exp(scores - best[..., None]), 0.0)
    total = jnp.sum(expo, -1)
    weights = (expo * value_scale).astype(jnp.bfloat16)
    summed = jnp.einsum("srgt,td->srgd", weights, values, preferred_element_type=jnp.float32)
    return (best, total, summed)


def local_general(
    hidden_in,
    norm_gain,
    qkv_weight,
    out_weight,
    cache_pool,
    cache_scale,
    request_length,
    block_table,
):
    devices = lax.axis_size("tensor")
    device = lax.axis_index("tensor")
    owners = devices // KVH
    stripe = devices * BLK
    requests = request_length.shape[0]
    request_owner = jnp.arange(requests, dtype=jnp.int32) % owners
    unit_rows = requests // owners * QR
    most = block_table.shape[1]
    local_width = hidden_in.shape[2]
    my_owner = device // KVH
    owner_requests, stripe_request, stripe_rank, slots, rank, stripes = request_layout(
        request_owner, request_length, block_table, owners, stripe
    )
    step_rows = jnp.arange(QR, dtype=jnp.int32)
    row_order = (owner_requests[:, :, None] * QR + step_rows[None, None, :]).reshape(
        owners * unit_rows
    )
    inverse = ((request_owner * unit_rows + rank * QR)[:, None] + step_rows[None, :]).reshape(
        requests * QR
    )
    row_request = jnp.repeat(owner_requests[my_owner], QR)
    row_length = request_length[row_request]
    row_step = jnp.arange(unit_rows, dtype=jnp.int32) % QR
    same_request = row_request[:, None] == row_request[None, :]
    gain = norm_gain.astype(jnp.float32)
    weight_grouped = qkv_weight.reshape(local_width, KVH, GW)
    sent = cache_pool[jnp.transpose(slots)].reshape(most, devices, BLK, 2 * HD)
    sent_scale = cache_scale[jnp.transpose(slots)].reshape(most, devices, 2)
    landed, landed_scale = (
        lax.all_to_all(sent, "tensor", split_axis=1, concat_axis=1, tiled=True),
        lax.all_to_all(sent_scale, "tensor", split_axis=1, concat_axis=1, tiled=True),
    )
    cache_data = landed.reshape(most * stripe, 2 * HD)
    token_scale = jnp.broadcast_to(
        landed_scale.astype(jnp.float32)[:, :, None, :], (most, devices, BLK, 2)
    ).reshape(most * stripe, 2)
    token = jnp.arange(most * stripe, dtype=jnp.int32)
    token_stripe = token // stripe
    token_request = stripe_request[my_owner][token_stripe]
    token_position = stripe_rank[my_owner][token_stripe] * stripe + token % stripe
    token_length = jnp.where(token_request >= 0, request_length[jnp.maximum(token_request, 0)], 0)
    cache_mask = (
        (token_request[None, :] == row_request[:, None]) & (token_position < token_length)[None, :]
    )[None, :, None, :]
    outputs = []
    keys_seen = []
    values_seen = []
    for step in range(STEPS):
        block = hidden_in[step : step + 1]
        project_count = block.shape[0]
        values = block.astype(jnp.float32)
        sums = lax.psum(jnp.sum(values * values, -1), "tensor")
        normed = (values * lax.rsqrt(sums[..., None] / D + EPSILON) * gain).astype(jnp.bfloat16)
        ordered = jnp.take(normed, row_order, axis=1).reshape(
            project_count, owners, unit_rows, local_width
        )
        term = jnp.einsum(
            "sojd,dhg->ohsjg", ordered, weight_grouped, preferred_element_type=jnp.float32
        )
        term = term.reshape(owners * KVH * project_count * unit_rows, GW)
        mine = lax.psum_scatter(term, "tensor", scatter_dimension=0, tiled=True)
        joined_block = mine.astype(jnp.bfloat16).reshape(project_count, unit_rows, GW)
        prepare_count = joined_block.shape[0]
        steps_here = step + jnp.arange(prepare_count, dtype=jnp.int32)
        position = row_length[None, :] + QR * steps_here[:, None] + row_step[None, :]
        prepare_queries = rotate(
            joined_block[..., : GQ * HD]
            .reshape(prepare_count, unit_rows, GQ, HD)
            .astype(jnp.float32),
            position[:, :, None],
        ).astype(jnp.bfloat16)
        keys = rotate(
            joined_block[..., GQ * HD : GQ * HD + HD].astype(jnp.float32), position
        ).astype(jnp.bfloat16)
        queries, keys, values = (prepare_queries, keys, joined_block[..., GQ * HD + HD :])
        keys_seen.append(keys)
        values_seen.append(values)
        keys_all = jnp.concatenate(keys_seen, 0)
        attend_count = queries.shape[0]
        cache_best, cache_total, cache_summed = cache_partial(
            queries,
            cache_data[:, :HD],
            cache_data[:, HD:],
            token_scale[:, 0],
            token_scale[:, 1],
            cache_mask,
        )
        news = jnp.einsum(
            "srgd,pjd->srgpj", queries, keys_all, preferred_element_type=jnp.float32
        ) * HD ** (-0.5)
        query_step = step + jnp.arange(attend_count, dtype=jnp.int32)[:, None, None, None]
        key_step = jnp.arange(keys_all.shape[0], dtype=jnp.int32)[None, None, :, None]
        allowed = (key_step < query_step) | (key_step == query_step) & (
            row_step[None, None, None, :] <= row_step[None, :, None, None]
        )
        allowed = (allowed & same_request[None, :, None, :])[:, :, None, :, :]
        news = jnp.where(allowed, news, NEG_FILL)
        best = jnp.maximum(cache_best, jnp.max(news, (3, 4)))
        factor = jnp.exp(cache_best - best)
        expo = jnp.where(allowed, jnp.exp(news - best[..., None, None]), 0.0)
        total = cache_total * factor + jnp.sum(expo, (3, 4))
        summed = cache_summed * factor[..., None] + jnp.einsum(
            "srgpj,pjd->srgd",
            expo.astype(jnp.bfloat16),
            jnp.concatenate(values_seen, 0),
            preferred_element_type=jnp.float32,
        )
        attention = (
            (summed / total[..., None])
            .astype(jnp.bfloat16)
            .reshape(attend_count, unit_rows, GQ * HD)
        )
        count = attention.shape[0]
        gathered = lax.all_gather(attention, "tensor", axis=2, tiled=True).reshape(
            count, unit_rows, owners, QH * HD
        )
        mixed = jnp.einsum(
            "sjof,fd->sojd", gathered, out_weight, preferred_element_type=jnp.float32
        )
        mixed = jnp.take(mixed.reshape(count, owners * unit_rows, local_width), inverse, axis=1)
        outputs.append(
            (hidden_in[step : step + count].astype(jnp.float32) + mixed).astype(jnp.bfloat16)
        )
    return jnp.concatenate(outputs, 0)


VMEM_LIMIT = 48 * 1024 * 1024
SHORT = pl.CostEstimate(flops=1, bytes_accessed=1, transcendentals=0)
LONG = pl.CostEstimate(flops=2 * 10**10, bytes_accessed=1, transcendentals=0)
LOW_BITS = 4
PACKED = 16 // LOW_BITS
LEVELS = 32600.0 * 2**LOW_BITS
POWER_STEPS = 8.0
TILE = 16
MESH_BITS = (1, 2, 4, 8)


def swap(value, bit):
    devices = lax.axis_size("tensor")
    return lax.ppermute(value, "tensor", [(i, i ^ bit) for i in range(devices)])


def no_work(*refs):
    del refs


def together(arrays, after):
    anywhere = pl.BlockSpec(memory_space=pl.ANY)
    return pl.pallas_call(
        no_work,
        in_specs=[anywhere] * (len(arrays) + len(after)),
        out_specs=[anywhere] * len(arrays),
        out_shape=[jax.ShapeDtypeStruct(a.shape, a.dtype) for a in arrays],
        input_output_aliases={i: i for i in range(len(arrays))},
        compiler_params=pltpu.CompilerParams(vmem_limit_bytes=VMEM_LIMIT),
        cost_estimate=SHORT,
        name="together",
    )(*arrays, *after)


def coded_rows(rows):
    return rows + rows // PACKED


def encode(block):
    top = jnp.max(jnp.abs(block), 0, keepdims=True)
    power = jnp.ceil(jnp.log2(jnp.maximum(top, 1e-30)) * POWER_STEPS)
    codes = jnp.round(block * (jnp.exp2(power * (-1.0 / POWER_STEPS)) * LEVELS)).astype(jnp.int32)
    low = codes & (2**LOW_BITS - 1)
    part = block.shape[0] // PACKED
    packed = low[:part]
    for i in range(1, PACKED):
        packed = packed + (low[i * part : (i + 1) * part] << (LOW_BITS * i))
    high = (codes >> LOW_BITS).astype(jnp.int16)
    return jnp.concatenate([high, (packed - 32768).astype(jnp.int16)], 0), power


def decode(codes, power):
    rows = codes.shape[0] * PACKED // (PACKED + 1)
    high = codes[:rows].astype(jnp.int32) << LOW_BITS
    packed = codes[rows:].astype(jnp.int32) + 32768
    low = jnp.concatenate(
        [(packed >> (LOW_BITS * i)) & (2**LOW_BITS - 1) for i in range(PACKED)], 0
    )
    scale = jnp.exp2(power * (1.0 / POWER_STEPS)) * (1.0 / LEVELS)
    return (high + low).astype(jnp.float32) * scale


def pick_row(rows, index):
    ids = lax.broadcasted_iota(jnp.int32, rows.shape, 0)
    return jnp.sum(jnp.where(ids == index, rows, 0.0), 0, keepdims=True)


def store_codes(sent, powers, block, index, steps):
    rows = coded_rows(block.shape[0])
    codes, power = encode(block)
    sent[pl.ds(pl.multiple_of(index * rows, TILE), rows), :] = codes

    powers[pl.ds(index, 1), :] = power

    @pl.when(index == steps - 1)
    def _():
        sent[pl.ds(steps * rows, TILE), :] = powers[...].astype(jnp.int32).astype(jnp.int16)


PART_HEADS = (3, 5)


def project_kernel(part, core, normed, weights, *refs):
    kept, sent, powers, slabs, arrived = refs[-5:]
    index = pl.program_id(0)
    half = kept.shape[2]
    heads = PART_HEADS[part] * HD
    first = sum(PART_HEADS[:part]) * HD

    def copies(group):
        found = []
        for side in range(2):
            owner = core[0] if side == 0 else 1 - core[0]
            spans = [(group * GW + owner * (GQ // 2 * HD) + first, 0, heads)]
            if half > heads:
                spans.append((group * GW + (GQ + owner) * HD, heads, HD))
            for number, (start, offset, size) in enumerate(spans):
                found.append(
                    pltpu.make_async_copy(
                        weights.at[:, pl.ds(pl.multiple_of(start, HD), size)],
                        slabs.at[group, :, pl.ds(side * half + offset, size)],
                        arrived.at[group, side, number],
                    )
                )
        return found

    @pl.when(index == 0)
    def _():
        for group in range(KVH):
            for copy in copies(group):
                copy.start()
        powers[...] = jnp.zeros_like(powers)

    for copy in copies(index):
        copy.wait()

    found = []
    rows = coded_rows(normed.shape[0])
    for side in range(2):
        for start in range(0, half, 2 * HD):
            at = slice(start, min(start + 2 * HD, half))
            product = jnp.dot(
                normed[...],
                slabs[index, :, side * half + at.start : side * half + at.stop],
                preferred_element_type=jnp.float32,
            )
            if side == 0:
                kept[0, :, at] = product
            else:
                codes, power = encode(product)
                sent[pl.ds(pl.multiple_of(index * rows, TILE), rows), at] = codes
                found.append(power)
    powers[pl.ds(index, 1), :] = jnp.concatenate(found, 1)

    @pl.when(index == KVH - 1)
    def _():
        sent[pl.ds(KVH * rows, TILE), :] = powers[...].astype(jnp.int32).astype(jnp.int16)


def project(core, normed, qkv_weight, part, after):
    rows, width = normed.shape
    columns = PART_HEADS[part] * HD + (HD if part == 0 else 0)
    sent_rows = KVH * coded_rows(rows) + TILE
    return pl.pallas_call(
        functools.partial(project_kernel, part),
        grid_spec=pltpu.PrefetchScalarGridSpec(
            num_scalar_prefetch=1,
            grid=(KVH,),
            in_specs=[pl.BlockSpec((rows, width), lambda t, c: (0, 0))]
            + [pl.BlockSpec(memory_space=pl.ANY)] * (1 + len(after)),
            out_specs=[
                pl.BlockSpec((1, rows, columns), lambda t, c: (t, 0, 0)),
                pl.BlockSpec((sent_rows, columns), lambda t, c: (0, 0)),
            ],
            scratch_shapes=[
                pltpu.VMEM((TILE, columns), jnp.float32),
                pltpu.VMEM((KVH, width, 2 * columns), jnp.bfloat16),
                pltpu.SemaphoreType.DMA((KVH, 2, 2)),
            ],
        ),
        out_shape=[
            jax.ShapeDtypeStruct((KVH, rows, columns), jnp.float32),
            jax.ShapeDtypeStruct((sent_rows, columns), jnp.int16),
        ],
        compiler_params=pltpu.CompilerParams(vmem_limit_bytes=VMEM_LIMIT),
        cost_estimate=SHORT,
        name="project",
    )(core, normed, qkv_weight, *after)


def fold_kernel(steps, low, bit, held, held_out, landed, landed_out, landed_powers, *refs):
    kept, sent, powers = refs[-3:]
    index = pl.program_id(0)
    rows_of_powers = landed_powers[...].astype(jnp.int32).astype(jnp.float32)
    first = index // low * (2 * low) + index % low

    def total(side, block, codes):
        power = pick_row(rows_of_powers, first + side * low)
        return block[0] + decode(codes[...], power)

    @pl.when(index == 0)
    def _():
        powers[...] = jnp.zeros_like(powers)

    kept[0] = total(bit[0], held, landed)
    store_codes(sent, powers, total(1 - bit[0], held_out, landed_out), index, steps)


def fold(bit, held, landed, low, after):
    blocks, rows, columns = held.shape
    steps = blocks // 2
    coded = coded_rows(rows)

    def block(i, b, out):
        side = 1 - b[0] if out else b[0]
        return i // low * (2 * low) + side * low + i % low

    return pl.pallas_call(
        functools.partial(fold_kernel, steps, low),
        grid_spec=pltpu.PrefetchScalarGridSpec(
            num_scalar_prefetch=1,
            grid=(steps,),
            in_specs=[
                pl.BlockSpec((1, rows, columns), lambda i, b: (block(i, b, False), 0, 0)),
                pl.BlockSpec((1, rows, columns), lambda i, b: (block(i, b, True), 0, 0)),
                pl.BlockSpec((coded, columns), lambda i, b: (block(i, b, False), 0)),
                pl.BlockSpec((coded, columns), lambda i, b: (block(i, b, True), 0)),
                pl.BlockSpec((TILE, columns), lambda i, b: (blocks * coded // TILE, 0)),
            ]
            + [pl.BlockSpec(memory_space=pl.ANY)] * len(after),
            out_specs=[
                pl.BlockSpec((1, rows, columns), lambda i, b: (i, 0, 0)),
                pl.BlockSpec((steps * coded + TILE, columns), lambda i, b: (0, 0)),
            ],
            scratch_shapes=[pltpu.VMEM((TILE, columns), jnp.float32)],
        ),
        out_shape=[
            jax.ShapeDtypeStruct((steps, rows, columns), jnp.float32),
            jax.ShapeDtypeStruct((steps * coded + TILE, columns), jnp.int16),
        ],
        compiler_params=pltpu.CompilerParams(vmem_limit_bytes=VMEM_LIMIT),
        cost_estimate=SHORT,
        name="fold",
    )(bit, held, held, landed, landed, landed, *after)


def finish_kernel(heads, after_count, core, held, landed, cosine, sine, *refs):
    queries, *pair = refs[after_count:]
    coded = coded_rows(held.shape[1])
    power = landed[pl.ds(coded, TILE), :].astype(jnp.int32).astype(jnp.float32)[0:1]
    total = held[0] + decode(landed[pl.ds(0, coded), :], power)
    joined = total.astype(jnp.bfloat16)
    for head in range(joined.shape[1] // HD):
        raw = joined[:, head * HD : (head + 1) * HD].astype(jnp.float32)
        turned = raw * cosine[...] + pltpu.roll(raw, HD // 2, 1) * sine[...]
        if head < heads:
            queries[:, head * HD : (head + 1) * HD] = turned.astype(jnp.bfloat16)
        else:
            pair[0][...] = jnp.where(core[0] == 0, turned, raw).astype(jnp.bfloat16)


def finish(core, held, landed, cosine, sine, heads, after):
    _, rows, columns = held.shape
    whole = pl.BlockSpec(memory_space=pltpu.VMEM)
    shapes = [jax.ShapeDtypeStruct((rows, heads * HD), jnp.bfloat16)]
    if columns > heads * HD:
        shapes.append(jax.ShapeDtypeStruct((rows, HD), jnp.bfloat16))
    return pl.pallas_call(
        functools.partial(finish_kernel, heads, len(after)),
        in_specs=[pl.BlockSpec(memory_space=pltpu.SMEM)]
        + [whole] * 4
        + [pl.BlockSpec(memory_space=pl.ANY)] * len(after),
        out_specs=[whole] * len(shapes),
        out_shape=shapes,
        compiler_params=pltpu.CompilerParams(vmem_limit_bytes=VMEM_LIMIT),
        cost_estimate=LONG,
        name="finish",
    )(core, held, landed, cosine, sine, *after)


def mix_kernel(count, places, *refs):
    pieces = refs[:count]
    weights, start, mixed, total, wide, arrived = refs[count:]
    depth = wide.shape[1]
    columns = wide.shape[2] // 2
    flat = []
    for piece in pieces:
        flat += [piece] if len(piece.shape) == 2 else [piece.at[i] for i in range(piece.shape[0])]
    copies = [
        pltpu.make_async_copy(
            weights.at[pl.ds(pl.multiple_of(places[i] * depth, depth), depth), :],
            wide.at[i],
            arrived.at[i],
        )
        for i in range(len(flat))
    ]
    for copy in copies:
        copy.start()
    cuts = [0, 1, 2, 4, len(flat)]
    cuts = sorted(set(min(cut, len(flat)) for cut in cuts))
    for first, last in zip(cuts, cuts[1:]):
        for copy in copies[first:last]:
            copy.wait()
        for side in range(2):
            span = pl.ds(side * columns, columns)
            source = start if first == 0 else total
            value = source[:, span].astype(jnp.float32)
            for i in range(first, last):
                value = value + jnp.dot(
                    flat[i][...], wide[i, :, span], preferred_element_type=jnp.float32
                )
            target = mixed if last == len(flat) else total
            target[:, span] = value.astype(target.dtype)


def mix(places, pieces, out_weight, start, dtype):
    columns = out_weight.shape[1]
    rows, width = pieces[0].shape[-2:]
    count = sum(1 if len(p.shape) == 2 else p.shape[0] for p in pieces)
    whole = pl.BlockSpec(memory_space=pltpu.VMEM)
    return pl.pallas_call(
        functools.partial(mix_kernel, len(pieces)),
        in_specs=[pl.BlockSpec(memory_space=pltpu.SMEM)]
        + [whole] * len(pieces)
        + [pl.BlockSpec(memory_space=pl.ANY), whole],
        out_specs=whole,
        scratch_shapes=[
            pltpu.VMEM((rows, columns), jnp.float32),
            pltpu.VMEM((count, width, columns), jnp.bfloat16),
            pltpu.SemaphoreType.DMA((count,)),
        ],
        out_shape=jax.ShapeDtypeStruct((rows, columns), dtype),
        compiler_params=pltpu.CompilerParams(vmem_limit_bytes=VMEM_LIMIT),
        cost_estimate=SHORT,
        name="mix",
    )(places, *pieces, out_weight, start)


def pack_kernel(groups, count, *refs):
    flat = []
    for ref in refs[:count]:
        flat += [ref] if len(ref.shape) == 2 else [ref.at[i] for i in range(ref.shape[0])]
    for group, target in zip(groups, refs[-len(groups) :]):
        for place, index in enumerate(group):
            target[place] = flat[index][...]


def pack(pieces, groups, after):
    whole = pl.BlockSpec(memory_space=pltpu.VMEM)
    shape = pieces[0].shape[-2:]
    return pl.pallas_call(
        functools.partial(pack_kernel, groups, len(pieces)),
        in_specs=[whole] * len(pieces) + [pl.BlockSpec(memory_space=pl.ANY)] * len(after),
        out_specs=[whole] * len(groups),
        out_shape=[jax.ShapeDtypeStruct((len(g),) + shape, pieces[0].dtype) for g in groups],
        compiler_params=pltpu.CompilerParams(vmem_limit_bytes=VMEM_LIMIT),
        cost_estimate=SHORT,
        name="pack",
    )(*pieces, *after)


def gather_and_mix(attention, out_weight, start, device):
    def add(mixed, pieces, offsets, dtype=jnp.float32):
        places = jnp.stack([device ^ offset for offset in offsets])
        return mix(places, pieces, out_weight, mixed, dtype)

    near = swap(attention, 4)
    across = swap(attention, 2)
    far = swap(attention, 8)
    partner = swap(attention, 1)
    near, attention = together([near, attention], [across, partner])

    across_near = swap(near, 2)
    farthest = swap(attention, 12)
    (first,) = pack([near, across], [(0, 1)], [])
    first_partner = swap(first, 1)
    mixed = add(start, [attention, partner], (0, 1))
    (far,) = together([far], [across_near, first_partner, mixed])

    across_far = swap(far, 2)
    mixed = add(mixed, [first, first_partner], (4, 2, 5, 3))
    (second,) = pack([far, across_near, across_far, farthest], [(0, 1, 2, 3)], [mixed])

    last = swap(farthest, 2)
    second_partner = swap(second, 1)
    mixed = add(mixed, [second, second_partner], (8, 6, 10, 12, 9, 7, 11, 13))
    (last,) = together([last], [mixed])

    last_partner = swap(last, 1)
    return add(mixed, [last, last_partner], (14, 15), jnp.bfloat16)


def attend_kernel(
    slot_request,
    queries,
    new_keys,
    new_values,
    own,
    other,
    key_scale,
    value_scale,
    cache_bias,
    new_bias,
    attention,
    slot_best,
    slot_total,
    slot_sum,
    best,
    total,
    summed,
):
    slots = slot_best.shape[0]
    requests, count, _ = queries.shape
    transposed = (((1,), (1,)), ((), ()))
    for request in range(requests):
        scores = (
            lax.dot_general(
                queries[request],
                new_keys[request],
                transposed,
                preferred_element_type=jnp.float32,
            )
            * HD ** (-0.5)
            + new_bias[...]
        )
        top = jnp.max(scores, -1, keepdims=True)
        expo = jnp.exp(scores - top)
        best[request] = jnp.broadcast_to(top, (count, HD))
        total[request] = jnp.broadcast_to(jnp.sum(expo, -1, keepdims=True), (count, HD))
        summed[request] = jnp.dot(
            expo.astype(jnp.bfloat16), new_values[request], preferred_element_type=jnp.float32
        )
    for slot in range(slots):
        request = slot_request[slot]
        query = queries[request]
        raw = [
            part[:, slot * BLK : (slot + 1) * BLK, :].reshape(KVH * BLK, 2 * HD)
            for part in (own, other)
        ]
        scores = jnp.concatenate(
            [
                lax.dot_general(
                    query, kv[:, :HD], transposed, preferred_element_type=jnp.float32
                )
                for kv in raw
            ],
            1,
        )
        scores = scores * key_scale[slot : slot + 1, :] + cache_bias[slot : slot + 1, :]
        top = jnp.max(scores, -1, keepdims=True)
        expo = jnp.exp(scores - top)
        weights = (expo * value_scale[slot : slot + 1, :]).astype(jnp.bfloat16)
        slot_best[slot] = jnp.broadcast_to(top, (count, HD))
        slot_total[slot] = jnp.broadcast_to(jnp.sum(expo, -1, keepdims=True), (count, HD))
        values = jnp.concatenate([kv[:, HD:] for kv in raw], 0)
        slot_sum[slot] = jnp.dot(weights, values, preferred_element_type=jnp.float32)
    for slot in range(slots):
        request = slot_request[slot]
        before = best[request]
        here = slot_best[slot]
        top = jnp.maximum(before, here)
        keep = jnp.exp(before - top)
        add = jnp.exp(here - top)
        best[request] = top
        total[request] = total[request] * keep + slot_total[slot] * add
        summed[request] = summed[request] * keep + slot_sum[slot] * add
    for request in range(requests):
        attention[request] = (summed[request] / total[request]).astype(jnp.bfloat16)


def attend(slot_request, *arrays):
    queries = arrays[0]
    slots = arrays[5].shape[0]
    requests, count, _ = queries.shape
    whole = pl.BlockSpec(memory_space=pltpu.VMEM)
    return pl.pallas_call(
        attend_kernel,
        in_specs=[pl.BlockSpec(memory_space=pltpu.SMEM)] + [whole] * len(arrays),
        out_specs=whole,
        out_shape=jax.ShapeDtypeStruct((requests, count, HD), jnp.bfloat16),
        scratch_shapes=[pltpu.VMEM((slots, count, HD), jnp.float32)] * 3
        + [pltpu.VMEM((requests, count, HD), jnp.float32)] * 3,
        compiler_params=pltpu.CompilerParams(vmem_limit_bytes=VMEM_LIMIT),
        cost_estimate=SHORT,
        name="attend",
    )(slot_request, *arrays)


def slot_layout(request_length, block_table, slots, stripe):
    requests, most = block_table.shape
    stripes = (request_length + stripe - 1) // stripe
    columns = jnp.arange(most, dtype=jnp.int32)
    held = columns[None, :] < stripes[:, None]
    hit = held[:, :, None] & (
        block_table[:, :, None] == jnp.arange(slots, dtype=jnp.int32)[None, None, :]
    )
    hit = hit.astype(jnp.int32)
    order = jnp.arange(requests, dtype=jnp.int32)
    request = jnp.sum(hit * order[:, None, None], (0, 1))
    rank = jnp.sum(hit * columns[None, :, None], (0, 1))
    length = jnp.sum(hit * request_length[:, None, None], (0, 1))
    return request, rank, length


def arrange_kernel(chip, pool, scales, after, *sent):
    slots = pool.shape[0]
    for k, target in enumerate(sent):
        head = chip[0] ^ k
        target[: slots * BLK, :] = pool[:, head].reshape(slots * BLK, 2 * HD)
        target[slots * BLK :, :] = scales[head]


def arrange(chip, cache_pool, scales, after):
    rows = cache_pool.shape[0] * BLK + TILE
    whole = pl.BlockSpec(memory_space=pltpu.VMEM)
    return pl.pallas_call(
        arrange_kernel,
        in_specs=[
            pl.BlockSpec(memory_space=pltpu.SMEM),
            whole,
            whole,
            pl.BlockSpec(memory_space=pl.ANY),
        ],
        out_specs=[whole] * KVH,
        out_shape=[jax.ShapeDtypeStruct((rows, 2 * HD), jnp.bfloat16)] * KVH,
        compiler_params=pltpu.CompilerParams(vmem_limit_bytes=VMEM_LIMIT),
        cost_estimate=SHORT,
        name="arrange",
    )(chip, cache_pool, scales, after)


def local_pairs(
    hidden_in,
    norm_gain,
    qkv_weight,
    out_weight,
    cache_pool,
    cache_scale,
    request_length,
    block_table,
):
    devices = lax.axis_size("tensor")
    device = lax.axis_index("tensor")
    core = device % 2
    chip = device // 2
    stripe = devices * BLK
    slots = cache_pool.shape[0]
    requests = request_length.shape[0]
    rows = STEPS * requests * QR
    width = hidden_in.shape[2]
    heads = GQ // 2

    hidden = hidden_in.astype(jnp.float32)
    sums = jnp.sum(hidden * hidden, -1)
    bits = [jnp.reshape((device >> b) & 1, (1,)).astype(jnp.int32) for b in range(4)]
    scale_rows = jnp.pad(
        jnp.transpose(cache_scale, (1, 2, 0)).reshape(KVH, 1, 2 * slots),
        ((0, 0), (0, TILE - 1), (0, 2 * HD - 2 * slots)),
    )
    sums = sums + swap(sums, 2)
    chip_scalar = jnp.reshape(chip, (1,)).astype(jnp.int32)
    cache_pieces = list(arrange(chip_scalar, cache_pool, scale_rows, sums))

    def handed(k):
        cache_pieces[k] = swap(cache_pieces[k], 2 * k)

    for bit in (1, 4, 8):
        sums = sums + swap(sums, bit)
    normed = (
        hidden * lax.rsqrt(sums[..., None] / D + EPSILON) * norm_gain.astype(jnp.float32)
    ).astype(jnp.bfloat16)
    normed = normed.reshape(rows, width)

    step_ids = jnp.arange(STEPS, dtype=jnp.int32)
    row_ids = jnp.arange(QR, dtype=jnp.int32)
    position = (
        request_length[None, :, None] + QR * step_ids[:, None, None] + row_ids[None, None, :]
    )
    freqs = ROPE_BASE ** (-(jnp.arange(HD // 2, dtype=jnp.float32) * 2.0 / HD))
    angles = position.reshape(rows, 1).astype(jnp.float32) * freqs
    cosine = jnp.concatenate([jnp.cos(angles)] * 2, 1)
    sine = jnp.concatenate([-jnp.sin(angles), jnp.sin(angles)], 1)

    def folded(part, b, landed, low, *after):
        return fold(bits[b], part, landed, low, after)

    def finished(part, number, landed, *after):
        return finish(bits[0], part, landed, cosine, sine, PART_HEADS[number], after)

    for k in (1, 3, 4, 5):
        handed(k)
    held_a, sent_a = project(bits[0], normed, qkv_weight, 0, cache_pieces[:1])
    core_a = swap(sent_a, 1)
    held_b, sent_b = project(
        bits[0], normed, qkv_weight, 1, [held_a, cache_pieces[1], cache_pieces[3]]
    )
    sent_b, cache_pieces[2], cache_pieces[6], cache_pieces[7] = together(
        [sent_b, cache_pieces[2], cache_pieces[6], cache_pieces[7]], cache_pieces[4:6]
    )
    core_b = swap(sent_b, 1)
    held_a, sent_a = folded(held_a, 1, core_a, 1, sent_b)
    line_a = swap(sent_a, 2)
    for k in (2, 6, 7):
        handed(k)
    held_b, sent_b = folded(held_b, 2, core_b, 2, held_a)
    line_b = swap(sent_b, 4)
    late = [cache_pieces[k] for k in (2, 6, 7)]
    held_a, sent_a = folded(held_a, 2, line_a, 1, held_b, *late)
    line_a = swap(sent_a, 4)
    held_b, sent_b = folded(held_b, 1, line_b, 1, held_a)
    line_b = swap(sent_b, 2)
    (cache_own,) = pack(cache_pieces, [tuple(range(KVH))], [held_b])
    cache_other = swap(cache_own, 1)
    held_a, sent_a = folded(held_a, 3, line_a, 1, cache_own)
    line_a = swap(sent_a, 8)
    held_b, sent_b = folded(held_b, 3, line_b, 1, held_a)
    line_b = swap(sent_b, 8)
    query_a, pair = finished(held_a, 0, line_a, held_b)
    pair_other = swap(pair, 1)
    (query_b,) = finished(held_b, 1, line_b, query_a)
    query_chunks = [query_a, query_b]
    cache_parts = (cache_own, cache_other)
    keys = jnp.where(core == 0, pair, pair_other)
    raw_values = jnp.where(core == 0, pair_other, pair)
    queries = jnp.concatenate(query_chunks, 1).reshape(STEPS, requests, QR, heads, HD)
    queries = jnp.transpose(queries, (1, 0, 2, 3, 4)).reshape(requests, STEPS * QR * heads, HD)

    def by_request(value):
        value = jnp.transpose(value.reshape(STEPS, requests, QR, HD), (1, 0, 2, 3))
        value = value.reshape(requests, STEPS * QR, HD)
        return jnp.pad(value, ((0, 0), (0, TILE - STEPS * QR), (0, 0)))

    slot_request, slot_rank, slot_length = slot_layout(request_length, block_table, slots, stripe)
    source = chip ^ jnp.arange(KVH, dtype=jnp.int32)
    sources = jnp.stack([source * 2 + core, source * 2 + 1 - core])
    offset = sources[:, :, None] * BLK + jnp.arange(BLK, dtype=jnp.int32)[None, None, :]
    token = slot_rank[:, None] * stripe + offset.reshape(1, stripe)
    cache_bias = jnp.where(token < slot_length[:, None], 0.0, NEG_FILL).astype(jnp.float32)
    scales = jnp.concatenate([part[:, slots * BLK, : 2 * slots] for part in cache_parts])
    scales = scales.astype(jnp.float32).reshape(2 * KVH, 2, slots)
    scales = jnp.repeat(jnp.transpose(scales, (1, 2, 0)), BLK, axis=2)
    order = jnp.arange(STEPS * QR * heads, dtype=jnp.int32) // heads
    key_order = jnp.arange(TILE, dtype=jnp.int32)
    new_bias = jnp.where(key_order[None, :] <= order[:, None], 0.0, NEG_FILL).astype(jnp.float32)
    attention = attend(
        slot_request,
        queries,
        by_request(keys),
        by_request(raw_values),
        *cache_parts,
        scales[0] * HD ** (-0.5),
        scales[1],
        cache_bias,
        new_bias,
    )
    attention = jnp.transpose(
        attention.reshape(requests, STEPS, QR, heads, HD), (1, 0, 2, 3, 4)
    ).reshape(rows, heads * HD)
    mixed = gather_and_mix(attention, out_weight, hidden_in.reshape(rows, width), device)
    return mixed.reshape(hidden_in.shape)


def solution(mesh):
    return jax.shard_map(
        local_pairs if mesh.shape["tensor"] == 2 * KVH else local_general,
        mesh=mesh,
        in_specs=(
            P(None, "groups", "tensor"),
            P("tensor"),
            P("tensor", None),
            P(None, "tensor"),
            P(("groups", "tensor"), None, None, None),
            P(("groups", "tensor"), None, None),
            P("groups"),
            P("groups", None),
        ),
        out_specs=P(None, "groups", "tensor"),
        check_vma=False,
    )
```

```python
import functools

import jax
import jax.numpy as jnp
from jax import lax
from jax.experimental import pallas as pl
from jax.experimental.pallas import tpu as pltpu
from jax.sharding import PartitionSpec as P

D = 16384
QH = 128
KVH = 8
HD = 128
QR = 6
STEPS = 2
BLK = 16
GQ = 16
GW = 2304


EPSILON = 1e-05
ROPE_BASE = 500000.0
NEG_FILL = -1e30


def rotate(values, positions):
    half = values.shape[-1] // 2
    freqs = ROPE_BASE ** (-(jnp.arange(half, dtype=jnp.float32) * 2.0 / values.shape[-1]))
    angles = positions.astype(jnp.float32)[..., None] * freqs
    cosine = jnp.cos(angles)
    sine = jnp.sin(angles)
    first = values[..., :half]
    second = values[..., half:]
    return jnp.concatenate([first * cosine - second * sine, second * cosine + first * sine], -1)


def request_layout(request_owner, request_length, block_table, owners, stripe):
    requests = request_owner.shape[0]
    most = block_table.shape[1]
    order = jnp.arange(requests, dtype=jnp.int32)
    stripes = (request_length + stripe - 1) // stripe
    before = (
        (request_owner[None, :] == request_owner[:, None]) & (order[None, :] < order[:, None])
    ).astype(jnp.int32)
    rank = jnp.sum(before, 1)
    offset = jnp.sum(before * stripes[None, :], 1)
    owner_ids = jnp.arange(owners, dtype=jnp.int32)
    mine = request_owner[None, :] == owner_ids[:, None]
    member = mine[:, :, None] & (
        rank[None, :, None] == jnp.arange(requests // owners, dtype=jnp.int32)[None, None, :]
    )
    owner_requests = jnp.sum(member.astype(jnp.int32) * order[None, :, None], 1)
    columns = jnp.arange(most, dtype=jnp.int32)
    within = columns[None, None, :] - offset[None, :, None]
    hit = (mine[:, :, None] & (within >= 0) & (within < stripes[None, :, None])).astype(jnp.int32)
    stripe_request = jnp.sum(hit * order[None, :, None], 1) - (1 - jnp.sum(hit, 1))
    stripe_rank = jnp.sum(hit * within, 1)
    pick = (within[..., None] == columns[None, None, None, :]).astype(jnp.int32)
    slots = jnp.sum(hit[..., None] * pick * block_table[None, :, None, :], (1, 3))
    return (owner_requests, stripe_request, stripe_rank, slots, rank, stripes)


def cache_partial(queries, keys, values, key_scale, value_scale, mask):
    scores = jnp.einsum("srgd,td->srgt", queries, keys, preferred_element_type=jnp.float32)
    scores = jnp.where(mask, scores * key_scale * HD ** (-0.5), NEG_FILL)
    best = jnp.max(scores, -1)
    expo = jnp.where(mask, jnp.exp(scores - best[..., None]), 0.0)
    total = jnp.sum(expo, -1)
    weights = (expo * value_scale).astype(jnp.bfloat16)
    summed = jnp.einsum("srgt,td->srgd", weights, values, preferred_element_type=jnp.float32)
    return (best, total, summed)


def local_general(
    hidden_in,
    norm_gain,
    qkv_weight,
    out_weight,
    cache_pool,
    cache_scale,
    request_length,
    block_table,
):
    devices = lax.axis_size("tensor")
    device = lax.axis_index("tensor")
    owners = devices // KVH
    stripe = devices * BLK
    requests = request_length.shape[0]
    request_owner = jnp.arange(requests, dtype=jnp.int32) % owners
    unit_rows = requests // owners * QR
    most = block_table.shape[1]
    local_width = hidden_in.shape[2]
    my_owner = device // KVH
    owner_requests, stripe_request, stripe_rank, slots, rank, stripes = request_layout(
        request_owner, request_length, block_table, owners, stripe
    )
    step_rows = jnp.arange(QR, dtype=jnp.int32)
    row_order = (owner_requests[:, :, None] * QR + step_rows[None, None, :]).reshape(
        owners * unit_rows
    )
    inverse = ((request_owner * unit_rows + rank * QR)[:, None] + step_rows[None, :]).reshape(
        requests * QR
    )
    row_request = jnp.repeat(owner_requests[my_owner], QR)
    row_length = request_length[row_request]
    row_step = jnp.arange(unit_rows, dtype=jnp.int32) % QR
    same_request = row_request[:, None] == row_request[None, :]
    gain = norm_gain.astype(jnp.float32)
    weight_grouped = qkv_weight.reshape(local_width, KVH, GW)
    sent = cache_pool[jnp.transpose(slots)].reshape(most, devices, BLK, 2 * HD)
    sent_scale = cache_scale[jnp.transpose(slots)].reshape(most, devices, 2)
    landed, landed_scale = (
        lax.all_to_all(sent, "tensor", split_axis=1, concat_axis=1, tiled=True),
        lax.all_to_all(sent_scale, "tensor", split_axis=1, concat_axis=1, tiled=True),
    )
    cache_data = landed.reshape(most * stripe, 2 * HD)
    token_scale = jnp.broadcast_to(
        landed_scale.astype(jnp.float32)[:, :, None, :], (most, devices, BLK, 2)
    ).reshape(most * stripe, 2)
    token = jnp.arange(most * stripe, dtype=jnp.int32)
    token_stripe = token // stripe
    token_request = stripe_request[my_owner][token_stripe]
    token_position = stripe_rank[my_owner][token_stripe] * stripe + token % stripe
    token_length = jnp.where(token_request >= 0, request_length[jnp.maximum(token_request, 0)], 0)
    cache_mask = (
        (token_request[None, :] == row_request[:, None]) & (token_position < token_length)[None, :]
    )[None, :, None, :]
    outputs = []
    keys_seen = []
    values_seen = []
    for step in range(STEPS):
        block = hidden_in[step : step + 1]
        project_count = block.shape[0]
        values = block.astype(jnp.float32)
        sums = lax.psum(jnp.sum(values * values, -1), "tensor")
        normed = (values * lax.rsqrt(sums[..., None] / D + EPSILON) * gain).astype(jnp.bfloat16)
        ordered = jnp.take(normed, row_order, axis=1).reshape(
            project_count, owners, unit_rows, local_width
        )
        term = jnp.einsum(
            "sojd,dhg->ohsjg", ordered, weight_grouped, preferred_element_type=jnp.float32
        )
        term = term.reshape(owners * KVH * project_count * unit_rows, GW)
        mine = lax.psum_scatter(term, "tensor", scatter_dimension=0, tiled=True)
        joined_block = mine.astype(jnp.bfloat16).reshape(project_count, unit_rows, GW)
        prepare_count = joined_block.shape[0]
        steps_here = step + jnp.arange(prepare_count, dtype=jnp.int32)
        position = row_length[None, :] + QR * steps_here[:, None] + row_step[None, :]
        prepare_queries = rotate(
            joined_block[..., : GQ * HD]
            .reshape(prepare_count, unit_rows, GQ, HD)
            .astype(jnp.float32),
            position[:, :, None],
        ).astype(jnp.bfloat16)
        keys = rotate(
            joined_block[..., GQ * HD : GQ * HD + HD].astype(jnp.float32), position
        ).astype(jnp.bfloat16)
        queries, keys, values = (prepare_queries, keys, joined_block[..., GQ * HD + HD :])
        keys_seen.append(keys)
        values_seen.append(values)
        keys_all = jnp.concatenate(keys_seen, 0)
        attend_count = queries.shape[0]
        cache_best, cache_total, cache_summed = cache_partial(
            queries,
            cache_data[:, :HD],
            cache_data[:, HD:],
            token_scale[:, 0],
            token_scale[:, 1],
            cache_mask,
        )
        news = jnp.einsum(
            "srgd,pjd->srgpj", queries, keys_all, preferred_element_type=jnp.float32
        ) * HD ** (-0.5)
        query_step = step + jnp.arange(attend_count, dtype=jnp.int32)[:, None, None, None]
        key_step = jnp.arange(keys_all.shape[0], dtype=jnp.int32)[None, None, :, None]
        allowed = (key_step < query_step) | (key_step == query_step) & (
            row_step[None, None, None, :] <= row_step[None, :, None, None]
        )
        allowed = (allowed & same_request[None, :, None, :])[:, :, None, :, :]
        news = jnp.where(allowed, news, NEG_FILL)
        best = jnp.maximum(cache_best, jnp.max(news, (3, 4)))
        factor = jnp.exp(cache_best - best)
        expo = jnp.where(allowed, jnp.exp(news - best[..., None, None]), 0.0)
        total = cache_total * factor + jnp.sum(expo, (3, 4))
        summed = cache_summed * factor[..., None] + jnp.einsum(
            "srgpj,pjd->srgd",
            expo.astype(jnp.bfloat16),
            jnp.concatenate(values_seen, 0),
            preferred_element_type=jnp.float32,
        )
        attention = (
            (summed / total[..., None])
            .astype(jnp.bfloat16)
            .reshape(attend_count, unit_rows, GQ * HD)
        )
        count = attention.shape[0]
        gathered = lax.all_gather(attention, "tensor", axis=2, tiled=True).reshape(
            count, unit_rows, owners, QH * HD
        )
        mixed = jnp.einsum(
            "sjof,fd->sojd", gathered, out_weight, preferred_element_type=jnp.float32
        )
        mixed = jnp.take(mixed.reshape(count, owners * unit_rows, local_width), inverse, axis=1)
        outputs.append(
            (hidden_in[step : step + count].astype(jnp.float32) + mixed).astype(jnp.bfloat16)
        )
    return jnp.concatenate(outputs, 0)


VMEM_LIMIT = 48 * 1024 * 1024
SHORT = pl.CostEstimate(flops=1, bytes_accessed=1, transcendentals=0)
LONG = pl.CostEstimate(flops=2 * 10**10, bytes_accessed=1, transcendentals=0)
LOW_BITS = 4
PACKED = 16 // LOW_BITS
LEVELS = 32600.0 * 2**LOW_BITS
POWER_STEPS = 8.0
TILE = 16
MESH_BITS = (1, 2, 4, 8)


def swap(value, bit):
    devices = lax.axis_size("tensor")
    return lax.ppermute(value, "tensor", [(i, i ^ bit) for i in range(devices)])


def no_work(*refs):
    del refs


def together(arrays, after):
    anywhere = pl.BlockSpec(memory_space=pl.ANY)
    return pl.pallas_call(
        no_work,
        in_specs=[anywhere] * (len(arrays) + len(after)),
        out_specs=[anywhere] * len(arrays),
        out_shape=[jax.ShapeDtypeStruct(a.shape, a.dtype) for a in arrays],
        input_output_aliases={i: i for i in range(len(arrays))},
        compiler_params=pltpu.CompilerParams(vmem_limit_bytes=VMEM_LIMIT),
        cost_estimate=SHORT,
        name="together",
    )(*arrays, *after)


def coded_rows(rows):
    return rows + rows // PACKED


def encode(block):
    top = jnp.max(jnp.abs(block), 0, keepdims=True)
    power = jnp.ceil(jnp.log2(jnp.maximum(top, 1e-30)) * POWER_STEPS)
    codes = jnp.round(block * (jnp.exp2(power * (-1.0 / POWER_STEPS)) * LEVELS)).astype(jnp.int32)
    low = codes & (2**LOW_BITS - 1)
    part = block.shape[0] // PACKED
    packed = low[:part]
    for i in range(1, PACKED):
        packed = packed + (low[i * part : (i + 1) * part] << (LOW_BITS * i))
    high = (codes >> LOW_BITS).astype(jnp.int16)
    return jnp.concatenate([high, (packed - 32768).astype(jnp.int16)], 0), power


def decode(codes, power):
    rows = codes.shape[0] * PACKED // (PACKED + 1)
    high = codes[:rows].astype(jnp.int32) << LOW_BITS
    packed = codes[rows:].astype(jnp.int32) + 32768
    low = jnp.concatenate(
        [(packed >> (LOW_BITS * i)) & (2**LOW_BITS - 1) for i in range(PACKED)], 0
    )
    scale = jnp.exp2(power * (1.0 / POWER_STEPS)) * (1.0 / LEVELS)
    return (high + low).astype(jnp.float32) * scale


def pick_row(rows, index):
    ids = lax.broadcasted_iota(jnp.int32, rows.shape, 0)
    return jnp.sum(jnp.where(ids == index, rows, 0.0), 0, keepdims=True)


def store_codes(sent, powers, block, index, steps):
    rows = coded_rows(block.shape[0])
    codes, power = encode(block)
    sent[pl.ds(pl.multiple_of(index * rows, TILE), rows), :] = codes

    powers[pl.ds(index, 1), :] = power

    @pl.when(index == steps - 1)
    def _():
        sent[pl.ds(steps * rows, TILE), :] = powers[...].astype(jnp.int32).astype(jnp.int16)


PART_HEADS = (3, 5)


def project_kernel(part, core, normed, weights, *refs):
    kept, sent, powers, slabs, arrived = refs[-5:]
    index = pl.program_id(0)
    half = kept.shape[2]
    heads = PART_HEADS[part] * HD
    first = sum(PART_HEADS[:part]) * HD

    def copies(group):
        found = []
        for side in range(2):
            owner = core[0] if side == 0 else 1 - core[0]
            spans = [(group * GW + owner * (GQ // 2 * HD) + first, 0, heads)]
            if half > heads:
                spans.append((group * GW + (GQ + owner) * HD, heads, HD))
            for number, (start, offset, size) in enumerate(spans):
                found.append(
                    pltpu.make_async_copy(
                        weights.at[:, pl.ds(pl.multiple_of(start, HD), size)],
                        slabs.at[group, :, pl.ds(side * half + offset, size)],
                        arrived.at[group, side, number],
                    )
                )
        return found

    @pl.when(index == 0)
    def _():
        for group in range(KVH):
            for copy in copies(group):
                copy.start()
        powers[...] = jnp.zeros_like(powers)

    for copy in copies(index):
        copy.wait()

    found = []
    rows = coded_rows(normed.shape[0])
    for side in range(2):
        for start in range(0, half, 2 * HD):
            at = slice(start, min(start + 2 * HD, half))
            product = jnp.dot(
                normed[...],
                slabs[index, :, side * half + at.start : side * half + at.stop],
                preferred_element_type=jnp.float32,
            )
            if side == 0:
                kept[0, :, at] = product
            else:
                codes, power = encode(product)
                sent[pl.ds(pl.multiple_of(index * rows, TILE), rows), at] = codes
                found.append(power)
    powers[pl.ds(index, 1), :] = jnp.concatenate(found, 1)

    @pl.when(index == KVH - 1)
    def _():
        sent[pl.ds(KVH * rows, TILE), :] = powers[...].astype(jnp.int32).astype(jnp.int16)


def project(core, normed, qkv_weight, part, after):
    rows, width = normed.shape
    columns = PART_HEADS[part] * HD + (HD if part == 0 else 0)
    sent_rows = KVH * coded_rows(rows) + TILE
    return pl.pallas_call(
        functools.partial(project_kernel, part),
        grid_spec=pltpu.PrefetchScalarGridSpec(
            num_scalar_prefetch=1,
            grid=(KVH,),
            in_specs=[pl.BlockSpec((rows, width), lambda t, c: (0, 0))]
            + [pl.BlockSpec(memory_space=pl.ANY)] * (1 + len(after)),
            out_specs=[
                pl.BlockSpec((1, rows, columns), lambda t, c: (t, 0, 0)),
                pl.BlockSpec((sent_rows, columns), lambda t, c: (0, 0)),
            ],
            scratch_shapes=[
                pltpu.VMEM((TILE, columns), jnp.float32),
                pltpu.VMEM((KVH, width, 2 * columns), jnp.bfloat16),
                pltpu.SemaphoreType.DMA((KVH, 2, 2)),
            ],
        ),
        out_shape=[
            jax.ShapeDtypeStruct((KVH, rows, columns), jnp.float32),
            jax.ShapeDtypeStruct((sent_rows, columns), jnp.int16),
        ],
        compiler_params=pltpu.CompilerParams(vmem_limit_bytes=VMEM_LIMIT),
        cost_estimate=SHORT,
        name="project",
    )(core, normed, qkv_weight, *after)


def fold_kernel(steps, low, bit, held, held_out, landed, landed_out, landed_powers, *refs):
    kept, sent, powers = refs[-3:]
    index = pl.program_id(0)
    rows_of_powers = landed_powers[...].astype(jnp.int32).astype(jnp.float32)
    first = index // low * (2 * low) + index % low

    def total(side, block, codes):
        power = pick_row(rows_of_powers, first + side * low)
        return block[0] + decode(codes[...], power)

    @pl.when(index == 0)
    def _():
        powers[...] = jnp.zeros_like(powers)

    kept[0] = total(bit[0], held, landed)
    store_codes(sent, powers, total(1 - bit[0], held_out, landed_out), index, steps)


def fold(bit, held, landed, low, after):
    blocks, rows, columns = held.shape
    steps = blocks // 2
    coded = coded_rows(rows)

    def block(i, b, out):
        side = 1 - b[0] if out else b[0]
        return i // low * (2 * low) + side * low + i % low

    return pl.pallas_call(
        functools.partial(fold_kernel, steps, low),
        grid_spec=pltpu.PrefetchScalarGridSpec(
            num_scalar_prefetch=1,
            grid=(steps,),
            in_specs=[
                pl.BlockSpec((1, rows, columns), lambda i, b: (block(i, b, False), 0, 0)),
                pl.BlockSpec((1, rows, columns), lambda i, b: (block(i, b, True), 0, 0)),
                pl.BlockSpec((coded, columns), lambda i, b: (block(i, b, False), 0)),
                pl.BlockSpec((coded, columns), lambda i, b: (block(i, b, True), 0)),
                pl.BlockSpec((TILE, columns), lambda i, b: (blocks * coded // TILE, 0)),
            ]
            + [pl.BlockSpec(memory_space=pl.ANY)] * len(after),
            out_specs=[
                pl.BlockSpec((1, rows, columns), lambda i, b: (i, 0, 0)),
                pl.BlockSpec((steps * coded + TILE, columns), lambda i, b: (0, 0)),
            ],
            scratch_shapes=[pltpu.VMEM((TILE, columns), jnp.float32)],
        ),
        out_shape=[
            jax.ShapeDtypeStruct((steps, rows, columns), jnp.float32),
            jax.ShapeDtypeStruct((steps * coded + TILE, columns), jnp.int16),
        ],
        compiler_params=pltpu.CompilerParams(vmem_limit_bytes=VMEM_LIMIT),
        cost_estimate=SHORT,
        name="fold",
    )(bit, held, held, landed, landed, landed, *after)


def finish_kernel(heads, after_count, core, held, landed, cosine, sine, *refs):
    queries, *pair = refs[after_count:]
    coded = coded_rows(held.shape[1])
    power = landed[pl.ds(coded, TILE), :].astype(jnp.int32).astype(jnp.float32)[0:1]
    total = held[0] + decode(landed[pl.ds(0, coded), :], power)
    joined = total.astype(jnp.bfloat16)
    for head in range(joined.shape[1] // HD):
        raw = joined[:, head * HD : (head + 1) * HD].astype(jnp.float32)
        turned = raw * cosine[...] + pltpu.roll(raw, HD // 2, 1) * sine[...]
        if head < heads:
            queries[:, head * HD : (head + 1) * HD] = turned.astype(jnp.bfloat16)
        else:
            pair[0][...] = jnp.where(core[0] == 0, turned, raw).astype(jnp.bfloat16)


def finish(core, held, landed, cosine, sine, heads, after):
    _, rows, columns = held.shape
    whole = pl.BlockSpec(memory_space=pltpu.VMEM)
    shapes = [jax.ShapeDtypeStruct((rows, heads * HD), jnp.bfloat16)]
    if columns > heads * HD:
        shapes.append(jax.ShapeDtypeStruct((rows, HD), jnp.bfloat16))
    return pl.pallas_call(
        functools.partial(finish_kernel, heads, len(after)),
        in_specs=[pl.BlockSpec(memory_space=pltpu.SMEM)]
        + [whole] * 4
        + [pl.BlockSpec(memory_space=pl.ANY)] * len(after),
        out_specs=[whole] * len(shapes),
        out_shape=shapes,
        compiler_params=pltpu.CompilerParams(vmem_limit_bytes=VMEM_LIMIT),
        cost_estimate=LONG,
        name="finish",
    )(core, held, landed, cosine, sine, *after)


def mix_kernel(count, places, *refs):
    pieces = refs[:count]
    weights, start, mixed, total, wide, arrived = refs[count:]
    depth = wide.shape[1]
    columns = wide.shape[2] // 2
    flat = []
    for piece in pieces:
        flat += [piece] if len(piece.shape) == 2 else [piece.at[i] for i in range(piece.shape[0])]
    copies = [
        pltpu.make_async_copy(
            weights.at[pl.ds(pl.multiple_of(places[i] * depth, depth), depth), :],
            wide.at[i],
            arrived.at[i],
        )
        for i in range(len(flat))
    ]
    for copy in copies:
        copy.start()
    cuts = [0, 1, 2, 4, len(flat)]
    cuts = sorted(set(min(cut, len(flat)) for cut in cuts))
    for first, last in zip(cuts, cuts[1:]):
        for copy in copies[first:last]:
            copy.wait()
        for side in range(2):
            span = pl.ds(side * columns, columns)
            source = start if first == 0 else total
            value = source[:, span].astype(jnp.float32)
            for i in range(first, last):
                value = value + jnp.dot(
                    flat[i][...], wide[i, :, span], preferred_element_type=jnp.float32
                )
            target = mixed if last == len(flat) else total
            target[:, span] = value.astype(target.dtype)


def mix(places, pieces, out_weight, start, dtype):
    columns = out_weight.shape[1]
    rows, width = pieces[0].shape[-2:]
    count = sum(1 if len(p.shape) == 2 else p.shape[0] for p in pieces)
    whole = pl.BlockSpec(memory_space=pltpu.VMEM)
    return pl.pallas_call(
        functools.partial(mix_kernel, len(pieces)),
        in_specs=[pl.BlockSpec(memory_space=pltpu.SMEM)]
        + [whole] * len(pieces)
        + [pl.BlockSpec(memory_space=pl.ANY), whole],
        out_specs=whole,
        scratch_shapes=[
            pltpu.VMEM((rows, columns), jnp.float32),
            pltpu.VMEM((count, width, columns), jnp.bfloat16),
            pltpu.SemaphoreType.DMA((count,)),
        ],
        out_shape=jax.ShapeDtypeStruct((rows, columns), dtype),
        compiler_params=pltpu.CompilerParams(vmem_limit_bytes=VMEM_LIMIT),
        cost_estimate=SHORT,
        name="mix",
    )(places, *pieces, out_weight, start)


def pack_kernel(groups, count, *refs):
    flat = []
    for ref in refs[:count]:
        flat += [ref] if len(ref.shape) == 2 else [ref.at[i] for i in range(ref.shape[0])]
    for group, target in zip(groups, refs[-len(groups) :]):
        for place, index in enumerate(group):
            target[place] = flat[index][...]


def pack(pieces, groups, after):
    whole = pl.BlockSpec(memory_space=pltpu.VMEM)
    shape = pieces[0].shape[-2:]
    return pl.pallas_call(
        functools.partial(pack_kernel, groups, len(pieces)),
        in_specs=[whole] * len(pieces) + [pl.BlockSpec(memory_space=pl.ANY)] * len(after),
        out_specs=[whole] * len(groups),
        out_shape=[jax.ShapeDtypeStruct((len(g),) + shape, pieces[0].dtype) for g in groups],
        compiler_params=pltpu.CompilerParams(vmem_limit_bytes=VMEM_LIMIT),
        cost_estimate=SHORT,
        name="pack",
    )(*pieces, *after)


def gather_and_mix(attention, out_weight, start, device):
    def add(mixed, pieces, offsets, dtype=jnp.float32):
        places = jnp.stack([device ^ offset for offset in offsets])
        return mix(places, pieces, out_weight, mixed, dtype)

    near = swap(attention, 4)
    across = swap(attention, 2)
    far = swap(attention, 8)
    partner = swap(attention, 1)
    first, onward = pack([near, across, far], [(0, 1, 2), (0, 2)], [partner])
    (attention,) = together([attention], [onward])

    across_onward = swap(onward, 2)
    farthest = swap(attention, 12)
    first_partner = swap(first, 1)
    mixed = add(start, [attention, partner], (0, 1))
    mixed = add(mixed, [first, first_partner], (4, 2, 8, 5, 3, 9))
    (second,) = pack([across_onward, farthest], [(0, 1, 2)], [mixed])

    last = swap(farthest, 2)
    second_partner = swap(second, 1)
    mixed = add(mixed, [second, second_partner], (6, 10, 12, 7, 11, 13))
    (last,) = together([last], [mixed])

    last_partner = swap(last, 1)
    return add(mixed, [last, last_partner], (14, 15), jnp.bfloat16)


def attend_kernel(
    slot_request,
    queries,
    new_keys,
    new_values,
    own,
    other,
    key_scale,
    value_scale,
    cache_bias,
    new_bias,
    attention,
    slot_best,
    slot_total,
    slot_sum,
    best,
    total,
    summed,
):
    slots = slot_best.shape[0]
    requests, count, _ = queries.shape
    transposed = (((1,), (1,)), ((), ()))
    for request in range(requests):
        scores = (
            lax.dot_general(
                queries[request],
                new_keys[request],
                transposed,
                preferred_element_type=jnp.float32,
            )
            * HD ** (-0.5)
            + new_bias[...]
        )
        top = jnp.max(scores, -1, keepdims=True)
        expo = jnp.exp(scores - top)
        best[request] = jnp.broadcast_to(top, (count, HD))
        total[request] = jnp.broadcast_to(jnp.sum(expo, -1, keepdims=True), (count, HD))
        summed[request] = jnp.dot(
            expo.astype(jnp.bfloat16), new_values[request], preferred_element_type=jnp.float32
        )
    for slot in range(slots):
        request = slot_request[slot]
        query = queries[request]
        raw = [
            part[:, slot * BLK : (slot + 1) * BLK, :].reshape(KVH * BLK, 2 * HD)
            for part in (own, other)
        ]
        scores = jnp.concatenate(
            [
                lax.dot_general(
                    query, kv[:, :HD], transposed, preferred_element_type=jnp.float32
                )
                for kv in raw
            ],
            1,
        )
        scores = scores * key_scale[slot : slot + 1, :] + cache_bias[slot : slot + 1, :]
        top = jnp.max(scores, -1, keepdims=True)
        expo = jnp.exp(scores - top)
        weights = (expo * value_scale[slot : slot + 1, :]).astype(jnp.bfloat16)
        slot_best[slot] = jnp.broadcast_to(top, (count, HD))
        slot_total[slot] = jnp.broadcast_to(jnp.sum(expo, -1, keepdims=True), (count, HD))
        values = jnp.concatenate([kv[:, HD:] for kv in raw], 0)
        slot_sum[slot] = jnp.dot(weights, values, preferred_element_type=jnp.float32)
    for slot in range(slots):
        request = slot_request[slot]
        before = best[request]
        here = slot_best[slot]
        top = jnp.maximum(before, here)
        keep = jnp.exp(before - top)
        add = jnp.exp(here - top)
        best[request] = top
        total[request] = total[request] * keep + slot_total[slot] * add
        summed[request] = summed[request] * keep + slot_sum[slot] * add
    for request in range(requests):
        attention[request] = (summed[request] / total[request]).astype(jnp.bfloat16)


def attend(slot_request, *arrays):
    queries = arrays[0]
    slots = arrays[5].shape[0]
    requests, count, _ = queries.shape
    whole = pl.BlockSpec(memory_space=pltpu.VMEM)
    return pl.pallas_call(
        attend_kernel,
        in_specs=[pl.BlockSpec(memory_space=pltpu.SMEM)] + [whole] * len(arrays),
        out_specs=whole,
        out_shape=jax.ShapeDtypeStruct((requests, count, HD), jnp.bfloat16),
        scratch_shapes=[pltpu.VMEM((slots, count, HD), jnp.float32)] * 3
        + [pltpu.VMEM((requests, count, HD), jnp.float32)] * 3,
        compiler_params=pltpu.CompilerParams(vmem_limit_bytes=VMEM_LIMIT),
        cost_estimate=SHORT,
        name="attend",
    )(slot_request, *arrays)


def slot_layout(request_length, block_table, slots, stripe):
    requests, most = block_table.shape
    stripes = (request_length + stripe - 1) // stripe
    columns = jnp.arange(most, dtype=jnp.int32)
    held = columns[None, :] < stripes[:, None]
    hit = held[:, :, None] & (
        block_table[:, :, None] == jnp.arange(slots, dtype=jnp.int32)[None, None, :]
    )
    hit = hit.astype(jnp.int32)
    order = jnp.arange(requests, dtype=jnp.int32)
    request = jnp.sum(hit * order[:, None, None], (0, 1))
    rank = jnp.sum(hit * columns[None, :, None], (0, 1))
    length = jnp.sum(hit * request_length[:, None, None], (0, 1))
    return request, rank, length


def arrange_kernel(chip, pool, scales, after, *sent):
    slots = pool.shape[0]
    for k, target in enumerate(sent):
        head = chip[0] ^ k
        target[: slots * BLK, :] = pool[:, head].reshape(slots * BLK, 2 * HD)
        target[slots * BLK :, :] = scales[head]


def arrange(chip, cache_pool, scales, after):
    rows = cache_pool.shape[0] * BLK + TILE
    whole = pl.BlockSpec(memory_space=pltpu.VMEM)
    return pl.pallas_call(
        arrange_kernel,
        in_specs=[
            pl.BlockSpec(memory_space=pltpu.SMEM),
            whole,
            whole,
            pl.BlockSpec(memory_space=pl.ANY),
        ],
        out_specs=[whole] * KVH,
        out_shape=[jax.ShapeDtypeStruct((rows, 2 * HD), jnp.bfloat16)] * KVH,
        compiler_params=pltpu.CompilerParams(vmem_limit_bytes=VMEM_LIMIT),
        cost_estimate=SHORT,
        name="arrange",
    )(chip, cache_pool, scales, after)


def local_pairs(
    hidden_in,
    norm_gain,
    qkv_weight,
    out_weight,
    cache_pool,
    cache_scale,
    request_length,
    block_table,
):
    devices = lax.axis_size("tensor")
    device = lax.axis_index("tensor")
    core = device % 2
    chip = device // 2
    stripe = devices * BLK
    slots = cache_pool.shape[0]
    requests = request_length.shape[0]
    rows = STEPS * requests * QR
    width = hidden_in.shape[2]
    heads = GQ // 2

    hidden = hidden_in.astype(jnp.float32)
    sums = jnp.sum(hidden * hidden, -1)
    bits = [jnp.reshape((device >> b) & 1, (1,)).astype(jnp.int32) for b in range(4)]
    scale_rows = jnp.pad(
        jnp.transpose(cache_scale, (1, 2, 0)).reshape(KVH, 1, 2 * slots),
        ((0, 0), (0, TILE - 1), (0, 2 * HD - 2 * slots)),
    )
    sums = sums + swap(sums, 2)
    chip_scalar = jnp.reshape(chip, (1,)).astype(jnp.int32)
    cache_pieces = list(arrange(chip_scalar, cache_pool, scale_rows, sums))

    def handed(k):
        cache_pieces[k] = swap(cache_pieces[k], 2 * k)

    for bit in (1, 4, 8):
        sums = sums + swap(sums, bit)
    normed = (
        hidden * lax.rsqrt(sums[..., None] / D + EPSILON) * norm_gain.astype(jnp.float32)
    ).astype(jnp.bfloat16)
    normed = normed.reshape(rows, width)

    step_ids = jnp.arange(STEPS, dtype=jnp.int32)
    row_ids = jnp.arange(QR, dtype=jnp.int32)
    position = (
        request_length[None, :, None] + QR * step_ids[:, None, None] + row_ids[None, None, :]
    )
    freqs = ROPE_BASE ** (-(jnp.arange(HD // 2, dtype=jnp.float32) * 2.0 / HD))
    angles = position.reshape(rows, 1).astype(jnp.float32) * freqs
    cosine = jnp.concatenate([jnp.cos(angles)] * 2, 1)
    sine = jnp.concatenate([-jnp.sin(angles), jnp.sin(angles)], 1)

    def folded(part, b, landed, low, *after):
        return fold(bits[b], part, landed, low, after)

    def finished(part, number, landed, *after):
        return finish(bits[0], part, landed, cosine, sine, PART_HEADS[number], after)

    for k in (1, 3, 4, 5):
        handed(k)
    held_a, sent_a = project(bits[0], normed, qkv_weight, 0, cache_pieces[:1])
    core_a = swap(sent_a, 1)
    held_b, sent_b = project(
        bits[0], normed, qkv_weight, 1, [held_a, cache_pieces[1], cache_pieces[3]]
    )
    sent_b, cache_pieces[2], cache_pieces[6], cache_pieces[7] = together(
        [sent_b, cache_pieces[2], cache_pieces[6], cache_pieces[7]], cache_pieces[4:6]
    )
    core_b = swap(sent_b, 1)
    held_a, sent_a = folded(held_a, 1, core_a, 1, sent_b)
    line_a = swap(sent_a, 2)
    for k in (2, 6, 7):
        handed(k)
    late = [cache_pieces[k] for k in (2, 6, 7)]
    held_b, sent_b = folded(held_b, 2, core_b, 2, held_a, *late)
    line_b = swap(sent_b, 4)
    held_a, sent_a = folded(held_a, 2, line_a, 1, held_b)
    line_a = swap(sent_a, 4)
    held_b, sent_b = folded(held_b, 1, line_b, 1, held_a)
    line_b = swap(sent_b, 2)
    (cache_own,) = pack(cache_pieces, [tuple(range(KVH))], [held_b])
    cache_other = swap(cache_own, 1)
    held_a, sent_a = folded(held_a, 3, line_a, 1, cache_own)
    line_a = swap(sent_a, 8)
    held_b, sent_b = folded(held_b, 3, line_b, 1, held_a)
    line_b = swap(sent_b, 8)
    query_a, pair = finished(held_a, 0, line_a, held_b)
    pair_other = swap(pair, 1)
    (query_b,) = finished(held_b, 1, line_b, query_a)
    query_chunks = [query_a, query_b]
    cache_parts = (cache_own, cache_other)
    keys = jnp.where(core == 0, pair, pair_other)
    raw_values = jnp.where(core == 0, pair_other, pair)
    queries = jnp.concatenate(query_chunks, 1).reshape(STEPS, requests, QR, heads, HD)
    queries = jnp.transpose(queries, (1, 0, 2, 3, 4)).reshape(requests, STEPS * QR * heads, HD)

    def by_request(value):
        value = jnp.transpose(value.reshape(STEPS, requests, QR, HD), (1, 0, 2, 3))
        value = value.reshape(requests, STEPS * QR, HD)
        return jnp.pad(value, ((0, 0), (0, TILE - STEPS * QR), (0, 0)))

    slot_request, slot_rank, slot_length = slot_layout(request_length, block_table, slots, stripe)
    source = chip ^ jnp.arange(KVH, dtype=jnp.int32)
    sources = jnp.stack([source * 2 + core, source * 2 + 1 - core])
    offset = sources[:, :, None] * BLK + jnp.arange(BLK, dtype=jnp.int32)[None, None, :]
    token = slot_rank[:, None] * stripe + offset.reshape(1, stripe)
    cache_bias = jnp.where(token < slot_length[:, None], 0.0, NEG_FILL).astype(jnp.float32)
    scales = jnp.concatenate([part[:, slots * BLK, : 2 * slots] for part in cache_parts])
    scales = scales.astype(jnp.float32).reshape(2 * KVH, 2, slots)
    scales = jnp.repeat(jnp.transpose(scales, (1, 2, 0)), BLK, axis=2)
    order = jnp.arange(STEPS * QR * heads, dtype=jnp.int32) // heads
    key_order = jnp.arange(TILE, dtype=jnp.int32)
    new_bias = jnp.where(key_order[None, :] <= order[:, None], 0.0, NEG_FILL).astype(jnp.float32)
    attention = attend(
        slot_request,
        queries,
        by_request(keys),
        by_request(raw_values),
        *cache_parts,
        scales[0] * HD ** (-0.5),
        scales[1],
        cache_bias,
        new_bias,
    )
    attention = jnp.transpose(
        attention.reshape(requests, STEPS, QR, heads, HD), (1, 0, 2, 3, 4)
    ).reshape(rows, heads * HD)
    mixed = gather_and_mix(attention, out_weight, hidden_in.reshape(rows, width), device)
    return mixed.reshape(hidden_in.shape)


def solution(mesh):
    return jax.shard_map(
        local_pairs if mesh.shape["tensor"] == 2 * KVH else local_general,
        mesh=mesh,
        in_specs=(
            P(None, "groups", "tensor"),
            P("tensor"),
            P("tensor", None),
            P(None, "tensor"),
            P(("groups", "tensor"), None, None, None),
            P(("groups", "tensor"), None, None),
            P("groups"),
            P("groups", None),
        ),
        out_specs=P(None, "groups", "tensor"),
        check_vma=False,
    )
```

```python
import functools

import jax
import jax.numpy as jnp
from jax import lax
from jax.experimental import pallas as pl
from jax.experimental.pallas import tpu as pltpu
from jax.sharding import PartitionSpec as P

D = 16384
QH = 128
KVH = 8
HD = 128
QR = 6
STEPS = 2
BLK = 16
GQ = 16
GW = 2304


EPSILON = 1e-05
ROPE_BASE = 500000.0
NEG_FILL = -1e30


def rotate(values, positions):
    half = values.shape[-1] // 2
    freqs = ROPE_BASE ** (-(jnp.arange(half, dtype=jnp.float32) * 2.0 / values.shape[-1]))
    angles = positions.astype(jnp.float32)[..., None] * freqs
    cosine = jnp.cos(angles)
    sine = jnp.sin(angles)
    first = values[..., :half]
    second = values[..., half:]
    return jnp.concatenate([first * cosine - second * sine, second * cosine + first * sine], -1)


def request_layout(request_owner, request_length, block_table, owners, stripe):
    requests = request_owner.shape[0]
    most = block_table.shape[1]
    order = jnp.arange(requests, dtype=jnp.int32)
    stripes = (request_length + stripe - 1) // stripe
    before = (
        (request_owner[None, :] == request_owner[:, None]) & (order[None, :] < order[:, None])
    ).astype(jnp.int32)
    rank = jnp.sum(before, 1)
    offset = jnp.sum(before * stripes[None, :], 1)
    owner_ids = jnp.arange(owners, dtype=jnp.int32)
    mine = request_owner[None, :] == owner_ids[:, None]
    member = mine[:, :, None] & (
        rank[None, :, None] == jnp.arange(requests // owners, dtype=jnp.int32)[None, None, :]
    )
    owner_requests = jnp.sum(member.astype(jnp.int32) * order[None, :, None], 1)
    columns = jnp.arange(most, dtype=jnp.int32)
    within = columns[None, None, :] - offset[None, :, None]
    hit = (mine[:, :, None] & (within >= 0) & (within < stripes[None, :, None])).astype(jnp.int32)
    stripe_request = jnp.sum(hit * order[None, :, None], 1) - (1 - jnp.sum(hit, 1))
    stripe_rank = jnp.sum(hit * within, 1)
    pick = (within[..., None] == columns[None, None, None, :]).astype(jnp.int32)
    slots = jnp.sum(hit[..., None] * pick * block_table[None, :, None, :], (1, 3))
    return (owner_requests, stripe_request, stripe_rank, slots, rank, stripes)


def cache_partial(queries, keys, values, key_scale, value_scale, mask):
    scores = jnp.einsum("srgd,td->srgt", queries, keys, preferred_element_type=jnp.float32)
    scores = jnp.where(mask, scores * key_scale * HD ** (-0.5), NEG_FILL)
    best = jnp.max(scores, -1)
    expo = jnp.where(mask, jnp.exp(scores - best[..., None]), 0.0)
    total = jnp.sum(expo, -1)
    weights = (expo * value_scale).astype(jnp.bfloat16)
    summed = jnp.einsum("srgt,td->srgd", weights, values, preferred_element_type=jnp.float32)
    return (best, total, summed)


def local_general(
    hidden_in,
    norm_gain,
    qkv_weight,
    out_weight,
    cache_pool,
    cache_scale,
    request_length,
    block_table,
):
    devices = lax.axis_size("tensor")
    device = lax.axis_index("tensor")
    owners = devices // KVH
    stripe = devices * BLK
    requests = request_length.shape[0]
    request_owner = jnp.arange(requests, dtype=jnp.int32) % owners
    unit_rows = requests // owners * QR
    most = block_table.shape[1]
    local_width = hidden_in.shape[2]
    my_owner = device // KVH
    owner_requests, stripe_request, stripe_rank, slots, rank, stripes = request_layout(
        request_owner, request_length, block_table, owners, stripe
    )
    step_rows = jnp.arange(QR, dtype=jnp.int32)
    row_order = (owner_requests[:, :, None] * QR + step_rows[None, None, :]).reshape(
        owners * unit_rows
    )
    inverse = ((request_owner * unit_rows + rank * QR)[:, None] + step_rows[None, :]).reshape(
        requests * QR
    )
    row_request = jnp.repeat(owner_requests[my_owner], QR)
    row_length = request_length[row_request]
    row_step = jnp.arange(unit_rows, dtype=jnp.int32) % QR
    same_request = row_request[:, None] == row_request[None, :]
    gain = norm_gain.astype(jnp.float32)
    weight_grouped = qkv_weight.reshape(local_width, KVH, GW)
    sent = cache_pool[jnp.transpose(slots)].reshape(most, devices, BLK, 2 * HD)
    sent_scale = cache_scale[jnp.transpose(slots)].reshape(most, devices, 2)
    landed, landed_scale = (
        lax.all_to_all(sent, "tensor", split_axis=1, concat_axis=1, tiled=True),
        lax.all_to_all(sent_scale, "tensor", split_axis=1, concat_axis=1, tiled=True),
    )
    cache_data = landed.reshape(most * stripe, 2 * HD)
    token_scale = jnp.broadcast_to(
        landed_scale.astype(jnp.float32)[:, :, None, :], (most, devices, BLK, 2)
    ).reshape(most * stripe, 2)
    token = jnp.arange(most * stripe, dtype=jnp.int32)
    token_stripe = token // stripe
    token_request = stripe_request[my_owner][token_stripe]
    token_position = stripe_rank[my_owner][token_stripe] * stripe + token % stripe
    token_length = jnp.where(token_request >= 0, request_length[jnp.maximum(token_request, 0)], 0)
    cache_mask = (
        (token_request[None, :] == row_request[:, None]) & (token_position < token_length)[None, :]
    )[None, :, None, :]
    outputs = []
    keys_seen = []
    values_seen = []
    for step in range(STEPS):
        block = hidden_in[step : step + 1]
        project_count = block.shape[0]
        values = block.astype(jnp.float32)
        sums = lax.psum(jnp.sum(values * values, -1), "tensor")
        normed = (values * lax.rsqrt(sums[..., None] / D + EPSILON) * gain).astype(jnp.bfloat16)
        ordered = jnp.take(normed, row_order, axis=1).reshape(
            project_count, owners, unit_rows, local_width
        )
        term = jnp.einsum(
            "sojd,dhg->ohsjg", ordered, weight_grouped, preferred_element_type=jnp.float32
        )
        term = term.reshape(owners * KVH * project_count * unit_rows, GW)
        mine = lax.psum_scatter(term, "tensor", scatter_dimension=0, tiled=True)
        joined_block = mine.astype(jnp.bfloat16).reshape(project_count, unit_rows, GW)
        prepare_count = joined_block.shape[0]
        steps_here = step + jnp.arange(prepare_count, dtype=jnp.int32)
        position = row_length[None, :] + QR * steps_here[:, None] + row_step[None, :]
        prepare_queries = rotate(
            joined_block[..., : GQ * HD]
            .reshape(prepare_count, unit_rows, GQ, HD)
            .astype(jnp.float32),
            position[:, :, None],
        ).astype(jnp.bfloat16)
        keys = rotate(
            joined_block[..., GQ * HD : GQ * HD + HD].astype(jnp.float32), position
        ).astype(jnp.bfloat16)
        queries, keys, values = (prepare_queries, keys, joined_block[..., GQ * HD + HD :])
        keys_seen.append(keys)
        values_seen.append(values)
        keys_all = jnp.concatenate(keys_seen, 0)
        attend_count = queries.shape[0]
        cache_best, cache_total, cache_summed = cache_partial(
            queries,
            cache_data[:, :HD],
            cache_data[:, HD:],
            token_scale[:, 0],
            token_scale[:, 1],
            cache_mask,
        )
        news = jnp.einsum(
            "srgd,pjd->srgpj", queries, keys_all, preferred_element_type=jnp.float32
        ) * HD ** (-0.5)
        query_step = step + jnp.arange(attend_count, dtype=jnp.int32)[:, None, None, None]
        key_step = jnp.arange(keys_all.shape[0], dtype=jnp.int32)[None, None, :, None]
        allowed = (key_step < query_step) | (key_step == query_step) & (
            row_step[None, None, None, :] <= row_step[None, :, None, None]
        )
        allowed = (allowed & same_request[None, :, None, :])[:, :, None, :, :]
        news = jnp.where(allowed, news, NEG_FILL)
        best = jnp.maximum(cache_best, jnp.max(news, (3, 4)))
        factor = jnp.exp(cache_best - best)
        expo = jnp.where(allowed, jnp.exp(news - best[..., None, None]), 0.0)
        total = cache_total * factor + jnp.sum(expo, (3, 4))
        summed = cache_summed * factor[..., None] + jnp.einsum(
            "srgpj,pjd->srgd",
            expo.astype(jnp.bfloat16),
            jnp.concatenate(values_seen, 0),
            preferred_element_type=jnp.float32,
        )
        attention = (
            (summed / total[..., None])
            .astype(jnp.bfloat16)
            .reshape(attend_count, unit_rows, GQ * HD)
        )
        count = attention.shape[0]
        gathered = lax.all_gather(attention, "tensor", axis=2, tiled=True).reshape(
            count, unit_rows, owners, QH * HD
        )
        mixed = jnp.einsum(
            "sjof,fd->sojd", gathered, out_weight, preferred_element_type=jnp.float32
        )
        mixed = jnp.take(mixed.reshape(count, owners * unit_rows, local_width), inverse, axis=1)
        outputs.append(
            (hidden_in[step : step + count].astype(jnp.float32) + mixed).astype(jnp.bfloat16)
        )
    return jnp.concatenate(outputs, 0)


VMEM_LIMIT = 48 * 1024 * 1024
SHORT = pl.CostEstimate(flops=1, bytes_accessed=1, transcendentals=0)
LONG = pl.CostEstimate(flops=2 * 10**10, bytes_accessed=1, transcendentals=0)
LOW_BITS = 4
PACKED = 16 // LOW_BITS
LEVELS = 32600.0 * 2**LOW_BITS
POWER_STEPS = 8.0
TILE = 16
MESH_BITS = (1, 2, 4, 8)


def swap(value, bit):
    devices = lax.axis_size("tensor")
    return lax.ppermute(value, "tensor", [(i, i ^ bit) for i in range(devices)])


def no_work(*refs):
    del refs


def together(arrays, after):
    anywhere = pl.BlockSpec(memory_space=pl.ANY)
    return pl.pallas_call(
        no_work,
        in_specs=[anywhere] * (len(arrays) + len(after)),
        out_specs=[anywhere] * len(arrays),
        out_shape=[jax.ShapeDtypeStruct(a.shape, a.dtype) for a in arrays],
        input_output_aliases={i: i for i in range(len(arrays))},
        compiler_params=pltpu.CompilerParams(vmem_limit_bytes=VMEM_LIMIT),
        cost_estimate=SHORT,
        name="together",
    )(*arrays, *after)


def coded_rows(rows):
    return rows + rows // PACKED


def encode(block):
    top = jnp.max(jnp.abs(block), 0, keepdims=True)
    power = jnp.ceil(jnp.log2(jnp.maximum(top, 1e-30)) * POWER_STEPS)
    codes = jnp.round(block * (jnp.exp2(power * (-1.0 / POWER_STEPS)) * LEVELS)).astype(jnp.int32)
    low = codes & (2**LOW_BITS - 1)
    part = block.shape[0] // PACKED
    packed = low[:part]
    for i in range(1, PACKED):
        packed = packed + (low[i * part : (i + 1) * part] << (LOW_BITS * i))
    high = (codes >> LOW_BITS).astype(jnp.int16)
    return jnp.concatenate([high, (packed - 32768).astype(jnp.int16)], 0), power


def decode(codes, power):
    rows = codes.shape[0] * PACKED // (PACKED + 1)
    high = codes[:rows].astype(jnp.int32) << LOW_BITS
    packed = codes[rows:].astype(jnp.int32) + 32768
    low = jnp.concatenate(
        [(packed >> (LOW_BITS * i)) & (2**LOW_BITS - 1) for i in range(PACKED)], 0
    )
    scale = jnp.exp2(power * (1.0 / POWER_STEPS)) * (1.0 / LEVELS)
    return (high + low).astype(jnp.float32) * scale


def pick_row(rows, index):
    ids = lax.broadcasted_iota(jnp.int32, rows.shape, 0)
    return jnp.sum(jnp.where(ids == index, rows, 0.0), 0, keepdims=True)


def store_codes(sent, powers, block, index, steps):
    rows = coded_rows(block.shape[0])
    codes, power = encode(block)
    sent[pl.ds(pl.multiple_of(index * rows, TILE), rows), :] = codes

    powers[pl.ds(index, 1), :] = power

    @pl.when(index == steps - 1)
    def _():
        sent[pl.ds(steps * rows, TILE), :] = powers[...].astype(jnp.int32).astype(jnp.int16)


PART_HEADS = (3, 5)


def project_kernel(part, core, normed, weights, *refs):
    kept, sent, powers, slabs, arrived = refs[-5:]
    index = pl.program_id(0)
    half = kept.shape[2]
    heads = PART_HEADS[part] * HD
    first = sum(PART_HEADS[:part]) * HD

    def copies(group):
        found = []
        for side in range(2):
            owner = core[0] if side == 0 else 1 - core[0]
            spans = [(group * GW + owner * (GQ // 2 * HD) + first, 0, heads)]
            if half > heads:
                spans.append((group * GW + (GQ + owner) * HD, heads, HD))
            for number, (start, offset, size) in enumerate(spans):
                found.append(
                    pltpu.make_async_copy(
                        weights.at[:, pl.ds(pl.multiple_of(start, HD), size)],
                        slabs.at[group, :, pl.ds(side * half + offset, size)],
                        arrived.at[group, side, number],
                    )
                )
        return found

    @pl.when(index == 0)
    def _():
        for group in range(KVH):
            for copy in copies(group):
                copy.start()
        powers[...] = jnp.zeros_like(powers)

    for copy in copies(index):
        copy.wait()

    found = []
    rows = coded_rows(normed.shape[0])
    place = pl.ds(pl.multiple_of(index * rows, TILE), rows)
    for start in range(0, 2 * half, 2 * HD):
        stop = start + 2 * HD
        product = jnp.dot(
            normed[...], slabs[index, :, start:stop], preferred_element_type=jnp.float32
        )
        if start < half:
            kept[0, :, start : min(stop, half)] = product[:, : half - start]
        if stop > half:
            first = max(start, half)
            codes, power = encode(product[:, first - start :])
            sent[place, first - half : stop - half] = codes
            found.append(power)
    powers[pl.ds(index, 1), :] = jnp.concatenate(found, 1)

    @pl.when(index == KVH - 1)
    def _():
        sent[pl.ds(KVH * rows, TILE), :] = powers[...].astype(jnp.int32).astype(jnp.int16)


def project(core, normed, qkv_weight, part, after):
    rows, width = normed.shape
    columns = PART_HEADS[part] * HD + (HD if part == 0 else 0)
    sent_rows = KVH * coded_rows(rows) + TILE
    return pl.pallas_call(
        functools.partial(project_kernel, part),
        grid_spec=pltpu.PrefetchScalarGridSpec(
            num_scalar_prefetch=1,
            grid=(KVH,),
            in_specs=[pl.BlockSpec((rows, width), lambda t, c: (0, 0))]
            + [pl.BlockSpec(memory_space=pl.ANY)] * (1 + len(after)),
            out_specs=[
                pl.BlockSpec((1, rows, columns), lambda t, c: (t, 0, 0)),
                pl.BlockSpec((sent_rows, columns), lambda t, c: (0, 0)),
            ],
            scratch_shapes=[
                pltpu.VMEM((TILE, columns), jnp.float32),
                pltpu.VMEM((KVH, width, 2 * columns), jnp.bfloat16),
                pltpu.SemaphoreType.DMA((KVH, 2, 2)),
            ],
        ),
        out_shape=[
            jax.ShapeDtypeStruct((KVH, rows, columns), jnp.float32),
            jax.ShapeDtypeStruct((sent_rows, columns), jnp.int16),
        ],
        compiler_params=pltpu.CompilerParams(vmem_limit_bytes=VMEM_LIMIT),
        cost_estimate=SHORT,
        name="project",
    )(core, normed, qkv_weight, *after)


def fold_kernel(steps, low, bit, held, held_out, landed, landed_out, landed_powers, *refs):
    kept, sent, powers = refs[-3:]
    index = pl.program_id(0)
    rows_of_powers = landed_powers[...].astype(jnp.int32).astype(jnp.float32)
    first = index // low * (2 * low) + index % low

    def total(side, block, codes):
        power = pick_row(rows_of_powers, first + side * low)
        return block[0] + decode(codes[...], power)

    @pl.when(index == 0)
    def _():
        powers[...] = jnp.zeros_like(powers)

    kept[0] = total(bit[0], held, landed)
    store_codes(sent, powers, total(1 - bit[0], held_out, landed_out), index, steps)


def fold(bit, held, landed, low, after):
    blocks, rows, columns = held.shape
    steps = blocks // 2
    coded = coded_rows(rows)

    def block(i, b, out):
        side = 1 - b[0] if out else b[0]
        return i // low * (2 * low) + side * low + i % low

    return pl.pallas_call(
        functools.partial(fold_kernel, steps, low),
        grid_spec=pltpu.PrefetchScalarGridSpec(
            num_scalar_prefetch=1,
            grid=(steps,),
            in_specs=[
                pl.BlockSpec((1, rows, columns), lambda i, b: (block(i, b, False), 0, 0)),
                pl.BlockSpec((1, rows, columns), lambda i, b: (block(i, b, True), 0, 0)),
                pl.BlockSpec((coded, columns), lambda i, b: (block(i, b, False), 0)),
                pl.BlockSpec((coded, columns), lambda i, b: (block(i, b, True), 0)),
                pl.BlockSpec((TILE, columns), lambda i, b: (blocks * coded // TILE, 0)),
            ]
            + [pl.BlockSpec(memory_space=pl.ANY)] * len(after),
            out_specs=[
                pl.BlockSpec((1, rows, columns), lambda i, b: (i, 0, 0)),
                pl.BlockSpec((steps * coded + TILE, columns), lambda i, b: (0, 0)),
            ],
            scratch_shapes=[pltpu.VMEM((TILE, columns), jnp.float32)],
        ),
        out_shape=[
            jax.ShapeDtypeStruct((steps, rows, columns), jnp.float32),
            jax.ShapeDtypeStruct((steps * coded + TILE, columns), jnp.int16),
        ],
        compiler_params=pltpu.CompilerParams(vmem_limit_bytes=VMEM_LIMIT),
        cost_estimate=SHORT,
        name="fold",
    )(bit, held, held, landed, landed, landed, *after)


def finish_kernel(heads, after_count, core, held, landed, cosine, sine, *refs):
    queries, *pair = refs[after_count:]
    coded = coded_rows(held.shape[1])
    power = landed[pl.ds(coded, TILE), :].astype(jnp.int32).astype(jnp.float32)[0:1]
    total = held[0] + decode(landed[pl.ds(0, coded), :], power)
    joined = total.astype(jnp.bfloat16)
    for head in range(joined.shape[1] // HD):
        raw = joined[:, head * HD : (head + 1) * HD].astype(jnp.float32)
        turned = raw * cosine[...] + pltpu.roll(raw, HD // 2, 1) * sine[...]
        if head < heads:
            queries[:, head * HD : (head + 1) * HD] = turned.astype(jnp.bfloat16)
        else:
            pair[0][...] = jnp.where(core[0] == 0, turned, raw).astype(jnp.bfloat16)


def finish(core, held, landed, cosine, sine, heads, after):
    _, rows, columns = held.shape
    whole = pl.BlockSpec(memory_space=pltpu.VMEM)
    shapes = [jax.ShapeDtypeStruct((rows, heads * HD), jnp.bfloat16)]
    if columns > heads * HD:
        shapes.append(jax.ShapeDtypeStruct((rows, HD), jnp.bfloat16))
    return pl.pallas_call(
        functools.partial(finish_kernel, heads, len(after)),
        in_specs=[pl.BlockSpec(memory_space=pltpu.SMEM)]
        + [whole] * 4
        + [pl.BlockSpec(memory_space=pl.ANY)] * len(after),
        out_specs=[whole] * len(shapes),
        out_shape=shapes,
        compiler_params=pltpu.CompilerParams(vmem_limit_bytes=VMEM_LIMIT),
        cost_estimate=LONG,
        name="finish",
    )(core, held, landed, cosine, sine, *after)


def mix_kernel(count, places, *refs):
    pieces = refs[:count]
    weights, start, mixed, total, wide, arrived = refs[count:]
    depth = wide.shape[1]
    columns = wide.shape[2] // 2
    flat = []
    for piece in pieces:
        flat += [piece] if len(piece.shape) == 2 else [piece.at[i] for i in range(piece.shape[0])]
    copies = [
        pltpu.make_async_copy(
            weights.at[pl.ds(pl.multiple_of(places[i] * depth, depth), depth), :],
            wide.at[i],
            arrived.at[i],
        )
        for i in range(len(flat))
    ]
    for copy in copies:
        copy.start()
    cuts = [0, 1, 2, 4, len(flat)]
    cuts = sorted(set(min(cut, len(flat)) for cut in cuts))
    for first, last in zip(cuts, cuts[1:]):
        for copy in copies[first:last]:
            copy.wait()
        for side in range(2):
            span = pl.ds(side * columns, columns)
            source = start if first == 0 else total
            value = source[:, span].astype(jnp.float32)
            for i in range(first, last):
                value = value + jnp.dot(
                    flat[i][...], wide[i, :, span], preferred_element_type=jnp.float32
                )
            target = mixed if last == len(flat) else total
            target[:, span] = value.astype(target.dtype)


def mix(places, pieces, out_weight, start, dtype):
    columns = out_weight.shape[1]
    rows, width = pieces[0].shape[-2:]
    count = sum(1 if len(p.shape) == 2 else p.shape[0] for p in pieces)
    whole = pl.BlockSpec(memory_space=pltpu.VMEM)
    return pl.pallas_call(
        functools.partial(mix_kernel, len(pieces)),
        in_specs=[pl.BlockSpec(memory_space=pltpu.SMEM)]
        + [whole] * len(pieces)
        + [pl.BlockSpec(memory_space=pl.ANY), whole],
        out_specs=whole,
        scratch_shapes=[
            pltpu.VMEM((rows, columns), jnp.float32),
            pltpu.VMEM((count, width, columns), jnp.bfloat16),
            pltpu.SemaphoreType.DMA((count,)),
        ],
        out_shape=jax.ShapeDtypeStruct((rows, columns), dtype),
        compiler_params=pltpu.CompilerParams(vmem_limit_bytes=VMEM_LIMIT),
        cost_estimate=SHORT,
        name="mix",
    )(places, *pieces, out_weight, start)


def pack_kernel(groups, count, *refs):
    flat = []
    for ref in refs[:count]:
        flat += [ref] if len(ref.shape) == 2 else [ref.at[i] for i in range(ref.shape[0])]
    for group, target in zip(groups, refs[-len(groups) :]):
        for place, index in enumerate(group):
            target[place] = flat[index][...]


def pack(pieces, groups, after):
    whole = pl.BlockSpec(memory_space=pltpu.VMEM)
    shape = pieces[0].shape[-2:]
    return pl.pallas_call(
        functools.partial(pack_kernel, groups, len(pieces)),
        in_specs=[whole] * len(pieces) + [pl.BlockSpec(memory_space=pl.ANY)] * len(after),
        out_specs=[whole] * len(groups),
        out_shape=[jax.ShapeDtypeStruct((len(g),) + shape, pieces[0].dtype) for g in groups],
        compiler_params=pltpu.CompilerParams(vmem_limit_bytes=VMEM_LIMIT),
        cost_estimate=SHORT,
        name="pack",
    )(*pieces, *after)


def gather_and_mix(attention, out_weight, start, device):
    def add(mixed, pieces, offsets, dtype=jnp.float32):
        places = jnp.stack([device ^ offset for offset in offsets])
        return mix(places, pieces, out_weight, mixed, dtype)

    near = swap(attention, 4)
    across = swap(attention, 2)
    far = swap(attention, 8)
    partner = swap(attention, 1)
    first, onward = pack([near, across, far], [(0, 1, 2), (0, 2)], [partner])
    (attention,) = together([attention], [onward])

    across_onward = swap(onward, 2)
    farthest = swap(attention, 12)
    first_partner = swap(first, 1)
    mixed = add(start, [attention, partner], (0, 1))
    mixed = add(mixed, [first, first_partner], (4, 2, 8, 5, 3, 9))
    (second,) = pack([across_onward, farthest], [(0, 1, 2)], [mixed])

    last = swap(farthest, 2)
    second_partner = swap(second, 1)
    mixed = add(mixed, [second, second_partner], (6, 10, 12, 7, 11, 13))
    (last,) = together([last], [mixed])

    last_partner = swap(last, 1)
    return add(mixed, [last, last_partner], (14, 15), jnp.bfloat16)


def attend_kernel(
    slot_request,
    queries,
    new_keys,
    new_values,
    own,
    other,
    key_scale,
    value_scale,
    cache_bias,
    new_bias,
    attention,
    slot_best,
    slot_total,
    slot_sum,
    best,
    total,
    summed,
):
    slots = slot_best.shape[0]
    requests, count, _ = queries.shape
    transposed = (((1,), (1,)), ((), ()))
    for request in range(requests):
        scores = (
            lax.dot_general(
                queries[request],
                new_keys[request],
                transposed,
                preferred_element_type=jnp.float32,
            )
            * HD ** (-0.5)
            + new_bias[...]
        )
        top = jnp.max(scores, -1, keepdims=True)
        expo = jnp.exp(scores - top)
        best[request] = jnp.broadcast_to(top, (count, HD))
        total[request] = jnp.broadcast_to(jnp.sum(expo, -1, keepdims=True), (count, HD))
        summed[request] = jnp.dot(
            expo.astype(jnp.bfloat16), new_values[request], preferred_element_type=jnp.float32
        )
    for slot in range(slots):
        request = slot_request[slot]
        query = queries[request]
        raw = [
            part[:, slot * BLK : (slot + 1) * BLK, :].reshape(KVH * BLK, 2 * HD)
            for part in (own, other)
        ]
        scores = jnp.concatenate(
            [
                lax.dot_general(
                    query, kv[:, :HD], transposed, preferred_element_type=jnp.float32
                )
                for kv in raw
            ],
            1,
        )
        scores = scores * key_scale[slot : slot + 1, :] + cache_bias[slot : slot + 1, :]
        top = jnp.max(scores, -1, keepdims=True)
        expo = jnp.exp(scores - top)
        weights = (expo * value_scale[slot : slot + 1, :]).astype(jnp.bfloat16)
        slot_best[slot] = jnp.broadcast_to(top, (count, HD))
        slot_total[slot] = jnp.broadcast_to(jnp.sum(expo, -1, keepdims=True), (count, HD))
        values = jnp.concatenate([kv[:, HD:] for kv in raw], 0)
        slot_sum[slot] = jnp.dot(weights, values, preferred_element_type=jnp.float32)
    for slot in range(slots):
        request = slot_request[slot]
        before = best[request]
        here = slot_best[slot]
        top = jnp.maximum(before, here)
        keep = jnp.exp(before - top)
        add = jnp.exp(here - top)
        best[request] = top
        total[request] = total[request] * keep + slot_total[slot] * add
        summed[request] = summed[request] * keep + slot_sum[slot] * add
    for request in range(requests):
        attention[request] = (summed[request] / total[request]).astype(jnp.bfloat16)


def attend(slot_request, *arrays):
    queries = arrays[0]
    slots = arrays[5].shape[0]
    requests, count, _ = queries.shape
    whole = pl.BlockSpec(memory_space=pltpu.VMEM)
    return pl.pallas_call(
        attend_kernel,
        in_specs=[pl.BlockSpec(memory_space=pltpu.SMEM)] + [whole] * len(arrays),
        out_specs=whole,
        out_shape=jax.ShapeDtypeStruct((requests, count, HD), jnp.bfloat16),
        scratch_shapes=[pltpu.VMEM((slots, count, HD), jnp.float32)] * 3
        + [pltpu.VMEM((requests, count, HD), jnp.float32)] * 3,
        compiler_params=pltpu.CompilerParams(vmem_limit_bytes=VMEM_LIMIT),
        cost_estimate=SHORT,
        name="attend",
    )(slot_request, *arrays)


def slot_layout(request_length, block_table, slots, stripe):
    requests, most = block_table.shape
    stripes = (request_length + stripe - 1) // stripe
    columns = jnp.arange(most, dtype=jnp.int32)
    held = columns[None, :] < stripes[:, None]
    hit = held[:, :, None] & (
        block_table[:, :, None] == jnp.arange(slots, dtype=jnp.int32)[None, None, :]
    )
    hit = hit.astype(jnp.int32)
    order = jnp.arange(requests, dtype=jnp.int32)
    request = jnp.sum(hit * order[:, None, None], (0, 1))
    rank = jnp.sum(hit * columns[None, :, None], (0, 1))
    length = jnp.sum(hit * request_length[:, None, None], (0, 1))
    return request, rank, length


def arrange_kernel(chip, pool, scales, after, *sent):
    slots = pool.shape[0]
    for k, target in enumerate(sent):
        head = chip[0] ^ k
        target[: slots * BLK, :] = pool[:, head].reshape(slots * BLK, 2 * HD)
        target[slots * BLK :, :] = scales[head]


def arrange(chip, cache_pool, scales, after):
    rows = cache_pool.shape[0] * BLK + TILE
    whole = pl.BlockSpec(memory_space=pltpu.VMEM)
    return pl.pallas_call(
        arrange_kernel,
        in_specs=[
            pl.BlockSpec(memory_space=pltpu.SMEM),
            whole,
            whole,
            pl.BlockSpec(memory_space=pl.ANY),
        ],
        out_specs=[whole] * KVH,
        out_shape=[jax.ShapeDtypeStruct((rows, 2 * HD), jnp.bfloat16)] * KVH,
        compiler_params=pltpu.CompilerParams(vmem_limit_bytes=VMEM_LIMIT),
        cost_estimate=SHORT,
        name="arrange",
    )(chip, cache_pool, scales, after)


def local_pairs(
    hidden_in,
    norm_gain,
    qkv_weight,
    out_weight,
    cache_pool,
    cache_scale,
    request_length,
    block_table,
):
    devices = lax.axis_size("tensor")
    device = lax.axis_index("tensor")
    core = device % 2
    chip = device // 2
    stripe = devices * BLK
    slots = cache_pool.shape[0]
    requests = request_length.shape[0]
    rows = STEPS * requests * QR
    width = hidden_in.shape[2]
    heads = GQ // 2

    hidden = hidden_in.astype(jnp.float32)
    sums = jnp.sum(hidden * hidden, -1)
    bits = [jnp.reshape((device >> b) & 1, (1,)).astype(jnp.int32) for b in range(4)]
    scale_rows = jnp.pad(
        jnp.transpose(cache_scale, (1, 2, 0)).reshape(KVH, 1, 2 * slots),
        ((0, 0), (0, TILE - 1), (0, 2 * HD - 2 * slots)),
    )
    sums = sums + swap(sums, 2)
    chip_scalar = jnp.reshape(chip, (1,)).astype(jnp.int32)
    cache_pieces = list(arrange(chip_scalar, cache_pool, scale_rows, sums))

    def handed(k):
        cache_pieces[k] = swap(cache_pieces[k], 2 * k)

    for bit in (1, 4, 8):
        sums = sums + swap(sums, bit)
    normed = (
        hidden * lax.rsqrt(sums[..., None] / D + EPSILON) * norm_gain.astype(jnp.float32)
    ).astype(jnp.bfloat16)
    normed = normed.reshape(rows, width)

    step_ids = jnp.arange(STEPS, dtype=jnp.int32)
    row_ids = jnp.arange(QR, dtype=jnp.int32)
    position = (
        request_length[None, :, None] + QR * step_ids[:, None, None] + row_ids[None, None, :]
    )
    freqs = ROPE_BASE ** (-(jnp.arange(HD // 2, dtype=jnp.float32) * 2.0 / HD))
    angles = position.reshape(rows, 1).astype(jnp.float32) * freqs
    cosine = jnp.concatenate([jnp.cos(angles)] * 2, 1)
    sine = jnp.concatenate([-jnp.sin(angles), jnp.sin(angles)], 1)

    def folded(part, b, landed, low, *after):
        return fold(bits[b], part, landed, low, after)

    def finished(part, number, landed, *after):
        return finish(bits[0], part, landed, cosine, sine, PART_HEADS[number], after)

    for k in (1, 3, 4, 5, 6):
        handed(k)
    held_a, sent_a = project(bits[0], normed, qkv_weight, 0, cache_pieces[:1])
    core_a = swap(sent_a, 1)
    held_b, sent_b = project(
        bits[0], normed, qkv_weight, 1, [held_a, cache_pieces[1], cache_pieces[3]]
    )
    sent_b, cache_pieces[2], cache_pieces[7] = together(
        [sent_b, cache_pieces[2], cache_pieces[7]], cache_pieces[4:7]
    )
    core_b = swap(sent_b, 1)
    for k in (2, 7):
        handed(k)
    held_a, sent_a = folded(held_a, 2, core_a, 2, sent_b)
    line_a = swap(sent_a, 4)
    held_b, sent_b = folded(held_b, 1, core_b, 1, held_a, cache_pieces[2], cache_pieces[7])
    line_b = swap(sent_b, 2)
    held_a, sent_a = folded(held_a, 1, line_a, 1, held_b)
    line_a = swap(sent_a, 2)
    held_b, sent_b = folded(held_b, 2, line_b, 1, held_a)
    line_b = swap(sent_b, 4)
    (cache_own,) = pack(cache_pieces, [tuple(range(KVH))], [held_b])
    cache_other = swap(cache_own, 1)
    held_a, sent_a = folded(held_a, 3, line_a, 1, cache_own)
    line_a = swap(sent_a, 8)
    held_b, sent_b = folded(held_b, 3, line_b, 1, held_a)
    line_b = swap(sent_b, 8)
    query_a, pair = finished(held_a, 0, line_a, held_b)
    pair_other = swap(pair, 1)
    (query_b,) = finished(held_b, 1, line_b, query_a)
    query_chunks = [query_a, query_b]
    cache_parts = (cache_own, cache_other)
    keys = jnp.where(core == 0, pair, pair_other)
    raw_values = jnp.where(core == 0, pair_other, pair)
    queries = jnp.concatenate(query_chunks, 1).reshape(STEPS, requests, QR, heads, HD)
    queries = jnp.transpose(queries, (1, 0, 2, 3, 4)).reshape(requests, STEPS * QR * heads, HD)

    def by_request(value):
        value = jnp.transpose(value.reshape(STEPS, requests, QR, HD), (1, 0, 2, 3))
        value = value.reshape(requests, STEPS * QR, HD)
        return jnp.pad(value, ((0, 0), (0, TILE - STEPS * QR), (0, 0)))

    slot_request, slot_rank, slot_length = slot_layout(request_length, block_table, slots, stripe)
    source = chip ^ jnp.arange(KVH, dtype=jnp.int32)
    sources = jnp.stack([source * 2 + core, source * 2 + 1 - core])
    offset = sources[:, :, None] * BLK + jnp.arange(BLK, dtype=jnp.int32)[None, None, :]
    token = slot_rank[:, None] * stripe + offset.reshape(1, stripe)
    cache_bias = jnp.where(token < slot_length[:, None], 0.0, NEG_FILL).astype(jnp.float32)
    scales = jnp.concatenate([part[:, slots * BLK, : 2 * slots] for part in cache_parts])
    scales = scales.astype(jnp.float32).reshape(2 * KVH, 2, slots)
    scales = jnp.repeat(jnp.transpose(scales, (1, 2, 0)), BLK, axis=2)
    order = jnp.arange(STEPS * QR * heads, dtype=jnp.int32) // heads
    key_order = jnp.arange(TILE, dtype=jnp.int32)
    new_bias = jnp.where(key_order[None, :] <= order[:, None], 0.0, NEG_FILL).astype(jnp.float32)
    attention = attend(
        slot_request,
        queries,
        by_request(keys),
        by_request(raw_values),
        *cache_parts,
        scales[0] * HD ** (-0.5),
        scales[1],
        cache_bias,
        new_bias,
    )
    attention = jnp.transpose(
        attention.reshape(requests, STEPS, QR, heads, HD), (1, 0, 2, 3, 4)
    ).reshape(rows, heads * HD)
    mixed = gather_and_mix(attention, out_weight, hidden_in.reshape(rows, width), device)
    return mixed.reshape(hidden_in.shape)


def solution(mesh):
    return jax.shard_map(
        local_pairs if mesh.shape["tensor"] == 2 * KVH else local_general,
        mesh=mesh,
        in_specs=(
            P(None, "groups", "tensor"),
            P("tensor"),
            P("tensor", None),
            P(None, "tensor"),
            P(("groups", "tensor"), None, None, None),
            P(("groups", "tensor"), None, None),
            P("groups"),
            P("groups", None),
        ),
        out_specs=P(None, "groups", "tensor"),
        check_vma=False,
    )
```

```python
import functools

import jax
import jax.numpy as jnp
from jax import lax
from jax.experimental import pallas as pl
from jax.experimental.pallas import tpu as pltpu
from jax.sharding import PartitionSpec as P

D = 16384
QH = 128
KVH = 8
HD = 128
QR = 6
STEPS = 2
BLK = 16
GQ = 16
GW = 2304


EPSILON = 1e-05
ROPE_BASE = 500000.0
NEG_FILL = -1e30


def rotate(values, positions):
    half = values.shape[-1] // 2
    freqs = ROPE_BASE ** (-(jnp.arange(half, dtype=jnp.float32) * 2.0 / values.shape[-1]))
    angles = positions.astype(jnp.float32)[..., None] * freqs
    cosine = jnp.cos(angles)
    sine = jnp.sin(angles)
    first = values[..., :half]
    second = values[..., half:]
    return jnp.concatenate([first * cosine - second * sine, second * cosine + first * sine], -1)


def request_layout(request_owner, request_length, block_table, owners, stripe):
    requests = request_owner.shape[0]
    most = block_table.shape[1]
    order = jnp.arange(requests, dtype=jnp.int32)
    stripes = (request_length + stripe - 1) // stripe
    before = (
        (request_owner[None, :] == request_owner[:, None]) & (order[None, :] < order[:, None])
    ).astype(jnp.int32)
    rank = jnp.sum(before, 1)
    offset = jnp.sum(before * stripes[None, :], 1)
    owner_ids = jnp.arange(owners, dtype=jnp.int32)
    mine = request_owner[None, :] == owner_ids[:, None]
    member = mine[:, :, None] & (
        rank[None, :, None] == jnp.arange(requests // owners, dtype=jnp.int32)[None, None, :]
    )
    owner_requests = jnp.sum(member.astype(jnp.int32) * order[None, :, None], 1)
    columns = jnp.arange(most, dtype=jnp.int32)
    within = columns[None, None, :] - offset[None, :, None]
    hit = (mine[:, :, None] & (within >= 0) & (within < stripes[None, :, None])).astype(jnp.int32)
    stripe_request = jnp.sum(hit * order[None, :, None], 1) - (1 - jnp.sum(hit, 1))
    stripe_rank = jnp.sum(hit * within, 1)
    pick = (within[..., None] == columns[None, None, None, :]).astype(jnp.int32)
    slots = jnp.sum(hit[..., None] * pick * block_table[None, :, None, :], (1, 3))
    return (owner_requests, stripe_request, stripe_rank, slots, rank, stripes)


def cache_partial(queries, keys, values, key_scale, value_scale, mask):
    scores = jnp.einsum("srgd,td->srgt", queries, keys, preferred_element_type=jnp.float32)
    scores = jnp.where(mask, scores * key_scale * HD ** (-0.5), NEG_FILL)
    best = jnp.max(scores, -1)
    expo = jnp.where(mask, jnp.exp(scores - best[..., None]), 0.0)
    total = jnp.sum(expo, -1)
    weights = (expo * value_scale).astype(jnp.bfloat16)
    summed = jnp.einsum("srgt,td->srgd", weights, values, preferred_element_type=jnp.float32)
    return (best, total, summed)


def local_general(
    hidden_in,
    norm_gain,
    qkv_weight,
    out_weight,
    cache_pool,
    cache_scale,
    request_length,
    block_table,
):
    devices = lax.axis_size("tensor")
    device = lax.axis_index("tensor")
    owners = devices // KVH
    stripe = devices * BLK
    requests = request_length.shape[0]
    request_owner = jnp.arange(requests, dtype=jnp.int32) % owners
    unit_rows = requests // owners * QR
    most = block_table.shape[1]
    local_width = hidden_in.shape[2]
    my_owner = device // KVH
    owner_requests, stripe_request, stripe_rank, slots, rank, stripes = request_layout(
        request_owner, request_length, block_table, owners, stripe
    )
    step_rows = jnp.arange(QR, dtype=jnp.int32)
    row_order = (owner_requests[:, :, None] * QR + step_rows[None, None, :]).reshape(
        owners * unit_rows
    )
    inverse = ((request_owner * unit_rows + rank * QR)[:, None] + step_rows[None, :]).reshape(
        requests * QR
    )
    row_request = jnp.repeat(owner_requests[my_owner], QR)
    row_length = request_length[row_request]
    row_step = jnp.arange(unit_rows, dtype=jnp.int32) % QR
    same_request = row_request[:, None] == row_request[None, :]
    gain = norm_gain.astype(jnp.float32)
    weight_grouped = qkv_weight.reshape(local_width, KVH, GW)
    sent = cache_pool[jnp.transpose(slots)].reshape(most, devices, BLK, 2 * HD)
    sent_scale = cache_scale[jnp.transpose(slots)].reshape(most, devices, 2)
    landed, landed_scale = (
        lax.all_to_all(sent, "tensor", split_axis=1, concat_axis=1, tiled=True),
        lax.all_to_all(sent_scale, "tensor", split_axis=1, concat_axis=1, tiled=True),
    )
    cache_data = landed.reshape(most * stripe, 2 * HD)
    token_scale = jnp.broadcast_to(
        landed_scale.astype(jnp.float32)[:, :, None, :], (most, devices, BLK, 2)
    ).reshape(most * stripe, 2)
    token = jnp.arange(most * stripe, dtype=jnp.int32)
    token_stripe = token // stripe
    token_request = stripe_request[my_owner][token_stripe]
    token_position = stripe_rank[my_owner][token_stripe] * stripe + token % stripe
    token_length = jnp.where(token_request >= 0, request_length[jnp.maximum(token_request, 0)], 0)
    cache_mask = (
        (token_request[None, :] == row_request[:, None]) & (token_position < token_length)[None, :]
    )[None, :, None, :]
    outputs = []
    keys_seen = []
    values_seen = []
    for step in range(STEPS):
        block = hidden_in[step : step + 1]
        project_count = block.shape[0]
        values = block.astype(jnp.float32)
        sums = lax.psum(jnp.sum(values * values, -1), "tensor")
        normed = (values * lax.rsqrt(sums[..., None] / D + EPSILON) * gain).astype(jnp.bfloat16)
        ordered = jnp.take(normed, row_order, axis=1).reshape(
            project_count, owners, unit_rows, local_width
        )
        term = jnp.einsum(
            "sojd,dhg->ohsjg", ordered, weight_grouped, preferred_element_type=jnp.float32
        )
        term = term.reshape(owners * KVH * project_count * unit_rows, GW)
        mine = lax.psum_scatter(term, "tensor", scatter_dimension=0, tiled=True)
        joined_block = mine.astype(jnp.bfloat16).reshape(project_count, unit_rows, GW)
        prepare_count = joined_block.shape[0]
        steps_here = step + jnp.arange(prepare_count, dtype=jnp.int32)
        position = row_length[None, :] + QR * steps_here[:, None] + row_step[None, :]
        prepare_queries = rotate(
            joined_block[..., : GQ * HD]
            .reshape(prepare_count, unit_rows, GQ, HD)
            .astype(jnp.float32),
            position[:, :, None],
        ).astype(jnp.bfloat16)
        keys = rotate(
            joined_block[..., GQ * HD : GQ * HD + HD].astype(jnp.float32), position
        ).astype(jnp.bfloat16)
        queries, keys, values = (prepare_queries, keys, joined_block[..., GQ * HD + HD :])
        keys_seen.append(keys)
        values_seen.append(values)
        keys_all = jnp.concatenate(keys_seen, 0)
        attend_count = queries.shape[0]
        cache_best, cache_total, cache_summed = cache_partial(
            queries,
            cache_data[:, :HD],
            cache_data[:, HD:],
            token_scale[:, 0],
            token_scale[:, 1],
            cache_mask,
        )
        news = jnp.einsum(
            "srgd,pjd->srgpj", queries, keys_all, preferred_element_type=jnp.float32
        ) * HD ** (-0.5)
        query_step = step + jnp.arange(attend_count, dtype=jnp.int32)[:, None, None, None]
        key_step = jnp.arange(keys_all.shape[0], dtype=jnp.int32)[None, None, :, None]
        allowed = (key_step < query_step) | (key_step == query_step) & (
            row_step[None, None, None, :] <= row_step[None, :, None, None]
        )
        allowed = (allowed & same_request[None, :, None, :])[:, :, None, :, :]
        news = jnp.where(allowed, news, NEG_FILL)
        best = jnp.maximum(cache_best, jnp.max(news, (3, 4)))
        factor = jnp.exp(cache_best - best)
        expo = jnp.where(allowed, jnp.exp(news - best[..., None, None]), 0.0)
        total = cache_total * factor + jnp.sum(expo, (3, 4))
        summed = cache_summed * factor[..., None] + jnp.einsum(
            "srgpj,pjd->srgd",
            expo.astype(jnp.bfloat16),
            jnp.concatenate(values_seen, 0),
            preferred_element_type=jnp.float32,
        )
        attention = (
            (summed / total[..., None])
            .astype(jnp.bfloat16)
            .reshape(attend_count, unit_rows, GQ * HD)
        )
        count = attention.shape[0]
        gathered = lax.all_gather(attention, "tensor", axis=2, tiled=True).reshape(
            count, unit_rows, owners, QH * HD
        )
        mixed = jnp.einsum(
            "sjof,fd->sojd", gathered, out_weight, preferred_element_type=jnp.float32
        )
        mixed = jnp.take(mixed.reshape(count, owners * unit_rows, local_width), inverse, axis=1)
        outputs.append(
            (hidden_in[step : step + count].astype(jnp.float32) + mixed).astype(jnp.bfloat16)
        )
    return jnp.concatenate(outputs, 0)


VMEM_LIMIT = 48 * 1024 * 1024
SHORT = pl.CostEstimate(flops=1, bytes_accessed=1, transcendentals=0)
LONG = pl.CostEstimate(flops=2 * 10**10, bytes_accessed=1, transcendentals=0)
LOW_BITS = 4
PACKED = 16 // LOW_BITS
LEVELS = 32600.0 * 2**LOW_BITS
POWER_STEPS = 8.0
TILE = 16
MESH_BITS = (1, 2, 4, 8)


def swap(value, bit):
    devices = lax.axis_size("tensor")
    return lax.ppermute(value, "tensor", [(i, i ^ bit) for i in range(devices)])


def no_work(*refs):
    del refs


def together(arrays, after):
    anywhere = pl.BlockSpec(memory_space=pl.ANY)
    return pl.pallas_call(
        no_work,
        in_specs=[anywhere] * (len(arrays) + len(after)),
        out_specs=[anywhere] * len(arrays),
        out_shape=[jax.ShapeDtypeStruct(a.shape, a.dtype) for a in arrays],
        input_output_aliases={i: i for i in range(len(arrays))},
        compiler_params=pltpu.CompilerParams(vmem_limit_bytes=VMEM_LIMIT),
        cost_estimate=SHORT,
        name="together",
    )(*arrays, *after)


def coded_rows(rows):
    return rows + rows // PACKED


def encode(block):
    top = jnp.max(jnp.abs(block), 0, keepdims=True)
    power = jnp.ceil(jnp.log2(jnp.maximum(top, 1e-30)) * POWER_STEPS)
    codes = jnp.round(block * (jnp.exp2(power * (-1.0 / POWER_STEPS)) * LEVELS)).astype(jnp.int32)
    low = codes & (2**LOW_BITS - 1)
    part = block.shape[0] // PACKED
    packed = low[:part]
    for i in range(1, PACKED):
        packed = packed + (low[i * part : (i + 1) * part] << (LOW_BITS * i))
    high = (codes >> LOW_BITS).astype(jnp.int16)
    return jnp.concatenate([high, (packed - 32768).astype(jnp.int16)], 0), power


def decode(codes, power):
    rows = codes.shape[0] * PACKED // (PACKED + 1)
    high = codes[:rows].astype(jnp.int32) << LOW_BITS
    packed = codes[rows:].astype(jnp.int32) + 32768
    low = jnp.concatenate(
        [(packed >> (LOW_BITS * i)) & (2**LOW_BITS - 1) for i in range(PACKED)], 0
    )
    scale = jnp.exp2(power * (1.0 / POWER_STEPS)) * (1.0 / LEVELS)
    return (high + low).astype(jnp.float32) * scale


def pick_row(rows, index):
    ids = lax.broadcasted_iota(jnp.int32, rows.shape, 0)
    return jnp.sum(jnp.where(ids == index, rows, 0.0), 0, keepdims=True)


def store_codes(sent, powers, block, index, steps):
    rows = coded_rows(block.shape[0])
    codes, power = encode(block)
    sent[pl.ds(pl.multiple_of(index * rows, TILE), rows), :] = codes

    powers[pl.ds(index, 1), :] = power

    @pl.when(index == steps - 1)
    def _():
        sent[pl.ds(steps * rows, TILE), :] = powers[...].astype(jnp.int32).astype(jnp.int16)


PART_HEADS = (3, 5)


def project_kernel(part, core, normed, weights, *refs):
    kept, sent, powers, slabs, arrived = refs[-5:]
    index = pl.program_id(0)
    half = kept.shape[2]
    heads = PART_HEADS[part] * HD
    first = sum(PART_HEADS[:part]) * HD

    def copies(group):
        found = []
        for side in range(2):
            owner = core[0] if side == 0 else 1 - core[0]
            spans = [(group * GW + owner * (GQ // 2 * HD) + first, 0, heads)]
            if half > heads:
                spans.append((group * GW + (GQ + owner) * HD, heads, HD))
            for number, (start, offset, size) in enumerate(spans):
                found.append(
                    pltpu.make_async_copy(
                        weights.at[:, pl.ds(pl.multiple_of(start, HD), size)],
                        slabs.at[group, :, pl.ds(side * half + offset, size)],
                        arrived.at[group, side, number],
                    )
                )
        return found

    @pl.when(index == 0)
    def _():
        for group in range(KVH):
            for copy in copies(group):
                copy.start()
        powers[...] = jnp.zeros_like(powers)

    for copy in copies(index):
        copy.wait()

    found = []
    rows = coded_rows(normed.shape[0])
    place = pl.ds(pl.multiple_of(index * rows, TILE), rows)
    for start in range(0, 2 * half, 2 * HD):
        stop = start + 2 * HD
        product = jnp.dot(
            normed[...], slabs[index, :, start:stop], preferred_element_type=jnp.float32
        )
        if start < half:
            kept[0, :, start : min(stop, half)] = product[:, : half - start]
        if stop > half:
            first = max(start, half)
            codes, power = encode(product[:, first - start :])
            sent[place, first - half : stop - half] = codes
            found.append(power)
    powers[pl.ds(index, 1), :] = jnp.concatenate(found, 1)

    @pl.when(index == KVH - 1)
    def _():
        sent[pl.ds(KVH * rows, TILE), :] = powers[...].astype(jnp.int32).astype(jnp.int16)


def project(core, normed, qkv_weight, part, after):
    rows, width = normed.shape
    columns = PART_HEADS[part] * HD + (HD if part == 0 else 0)
    sent_rows = KVH * coded_rows(rows) + TILE
    return pl.pallas_call(
        functools.partial(project_kernel, part),
        grid_spec=pltpu.PrefetchScalarGridSpec(
            num_scalar_prefetch=1,
            grid=(KVH,),
            in_specs=[pl.BlockSpec((rows, width), lambda t, c: (0, 0))]
            + [pl.BlockSpec(memory_space=pl.ANY)] * (1 + len(after)),
            out_specs=[
                pl.BlockSpec((1, rows, columns), lambda t, c: (t, 0, 0)),
                pl.BlockSpec((sent_rows, columns), lambda t, c: (0, 0)),
            ],
            scratch_shapes=[
                pltpu.VMEM((TILE, columns), jnp.float32),
                pltpu.VMEM((KVH, width, 2 * columns), jnp.bfloat16),
                pltpu.SemaphoreType.DMA((KVH, 2, 2)),
            ],
        ),
        out_shape=[
            pltpu.HBM((KVH, rows, columns), jnp.float32),
            jax.ShapeDtypeStruct((sent_rows, columns), jnp.int16),
        ],
        compiler_params=pltpu.CompilerParams(vmem_limit_bytes=VMEM_LIMIT),
        cost_estimate=SHORT,
        name="project",
    )(core, normed, qkv_weight, *after)


def fold_kernel(steps, low, bit, held, held_out, landed, landed_out, landed_powers, *refs):
    kept, sent, powers = refs[-3:]
    index = pl.program_id(0)
    rows_of_powers = landed_powers[...].astype(jnp.int32).astype(jnp.float32)
    first = index // low * (2 * low) + index % low

    def total(side, block, codes):
        power = pick_row(rows_of_powers, first + side * low)
        return block[0] + decode(codes[...], power)

    @pl.when(index == 0)
    def _():
        powers[...] = jnp.zeros_like(powers)

    kept[0] = total(bit[0], held, landed)
    store_codes(sent, powers, total(1 - bit[0], held_out, landed_out), index, steps)


def fold(bit, held, landed, low, after):
    blocks, rows, columns = held.shape
    steps = blocks // 2
    coded = coded_rows(rows)

    def block(i, b, out):
        side = 1 - b[0] if out else b[0]
        return i // low * (2 * low) + side * low + i % low

    return pl.pallas_call(
        functools.partial(fold_kernel, steps, low),
        grid_spec=pltpu.PrefetchScalarGridSpec(
            num_scalar_prefetch=1,
            grid=(steps,),
            in_specs=[
                pl.BlockSpec((1, rows, columns), lambda i, b: (block(i, b, False), 0, 0)),
                pl.BlockSpec((1, rows, columns), lambda i, b: (block(i, b, True), 0, 0)),
                pl.BlockSpec((coded, columns), lambda i, b: (block(i, b, False), 0)),
                pl.BlockSpec((coded, columns), lambda i, b: (block(i, b, True), 0)),
                pl.BlockSpec((TILE, columns), lambda i, b: (blocks * coded // TILE, 0)),
            ]
            + [pl.BlockSpec(memory_space=pl.ANY)] * len(after),
            out_specs=[
                pl.BlockSpec((1, rows, columns), lambda i, b: (i, 0, 0)),
                pl.BlockSpec((steps * coded + TILE, columns), lambda i, b: (0, 0)),
            ],
            scratch_shapes=[pltpu.VMEM((TILE, columns), jnp.float32)],
        ),
        out_shape=[
            jax.ShapeDtypeStruct((steps, rows, columns), jnp.float32),
            jax.ShapeDtypeStruct((steps * coded + TILE, columns), jnp.int16),
        ],
        compiler_params=pltpu.CompilerParams(vmem_limit_bytes=VMEM_LIMIT),
        cost_estimate=SHORT,
        name="fold",
    )(bit, held, held, landed, landed, landed, *after)


def finish_kernel(heads, after_count, core, held, landed, cosine, sine, *refs):
    queries, *pair = refs[after_count:]
    coded = coded_rows(held.shape[1])
    power = landed[pl.ds(coded, TILE), :].astype(jnp.int32).astype(jnp.float32)[0:1]
    total = held[0] + decode(landed[pl.ds(0, coded), :], power)
    joined = total.astype(jnp.bfloat16)
    for head in range(joined.shape[1] // HD):
        raw = joined[:, head * HD : (head + 1) * HD].astype(jnp.float32)
        turned = raw * cosine[...] + pltpu.roll(raw, HD // 2, 1) * sine[...]
        if head < heads:
            queries[:, head * HD : (head + 1) * HD] = turned.astype(jnp.bfloat16)
        else:
            pair[0][...] = jnp.where(core[0] == 0, turned, raw).astype(jnp.bfloat16)


def finish(core, held, landed, cosine, sine, heads, after):
    _, rows, columns = held.shape
    whole = pl.BlockSpec(memory_space=pltpu.VMEM)
    shapes = [jax.ShapeDtypeStruct((rows, heads * HD), jnp.bfloat16)]
    if columns > heads * HD:
        shapes.append(jax.ShapeDtypeStruct((rows, HD), jnp.bfloat16))
    return pl.pallas_call(
        functools.partial(finish_kernel, heads, len(after)),
        in_specs=[pl.BlockSpec(memory_space=pltpu.SMEM)]
        + [whole] * 4
        + [pl.BlockSpec(memory_space=pl.ANY)] * len(after),
        out_specs=[whole] * len(shapes),
        out_shape=shapes,
        compiler_params=pltpu.CompilerParams(vmem_limit_bytes=VMEM_LIMIT),
        cost_estimate=LONG,
        name="finish",
    )(core, held, landed, cosine, sine, *after)


def mix_kernel(count, places, *refs):
    pieces = refs[:count]
    weights, start, mixed, total, wide, arrived = refs[count:]
    depth = wide.shape[1]
    columns = wide.shape[2] // 2
    flat = []
    for piece in pieces:
        flat += [piece] if len(piece.shape) == 2 else [piece.at[i] for i in range(piece.shape[0])]
    copies = [
        pltpu.make_async_copy(
            weights.at[pl.ds(pl.multiple_of(places[i] * depth, depth), depth), :],
            wide.at[i],
            arrived.at[i],
        )
        for i in range(len(flat))
    ]
    for copy in copies:
        copy.start()
    cuts = [0, 1, 2, 4, len(flat)]
    cuts = sorted(set(min(cut, len(flat)) for cut in cuts))
    for first, last in zip(cuts, cuts[1:]):
        for copy in copies[first:last]:
            copy.wait()
        for side in range(2):
            span = pl.ds(side * columns, columns)
            source = start if first == 0 else total
            value = source[:, span].astype(jnp.float32)
            for i in range(first, last):
                value = value + jnp.dot(
                    flat[i][...], wide[i, :, span], preferred_element_type=jnp.float32
                )
            target = mixed if last == len(flat) else total
            target[:, span] = value.astype(target.dtype)


def mix(places, pieces, out_weight, start, dtype):
    columns = out_weight.shape[1]
    rows, width = pieces[0].shape[-2:]
    count = sum(1 if len(p.shape) == 2 else p.shape[0] for p in pieces)
    whole = pl.BlockSpec(memory_space=pltpu.VMEM)
    return pl.pallas_call(
        functools.partial(mix_kernel, len(pieces)),
        in_specs=[pl.BlockSpec(memory_space=pltpu.SMEM)]
        + [whole] * len(pieces)
        + [pl.BlockSpec(memory_space=pl.ANY), whole],
        out_specs=whole,
        scratch_shapes=[
            pltpu.VMEM((rows, columns), jnp.float32),
            pltpu.VMEM((count, width, columns), jnp.bfloat16),
            pltpu.SemaphoreType.DMA((count,)),
        ],
        out_shape=jax.ShapeDtypeStruct((rows, columns), dtype),
        compiler_params=pltpu.CompilerParams(vmem_limit_bytes=VMEM_LIMIT),
        cost_estimate=SHORT,
        name="mix",
    )(places, *pieces, out_weight, start)


def pack_kernel(groups, count, *refs):
    flat = []
    for ref in refs[:count]:
        flat += [ref] if len(ref.shape) == 2 else [ref.at[i] for i in range(ref.shape[0])]
    for group, target in zip(groups, refs[-len(groups) :]):
        for place, index in enumerate(group):
            target[place] = flat[index][...]


def pack(pieces, groups, after):
    whole = pl.BlockSpec(memory_space=pltpu.VMEM)
    shape = pieces[0].shape[-2:]
    return pl.pallas_call(
        functools.partial(pack_kernel, groups, len(pieces)),
        in_specs=[whole] * len(pieces) + [pl.BlockSpec(memory_space=pl.ANY)] * len(after),
        out_specs=[whole] * len(groups),
        out_shape=[jax.ShapeDtypeStruct((len(g),) + shape, pieces[0].dtype) for g in groups],
        compiler_params=pltpu.CompilerParams(vmem_limit_bytes=VMEM_LIMIT),
        cost_estimate=SHORT,
        name="pack",
    )(*pieces, *after)


def gather_and_mix(attention, out_weight, start, device):
    def add(mixed, pieces, offsets, dtype=jnp.float32):
        places = jnp.stack([device ^ offset for offset in offsets])
        return mix(places, pieces, out_weight, mixed, dtype)

    near = swap(attention, 4)
    across = swap(attention, 2)
    far = swap(attention, 8)
    partner = swap(attention, 1)
    first, onward = pack([near, across, far], [(0, 1, 2), (0, 2)], [partner])
    (attention,) = together([attention], [onward])

    across_onward = swap(onward, 2)
    farthest = swap(attention, 12)
    first_partner = swap(first, 1)
    mixed = add(start, [attention, partner], (0, 1))
    mixed = add(mixed, [first, first_partner], (4, 2, 8, 5, 3, 9))
    (second,) = pack([across_onward, farthest], [(0, 1, 2)], [mixed])

    last = swap(farthest, 2)
    second_partner = swap(second, 1)
    mixed = add(mixed, [second, second_partner], (6, 10, 12, 7, 11, 13))
    (last,) = together([last], [mixed])

    last_partner = swap(last, 1)
    return add(mixed, [last, last_partner], (14, 15), jnp.bfloat16)


def attend_kernel(
    slot_request,
    queries,
    new_keys,
    new_values,
    own,
    other,
    key_scale,
    value_scale,
    cache_bias,
    new_bias,
    attention,
    slot_best,
    slot_total,
    slot_sum,
    best,
    total,
    summed,
):
    slots = slot_best.shape[0]
    requests, count, _ = queries.shape
    transposed = (((1,), (1,)), ((), ()))
    for request in range(requests):
        scores = (
            lax.dot_general(
                queries[request],
                new_keys[request],
                transposed,
                preferred_element_type=jnp.float32,
            )
            * HD ** (-0.5)
            + new_bias[...]
        )
        top = jnp.max(scores, -1, keepdims=True)
        expo = jnp.exp(scores - top)
        best[request] = jnp.broadcast_to(top, (count, HD))
        total[request] = jnp.broadcast_to(jnp.sum(expo, -1, keepdims=True), (count, HD))
        summed[request] = jnp.dot(
            expo.astype(jnp.bfloat16), new_values[request], preferred_element_type=jnp.float32
        )
    for slot in range(slots):
        request = slot_request[slot]
        query = queries[request]
        raw = [
            part[:, slot * BLK : (slot + 1) * BLK, :].reshape(KVH * BLK, 2 * HD)
            for part in (own, other)
        ]
        scores = jnp.concatenate(
            [
                lax.dot_general(
                    query, kv[:, :HD], transposed, preferred_element_type=jnp.float32
                )
                for kv in raw
            ],
            1,
        )
        scores = scores * key_scale[slot : slot + 1, :] + cache_bias[slot : slot + 1, :]
        top = jnp.max(scores, -1, keepdims=True)
        expo = jnp.exp(scores - top)
        weights = (expo * value_scale[slot : slot + 1, :]).astype(jnp.bfloat16)
        slot_best[slot] = jnp.broadcast_to(top, (count, HD))
        slot_total[slot] = jnp.broadcast_to(jnp.sum(expo, -1, keepdims=True), (count, HD))
        values = jnp.concatenate([kv[:, HD:] for kv in raw], 0)
        slot_sum[slot] = jnp.dot(weights, values, preferred_element_type=jnp.float32)
    for slot in range(slots):
        request = slot_request[slot]
        before = best[request]
        here = slot_best[slot]
        top = jnp.maximum(before, here)
        keep = jnp.exp(before - top)
        add = jnp.exp(here - top)
        best[request] = top
        total[request] = total[request] * keep + slot_total[slot] * add
        summed[request] = summed[request] * keep + slot_sum[slot] * add
    for request in range(requests):
        attention[request] = (summed[request] / total[request]).astype(jnp.bfloat16)


def attend(slot_request, *arrays):
    queries = arrays[0]
    slots = arrays[5].shape[0]
    requests, count, _ = queries.shape
    whole = pl.BlockSpec(memory_space=pltpu.VMEM)
    return pl.pallas_call(
        attend_kernel,
        in_specs=[pl.BlockSpec(memory_space=pltpu.SMEM)] + [whole] * len(arrays),
        out_specs=whole,
        out_shape=jax.ShapeDtypeStruct((requests, count, HD), jnp.bfloat16),
        scratch_shapes=[pltpu.VMEM((slots, count, HD), jnp.float32)] * 3
        + [pltpu.VMEM((requests, count, HD), jnp.float32)] * 3,
        compiler_params=pltpu.CompilerParams(vmem_limit_bytes=VMEM_LIMIT),
        cost_estimate=SHORT,
        name="attend",
    )(slot_request, *arrays)


def slot_layout(request_length, block_table, slots, stripe):
    requests, most = block_table.shape
    stripes = (request_length + stripe - 1) // stripe
    columns = jnp.arange(most, dtype=jnp.int32)
    held = columns[None, :] < stripes[:, None]
    hit = held[:, :, None] & (
        block_table[:, :, None] == jnp.arange(slots, dtype=jnp.int32)[None, None, :]
    )
    hit = hit.astype(jnp.int32)
    order = jnp.arange(requests, dtype=jnp.int32)
    request = jnp.sum(hit * order[:, None, None], (0, 1))
    rank = jnp.sum(hit * columns[None, :, None], (0, 1))
    length = jnp.sum(hit * request_length[:, None, None], (0, 1))
    return request, rank, length


def arrange_kernel(chip, pool, scales, after, *sent):
    slots = pool.shape[0]
    for k, target in enumerate(sent):
        head = chip[0] ^ k
        target[: slots * BLK, :] = pool[:, head].reshape(slots * BLK, 2 * HD)
        target[slots * BLK :, :] = scales[head]


def arrange(chip, cache_pool, scales, after):
    rows = cache_pool.shape[0] * BLK + TILE
    whole = pl.BlockSpec(memory_space=pltpu.VMEM)
    return pl.pallas_call(
        arrange_kernel,
        in_specs=[
            pl.BlockSpec(memory_space=pltpu.SMEM),
            whole,
            whole,
            pl.BlockSpec(memory_space=pl.ANY),
        ],
        out_specs=[whole] * KVH,
        out_shape=[jax.ShapeDtypeStruct((rows, 2 * HD), jnp.bfloat16)] * KVH,
        compiler_params=pltpu.CompilerParams(vmem_limit_bytes=VMEM_LIMIT),
        cost_estimate=SHORT,
        name="arrange",
    )(chip, cache_pool, scales, after)


def local_pairs(
    hidden_in,
    norm_gain,
    qkv_weight,
    out_weight,
    cache_pool,
    cache_scale,
    request_length,
    block_table,
):
    devices = lax.axis_size("tensor")
    device = lax.axis_index("tensor")
    core = device % 2
    chip = device // 2
    stripe = devices * BLK
    slots = cache_pool.shape[0]
    requests = request_length.shape[0]
    rows = STEPS * requests * QR
    width = hidden_in.shape[2]
    heads = GQ // 2

    hidden = hidden_in.astype(jnp.float32)
    sums = jnp.sum(hidden * hidden, -1)
    bits = [jnp.reshape((device >> b) & 1, (1,)).astype(jnp.int32) for b in range(4)]
    scale_rows = jnp.pad(
        jnp.transpose(cache_scale, (1, 2, 0)).reshape(KVH, 1, 2 * slots),
        ((0, 0), (0, TILE - 1), (0, 2 * HD - 2 * slots)),
    )
    sums = sums + swap(sums, 2)
    chip_scalar = jnp.reshape(chip, (1,)).astype(jnp.int32)
    cache_pieces = list(arrange(chip_scalar, cache_pool, scale_rows, sums))

    def handed(k):
        cache_pieces[k] = swap(cache_pieces[k], 2 * k)

    for bit in (1, 4, 8):
        sums = sums + swap(sums, bit)
    normed = (
        hidden * lax.rsqrt(sums[..., None] / D + EPSILON) * norm_gain.astype(jnp.float32)
    ).astype(jnp.bfloat16)
    normed = normed.reshape(rows, width)

    step_ids = jnp.arange(STEPS, dtype=jnp.int32)
    row_ids = jnp.arange(QR, dtype=jnp.int32)
    position = (
        request_length[None, :, None] + QR * step_ids[:, None, None] + row_ids[None, None, :]
    )
    freqs = ROPE_BASE ** (-(jnp.arange(HD // 2, dtype=jnp.float32) * 2.0 / HD))
    angles = position.reshape(rows, 1).astype(jnp.float32) * freqs
    cosine = jnp.concatenate([jnp.cos(angles)] * 2, 1)
    sine = jnp.concatenate([-jnp.sin(angles), jnp.sin(angles)], 1)

    def folded(part, b, landed, low, *after):
        return fold(bits[b], part, landed, low, after)

    def finished(part, number, landed, *after):
        return finish(bits[0], part, landed, cosine, sine, PART_HEADS[number], after)

    for k in (1, 3, 4, 5, 6):
        handed(k)
    held_a, sent_a = project(bits[0], normed, qkv_weight, 0, cache_pieces[:1])
    core_a = swap(sent_a, 1)
    held_b, sent_b = project(
        bits[0], normed, qkv_weight, 1, [held_a, cache_pieces[1], cache_pieces[3]]
    )
    sent_b, cache_pieces[2], cache_pieces[7] = together(
        [sent_b, cache_pieces[2], cache_pieces[7]], cache_pieces[4:7]
    )
    core_b = swap(sent_b, 1)
    for k in (2, 7):
        handed(k)
    held_a, sent_a = folded(held_a, 2, core_a, 2, sent_b)
    line_a = swap(sent_a, 4)
    held_b, sent_b = folded(held_b, 1, core_b, 1, held_a, cache_pieces[2], cache_pieces[7])
    line_b = swap(sent_b, 2)
    held_a, sent_a = folded(held_a, 1, line_a, 1, held_b)
    line_a = swap(sent_a, 2)
    held_b, sent_b = folded(held_b, 2, line_b, 1, held_a)
    line_b = swap(sent_b, 4)
    (cache_own,) = pack(cache_pieces, [tuple(range(KVH))], [held_b])
    cache_other = swap(cache_own, 1)
    held_a, sent_a = folded(held_a, 3, line_a, 1, cache_own)
    line_a = swap(sent_a, 8)
    held_b, sent_b = folded(held_b, 3, line_b, 1, held_a)
    line_b = swap(sent_b, 8)
    query_a, pair = finished(held_a, 0, line_a, held_b)
    (pair,) = together([pair], [line_b])
    pair_other = swap(pair, 1)
    (query_b,) = finished(held_b, 1, line_b, query_a)
    query_chunks = [query_a, query_b]
    cache_parts = (cache_own, cache_other)
    keys = jnp.where(core == 0, pair, pair_other)
    raw_values = jnp.where(core == 0, pair_other, pair)
    queries = jnp.concatenate(query_chunks, 1).reshape(STEPS, requests, QR, heads, HD)
    queries = jnp.transpose(queries, (1, 0, 2, 3, 4)).reshape(requests, STEPS * QR * heads, HD)

    def by_request(value):
        value = jnp.transpose(value.reshape(STEPS, requests, QR, HD), (1, 0, 2, 3))
        value = value.reshape(requests, STEPS * QR, HD)
        return jnp.pad(value, ((0, 0), (0, TILE - STEPS * QR), (0, 0)))

    slot_request, slot_rank, slot_length = slot_layout(request_length, block_table, slots, stripe)
    source = chip ^ jnp.arange(KVH, dtype=jnp.int32)
    sources = jnp.stack([source * 2 + core, source * 2 + 1 - core])
    offset = sources[:, :, None] * BLK + jnp.arange(BLK, dtype=jnp.int32)[None, None, :]
    token = slot_rank[:, None] * stripe + offset.reshape(1, stripe)
    cache_bias = jnp.where(token < slot_length[:, None], 0.0, NEG_FILL).astype(jnp.float32)
    scales = jnp.concatenate([part[:, slots * BLK, : 2 * slots] for part in cache_parts])
    scales = scales.astype(jnp.float32).reshape(2 * KVH, 2, slots)
    scales = jnp.repeat(jnp.transpose(scales, (1, 2, 0)), BLK, axis=2)
    order = jnp.arange(STEPS * QR * heads, dtype=jnp.int32) // heads
    key_order = jnp.arange(TILE, dtype=jnp.int32)
    new_bias = jnp.where(key_order[None, :] <= order[:, None], 0.0, NEG_FILL).astype(jnp.float32)
    attention = attend(
        slot_request,
        queries,
        by_request(keys),
        by_request(raw_values),
        *cache_parts,
        scales[0] * HD ** (-0.5),
        scales[1],
        cache_bias,
        new_bias,
    )
    attention = jnp.transpose(
        attention.reshape(requests, STEPS, QR, heads, HD), (1, 0, 2, 3, 4)
    ).reshape(rows, heads * HD)
    mixed = gather_and_mix(attention, out_weight, hidden_in.reshape(rows, width), device)
    return mixed.reshape(hidden_in.shape)


def solution(mesh):
    return jax.shard_map(
        local_pairs if mesh.shape["tensor"] == 2 * KVH else local_general,
        mesh=mesh,
        in_specs=(
            P(None, "groups", "tensor"),
            P("tensor"),
            P("tensor", None),
            P(None, "tensor"),
            P(("groups", "tensor"), None, None, None),
            P(("groups", "tensor"), None, None),
            P("groups"),
            P("groups", None),
        ),
        out_specs=P(None, "groups", "tensor"),
        check_vma=False,
    )
```

```python
import functools

import jax
import jax.numpy as jnp
from jax import lax
from jax.experimental import pallas as pl
from jax.experimental.pallas import tpu as pltpu
from jax.sharding import PartitionSpec as P

D = 16384
QH = 128
KVH = 8
HD = 128
QR = 6
STEPS = 2
BLK = 16
GQ = 16
GW = 2304


EPSILON = 1e-05
ROPE_BASE = 500000.0
NEG_FILL = -1e30


def rotate(values, positions):
    half = values.shape[-1] // 2
    freqs = ROPE_BASE ** (-(jnp.arange(half, dtype=jnp.float32) * 2.0 / values.shape[-1]))
    angles = positions.astype(jnp.float32)[..., None] * freqs
    cosine = jnp.cos(angles)
    sine = jnp.sin(angles)
    first = values[..., :half]
    second = values[..., half:]
    return jnp.concatenate([first * cosine - second * sine, second * cosine + first * sine], -1)


def request_layout(request_owner, request_length, block_table, owners, stripe):
    requests = request_owner.shape[0]
    most = block_table.shape[1]
    order = jnp.arange(requests, dtype=jnp.int32)
    stripes = (request_length + stripe - 1) // stripe
    before = (
        (request_owner[None, :] == request_owner[:, None]) & (order[None, :] < order[:, None])
    ).astype(jnp.int32)
    rank = jnp.sum(before, 1)
    offset = jnp.sum(before * stripes[None, :], 1)
    owner_ids = jnp.arange(owners, dtype=jnp.int32)
    mine = request_owner[None, :] == owner_ids[:, None]
    member = mine[:, :, None] & (
        rank[None, :, None] == jnp.arange(requests // owners, dtype=jnp.int32)[None, None, :]
    )
    owner_requests = jnp.sum(member.astype(jnp.int32) * order[None, :, None], 1)
    columns = jnp.arange(most, dtype=jnp.int32)
    within = columns[None, None, :] - offset[None, :, None]
    hit = (mine[:, :, None] & (within >= 0) & (within < stripes[None, :, None])).astype(jnp.int32)
    stripe_request = jnp.sum(hit * order[None, :, None], 1) - (1 - jnp.sum(hit, 1))
    stripe_rank = jnp.sum(hit * within, 1)
    pick = (within[..., None] == columns[None, None, None, :]).astype(jnp.int32)
    slots = jnp.sum(hit[..., None] * pick * block_table[None, :, None, :], (1, 3))
    return (owner_requests, stripe_request, stripe_rank, slots, rank, stripes)


def cache_partial(queries, keys, values, key_scale, value_scale, mask):
    scores = jnp.einsum("srgd,td->srgt", queries, keys, preferred_element_type=jnp.float32)
    scores = jnp.where(mask, scores * key_scale * HD ** (-0.5), NEG_FILL)
    best = jnp.max(scores, -1)
    expo = jnp.where(mask, jnp.exp(scores - best[..., None]), 0.0)
    total = jnp.sum(expo, -1)
    weights = (expo * value_scale).astype(jnp.bfloat16)
    summed = jnp.einsum("srgt,td->srgd", weights, values, preferred_element_type=jnp.float32)
    return (best, total, summed)


def local_general(
    hidden_in,
    norm_gain,
    qkv_weight,
    out_weight,
    cache_pool,
    cache_scale,
    request_length,
    block_table,
):
    devices = lax.axis_size("tensor")
    device = lax.axis_index("tensor")
    owners = devices // KVH
    stripe = devices * BLK
    requests = request_length.shape[0]
    request_owner = jnp.arange(requests, dtype=jnp.int32) % owners
    unit_rows = requests // owners * QR
    most = block_table.shape[1]
    local_width = hidden_in.shape[2]
    my_owner = device // KVH
    owner_requests, stripe_request, stripe_rank, slots, rank, stripes = request_layout(
        request_owner, request_length, block_table, owners, stripe
    )
    step_rows = jnp.arange(QR, dtype=jnp.int32)
    row_order = (owner_requests[:, :, None] * QR + step_rows[None, None, :]).reshape(
        owners * unit_rows
    )
    inverse = ((request_owner * unit_rows + rank * QR)[:, None] + step_rows[None, :]).reshape(
        requests * QR
    )
    row_request = jnp.repeat(owner_requests[my_owner], QR)
    row_length = request_length[row_request]
    row_step = jnp.arange(unit_rows, dtype=jnp.int32) % QR
    same_request = row_request[:, None] == row_request[None, :]
    gain = norm_gain.astype(jnp.float32)
    weight_grouped = qkv_weight.reshape(local_width, KVH, GW)
    sent = cache_pool[jnp.transpose(slots)].reshape(most, devices, BLK, 2 * HD)
    sent_scale = cache_scale[jnp.transpose(slots)].reshape(most, devices, 2)
    landed, landed_scale = (
        lax.all_to_all(sent, "tensor", split_axis=1, concat_axis=1, tiled=True),
        lax.all_to_all(sent_scale, "tensor", split_axis=1, concat_axis=1, tiled=True),
    )
    cache_data = landed.reshape(most * stripe, 2 * HD)
    token_scale = jnp.broadcast_to(
        landed_scale.astype(jnp.float32)[:, :, None, :], (most, devices, BLK, 2)
    ).reshape(most * stripe, 2)
    token = jnp.arange(most * stripe, dtype=jnp.int32)
    token_stripe = token // stripe
    token_request = stripe_request[my_owner][token_stripe]
    token_position = stripe_rank[my_owner][token_stripe] * stripe + token % stripe
    token_length = jnp.where(token_request >= 0, request_length[jnp.maximum(token_request, 0)], 0)
    cache_mask = (
        (token_request[None, :] == row_request[:, None]) & (token_position < token_length)[None, :]
    )[None, :, None, :]
    outputs = []
    keys_seen = []
    values_seen = []
    for step in range(STEPS):
        block = hidden_in[step : step + 1]
        project_count = block.shape[0]
        values = block.astype(jnp.float32)
        sums = lax.psum(jnp.sum(values * values, -1), "tensor")
        normed = (values * lax.rsqrt(sums[..., None] / D + EPSILON) * gain).astype(jnp.bfloat16)
        ordered = jnp.take(normed, row_order, axis=1).reshape(
            project_count, owners, unit_rows, local_width
        )
        term = jnp.einsum(
            "sojd,dhg->ohsjg", ordered, weight_grouped, preferred_element_type=jnp.float32
        )
        term = term.reshape(owners * KVH * project_count * unit_rows, GW)
        mine = lax.psum_scatter(term, "tensor", scatter_dimension=0, tiled=True)
        joined_block = mine.astype(jnp.bfloat16).reshape(project_count, unit_rows, GW)
        prepare_count = joined_block.shape[0]
        steps_here = step + jnp.arange(prepare_count, dtype=jnp.int32)
        position = row_length[None, :] + QR * steps_here[:, None] + row_step[None, :]
        prepare_queries = rotate(
            joined_block[..., : GQ * HD]
            .reshape(prepare_count, unit_rows, GQ, HD)
            .astype(jnp.float32),
            position[:, :, None],
        ).astype(jnp.bfloat16)
        keys = rotate(
            joined_block[..., GQ * HD : GQ * HD + HD].astype(jnp.float32), position
        ).astype(jnp.bfloat16)
        queries, keys, values = (prepare_queries, keys, joined_block[..., GQ * HD + HD :])
        keys_seen.append(keys)
        values_seen.append(values)
        keys_all = jnp.concatenate(keys_seen, 0)
        attend_count = queries.shape[0]
        cache_best, cache_total, cache_summed = cache_partial(
            queries,
            cache_data[:, :HD],
            cache_data[:, HD:],
            token_scale[:, 0],
            token_scale[:, 1],
            cache_mask,
        )
        news = jnp.einsum(
            "srgd,pjd->srgpj", queries, keys_all, preferred_element_type=jnp.float32
        ) * HD ** (-0.5)
        query_step = step + jnp.arange(attend_count, dtype=jnp.int32)[:, None, None, None]
        key_step = jnp.arange(keys_all.shape[0], dtype=jnp.int32)[None, None, :, None]
        allowed = (key_step < query_step) | (key_step == query_step) & (
            row_step[None, None, None, :] <= row_step[None, :, None, None]
        )
        allowed = (allowed & same_request[None, :, None, :])[:, :, None, :, :]
        news = jnp.where(allowed, news, NEG_FILL)
        best = jnp.maximum(cache_best, jnp.max(news, (3, 4)))
        factor = jnp.exp(cache_best - best)
        expo = jnp.where(allowed, jnp.exp(news - best[..., None, None]), 0.0)
        total = cache_total * factor + jnp.sum(expo, (3, 4))
        summed = cache_summed * factor[..., None] + jnp.einsum(
            "srgpj,pjd->srgd",
            expo.astype(jnp.bfloat16),
            jnp.concatenate(values_seen, 0),
            preferred_element_type=jnp.float32,
        )
        attention = (
            (summed / total[..., None])
            .astype(jnp.bfloat16)
            .reshape(attend_count, unit_rows, GQ * HD)
        )
        count = attention.shape[0]
        gathered = lax.all_gather(attention, "tensor", axis=2, tiled=True).reshape(
            count, unit_rows, owners, QH * HD
        )
        mixed = jnp.einsum(
            "sjof,fd->sojd", gathered, out_weight, preferred_element_type=jnp.float32
        )
        mixed = jnp.take(mixed.reshape(count, owners * unit_rows, local_width), inverse, axis=1)
        outputs.append(
            (hidden_in[step : step + count].astype(jnp.float32) + mixed).astype(jnp.bfloat16)
        )
    return jnp.concatenate(outputs, 0)


VMEM_LIMIT = 48 * 1024 * 1024
SHORT = pl.CostEstimate(flops=1, bytes_accessed=1, transcendentals=0)
LONG = pl.CostEstimate(flops=2 * 10**10, bytes_accessed=1, transcendentals=0)
LOW_BITS = 4
PACKED = 16 // LOW_BITS
LEVELS = 32600.0 * 2**LOW_BITS
POWER_STEPS = 8.0
FIRST = (1, 3, 4)
TILE = 16
MESH_BITS = (1, 2, 4, 8)


def swap(value, bit):
    devices = lax.axis_size("tensor")
    return lax.ppermute(value, "tensor", [(i, i ^ bit) for i in range(devices)])


def no_work(*refs):
    del refs


def together(arrays, after):
    anywhere = pl.BlockSpec(memory_space=pl.ANY)
    return pl.pallas_call(
        no_work,
        in_specs=[anywhere] * (len(arrays) + len(after)),
        out_specs=[anywhere] * len(arrays),
        out_shape=[jax.ShapeDtypeStruct(a.shape, a.dtype) for a in arrays],
        input_output_aliases={i: i for i in range(len(arrays))},
        compiler_params=pltpu.CompilerParams(vmem_limit_bytes=VMEM_LIMIT),
        cost_estimate=SHORT,
        name="together",
    )(*arrays, *after)


def coded_rows(rows):
    return rows + rows // PACKED


def encode(block):
    top = jnp.max(jnp.abs(block), 0, keepdims=True)
    power = jnp.ceil(jnp.log2(jnp.maximum(top, 1e-30)) * POWER_STEPS)
    codes = jnp.round(block * (jnp.exp2(power * (-1.0 / POWER_STEPS)) * LEVELS)).astype(jnp.int32)
    low = codes & (2**LOW_BITS - 1)
    part = block.shape[0] // PACKED
    packed = low[:part]
    for i in range(1, PACKED):
        packed = packed + (low[i * part : (i + 1) * part] << (LOW_BITS * i))
    high = (codes >> LOW_BITS).astype(jnp.int16)
    return jnp.concatenate([high, (packed - 32768).astype(jnp.int16)], 0), power


def decode(codes, power):
    rows = codes.shape[0] * PACKED // (PACKED + 1)
    high = codes[:rows].astype(jnp.int32) << LOW_BITS
    packed = codes[rows:].astype(jnp.int32) + 32768
    low = jnp.concatenate(
        [(packed >> (LOW_BITS * i)) & (2**LOW_BITS - 1) for i in range(PACKED)], 0
    )
    scale = jnp.exp2(power * (1.0 / POWER_STEPS)) * (1.0 / LEVELS)
    return (high + low).astype(jnp.float32) * scale


def pick_row(rows, index):
    ids = lax.broadcasted_iota(jnp.int32, rows.shape, 0)
    return jnp.sum(jnp.where(ids == index, rows, 0.0), 0, keepdims=True)


def store_codes(sent, powers, block, index, steps):
    rows = coded_rows(block.shape[0])
    codes, power = encode(block)
    sent[pl.ds(pl.multiple_of(index * rows, TILE), rows), :] = codes

    powers[pl.ds(index, 1), :] = power

    @pl.when(index == steps - 1)
    def _():
        sent[pl.ds(steps * rows, TILE), :] = powers[...].astype(jnp.int32).astype(jnp.int16)


PART_HEADS = (3, 5)


def project_kernel(part, core, normed, weights, *refs):
    kept, sent, powers, slabs, arrived = refs[-5:]
    index = pl.program_id(0)
    half = kept.shape[2]
    heads = PART_HEADS[part] * HD
    first = sum(PART_HEADS[:part]) * HD

    def copies(group):
        found = []
        for side in range(2):
            owner = core[0] if side == 0 else 1 - core[0]
            spans = [(group * GW + owner * (GQ // 2 * HD) + first, 0, heads)]
            if half > heads:
                spans.append((group * GW + (GQ + owner) * HD, heads, HD))
            for number, (start, offset, size) in enumerate(spans):
                found.append(
                    pltpu.make_async_copy(
                        weights.at[:, pl.ds(pl.multiple_of(start, HD), size)],
                        slabs.at[group, :, pl.ds(side * half + offset, size)],
                        arrived.at[group, side, number],
                    )
                )
        return found

    @pl.when(index == 0)
    def _():
        for group in range(KVH):
            for copy in copies(group):
                copy.start()
        powers[...] = jnp.zeros_like(powers)

    for copy in copies(index):
        copy.wait()

    found = []
    rows = coded_rows(normed.shape[0])
    place = pl.ds(pl.multiple_of(index * rows, TILE), rows)
    for start in range(0, 2 * half, 2 * HD):
        stop = start + 2 * HD
        product = jnp.dot(
            normed[...], slabs[index, :, start:stop], preferred_element_type=jnp.float32
        )
        if start < half:
            kept[0, :, start : min(stop, half)] = product[:, : half - start]
        if stop > half:
            first = max(start, half)
            codes, power = encode(product[:, first - start :])
            sent[place, first - half : stop - half] = codes
            found.append(power)
    powers[pl.ds(index, 1), :] = jnp.concatenate(found, 1)

    @pl.when(index == KVH - 1)
    def _():
        sent[pl.ds(KVH * rows, TILE), :] = powers[...].astype(jnp.int32).astype(jnp.int16)


def project(core, normed, qkv_weight, part, cost, after):
    rows, width = normed.shape
    columns = PART_HEADS[part] * HD + (HD if part == 0 else 0)
    sent_rows = KVH * coded_rows(rows) + TILE
    return pl.pallas_call(
        functools.partial(project_kernel, part),
        grid_spec=pltpu.PrefetchScalarGridSpec(
            num_scalar_prefetch=1,
            grid=(KVH,),
            in_specs=[pl.BlockSpec((rows, width), lambda t, c: (0, 0))]
            + [pl.BlockSpec(memory_space=pl.ANY)] * (1 + len(after)),
            out_specs=[
                pl.BlockSpec((1, rows, columns), lambda t, c: (t, 0, 0)),
                pl.BlockSpec((sent_rows, columns), lambda t, c: (0, 0)),
            ],
            scratch_shapes=[
                pltpu.VMEM((TILE, columns), jnp.float32),
                pltpu.VMEM((KVH, width, 2 * columns), jnp.bfloat16),
                pltpu.SemaphoreType.DMA((KVH, 2, 2)),
            ],
        ),
        out_shape=[
            pltpu.HBM((KVH, rows, columns), jnp.float32),
            jax.ShapeDtypeStruct((sent_rows, columns), jnp.int16),
        ],
        compiler_params=pltpu.CompilerParams(vmem_limit_bytes=VMEM_LIMIT),
        cost_estimate=cost,
        name="project",
    )(core, normed, qkv_weight, *after)


def fold_kernel(steps, low, bit, held, held_out, landed, landed_out, landed_powers, *refs):
    kept, sent, powers = refs[-3:]
    index = pl.program_id(0)
    rows_of_powers = landed_powers[...].astype(jnp.int32).astype(jnp.float32)
    first = index // low * (2 * low) + index % low

    def total(side, block, codes):
        power = pick_row(rows_of_powers, first + side * low)
        return block[0] + decode(codes[...], power)

    @pl.when(index == 0)
    def _():
        powers[...] = jnp.zeros_like(powers)

    kept[0] = total(bit[0], held, landed)
    store_codes(sent, powers, total(1 - bit[0], held_out, landed_out), index, steps)


def fold(bit, held, landed, low, after):
    blocks, rows, columns = held.shape
    steps = blocks // 2
    coded = coded_rows(rows)

    def block(i, b, out):
        side = 1 - b[0] if out else b[0]
        return i // low * (2 * low) + side * low + i % low

    return pl.pallas_call(
        functools.partial(fold_kernel, steps, low),
        grid_spec=pltpu.PrefetchScalarGridSpec(
            num_scalar_prefetch=1,
            grid=(steps,),
            in_specs=[
                pl.BlockSpec((1, rows, columns), lambda i, b: (block(i, b, False), 0, 0)),
                pl.BlockSpec((1, rows, columns), lambda i, b: (block(i, b, True), 0, 0)),
                pl.BlockSpec((coded, columns), lambda i, b: (block(i, b, False), 0)),
                pl.BlockSpec((coded, columns), lambda i, b: (block(i, b, True), 0)),
                pl.BlockSpec((TILE, columns), lambda i, b: (blocks * coded // TILE, 0)),
            ]
            + [pl.BlockSpec(memory_space=pl.ANY)] * len(after),
            out_specs=[
                pl.BlockSpec((1, rows, columns), lambda i, b: (i, 0, 0)),
                pl.BlockSpec((steps * coded + TILE, columns), lambda i, b: (0, 0)),
            ],
            scratch_shapes=[pltpu.VMEM((TILE, columns), jnp.float32)],
        ),
        out_shape=[
            jax.ShapeDtypeStruct((steps, rows, columns), jnp.float32),
            jax.ShapeDtypeStruct((steps * coded + TILE, columns), jnp.int16),
        ],
        compiler_params=pltpu.CompilerParams(vmem_limit_bytes=VMEM_LIMIT),
        cost_estimate=SHORT,
        name="fold",
    )(bit, held, held, landed, landed, landed, *after)


def finish_kernel(heads, after_count, core, held, landed, cosine, sine, *refs):
    queries, *pair = refs[after_count:]
    coded = coded_rows(held.shape[1])
    power = landed[pl.ds(coded, TILE), :].astype(jnp.int32).astype(jnp.float32)[0:1]
    total = held[0] + decode(landed[pl.ds(0, coded), :], power)
    joined = total.astype(jnp.bfloat16)
    for head in range(joined.shape[1] // HD):
        raw = joined[:, head * HD : (head + 1) * HD].astype(jnp.float32)
        turned = raw * cosine[...] + pltpu.roll(raw, HD // 2, 1) * sine[...]
        if head < heads:
            queries[:, head * HD : (head + 1) * HD] = turned.astype(jnp.bfloat16)
        else:
            pair[0][...] = jnp.where(core[0] == 0, turned, raw).astype(jnp.bfloat16)


def finish(core, held, landed, cosine, sine, heads, after):
    _, rows, columns = held.shape
    whole = pl.BlockSpec(memory_space=pltpu.VMEM)
    shapes = [jax.ShapeDtypeStruct((rows, heads * HD), jnp.bfloat16)]
    if columns > heads * HD:
        shapes.append(jax.ShapeDtypeStruct((rows, HD), jnp.bfloat16))
    return pl.pallas_call(
        functools.partial(finish_kernel, heads, len(after)),
        in_specs=[pl.BlockSpec(memory_space=pltpu.SMEM)]
        + [whole] * 4
        + [pl.BlockSpec(memory_space=pl.ANY)] * len(after),
        out_specs=[whole] * len(shapes),
        out_shape=shapes,
        compiler_params=pltpu.CompilerParams(vmem_limit_bytes=VMEM_LIMIT),
        cost_estimate=LONG,
        name="finish",
    )(core, held, landed, cosine, sine, *after)


def mix_kernel(count, places, *refs):
    pieces = refs[:count]
    weights, start, mixed, total, wide, arrived = refs[count:]
    depth = wide.shape[1]
    columns = wide.shape[2] // 2
    flat = []
    for piece in pieces:
        flat += [piece] if len(piece.shape) == 2 else [piece.at[i] for i in range(piece.shape[0])]
    copies = [
        pltpu.make_async_copy(
            weights.at[pl.ds(pl.multiple_of(places[i] * depth, depth), depth), :],
            wide.at[i],
            arrived.at[i],
        )
        for i in range(len(flat))
    ]
    for copy in copies:
        copy.start()
    cuts = [0, 1, 2, 4, len(flat)]
    cuts = sorted(set(min(cut, len(flat)) for cut in cuts))
    for first, last in zip(cuts, cuts[1:]):
        for copy in copies[first:last]:
            copy.wait()
        for side in range(2):
            span = pl.ds(side * columns, columns)
            source = start if first == 0 else total
            value = source[:, span].astype(jnp.float32)
            for i in range(first, last):
                value = value + jnp.dot(
                    flat[i][...], wide[i, :, span], preferred_element_type=jnp.float32
                )
            target = mixed if last == len(flat) else total
            target[:, span] = value.astype(target.dtype)


def mix(places, pieces, out_weight, start, dtype):
    columns = out_weight.shape[1]
    rows, width = pieces[0].shape[-2:]
    count = sum(1 if len(p.shape) == 2 else p.shape[0] for p in pieces)
    whole = pl.BlockSpec(memory_space=pltpu.VMEM)
    return pl.pallas_call(
        functools.partial(mix_kernel, len(pieces)),
        in_specs=[pl.BlockSpec(memory_space=pltpu.SMEM)]
        + [whole] * len(pieces)
        + [pl.BlockSpec(memory_space=pl.ANY), whole],
        out_specs=whole,
        scratch_shapes=[
            pltpu.VMEM((rows, columns), jnp.float32),
            pltpu.VMEM((count, width, columns), jnp.bfloat16),
            pltpu.SemaphoreType.DMA((count,)),
        ],
        out_shape=jax.ShapeDtypeStruct((rows, columns), dtype),
        compiler_params=pltpu.CompilerParams(vmem_limit_bytes=VMEM_LIMIT),
        cost_estimate=SHORT,
        name="mix",
    )(places, *pieces, out_weight, start)


def pack_kernel(groups, count, *refs):
    flat = []
    for ref in refs[:count]:
        flat += [ref] if len(ref.shape) == 2 else [ref.at[i] for i in range(ref.shape[0])]
    for group, target in zip(groups, refs[-len(groups) :]):
        for place, index in enumerate(group):
            target[place] = flat[index][...]


def pack(pieces, groups, after):
    whole = pl.BlockSpec(memory_space=pltpu.VMEM)
    shape = pieces[0].shape[-2:]
    return pl.pallas_call(
        functools.partial(pack_kernel, groups, len(pieces)),
        in_specs=[whole] * len(pieces) + [pl.BlockSpec(memory_space=pl.ANY)] * len(after),
        out_specs=[whole] * len(groups),
        out_shape=[jax.ShapeDtypeStruct((len(g),) + shape, pieces[0].dtype) for g in groups],
        compiler_params=pltpu.CompilerParams(vmem_limit_bytes=VMEM_LIMIT),
        cost_estimate=SHORT,
        name="pack",
    )(*pieces, *after)


def gather_and_mix(attention, out_weight, start, device):
    def add(mixed, pieces, offsets, dtype=jnp.float32):
        places = jnp.stack([device ^ offset for offset in offsets])
        return mix(places, pieces, out_weight, mixed, dtype)

    near = swap(attention, 4)
    across = swap(attention, 2)
    far = swap(attention, 8)
    partner = swap(attention, 1)
    first, onward = pack([near, across, far], [(0, 1, 2), (0, 2)], [partner])
    (attention,) = together([attention], [onward])

    across_onward = swap(onward, 2)
    farthest = swap(attention, 12)
    first_partner = swap(first, 1)
    mixed = add(start, [attention, partner], (0, 1))
    mixed = add(mixed, [first, first_partner], (4, 2, 8, 5, 3, 9))
    (second,) = pack([across_onward, farthest], [(0, 1, 2)], [mixed])

    last = swap(farthest, 2)
    second_partner = swap(second, 1)
    mixed = add(mixed, [second, second_partner], (6, 10, 12, 7, 11, 13))
    (last,) = together([last], [mixed])

    last_partner = swap(last, 1)
    return add(mixed, [last, last_partner], (14, 15), jnp.bfloat16)


def attend_kernel(
    slot_request,
    queries,
    new_keys,
    new_values,
    own,
    other,
    key_scale,
    value_scale,
    cache_bias,
    new_bias,
    attention,
    slot_best,
    slot_total,
    slot_sum,
    best,
    total,
    summed,
):
    slots = slot_best.shape[0]
    requests, count, _ = queries.shape
    transposed = (((1,), (1,)), ((), ()))
    for request in range(requests):
        scores = (
            lax.dot_general(
                queries[request],
                new_keys[request],
                transposed,
                preferred_element_type=jnp.float32,
            )
            * HD ** (-0.5)
            + new_bias[...]
        )
        top = jnp.max(scores, -1, keepdims=True)
        expo = jnp.exp(scores - top)
        best[request] = jnp.broadcast_to(top, (count, HD))
        total[request] = jnp.broadcast_to(jnp.sum(expo, -1, keepdims=True), (count, HD))
        summed[request] = jnp.dot(
            expo.astype(jnp.bfloat16), new_values[request], preferred_element_type=jnp.float32
        )
    for slot in range(slots):
        request = slot_request[slot]
        query = queries[request]
        raw = [
            part[:, slot * BLK : (slot + 1) * BLK, :].reshape(KVH * BLK, 2 * HD)
            for part in (own, other)
        ]
        scores = jnp.concatenate(
            [
                lax.dot_general(
                    query, kv[:, :HD], transposed, preferred_element_type=jnp.float32
                )
                for kv in raw
            ],
            1,
        )
        scores = scores * key_scale[slot : slot + 1, :] + cache_bias[slot : slot + 1, :]
        top = jnp.max(scores, -1, keepdims=True)
        expo = jnp.exp(scores - top)
        weights = (expo * value_scale[slot : slot + 1, :]).astype(jnp.bfloat16)
        slot_best[slot] = jnp.broadcast_to(top, (count, HD))
        slot_total[slot] = jnp.broadcast_to(jnp.sum(expo, -1, keepdims=True), (count, HD))
        values = jnp.concatenate([kv[:, HD:] for kv in raw], 0)
        slot_sum[slot] = jnp.dot(weights, values, preferred_element_type=jnp.float32)
    for slot in range(slots):
        request = slot_request[slot]
        before = best[request]
        here = slot_best[slot]
        top = jnp.maximum(before, here)
        keep = jnp.exp(before - top)
        add = jnp.exp(here - top)
        best[request] = top
        total[request] = total[request] * keep + slot_total[slot] * add
        summed[request] = summed[request] * keep + slot_sum[slot] * add
    for request in range(requests):
        attention[request] = (summed[request] / total[request]).astype(jnp.bfloat16)


def attend(slot_request, *arrays):
    queries = arrays[0]
    slots = arrays[5].shape[0]
    requests, count, _ = queries.shape
    whole = pl.BlockSpec(memory_space=pltpu.VMEM)
    return pl.pallas_call(
        attend_kernel,
        in_specs=[pl.BlockSpec(memory_space=pltpu.SMEM)] + [whole] * len(arrays),
        out_specs=whole,
        out_shape=jax.ShapeDtypeStruct((requests, count, HD), jnp.bfloat16),
        scratch_shapes=[pltpu.VMEM((slots, count, HD), jnp.float32)] * 3
        + [pltpu.VMEM((requests, count, HD), jnp.float32)] * 3,
        compiler_params=pltpu.CompilerParams(vmem_limit_bytes=VMEM_LIMIT),
        cost_estimate=SHORT,
        name="attend",
    )(slot_request, *arrays)


def slot_layout(request_length, block_table, slots, stripe):
    requests, most = block_table.shape
    stripes = (request_length + stripe - 1) // stripe
    columns = jnp.arange(most, dtype=jnp.int32)
    held = columns[None, :] < stripes[:, None]
    hit = held[:, :, None] & (
        block_table[:, :, None] == jnp.arange(slots, dtype=jnp.int32)[None, None, :]
    )
    hit = hit.astype(jnp.int32)
    order = jnp.arange(requests, dtype=jnp.int32)
    request = jnp.sum(hit * order[:, None, None], (0, 1))
    rank = jnp.sum(hit * columns[None, :, None], (0, 1))
    length = jnp.sum(hit * request_length[:, None, None], (0, 1))
    return request, rank, length


def arrange_kernel(chip, pool, scales, after, *sent):
    slots = pool.shape[0]
    for k, target in enumerate(sent):
        head = chip[0] ^ k
        target[: slots * BLK, :] = pool[:, head].reshape(slots * BLK, 2 * HD)
        target[slots * BLK :, :] = scales[head]


def arrange(chip, cache_pool, scales, after):
    rows = cache_pool.shape[0] * BLK + TILE
    whole = pl.BlockSpec(memory_space=pltpu.VMEM)
    return pl.pallas_call(
        arrange_kernel,
        in_specs=[
            pl.BlockSpec(memory_space=pltpu.SMEM),
            whole,
            whole,
            pl.BlockSpec(memory_space=pl.ANY),
        ],
        out_specs=[whole] * KVH,
        out_shape=[jax.ShapeDtypeStruct((rows, 2 * HD), jnp.bfloat16)] * KVH,
        compiler_params=pltpu.CompilerParams(vmem_limit_bytes=VMEM_LIMIT),
        cost_estimate=SHORT,
        name="arrange",
    )(chip, cache_pool, scales, after)


def local_pairs(
    hidden_in,
    norm_gain,
    qkv_weight,
    out_weight,
    cache_pool,
    cache_scale,
    request_length,
    block_table,
):
    devices = lax.axis_size("tensor")
    device = lax.axis_index("tensor")
    core = device % 2
    chip = device // 2
    stripe = devices * BLK
    slots = cache_pool.shape[0]
    requests = request_length.shape[0]
    rows = STEPS * requests * QR
    width = hidden_in.shape[2]
    heads = GQ // 2

    hidden = hidden_in.astype(jnp.float32)
    sums = jnp.sum(hidden * hidden, -1)
    bits = [jnp.reshape((device >> b) & 1, (1,)).astype(jnp.int32) for b in range(4)]
    scale_rows = jnp.pad(
        jnp.transpose(cache_scale, (1, 2, 0)).reshape(KVH, 1, 2 * slots),
        ((0, 0), (0, TILE - 1), (0, 2 * HD - 2 * slots)),
    )
    sums = sums + swap(sums, 2)
    chip_scalar = jnp.reshape(chip, (1,)).astype(jnp.int32)
    cache_pieces = list(arrange(chip_scalar, cache_pool, scale_rows, sums))

    def handed(k):
        cache_pieces[k] = swap(cache_pieces[k], 2 * k)

    for bit in (1, 4, 8):
        sums = sums + swap(sums, bit)
    normed = (
        hidden * lax.rsqrt(sums[..., None] / D + EPSILON) * norm_gain.astype(jnp.float32)
    ).astype(jnp.bfloat16)
    normed = normed.reshape(rows, width)

    step_ids = jnp.arange(STEPS, dtype=jnp.int32)
    row_ids = jnp.arange(QR, dtype=jnp.int32)
    position = (
        request_length[None, :, None] + QR * step_ids[:, None, None] + row_ids[None, None, :]
    )
    freqs = ROPE_BASE ** (-(jnp.arange(HD // 2, dtype=jnp.float32) * 2.0 / HD))
    angles = position.reshape(rows, 1).astype(jnp.float32) * freqs
    cosine = jnp.concatenate([jnp.cos(angles)] * 2, 1)
    sine = jnp.concatenate([-jnp.sin(angles), jnp.sin(angles)], 1)

    def folded(part, b, landed, low, *after):
        return fold(bits[b], part, landed, low, after)

    def finished(part, number, landed, *after):
        return finish(bits[0], part, landed, cosine, sine, PART_HEADS[number], after)

    for k in (1, 3, 4, 5, 6):
        handed(k)
    held_a, sent_a = project(bits[0], normed, qkv_weight, 0, SHORT, cache_pieces[:1])
    core_a = swap(sent_a, 1)
    first = [held_a] + [cache_pieces[k] for k in FIRST]
    held_b, sent_b = project(bits[0], normed, qkv_weight, 1, LONG, first)
    sent_b, cache_pieces[2], cache_pieces[7] = together(
        [sent_b, cache_pieces[2], cache_pieces[7]],
        [core_a] + [cache_pieces[k] for k in (1, 3, 4, 5, 6) if k not in FIRST],
    )
    core_b = swap(sent_b, 1)
    for k in (2, 7):
        handed(k)
    held_a, sent_a = folded(held_a, 2, core_a, 2, sent_b)
    line_a = swap(sent_a, 4)
    held_b, sent_b = folded(held_b, 1, core_b, 1, held_a, cache_pieces[2], cache_pieces[7])
    line_b = swap(sent_b, 2)
    held_a, sent_a = folded(held_a, 1, line_a, 1, held_b)
    line_a = swap(sent_a, 2)
    held_b, sent_b = folded(held_b, 2, line_b, 1, held_a)
    line_b = swap(sent_b, 4)
    (cache_own,) = pack(cache_pieces, [tuple(range(KVH))], [held_b])
    cache_other = swap(cache_own, 1)
    held_a, sent_a = folded(held_a, 3, line_a, 1, cache_own)
    line_a = swap(sent_a, 8)
    held_b, sent_b = folded(held_b, 3, line_b, 1, held_a)
    line_b = swap(sent_b, 8)
    query_a, pair = finished(held_a, 0, line_a, held_b)
    (pair,) = together([pair], [line_b])
    pair_other = swap(pair, 1)
    (query_b,) = finished(held_b, 1, line_b, query_a)
    query_chunks = [query_a, query_b]
    cache_parts = (cache_own, cache_other)
    keys = jnp.where(core == 0, pair, pair_other)
    raw_values = jnp.where(core == 0, pair_other, pair)
    queries = jnp.concatenate(query_chunks, 1).reshape(STEPS, requests, QR, heads, HD)
    queries = jnp.transpose(queries, (1, 0, 2, 3, 4)).reshape(requests, STEPS * QR * heads, HD)

    def by_request(value):
        value = jnp.transpose(value.reshape(STEPS, requests, QR, HD), (1, 0, 2, 3))
        value = value.reshape(requests, STEPS * QR, HD)
        return jnp.pad(value, ((0, 0), (0, TILE - STEPS * QR), (0, 0)))

    slot_request, slot_rank, slot_length = slot_layout(request_length, block_table, slots, stripe)
    source = chip ^ jnp.arange(KVH, dtype=jnp.int32)
    sources = jnp.stack([source * 2 + core, source * 2 + 1 - core])
    offset = sources[:, :, None] * BLK + jnp.arange(BLK, dtype=jnp.int32)[None, None, :]
    token = slot_rank[:, None] * stripe + offset.reshape(1, stripe)
    cache_bias = jnp.where(token < slot_length[:, None], 0.0, NEG_FILL).astype(jnp.float32)
    scales = jnp.concatenate([part[:, slots * BLK, : 2 * slots] for part in cache_parts])
    scales = scales.astype(jnp.float32).reshape(2 * KVH, 2, slots)
    scales = jnp.repeat(jnp.transpose(scales, (1, 2, 0)), BLK, axis=2)
    order = jnp.arange(STEPS * QR * heads, dtype=jnp.int32) // heads
    key_order = jnp.arange(TILE, dtype=jnp.int32)
    new_bias = jnp.where(key_order[None, :] <= order[:, None], 0.0, NEG_FILL).astype(jnp.float32)
    attention = attend(
        slot_request,
        queries,
        by_request(keys),
        by_request(raw_values),
        *cache_parts,
        scales[0] * HD ** (-0.5),
        scales[1],
        cache_bias,
        new_bias,
    )
    attention = jnp.transpose(
        attention.reshape(requests, STEPS, QR, heads, HD), (1, 0, 2, 3, 4)
    ).reshape(rows, heads * HD)
    mixed = gather_and_mix(attention, out_weight, hidden_in.reshape(rows, width), device)
    return mixed.reshape(hidden_in.shape)


def solution(mesh):
    return jax.shard_map(
        local_pairs if mesh.shape["tensor"] == 2 * KVH else local_general,
        mesh=mesh,
        in_specs=(
            P(None, "groups", "tensor"),
            P("tensor"),
            P("tensor", None),
            P(None, "tensor"),
            P(("groups", "tensor"), None, None, None),
            P(("groups", "tensor"), None, None),
            P("groups"),
            P("groups", None),
        ),
        out_specs=P(None, "groups", "tensor"),
        check_vma=False,
    )
```

```python
import functools

import jax
import jax.numpy as jnp
from jax import lax
from jax.experimental import pallas as pl
from jax.experimental.pallas import tpu as pltpu
from jax.sharding import PartitionSpec as P

D = 16384
QH = 128
KVH = 8
HD = 128
QR = 6
STEPS = 2
BLK = 16
GQ = 16
GW = 2304


EPSILON = 1e-05
ROPE_BASE = 500000.0
NEG_FILL = -1e30


def rotate(values, positions):
    half = values.shape[-1] // 2
    freqs = ROPE_BASE ** (-(jnp.arange(half, dtype=jnp.float32) * 2.0 / values.shape[-1]))
    angles = positions.astype(jnp.float32)[..., None] * freqs
    cosine = jnp.cos(angles)
    sine = jnp.sin(angles)
    first = values[..., :half]
    second = values[..., half:]
    return jnp.concatenate([first * cosine - second * sine, second * cosine + first * sine], -1)


def request_layout(request_owner, request_length, block_table, owners, stripe):
    requests = request_owner.shape[0]
    most = block_table.shape[1]
    order = jnp.arange(requests, dtype=jnp.int32)
    stripes = (request_length + stripe - 1) // stripe
    before = (
        (request_owner[None, :] == request_owner[:, None]) & (order[None, :] < order[:, None])
    ).astype(jnp.int32)
    rank = jnp.sum(before, 1)
    offset = jnp.sum(before * stripes[None, :], 1)
    owner_ids = jnp.arange(owners, dtype=jnp.int32)
    mine = request_owner[None, :] == owner_ids[:, None]
    member = mine[:, :, None] & (
        rank[None, :, None] == jnp.arange(requests // owners, dtype=jnp.int32)[None, None, :]
    )
    owner_requests = jnp.sum(member.astype(jnp.int32) * order[None, :, None], 1)
    columns = jnp.arange(most, dtype=jnp.int32)
    within = columns[None, None, :] - offset[None, :, None]
    hit = (mine[:, :, None] & (within >= 0) & (within < stripes[None, :, None])).astype(jnp.int32)
    stripe_request = jnp.sum(hit * order[None, :, None], 1) - (1 - jnp.sum(hit, 1))
    stripe_rank = jnp.sum(hit * within, 1)
    pick = (within[..., None] == columns[None, None, None, :]).astype(jnp.int32)
    slots = jnp.sum(hit[..., None] * pick * block_table[None, :, None, :], (1, 3))
    return (owner_requests, stripe_request, stripe_rank, slots, rank, stripes)


def cache_partial(queries, keys, values, key_scale, value_scale, mask):
    scores = jnp.einsum("srgd,td->srgt", queries, keys, preferred_element_type=jnp.float32)
    scores = jnp.where(mask, scores * key_scale * HD ** (-0.5), NEG_FILL)
    best = jnp.max(scores, -1)
    expo = jnp.where(mask, jnp.exp(scores - best[..., None]), 0.0)
    total = jnp.sum(expo, -1)
    weights = (expo * value_scale).astype(jnp.bfloat16)
    summed = jnp.einsum("srgt,td->srgd", weights, values, preferred_element_type=jnp.float32)
    return (best, total, summed)


def local_general(
    hidden_in,
    norm_gain,
    qkv_weight,
    out_weight,
    cache_pool,
    cache_scale,
    request_length,
    block_table,
):
    devices = lax.axis_size("tensor")
    device = lax.axis_index("tensor")
    owners = devices // KVH
    stripe = devices * BLK
    requests = request_length.shape[0]
    request_owner = jnp.arange(requests, dtype=jnp.int32) % owners
    unit_rows = requests // owners * QR
    most = block_table.shape[1]
    local_width = hidden_in.shape[2]
    my_owner = device // KVH
    owner_requests, stripe_request, stripe_rank, slots, rank, stripes = request_layout(
        request_owner, request_length, block_table, owners, stripe
    )
    step_rows = jnp.arange(QR, dtype=jnp.int32)
    row_order = (owner_requests[:, :, None] * QR + step_rows[None, None, :]).reshape(
        owners * unit_rows
    )
    inverse = ((request_owner * unit_rows + rank * QR)[:, None] + step_rows[None, :]).reshape(
        requests * QR
    )
    row_request = jnp.repeat(owner_requests[my_owner], QR)
    row_length = request_length[row_request]
    row_step = jnp.arange(unit_rows, dtype=jnp.int32) % QR
    same_request = row_request[:, None] == row_request[None, :]
    gain = norm_gain.astype(jnp.float32)
    weight_grouped = qkv_weight.reshape(local_width, KVH, GW)
    sent = cache_pool[jnp.transpose(slots)].reshape(most, devices, BLK, 2 * HD)
    sent_scale = cache_scale[jnp.transpose(slots)].reshape(most, devices, 2)
    landed, landed_scale = (
        lax.all_to_all(sent, "tensor", split_axis=1, concat_axis=1, tiled=True),
        lax.all_to_all(sent_scale, "tensor", split_axis=1, concat_axis=1, tiled=True),
    )
    cache_data = landed.reshape(most * stripe, 2 * HD)
    token_scale = jnp.broadcast_to(
        landed_scale.astype(jnp.float32)[:, :, None, :], (most, devices, BLK, 2)
    ).reshape(most * stripe, 2)
    token = jnp.arange(most * stripe, dtype=jnp.int32)
    token_stripe = token // stripe
    token_request = stripe_request[my_owner][token_stripe]
    token_position = stripe_rank[my_owner][token_stripe] * stripe + token % stripe
    token_length = jnp.where(token_request >= 0, request_length[jnp.maximum(token_request, 0)], 0)
    cache_mask = (
        (token_request[None, :] == row_request[:, None]) & (token_position < token_length)[None, :]
    )[None, :, None, :]
    outputs = []
    keys_seen = []
    values_seen = []
    for step in range(STEPS):
        block = hidden_in[step : step + 1]
        project_count = block.shape[0]
        values = block.astype(jnp.float32)
        sums = lax.psum(jnp.sum(values * values, -1), "tensor")
        normed = (values * lax.rsqrt(sums[..., None] / D + EPSILON) * gain).astype(jnp.bfloat16)
        ordered = jnp.take(normed, row_order, axis=1).reshape(
            project_count, owners, unit_rows, local_width
        )
        term = jnp.einsum(
            "sojd,dhg->ohsjg", ordered, weight_grouped, preferred_element_type=jnp.float32
        )
        term = term.reshape(owners * KVH * project_count * unit_rows, GW)
        mine = lax.psum_scatter(term, "tensor", scatter_dimension=0, tiled=True)
        joined_block = mine.astype(jnp.bfloat16).reshape(project_count, unit_rows, GW)
        prepare_count = joined_block.shape[0]
        steps_here = step + jnp.arange(prepare_count, dtype=jnp.int32)
        position = row_length[None, :] + QR * steps_here[:, None] + row_step[None, :]
        prepare_queries = rotate(
            joined_block[..., : GQ * HD]
            .reshape(prepare_count, unit_rows, GQ, HD)
            .astype(jnp.float32),
            position[:, :, None],
        ).astype(jnp.bfloat16)
        keys = rotate(
            joined_block[..., GQ * HD : GQ * HD + HD].astype(jnp.float32), position
        ).astype(jnp.bfloat16)
        queries, keys, values = (prepare_queries, keys, joined_block[..., GQ * HD + HD :])
        keys_seen.append(keys)
        values_seen.append(values)
        keys_all = jnp.concatenate(keys_seen, 0)
        attend_count = queries.shape[0]
        cache_best, cache_total, cache_summed = cache_partial(
            queries,
            cache_data[:, :HD],
            cache_data[:, HD:],
            token_scale[:, 0],
            token_scale[:, 1],
            cache_mask,
        )
        news = jnp.einsum(
            "srgd,pjd->srgpj", queries, keys_all, preferred_element_type=jnp.float32
        ) * HD ** (-0.5)
        query_step = step + jnp.arange(attend_count, dtype=jnp.int32)[:, None, None, None]
        key_step = jnp.arange(keys_all.shape[0], dtype=jnp.int32)[None, None, :, None]
        allowed = (key_step < query_step) | (key_step == query_step) & (
            row_step[None, None, None, :] <= row_step[None, :, None, None]
        )
        allowed = (allowed & same_request[None, :, None, :])[:, :, None, :, :]
        news = jnp.where(allowed, news, NEG_FILL)
        best = jnp.maximum(cache_best, jnp.max(news, (3, 4)))
        factor = jnp.exp(cache_best - best)
        expo = jnp.where(allowed, jnp.exp(news - best[..., None, None]), 0.0)
        total = cache_total * factor + jnp.sum(expo, (3, 4))
        summed = cache_summed * factor[..., None] + jnp.einsum(
            "srgpj,pjd->srgd",
            expo.astype(jnp.bfloat16),
            jnp.concatenate(values_seen, 0),
            preferred_element_type=jnp.float32,
        )
        attention = (
            (summed / total[..., None])
            .astype(jnp.bfloat16)
            .reshape(attend_count, unit_rows, GQ * HD)
        )
        count = attention.shape[0]
        gathered = lax.all_gather(attention, "tensor", axis=2, tiled=True).reshape(
            count, unit_rows, owners, QH * HD
        )
        mixed = jnp.einsum(
            "sjof,fd->sojd", gathered, out_weight, preferred_element_type=jnp.float32
        )
        mixed = jnp.take(mixed.reshape(count, owners * unit_rows, local_width), inverse, axis=1)
        outputs.append(
            (hidden_in[step : step + count].astype(jnp.float32) + mixed).astype(jnp.bfloat16)
        )
    return jnp.concatenate(outputs, 0)


VMEM_LIMIT = 48 * 1024 * 1024
SHORT = pl.CostEstimate(flops=1, bytes_accessed=1, transcendentals=0)
LONG = pl.CostEstimate(flops=2 * 10**10, bytes_accessed=1, transcendentals=0)
LOW_BITS = 4
PACKED = 16 // LOW_BITS
LEVELS = 32600.0 * 2**LOW_BITS
POWER_STEPS = 8.0
TILE = 16
MESH_BITS = (1, 2, 4, 8)


def swap(value, bit):
    devices = lax.axis_size("tensor")
    return lax.ppermute(value, "tensor", [(i, i ^ bit) for i in range(devices)])


def no_work(*refs):
    del refs


def together(arrays, after):
    anywhere = pl.BlockSpec(memory_space=pl.ANY)
    return pl.pallas_call(
        no_work,
        in_specs=[anywhere] * (len(arrays) + len(after)),
        out_specs=[anywhere] * len(arrays),
        out_shape=[jax.ShapeDtypeStruct(a.shape, a.dtype) for a in arrays],
        input_output_aliases={i: i for i in range(len(arrays))},
        compiler_params=pltpu.CompilerParams(vmem_limit_bytes=VMEM_LIMIT),
        cost_estimate=SHORT,
        name="together",
    )(*arrays, *after)


def coded_rows(rows):
    return rows + rows // PACKED


def encode(block):
    top = jnp.max(jnp.abs(block), 0, keepdims=True)
    power = jnp.ceil(jnp.log2(jnp.maximum(top, 1e-30)) * POWER_STEPS)
    codes = jnp.round(block * (jnp.exp2(power * (-1.0 / POWER_STEPS)) * LEVELS)).astype(jnp.int32)
    low = codes & (2**LOW_BITS - 1)
    part = block.shape[0] // PACKED
    packed = low[:part]
    for i in range(1, PACKED):
        packed = packed + (low[i * part : (i + 1) * part] << (LOW_BITS * i))
    high = (codes >> LOW_BITS).astype(jnp.int16)
    return jnp.concatenate([high, (packed - 32768).astype(jnp.int16)], 0), power


def decode(codes, power):
    rows = codes.shape[0] * PACKED // (PACKED + 1)
    high = codes[:rows].astype(jnp.int32) << LOW_BITS
    packed = codes[rows:].astype(jnp.int32) + 32768
    low = jnp.concatenate(
        [(packed >> (LOW_BITS * i)) & (2**LOW_BITS - 1) for i in range(PACKED)], 0
    )
    scale = jnp.exp2(power * (1.0 / POWER_STEPS)) * (1.0 / LEVELS)
    return (high + low).astype(jnp.float32) * scale


def pick_row(rows, index):
    ids = lax.broadcasted_iota(jnp.int32, rows.shape, 0)
    return jnp.sum(jnp.where(ids == index, rows, 0.0), 0, keepdims=True)


def store_codes(sent, powers, block, index, steps):
    rows = coded_rows(block.shape[0])
    codes, power = encode(block)
    sent[pl.ds(pl.multiple_of(index * rows, TILE), rows), :] = codes

    powers[pl.ds(index, 1), :] = power

    @pl.when(index == steps - 1)
    def _():
        sent[pl.ds(steps * rows, TILE), :] = powers[...].astype(jnp.int32).astype(jnp.int16)


PART_HEADS = (3, 5)


def project_kernel(part, core, normed, weights, *refs):
    kept, sent, powers, slabs, arrived = refs[-5:]
    index = pl.program_id(0)
    half = kept.shape[2]
    heads = PART_HEADS[part] * HD
    first = sum(PART_HEADS[:part]) * HD

    def copies(group):
        found = []
        for side in range(2):
            owner = core[0] if side == 0 else 1 - core[0]
            spans = [(group * GW + owner * (GQ // 2 * HD) + first, 0, heads)]
            if half > heads:
                spans.append((group * GW + (GQ + owner) * HD, heads, HD))
            for number, (start, offset, size) in enumerate(spans):
                found.append(
                    pltpu.make_async_copy(
                        weights.at[:, pl.ds(pl.multiple_of(start, HD), size)],
                        slabs.at[group, :, pl.ds(side * half + offset, size)],
                        arrived.at[group, side, number],
                    )
                )
        return found

    @pl.when(index == 0)
    def _():
        for group in range(KVH):
            for copy in copies(group):
                copy.start()
        powers[...] = jnp.zeros_like(powers)

    for copy in copies(index):
        copy.wait()

    found = []
    rows = coded_rows(normed.shape[0])
    place = pl.ds(pl.multiple_of(index * rows, TILE), rows)
    for start in range(0, 2 * half, 2 * HD):
        stop = start + 2 * HD
        product = jnp.dot(
            normed[...], slabs[index, :, start:stop], preferred_element_type=jnp.float32
        )
        if start < half:
            kept[0, :, start : min(stop, half)] = product[:, : half - start]
        if stop > half:
            first = max(start, half)
            codes, power = encode(product[:, first - start :])
            sent[place, first - half : stop - half] = codes
            found.append(power)
    powers[pl.ds(index, 1), :] = jnp.concatenate(found, 1)

    @pl.when(index == KVH - 1)
    def _():
        sent[pl.ds(KVH * rows, TILE), :] = powers[...].astype(jnp.int32).astype(jnp.int16)


def project(core, normed, qkv_weight, part, after):
    rows, width = normed.shape
    columns = PART_HEADS[part] * HD + (HD if part == 0 else 0)
    sent_rows = KVH * coded_rows(rows) + TILE
    return pl.pallas_call(
        functools.partial(project_kernel, part),
        grid_spec=pltpu.PrefetchScalarGridSpec(
            num_scalar_prefetch=1,
            grid=(KVH,),
            in_specs=[pl.BlockSpec((rows, width), lambda t, c: (0, 0))]
            + [pl.BlockSpec(memory_space=pl.ANY)] * (1 + len(after)),
            out_specs=[
                pl.BlockSpec((1, rows, columns), lambda t, c: (t, 0, 0)),
                pl.BlockSpec((sent_rows, columns), lambda t, c: (0, 0)),
            ],
            scratch_shapes=[
                pltpu.VMEM((TILE, columns), jnp.float32),
                pltpu.VMEM((KVH, width, 2 * columns), jnp.bfloat16),
                pltpu.SemaphoreType.DMA((KVH, 2, 2)),
            ],
        ),
        out_shape=[
            pltpu.HBM((KVH, rows, columns), jnp.float32),
            jax.ShapeDtypeStruct((sent_rows, columns), jnp.int16),
        ],
        compiler_params=pltpu.CompilerParams(vmem_limit_bytes=VMEM_LIMIT),
        cost_estimate=SHORT,
        name="project",
    )(core, normed, qkv_weight, *after)


def fold_kernel(steps, low, bit, held, held_out, landed, landed_out, landed_powers, *refs):
    kept, sent, powers = refs[-3:]
    index = pl.program_id(0)
    rows_of_powers = landed_powers[...].astype(jnp.int32).astype(jnp.float32)
    first = index // low * (2 * low) + index % low

    def total(side, block, codes):
        power = pick_row(rows_of_powers, first + side * low)
        return block[0] + decode(codes[...], power)

    @pl.when(index == 0)
    def _():
        powers[...] = jnp.zeros_like(powers)

    kept[0] = total(bit[0], held, landed)
    store_codes(sent, powers, total(1 - bit[0], held_out, landed_out), index, steps)


def fold(bit, held, landed, low, after):
    blocks, rows, columns = held.shape
    steps = blocks // 2
    coded = coded_rows(rows)

    def block(i, b, out):
        side = 1 - b[0] if out else b[0]
        return i // low * (2 * low) + side * low + i % low

    return pl.pallas_call(
        functools.partial(fold_kernel, steps, low),
        grid_spec=pltpu.PrefetchScalarGridSpec(
            num_scalar_prefetch=1,
            grid=(steps,),
            in_specs=[
                pl.BlockSpec((1, rows, columns), lambda i, b: (block(i, b, False), 0, 0)),
                pl.BlockSpec((1, rows, columns), lambda i, b: (block(i, b, True), 0, 0)),
                pl.BlockSpec((coded, columns), lambda i, b: (block(i, b, False), 0)),
                pl.BlockSpec((coded, columns), lambda i, b: (block(i, b, True), 0)),
                pl.BlockSpec((TILE, columns), lambda i, b: (blocks * coded // TILE, 0)),
            ]
            + [pl.BlockSpec(memory_space=pl.ANY)] * len(after),
            out_specs=[
                pl.BlockSpec((1, rows, columns), lambda i, b: (i, 0, 0)),
                pl.BlockSpec((steps * coded + TILE, columns), lambda i, b: (0, 0)),
            ],
            scratch_shapes=[pltpu.VMEM((TILE, columns), jnp.float32)],
        ),
        out_shape=[
            jax.ShapeDtypeStruct((steps, rows, columns), jnp.float32),
            jax.ShapeDtypeStruct((steps * coded + TILE, columns), jnp.int16),
        ],
        compiler_params=pltpu.CompilerParams(vmem_limit_bytes=VMEM_LIMIT),
        cost_estimate=SHORT,
        name="fold",
    )(bit, held, held, landed, landed, landed, *after)


def finish_kernel(heads, after_count, core, held, landed, cosine, sine, *refs):
    queries, *pair = refs[after_count:]
    coded = coded_rows(held.shape[1])
    power = landed[pl.ds(coded, TILE), :].astype(jnp.int32).astype(jnp.float32)[0:1]
    total = held[0] + decode(landed[pl.ds(0, coded), :], power)
    joined = total.astype(jnp.bfloat16)
    for head in range(joined.shape[1] // HD):
        raw = joined[:, head * HD : (head + 1) * HD].astype(jnp.float32)
        turned = raw * cosine[...] + pltpu.roll(raw, HD // 2, 1) * sine[...]
        if head < heads:
            queries[:, head * HD : (head + 1) * HD] = turned.astype(jnp.bfloat16)
        else:
            pair[0][...] = jnp.where(core[0] == 0, turned, raw).astype(jnp.bfloat16)


def finish(core, held, landed, cosine, sine, heads, after):
    _, rows, columns = held.shape
    whole = pl.BlockSpec(memory_space=pltpu.VMEM)
    shapes = [jax.ShapeDtypeStruct((rows, heads * HD), jnp.bfloat16)]
    if columns > heads * HD:
        shapes.append(jax.ShapeDtypeStruct((rows, HD), jnp.bfloat16))
    return pl.pallas_call(
        functools.partial(finish_kernel, heads, len(after)),
        in_specs=[pl.BlockSpec(memory_space=pltpu.SMEM)]
        + [whole] * 4
        + [pl.BlockSpec(memory_space=pl.ANY)] * len(after),
        out_specs=[whole] * len(shapes),
        out_shape=shapes,
        compiler_params=pltpu.CompilerParams(vmem_limit_bytes=VMEM_LIMIT),
        cost_estimate=LONG,
        name="finish",
    )(core, held, landed, cosine, sine, *after)


def mix_kernel(count, places, *refs):
    pieces = refs[:count]
    weights, start, mixed, total, wide, arrived = refs[count:]
    depth = wide.shape[1]
    columns = wide.shape[2] // 2
    flat = []
    for piece in pieces:
        flat += [piece] if len(piece.shape) == 2 else [piece.at[i] for i in range(piece.shape[0])]
    copies = [
        pltpu.make_async_copy(
            weights.at[pl.ds(pl.multiple_of(places[i] * depth, depth), depth), :],
            wide.at[i],
            arrived.at[i],
        )
        for i in range(len(flat))
    ]
    for copy in copies:
        copy.start()
    cuts = [0, 1, 2, 4, len(flat)]
    cuts = sorted(set(min(cut, len(flat)) for cut in cuts))
    for first, last in zip(cuts, cuts[1:]):
        for copy in copies[first:last]:
            copy.wait()
        for side in range(2):
            span = pl.ds(side * columns, columns)
            source = start if first == 0 else total
            value = source[:, span].astype(jnp.float32)
            for i in range(first, last):
                value = value + jnp.dot(
                    flat[i][...], wide[i, :, span], preferred_element_type=jnp.float32
                )
            target = mixed if last == len(flat) else total
            target[:, span] = value.astype(target.dtype)


def mix(places, pieces, out_weight, start, dtype):
    columns = out_weight.shape[1]
    rows, width = pieces[0].shape[-2:]
    count = sum(1 if len(p.shape) == 2 else p.shape[0] for p in pieces)
    whole = pl.BlockSpec(memory_space=pltpu.VMEM)
    return pl.pallas_call(
        functools.partial(mix_kernel, len(pieces)),
        in_specs=[pl.BlockSpec(memory_space=pltpu.SMEM)]
        + [whole] * len(pieces)
        + [pl.BlockSpec(memory_space=pl.ANY), whole],
        out_specs=whole,
        scratch_shapes=[
            pltpu.VMEM((rows, columns), jnp.float32),
            pltpu.VMEM((count, width, columns), jnp.bfloat16),
            pltpu.SemaphoreType.DMA((count,)),
        ],
        out_shape=jax.ShapeDtypeStruct((rows, columns), dtype),
        compiler_params=pltpu.CompilerParams(vmem_limit_bytes=VMEM_LIMIT),
        cost_estimate=SHORT,
        name="mix",
    )(places, *pieces, out_weight, start)


def pack_kernel(groups, count, *refs):
    flat = []
    for ref in refs[:count]:
        flat += [ref] if len(ref.shape) == 2 else [ref.at[i] for i in range(ref.shape[0])]
    for group, target in zip(groups, refs[-len(groups) :]):
        for place, index in enumerate(group):
            target[place] = flat[index][...]


def pack(pieces, groups, after):
    whole = pl.BlockSpec(memory_space=pltpu.VMEM)
    shape = pieces[0].shape[-2:]
    return pl.pallas_call(
        functools.partial(pack_kernel, groups, len(pieces)),
        in_specs=[whole] * len(pieces) + [pl.BlockSpec(memory_space=pl.ANY)] * len(after),
        out_specs=[whole] * len(groups),
        out_shape=[jax.ShapeDtypeStruct((len(g),) + shape, pieces[0].dtype) for g in groups],
        compiler_params=pltpu.CompilerParams(vmem_limit_bytes=VMEM_LIMIT),
        cost_estimate=SHORT,
        name="pack",
    )(*pieces, *after)


def gather_and_mix(attention, out_weight, start, device):
    def add(mixed, pieces, offsets, dtype=jnp.float32):
        places = jnp.stack([device ^ offset for offset in offsets])
        return mix(places, pieces, out_weight, mixed, dtype)

    near = swap(attention, 4)
    across = swap(attention, 2)
    far = swap(attention, 8)
    partner = swap(attention, 1)
    first, onward = pack([near, across, far], [(0, 1, 2), (0, 2)], [partner])
    (attention,) = together([attention], [onward])

    across_onward = swap(onward, 2)
    farthest = swap(attention, 12)
    first_partner = swap(first, 1)
    mixed = add(start, [attention, partner], (0, 1))
    mixed = add(mixed, [first, first_partner], (4, 2, 8, 5, 3, 9))
    (second,) = pack([across_onward, farthest], [(0, 1, 2)], [mixed])

    last = swap(farthest, 2)
    second_partner = swap(second, 1)
    mixed = add(mixed, [second, second_partner], (6, 10, 12, 7, 11, 13))
    (last,) = together([last], [mixed])

    last_partner = swap(last, 1)
    return add(mixed, [last, last_partner], (14, 15), jnp.bfloat16)


def attend_kernel(
    slot_request,
    queries,
    new_keys,
    new_values,
    own,
    other,
    key_scale,
    value_scale,
    cache_bias,
    new_bias,
    attention,
    slot_best,
    slot_total,
    slot_sum,
    best,
    total,
    summed,
):
    slots = slot_best.shape[0]
    requests, count, _ = queries.shape
    transposed = (((1,), (1,)), ((), ()))
    for request in range(requests):
        scores = (
            lax.dot_general(
                queries[request],
                new_keys[request],
                transposed,
                preferred_element_type=jnp.float32,
            )
            * HD ** (-0.5)
            + new_bias[...]
        )
        top = jnp.max(scores, -1, keepdims=True)
        expo = jnp.exp(scores - top)
        best[request] = jnp.broadcast_to(top, (count, HD))
        total[request] = jnp.broadcast_to(jnp.sum(expo, -1, keepdims=True), (count, HD))
        summed[request] = jnp.dot(
            expo.astype(jnp.bfloat16), new_values[request], preferred_element_type=jnp.float32
        )
    for slot in range(slots):
        request = slot_request[slot]
        query = queries[request]
        raw = [
            part[:, slot * BLK : (slot + 1) * BLK, :].reshape(KVH * BLK, 2 * HD)
            for part in (own, other)
        ]
        scores = jnp.concatenate(
            [
                lax.dot_general(
                    query, kv[:, :HD], transposed, preferred_element_type=jnp.float32
                )
                for kv in raw
            ],
            1,
        )
        scores = scores * key_scale[slot : slot + 1, :] + cache_bias[slot : slot + 1, :]
        top = jnp.max(scores, -1, keepdims=True)
        expo = jnp.exp(scores - top)
        weights = (expo * value_scale[slot : slot + 1, :]).astype(jnp.bfloat16)
        slot_best[slot] = jnp.broadcast_to(top, (count, HD))
        slot_total[slot] = jnp.broadcast_to(jnp.sum(expo, -1, keepdims=True), (count, HD))
        values = jnp.concatenate([kv[:, HD:] for kv in raw], 0)
        slot_sum[slot] = jnp.dot(weights, values, preferred_element_type=jnp.float32)
    for slot in range(slots):
        request = slot_request[slot]
        before = best[request]
        here = slot_best[slot]
        top = jnp.maximum(before, here)
        keep = jnp.exp(before - top)
        add = jnp.exp(here - top)
        best[request] = top
        total[request] = total[request] * keep + slot_total[slot] * add
        summed[request] = summed[request] * keep + slot_sum[slot] * add
    for request in range(requests):
        attention[request] = (summed[request] / total[request]).astype(jnp.bfloat16)


def attend(slot_request, *arrays):
    queries = arrays[0]
    slots = arrays[5].shape[0]
    requests, count, _ = queries.shape
    whole = pl.BlockSpec(memory_space=pltpu.VMEM)
    return pl.pallas_call(
        attend_kernel,
        in_specs=[pl.BlockSpec(memory_space=pltpu.SMEM)] + [whole] * len(arrays),
        out_specs=whole,
        out_shape=jax.ShapeDtypeStruct((requests, count, HD), jnp.bfloat16),
        scratch_shapes=[pltpu.VMEM((slots, count, HD), jnp.float32)] * 3
        + [pltpu.VMEM((requests, count, HD), jnp.float32)] * 3,
        compiler_params=pltpu.CompilerParams(vmem_limit_bytes=VMEM_LIMIT),
        cost_estimate=SHORT,
        name="attend",
    )(slot_request, *arrays)


def slot_layout(request_length, block_table, slots, stripe):
    requests, most = block_table.shape
    stripes = (request_length + stripe - 1) // stripe
    columns = jnp.arange(most, dtype=jnp.int32)
    held = columns[None, :] < stripes[:, None]
    hit = held[:, :, None] & (
        block_table[:, :, None] == jnp.arange(slots, dtype=jnp.int32)[None, None, :]
    )
    hit = hit.astype(jnp.int32)
    order = jnp.arange(requests, dtype=jnp.int32)
    request = jnp.sum(hit * order[:, None, None], (0, 1))
    rank = jnp.sum(hit * columns[None, :, None], (0, 1))
    length = jnp.sum(hit * request_length[:, None, None], (0, 1))
    return request, rank, length


def arrange_kernel(chip, pool, scales, after, *sent):
    slots = pool.shape[0]
    for k, target in enumerate(sent):
        head = chip[0] ^ k
        target[: slots * BLK, :] = pool[:, head].reshape(slots * BLK, 2 * HD)
        target[slots * BLK :, :] = scales[head]


def arrange(chip, cache_pool, scales, after):
    rows = cache_pool.shape[0] * BLK + TILE
    whole = pl.BlockSpec(memory_space=pltpu.VMEM)
    return pl.pallas_call(
        arrange_kernel,
        in_specs=[
            pl.BlockSpec(memory_space=pltpu.SMEM),
            whole,
            whole,
            pl.BlockSpec(memory_space=pl.ANY),
        ],
        out_specs=[whole] * KVH,
        out_shape=[jax.ShapeDtypeStruct((rows, 2 * HD), jnp.bfloat16)] * KVH,
        compiler_params=pltpu.CompilerParams(vmem_limit_bytes=VMEM_LIMIT),
        cost_estimate=SHORT,
        name="arrange",
    )(chip, cache_pool, scales, after)


def local_pairs(
    hidden_in,
    norm_gain,
    qkv_weight,
    out_weight,
    cache_pool,
    cache_scale,
    request_length,
    block_table,
):
    devices = lax.axis_size("tensor")
    device = lax.axis_index("tensor")
    core = device % 2
    chip = device // 2
    stripe = devices * BLK
    slots = cache_pool.shape[0]
    requests = request_length.shape[0]
    rows = STEPS * requests * QR
    width = hidden_in.shape[2]
    heads = GQ // 2

    hidden = hidden_in.astype(jnp.float32)
    sums = jnp.sum(hidden * hidden, -1)
    bits = [jnp.reshape((device >> b) & 1, (1,)).astype(jnp.int32) for b in range(4)]
    scale_rows = jnp.pad(
        jnp.transpose(cache_scale, (1, 2, 0)).reshape(KVH, 1, 2 * slots),
        ((0, 0), (0, TILE - 1), (0, 2 * HD - 2 * slots)),
    )
    sums = sums + swap(sums, 2)
    chip_scalar = jnp.reshape(chip, (1,)).astype(jnp.int32)
    cache_pieces = list(arrange(chip_scalar, cache_pool, scale_rows, sums))

    def handed(k):
        cache_pieces[k] = swap(cache_pieces[k], 2 * k)

    for bit in (1, 4, 8):
        sums = sums + swap(sums, bit)
    normed = (
        hidden * lax.rsqrt(sums[..., None] / D + EPSILON) * norm_gain.astype(jnp.float32)
    ).astype(jnp.bfloat16)
    normed = normed.reshape(rows, width)

    step_ids = jnp.arange(STEPS, dtype=jnp.int32)
    row_ids = jnp.arange(QR, dtype=jnp.int32)
    position = (
        request_length[None, :, None] + QR * step_ids[:, None, None] + row_ids[None, None, :]
    )
    freqs = ROPE_BASE ** (-(jnp.arange(HD // 2, dtype=jnp.float32) * 2.0 / HD))
    angles = position.reshape(rows, 1).astype(jnp.float32) * freqs
    cosine = jnp.concatenate([jnp.cos(angles)] * 2, 1)
    sine = jnp.concatenate([-jnp.sin(angles), jnp.sin(angles)], 1)

    def folded(part, b, landed, low, *after):
        return fold(bits[b], part, landed, low, after)

    def finished(part, number, landed, *after):
        return finish(bits[0], part, landed, cosine, sine, PART_HEADS[number], after)

    for k in (1, 3, 4, 5, 6):
        handed(k)
    held_a, sent_a = project(bits[0], normed, qkv_weight, 0, cache_pieces[:1])
    core_a = swap(sent_a, 1)
    held_b, sent_b = project(
        bits[0], normed, qkv_weight, 1, [held_a, cache_pieces[1], cache_pieces[3]]
    )
    sent_b, cache_pieces[2], cache_pieces[7] = together(
        [sent_b, cache_pieces[2], cache_pieces[7]], cache_pieces[4:7]
    )
    core_b = swap(sent_b, 1)
    for k in (2, 7):
        handed(k)
    held_a, sent_a = folded(held_a, 1, core_a, 1, sent_b)
    line_a = swap(sent_a, 2)
    held_b, sent_b = folded(held_b, 2, core_b, 2, held_a, cache_pieces[2], cache_pieces[7])
    line_b = swap(sent_b, 4)
    held_a, sent_a = folded(held_a, 2, line_a, 1, held_b)
    line_a = swap(sent_a, 4)
    held_b, sent_b = folded(held_b, 1, line_b, 1, held_a)
    line_b = swap(sent_b, 2)
    (cache_own,) = pack(cache_pieces, [tuple(range(KVH))], [held_b])
    cache_other = swap(cache_own, 1)
    held_a, sent_a = folded(held_a, 3, line_a, 1, cache_own)
    line_a = swap(sent_a, 8)
    held_b, sent_b = folded(held_b, 3, line_b, 1, held_a)
    line_b = swap(sent_b, 8)
    query_a, pair = finished(held_a, 0, line_a, held_b)
    (pair,) = together([pair], [line_b])
    pair_other = swap(pair, 1)
    (query_b,) = finished(held_b, 1, line_b, query_a)
    query_chunks = [query_a, query_b]
    cache_parts = (cache_own, cache_other)
    keys = jnp.where(core == 0, pair, pair_other)
    raw_values = jnp.where(core == 0, pair_other, pair)
    queries = jnp.concatenate(query_chunks, 1).reshape(STEPS, requests, QR, heads, HD)
    queries = jnp.transpose(queries, (1, 0, 2, 3, 4)).reshape(requests, STEPS * QR * heads, HD)

    def by_request(value):
        value = jnp.transpose(value.reshape(STEPS, requests, QR, HD), (1, 0, 2, 3))
        value = value.reshape(requests, STEPS * QR, HD)
        return jnp.pad(value, ((0, 0), (0, TILE - STEPS * QR), (0, 0)))

    slot_request, slot_rank, slot_length = slot_layout(request_length, block_table, slots, stripe)
    source = chip ^ jnp.arange(KVH, dtype=jnp.int32)
    sources = jnp.stack([source * 2 + core, source * 2 + 1 - core])
    offset = sources[:, :, None] * BLK + jnp.arange(BLK, dtype=jnp.int32)[None, None, :]
    token = slot_rank[:, None] * stripe + offset.reshape(1, stripe)
    cache_bias = jnp.where(token < slot_length[:, None], 0.0, NEG_FILL).astype(jnp.float32)
    scales = jnp.concatenate([part[:, slots * BLK, : 2 * slots] for part in cache_parts])
    scales = scales.astype(jnp.float32).reshape(2 * KVH, 2, slots)
    scales = jnp.repeat(jnp.transpose(scales, (1, 2, 0)), BLK, axis=2)
    order = jnp.arange(STEPS * QR * heads, dtype=jnp.int32) // heads
    key_order = jnp.arange(TILE, dtype=jnp.int32)
    new_bias = jnp.where(key_order[None, :] <= order[:, None], 0.0, NEG_FILL).astype(jnp.float32)
    attention = attend(
        slot_request,
        queries,
        by_request(keys),
        by_request(raw_values),
        *cache_parts,
        scales[0] * HD ** (-0.5),
        scales[1],
        cache_bias,
        new_bias,
    )
    attention = jnp.transpose(
        attention.reshape(requests, STEPS, QR, heads, HD), (1, 0, 2, 3, 4)
    ).reshape(rows, heads * HD)
    mixed = gather_and_mix(attention, out_weight, hidden_in.reshape(rows, width), device)
    return mixed.reshape(hidden_in.shape)


def solution(mesh):
    return jax.shard_map(
        local_pairs if mesh.shape["tensor"] == 2 * KVH else local_general,
        mesh=mesh,
        in_specs=(
            P(None, "groups", "tensor"),
            P("tensor"),
            P("tensor", None),
            P(None, "tensor"),
            P(("groups", "tensor"), None, None, None),
            P(("groups", "tensor"), None, None),
            P("groups"),
            P("groups", None),
        ),
        out_specs=P(None, "groups", "tensor"),
        check_vma=False,
    )
```

```python
import functools

import jax
import jax.numpy as jnp
from jax import lax
from jax.experimental import pallas as pl
from jax.experimental.pallas import tpu as pltpu
from jax.sharding import PartitionSpec as P

D = 16384
QH = 128
KVH = 8
HD = 128
QR = 6
STEPS = 2
BLK = 16
GQ = 16
GW = 2304


EPSILON = 1e-05
ROPE_BASE = 500000.0
NEG_FILL = -1e30


def rotate(values, positions):
    half = values.shape[-1] // 2
    freqs = ROPE_BASE ** (-(jnp.arange(half, dtype=jnp.float32) * 2.0 / values.shape[-1]))
    angles = positions.astype(jnp.float32)[..., None] * freqs
    cosine = jnp.cos(angles)
    sine = jnp.sin(angles)
    first = values[..., :half]
    second = values[..., half:]
    return jnp.concatenate([first * cosine - second * sine, second * cosine + first * sine], -1)


def request_layout(request_owner, request_length, block_table, owners, stripe):
    requests = request_owner.shape[0]
    most = block_table.shape[1]
    order = jnp.arange(requests, dtype=jnp.int32)
    stripes = (request_length + stripe - 1) // stripe
    before = (
        (request_owner[None, :] == request_owner[:, None]) & (order[None, :] < order[:, None])
    ).astype(jnp.int32)
    rank = jnp.sum(before, 1)
    offset = jnp.sum(before * stripes[None, :], 1)
    owner_ids = jnp.arange(owners, dtype=jnp.int32)
    mine = request_owner[None, :] == owner_ids[:, None]
    member = mine[:, :, None] & (
        rank[None, :, None] == jnp.arange(requests // owners, dtype=jnp.int32)[None, None, :]
    )
    owner_requests = jnp.sum(member.astype(jnp.int32) * order[None, :, None], 1)
    columns = jnp.arange(most, dtype=jnp.int32)
    within = columns[None, None, :] - offset[None, :, None]
    hit = (mine[:, :, None] & (within >= 0) & (within < stripes[None, :, None])).astype(jnp.int32)
    stripe_request = jnp.sum(hit * order[None, :, None], 1) - (1 - jnp.sum(hit, 1))
    stripe_rank = jnp.sum(hit * within, 1)
    pick = (within[..., None] == columns[None, None, None, :]).astype(jnp.int32)
    slots = jnp.sum(hit[..., None] * pick * block_table[None, :, None, :], (1, 3))
    return (owner_requests, stripe_request, stripe_rank, slots, rank, stripes)


def cache_partial(queries, keys, values, key_scale, value_scale, mask):
    scores = jnp.einsum("srgd,td->srgt", queries, keys, preferred_element_type=jnp.float32)
    scores = jnp.where(mask, scores * key_scale * HD ** (-0.5), NEG_FILL)
    best = jnp.max(scores, -1)
    expo = jnp.where(mask, jnp.exp(scores - best[..., None]), 0.0)
    total = jnp.sum(expo, -1)
    weights = (expo * value_scale).astype(jnp.bfloat16)
    summed = jnp.einsum("srgt,td->srgd", weights, values, preferred_element_type=jnp.float32)
    return (best, total, summed)


def local_general(
    hidden_in,
    norm_gain,
    qkv_weight,
    out_weight,
    cache_pool,
    cache_scale,
    request_length,
    block_table,
):
    devices = lax.axis_size("tensor")
    device = lax.axis_index("tensor")
    owners = devices // KVH
    stripe = devices * BLK
    requests = request_length.shape[0]
    request_owner = jnp.arange(requests, dtype=jnp.int32) % owners
    unit_rows = requests // owners * QR
    most = block_table.shape[1]
    local_width = hidden_in.shape[2]
    my_owner = device // KVH
    owner_requests, stripe_request, stripe_rank, slots, rank, stripes = request_layout(
        request_owner, request_length, block_table, owners, stripe
    )
    step_rows = jnp.arange(QR, dtype=jnp.int32)
    row_order = (owner_requests[:, :, None] * QR + step_rows[None, None, :]).reshape(
        owners * unit_rows
    )
    inverse = ((request_owner * unit_rows + rank * QR)[:, None] + step_rows[None, :]).reshape(
        requests * QR
    )
    row_request = jnp.repeat(owner_requests[my_owner], QR)
    row_length = request_length[row_request]
    row_step = jnp.arange(unit_rows, dtype=jnp.int32) % QR
    same_request = row_request[:, None] == row_request[None, :]
    gain = norm_gain.astype(jnp.float32)
    weight_grouped = qkv_weight.reshape(local_width, KVH, GW)
    sent = cache_pool[jnp.transpose(slots)].reshape(most, devices, BLK, 2 * HD)
    sent_scale = cache_scale[jnp.transpose(slots)].reshape(most, devices, 2)
    landed, landed_scale = (
        lax.all_to_all(sent, "tensor", split_axis=1, concat_axis=1, tiled=True),
        lax.all_to_all(sent_scale, "tensor", split_axis=1, concat_axis=1, tiled=True),
    )
    cache_data = landed.reshape(most * stripe, 2 * HD)
    token_scale = jnp.broadcast_to(
        landed_scale.astype(jnp.float32)[:, :, None, :], (most, devices, BLK, 2)
    ).reshape(most * stripe, 2)
    token = jnp.arange(most * stripe, dtype=jnp.int32)
    token_stripe = token // stripe
    token_request = stripe_request[my_owner][token_stripe]
    token_position = stripe_rank[my_owner][token_stripe] * stripe + token % stripe
    token_length = jnp.where(token_request >= 0, request_length[jnp.maximum(token_request, 0)], 0)
    cache_mask = (
        (token_request[None, :] == row_request[:, None]) & (token_position < token_length)[None, :]
    )[None, :, None, :]
    outputs = []
    keys_seen = []
    values_seen = []
    for step in range(STEPS):
        block = hidden_in[step : step + 1]
        project_count = block.shape[0]
        values = block.astype(jnp.float32)
        sums = lax.psum(jnp.sum(values * values, -1), "tensor")
        normed = (values * lax.rsqrt(sums[..., None] / D + EPSILON) * gain).astype(jnp.bfloat16)
        ordered = jnp.take(normed, row_order, axis=1).reshape(
            project_count, owners, unit_rows, local_width
        )
        term = jnp.einsum(
            "sojd,dhg->ohsjg", ordered, weight_grouped, preferred_element_type=jnp.float32
        )
        term = term.reshape(owners * KVH * project_count * unit_rows, GW)
        mine = lax.psum_scatter(term, "tensor", scatter_dimension=0, tiled=True)
        joined_block = mine.astype(jnp.bfloat16).reshape(project_count, unit_rows, GW)
        prepare_count = joined_block.shape[0]
        steps_here = step + jnp.arange(prepare_count, dtype=jnp.int32)
        position = row_length[None, :] + QR * steps_here[:, None] + row_step[None, :]
        prepare_queries = rotate(
            joined_block[..., : GQ * HD]
            .reshape(prepare_count, unit_rows, GQ, HD)
            .astype(jnp.float32),
            position[:, :, None],
        ).astype(jnp.bfloat16)
        keys = rotate(
            joined_block[..., GQ * HD : GQ * HD + HD].astype(jnp.float32), position
        ).astype(jnp.bfloat16)
        queries, keys, values = (prepare_queries, keys, joined_block[..., GQ * HD + HD :])
        keys_seen.append(keys)
        values_seen.append(values)
        keys_all = jnp.concatenate(keys_seen, 0)
        attend_count = queries.shape[0]
        cache_best, cache_total, cache_summed = cache_partial(
            queries,
            cache_data[:, :HD],
            cache_data[:, HD:],
            token_scale[:, 0],
            token_scale[:, 1],
            cache_mask,
        )
        news = jnp.einsum(
            "srgd,pjd->srgpj", queries, keys_all, preferred_element_type=jnp.float32
        ) * HD ** (-0.5)
        query_step = step + jnp.arange(attend_count, dtype=jnp.int32)[:, None, None, None]
        key_step = jnp.arange(keys_all.shape[0], dtype=jnp.int32)[None, None, :, None]
        allowed = (key_step < query_step) | (key_step == query_step) & (
            row_step[None, None, None, :] <= row_step[None, :, None, None]
        )
        allowed = (allowed & same_request[None, :, None, :])[:, :, None, :, :]
        news = jnp.where(allowed, news, NEG_FILL)
        best = jnp.maximum(cache_best, jnp.max(news, (3, 4)))
        factor = jnp.exp(cache_best - best)
        expo = jnp.where(allowed, jnp.exp(news - best[..., None, None]), 0.0)
        total = cache_total * factor + jnp.sum(expo, (3, 4))
        summed = cache_summed * factor[..., None] + jnp.einsum(
            "srgpj,pjd->srgd",
            expo.astype(jnp.bfloat16),
            jnp.concatenate(values_seen, 0),
            preferred_element_type=jnp.float32,
        )
        attention = (
            (summed / total[..., None])
            .astype(jnp.bfloat16)
            .reshape(attend_count, unit_rows, GQ * HD)
        )
        count = attention.shape[0]
        gathered = lax.all_gather(attention, "tensor", axis=2, tiled=True).reshape(
            count, unit_rows, owners, QH * HD
        )
        mixed = jnp.einsum(
            "sjof,fd->sojd", gathered, out_weight, preferred_element_type=jnp.float32
        )
        mixed = jnp.take(mixed.reshape(count, owners * unit_rows, local_width), inverse, axis=1)
        outputs.append(
            (hidden_in[step : step + count].astype(jnp.float32) + mixed).astype(jnp.bfloat16)
        )
    return jnp.concatenate(outputs, 0)


VMEM_LIMIT = 48 * 1024 * 1024
SHORT = pl.CostEstimate(flops=1, bytes_accessed=1, transcendentals=0)
LONG = pl.CostEstimate(flops=2 * 10**10, bytes_accessed=1, transcendentals=0)
LOW_BITS = 4
PACKED = 16 // LOW_BITS
LEVELS = 32600.0 * 2**LOW_BITS
POWER_STEPS = 8.0
TILE = 16
MESH_BITS = (1, 2, 4, 8)


def swap(value, bit):
    devices = lax.axis_size("tensor")
    return lax.ppermute(value, "tensor", [(i, i ^ bit) for i in range(devices)])


def no_work(*refs):
    del refs


def together(arrays, after):
    anywhere = pl.BlockSpec(memory_space=pl.ANY)
    return pl.pallas_call(
        no_work,
        in_specs=[anywhere] * (len(arrays) + len(after)),
        out_specs=[anywhere] * len(arrays),
        out_shape=[jax.ShapeDtypeStruct(a.shape, a.dtype) for a in arrays],
        input_output_aliases={i: i for i in range(len(arrays))},
        compiler_params=pltpu.CompilerParams(vmem_limit_bytes=VMEM_LIMIT),
        cost_estimate=SHORT,
        name="together",
    )(*arrays, *after)


def coded_rows(rows):
    return rows + rows // PACKED


def encode(block):
    top = jnp.max(jnp.abs(block), 0, keepdims=True)
    power = jnp.ceil(jnp.log2(jnp.maximum(top, 1e-30)) * POWER_STEPS)
    codes = jnp.round(block * (jnp.exp2(power * (-1.0 / POWER_STEPS)) * LEVELS)).astype(jnp.int32)
    low = codes & (2**LOW_BITS - 1)
    part = block.shape[0] // PACKED
    packed = low[:part]
    for i in range(1, PACKED):
        packed = packed + (low[i * part : (i + 1) * part] << (LOW_BITS * i))
    high = (codes >> LOW_BITS).astype(jnp.int16)
    return jnp.concatenate([high, (packed - 32768).astype(jnp.int16)], 0), power


def decode(codes, power):
    rows = codes.shape[0] * PACKED // (PACKED + 1)
    high = codes[:rows].astype(jnp.int32) << LOW_BITS
    packed = codes[rows:].astype(jnp.int32) + 32768
    low = jnp.concatenate(
        [(packed >> (LOW_BITS * i)) & (2**LOW_BITS - 1) for i in range(PACKED)], 0
    )
    scale = jnp.exp2(power * (1.0 / POWER_STEPS)) * (1.0 / LEVELS)
    return (high + low).astype(jnp.float32) * scale


def pick_row(rows, index):
    ids = lax.broadcasted_iota(jnp.int32, rows.shape, 0)
    return jnp.sum(jnp.where(ids == index, rows, 0.0), 0, keepdims=True)


def store_codes(sent, powers, block, index, steps):
    rows = coded_rows(block.shape[0])
    codes, power = encode(block)
    sent[pl.ds(pl.multiple_of(index * rows, TILE), rows), :] = codes

    powers[pl.ds(index, 1), :] = power

    @pl.when(index == steps - 1)
    def _():
        sent[pl.ds(steps * rows, TILE), :] = powers[...].astype(jnp.int32).astype(jnp.int16)


PART_HEADS = (3, 5)


def project_kernel(part, core, normed, weights, *refs):
    kept, sent, powers, slabs, arrived = refs[-5:]
    index = pl.program_id(0)
    half = kept.shape[2]
    heads = PART_HEADS[part] * HD
    first = sum(PART_HEADS[:part]) * HD

    def copies(group):
        found = []
        for side in range(2):
            owner = core[0] if side == 0 else 1 - core[0]
            spans = [(group * GW + owner * (GQ // 2 * HD) + first, 0, heads)]
            if half > heads:
                spans.append((group * GW + (GQ + owner) * HD, heads, HD))
            for number, (start, offset, size) in enumerate(spans):
                found.append(
                    pltpu.make_async_copy(
                        weights.at[:, pl.ds(pl.multiple_of(start, HD), size)],
                        slabs.at[group, :, pl.ds(side * half + offset, size)],
                        arrived.at[group, side, number],
                    )
                )
        return found

    @pl.when(index == 0)
    def _():
        for group in range(KVH):
            for copy in copies(group):
                copy.start()
        powers[...] = jnp.zeros_like(powers)

    for copy in copies(index):
        copy.wait()

    found = []
    rows = coded_rows(normed.shape[0])
    place = pl.ds(pl.multiple_of(index * rows, TILE), rows)
    for start in range(0, 2 * half, 2 * HD):
        stop = start + 2 * HD
        product = jnp.dot(
            normed[...], slabs[index, :, start:stop], preferred_element_type=jnp.float32
        )
        if start < half:
            kept[0, :, start : min(stop, half)] = product[:, : half - start]
        if stop > half:
            first = max(start, half)
            codes, power = encode(product[:, first - start :])
            sent[place, first - half : stop - half] = codes
            found.append(power)
    powers[pl.ds(index, 1), :] = jnp.concatenate(found, 1)

    @pl.when(index == KVH - 1)
    def _():
        sent[pl.ds(KVH * rows, TILE), :] = powers[...].astype(jnp.int32).astype(jnp.int16)


def project(core, normed, qkv_weight, part, after):
    rows, width = normed.shape
    columns = PART_HEADS[part] * HD + (HD if part == 0 else 0)
    sent_rows = KVH * coded_rows(rows) + TILE
    return pl.pallas_call(
        functools.partial(project_kernel, part),
        grid_spec=pltpu.PrefetchScalarGridSpec(
            num_scalar_prefetch=1,
            grid=(KVH,),
            in_specs=[pl.BlockSpec((rows, width), lambda t, c: (0, 0))]
            + [pl.BlockSpec(memory_space=pl.ANY)] * (1 + len(after)),
            out_specs=[
                pl.BlockSpec((1, rows, columns), lambda t, c: (t, 0, 0)),
                pl.BlockSpec((sent_rows, columns), lambda t, c: (0, 0)),
            ],
            scratch_shapes=[
                pltpu.VMEM((TILE, columns), jnp.float32),
                pltpu.VMEM((KVH, width, 2 * columns), jnp.bfloat16),
                pltpu.SemaphoreType.DMA((KVH, 2, 2)),
            ],
        ),
        out_shape=[
            pltpu.HBM((KVH, rows, columns), jnp.float32),
            jax.ShapeDtypeStruct((sent_rows, columns), jnp.int16),
        ],
        compiler_params=pltpu.CompilerParams(vmem_limit_bytes=VMEM_LIMIT),
        cost_estimate=SHORT,
        name="project",
    )(core, normed, qkv_weight, *after)


def fold_kernel(steps, low, bit, held, held_out, landed, landed_out, landed_powers, *refs):
    kept, sent, powers = refs[-3:]
    index = pl.program_id(0)
    rows_of_powers = landed_powers[...].astype(jnp.int32).astype(jnp.float32)
    first = index // low * (2 * low) + index % low

    def total(side, block, codes):
        power = pick_row(rows_of_powers, first + side * low)
        return block[0] + decode(codes[...], power)

    @pl.when(index == 0)
    def _():
        powers[...] = jnp.zeros_like(powers)

    kept[0] = total(bit[0], held, landed)
    store_codes(sent, powers, total(1 - bit[0], held_out, landed_out), index, steps)


def fold(bit, held, landed, low, cost, after):
    blocks, rows, columns = held.shape
    steps = blocks // 2
    coded = coded_rows(rows)

    def block(i, b, out):
        side = 1 - b[0] if out else b[0]
        return i // low * (2 * low) + side * low + i % low

    return pl.pallas_call(
        functools.partial(fold_kernel, steps, low),
        grid_spec=pltpu.PrefetchScalarGridSpec(
            num_scalar_prefetch=1,
            grid=(steps,),
            in_specs=[
                pl.BlockSpec((1, rows, columns), lambda i, b: (block(i, b, False), 0, 0)),
                pl.BlockSpec((1, rows, columns), lambda i, b: (block(i, b, True), 0, 0)),
                pl.BlockSpec((coded, columns), lambda i, b: (block(i, b, False), 0)),
                pl.BlockSpec((coded, columns), lambda i, b: (block(i, b, True), 0)),
                pl.BlockSpec((TILE, columns), lambda i, b: (blocks * coded // TILE, 0)),
            ]
            + [pl.BlockSpec(memory_space=pl.ANY)] * len(after),
            out_specs=[
                pl.BlockSpec((1, rows, columns), lambda i, b: (i, 0, 0)),
                pl.BlockSpec((steps * coded + TILE, columns), lambda i, b: (0, 0)),
            ],
            scratch_shapes=[pltpu.VMEM((TILE, columns), jnp.float32)],
        ),
        out_shape=[
            jax.ShapeDtypeStruct((steps, rows, columns), jnp.float32),
            jax.ShapeDtypeStruct((steps * coded + TILE, columns), jnp.int16),
        ],
        compiler_params=pltpu.CompilerParams(vmem_limit_bytes=VMEM_LIMIT),
        cost_estimate=cost,
        name="fold",
    )(bit, held, held, landed, landed, landed, *after)


def finish_kernel(heads, after_count, core, held, landed, cosine, sine, *refs):
    queries, *pair = refs[after_count:]
    coded = coded_rows(held.shape[1])
    power = landed[pl.ds(coded, TILE), :].astype(jnp.int32).astype(jnp.float32)[0:1]
    total = held[0] + decode(landed[pl.ds(0, coded), :], power)
    joined = total.astype(jnp.bfloat16)
    for head in range(joined.shape[1] // HD):
        raw = joined[:, head * HD : (head + 1) * HD].astype(jnp.float32)
        turned = raw * cosine[...] + pltpu.roll(raw, HD // 2, 1) * sine[...]
        if head < heads:
            queries[:, head * HD : (head + 1) * HD] = turned.astype(jnp.bfloat16)
        else:
            pair[0][...] = jnp.where(core[0] == 0, turned, raw).astype(jnp.bfloat16)


def finish(core, held, landed, cosine, sine, heads, after):
    _, rows, columns = held.shape
    whole = pl.BlockSpec(memory_space=pltpu.VMEM)
    shapes = [jax.ShapeDtypeStruct((rows, heads * HD), jnp.bfloat16)]
    if columns > heads * HD:
        shapes.append(jax.ShapeDtypeStruct((rows, HD), jnp.bfloat16))
    return pl.pallas_call(
        functools.partial(finish_kernel, heads, len(after)),
        in_specs=[pl.BlockSpec(memory_space=pltpu.SMEM)]
        + [whole] * 4
        + [pl.BlockSpec(memory_space=pl.ANY)] * len(after),
        out_specs=[whole] * len(shapes),
        out_shape=shapes,
        compiler_params=pltpu.CompilerParams(vmem_limit_bytes=VMEM_LIMIT),
        cost_estimate=LONG,
        name="finish",
    )(core, held, landed, cosine, sine, *after)


def mix_kernel(count, places, *refs):
    pieces = refs[:count]
    weights, start, mixed, total, wide, arrived = refs[count:]
    depth = wide.shape[1]
    columns = wide.shape[2] // 2
    flat = []
    for piece in pieces:
        flat += [piece] if len(piece.shape) == 2 else [piece.at[i] for i in range(piece.shape[0])]
    copies = [
        pltpu.make_async_copy(
            weights.at[pl.ds(pl.multiple_of(places[i] * depth, depth), depth), :],
            wide.at[i],
            arrived.at[i],
        )
        for i in range(len(flat))
    ]
    for copy in copies:
        copy.start()
    cuts = [0, 1, 2, 4, len(flat)]
    cuts = sorted(set(min(cut, len(flat)) for cut in cuts))
    for first, last in zip(cuts, cuts[1:]):
        for copy in copies[first:last]:
            copy.wait()
        for side in range(2):
            span = pl.ds(side * columns, columns)
            source = start if first == 0 else total
            value = source[:, span].astype(jnp.float32)
            for i in range(first, last):
                value = value + jnp.dot(
                    flat[i][...], wide[i, :, span], preferred_element_type=jnp.float32
                )
            target = mixed if last == len(flat) else total
            target[:, span] = value.astype(target.dtype)


def mix(places, pieces, out_weight, start, dtype):
    columns = out_weight.shape[1]
    rows, width = pieces[0].shape[-2:]
    count = sum(1 if len(p.shape) == 2 else p.shape[0] for p in pieces)
    whole = pl.BlockSpec(memory_space=pltpu.VMEM)
    return pl.pallas_call(
        functools.partial(mix_kernel, len(pieces)),
        in_specs=[pl.BlockSpec(memory_space=pltpu.SMEM)]
        + [whole] * len(pieces)
        + [pl.BlockSpec(memory_space=pl.ANY), whole],
        out_specs=whole,
        scratch_shapes=[
            pltpu.VMEM((rows, columns), jnp.float32),
            pltpu.VMEM((count, width, columns), jnp.bfloat16),
            pltpu.SemaphoreType.DMA((count,)),
        ],
        out_shape=jax.ShapeDtypeStruct((rows, columns), dtype),
        compiler_params=pltpu.CompilerParams(vmem_limit_bytes=VMEM_LIMIT),
        cost_estimate=SHORT,
        name="mix",
    )(places, *pieces, out_weight, start)


def pack_kernel(groups, count, *refs):
    flat = []
    for ref in refs[:count]:
        flat += [ref] if len(ref.shape) == 2 else [ref.at[i] for i in range(ref.shape[0])]
    for group, target in zip(groups, refs[-len(groups) :]):
        for place, index in enumerate(group):
            target[place] = flat[index][...]


def pack(pieces, groups, after):
    whole = pl.BlockSpec(memory_space=pltpu.VMEM)
    shape = pieces[0].shape[-2:]
    return pl.pallas_call(
        functools.partial(pack_kernel, groups, len(pieces)),
        in_specs=[whole] * len(pieces) + [pl.BlockSpec(memory_space=pl.ANY)] * len(after),
        out_specs=[whole] * len(groups),
        out_shape=[jax.ShapeDtypeStruct((len(g),) + shape, pieces[0].dtype) for g in groups],
        compiler_params=pltpu.CompilerParams(vmem_limit_bytes=VMEM_LIMIT),
        cost_estimate=SHORT,
        name="pack",
    )(*pieces, *after)


def gather_and_mix(attention, out_weight, start, device):
    def add(mixed, pieces, offsets, dtype=jnp.float32):
        places = jnp.stack([device ^ offset for offset in offsets])
        return mix(places, pieces, out_weight, mixed, dtype)

    near = swap(attention, 4)
    across = swap(attention, 2)
    far = swap(attention, 8)
    partner = swap(attention, 1)
    first, onward = pack([near, across, far], [(0, 1, 2), (0, 2)], [partner])
    (attention,) = together([attention], [onward])

    across_onward = swap(onward, 2)
    farthest = swap(attention, 12)
    first_partner = swap(first, 1)
    mixed = add(start, [attention, partner], (0, 1))
    mixed = add(mixed, [first, first_partner], (4, 2, 8, 5, 3, 9))
    (second,) = pack([across_onward, farthest], [(0, 1, 2)], [mixed])

    last = swap(farthest, 2)
    second_partner = swap(second, 1)
    mixed = add(mixed, [second, second_partner], (6, 10, 12, 7, 11, 13))
    (last,) = together([last], [mixed])

    last_partner = swap(last, 1)
    return add(mixed, [last, last_partner], (14, 15), jnp.bfloat16)


def attend_kernel(
    slot_request,
    queries,
    new_keys,
    new_values,
    own,
    other,
    key_scale,
    value_scale,
    cache_bias,
    new_bias,
    attention,
    slot_best,
    slot_total,
    slot_sum,
    best,
    total,
    summed,
):
    slots = slot_best.shape[0]
    requests, count, _ = queries.shape
    transposed = (((1,), (1,)), ((), ()))
    for request in range(requests):
        scores = (
            lax.dot_general(
                queries[request],
                new_keys[request],
                transposed,
                preferred_element_type=jnp.float32,
            )
            * HD ** (-0.5)
            + new_bias[...]
        )
        top = jnp.max(scores, -1, keepdims=True)
        expo = jnp.exp(scores - top)
        best[request] = jnp.broadcast_to(top, (count, HD))
        total[request] = jnp.broadcast_to(jnp.sum(expo, -1, keepdims=True), (count, HD))
        summed[request] = jnp.dot(
            expo.astype(jnp.bfloat16), new_values[request], preferred_element_type=jnp.float32
        )
    for slot in range(slots):
        request = slot_request[slot]
        query = queries[request]
        raw = [
            part[:, slot * BLK : (slot + 1) * BLK, :].reshape(KVH * BLK, 2 * HD)
            for part in (own, other)
        ]
        scores = jnp.concatenate(
            [
                lax.dot_general(
                    query, kv[:, :HD], transposed, preferred_element_type=jnp.float32
                )
                for kv in raw
            ],
            1,
        )
        scores = scores * key_scale[slot : slot + 1, :] + cache_bias[slot : slot + 1, :]
        top = jnp.max(scores, -1, keepdims=True)
        expo = jnp.exp(scores - top)
        weights = (expo * value_scale[slot : slot + 1, :]).astype(jnp.bfloat16)
        slot_best[slot] = jnp.broadcast_to(top, (count, HD))
        slot_total[slot] = jnp.broadcast_to(jnp.sum(expo, -1, keepdims=True), (count, HD))
        values = jnp.concatenate([kv[:, HD:] for kv in raw], 0)
        slot_sum[slot] = jnp.dot(weights, values, preferred_element_type=jnp.float32)
    for slot in range(slots):
        request = slot_request[slot]
        before = best[request]
        here = slot_best[slot]
        top = jnp.maximum(before, here)
        keep = jnp.exp(before - top)
        add = jnp.exp(here - top)
        best[request] = top
        total[request] = total[request] * keep + slot_total[slot] * add
        summed[request] = summed[request] * keep + slot_sum[slot] * add
    for request in range(requests):
        attention[request] = (summed[request] / total[request]).astype(jnp.bfloat16)


def attend(slot_request, *arrays):
    queries = arrays[0]
    slots = arrays[5].shape[0]
    requests, count, _ = queries.shape
    whole = pl.BlockSpec(memory_space=pltpu.VMEM)
    return pl.pallas_call(
        attend_kernel,
        in_specs=[pl.BlockSpec(memory_space=pltpu.SMEM)] + [whole] * len(arrays),
        out_specs=whole,
        out_shape=jax.ShapeDtypeStruct((requests, count, HD), jnp.bfloat16),
        scratch_shapes=[pltpu.VMEM((slots, count, HD), jnp.float32)] * 3
        + [pltpu.VMEM((requests, count, HD), jnp.float32)] * 3,
        compiler_params=pltpu.CompilerParams(vmem_limit_bytes=VMEM_LIMIT),
        cost_estimate=SHORT,
        name="attend",
    )(slot_request, *arrays)


def slot_layout(request_length, block_table, slots, stripe):
    requests, most = block_table.shape
    stripes = (request_length + stripe - 1) // stripe
    columns = jnp.arange(most, dtype=jnp.int32)
    held = columns[None, :] < stripes[:, None]
    hit = held[:, :, None] & (
        block_table[:, :, None] == jnp.arange(slots, dtype=jnp.int32)[None, None, :]
    )
    hit = hit.astype(jnp.int32)
    order = jnp.arange(requests, dtype=jnp.int32)
    request = jnp.sum(hit * order[:, None, None], (0, 1))
    rank = jnp.sum(hit * columns[None, :, None], (0, 1))
    length = jnp.sum(hit * request_length[:, None, None], (0, 1))
    return request, rank, length


def arrange_kernel(chip, pool, scales, after, *sent):
    slots = pool.shape[0]
    for k, target in enumerate(sent):
        head = chip[0] ^ k
        target[: slots * BLK, :] = pool[:, head].reshape(slots * BLK, 2 * HD)
        target[slots * BLK :, :] = scales[head]


def arrange(chip, cache_pool, scales, after):
    rows = cache_pool.shape[0] * BLK + TILE
    whole = pl.BlockSpec(memory_space=pltpu.VMEM)
    return pl.pallas_call(
        arrange_kernel,
        in_specs=[
            pl.BlockSpec(memory_space=pltpu.SMEM),
            whole,
            whole,
            pl.BlockSpec(memory_space=pl.ANY),
        ],
        out_specs=[whole] * KVH,
        out_shape=[jax.ShapeDtypeStruct((rows, 2 * HD), jnp.bfloat16)] * KVH,
        compiler_params=pltpu.CompilerParams(vmem_limit_bytes=VMEM_LIMIT),
        cost_estimate=SHORT,
        name="arrange",
    )(chip, cache_pool, scales, after)


def local_pairs(
    hidden_in,
    norm_gain,
    qkv_weight,
    out_weight,
    cache_pool,
    cache_scale,
    request_length,
    block_table,
):
    devices = lax.axis_size("tensor")
    device = lax.axis_index("tensor")
    core = device % 2
    chip = device // 2
    stripe = devices * BLK
    slots = cache_pool.shape[0]
    requests = request_length.shape[0]
    rows = STEPS * requests * QR
    width = hidden_in.shape[2]
    heads = GQ // 2

    hidden = hidden_in.astype(jnp.float32)
    sums = jnp.sum(hidden * hidden, -1)
    bits = [jnp.reshape((device >> b) & 1, (1,)).astype(jnp.int32) for b in range(4)]
    scale_rows = jnp.pad(
        jnp.transpose(cache_scale, (1, 2, 0)).reshape(KVH, 1, 2 * slots),
        ((0, 0), (0, TILE - 1), (0, 2 * HD - 2 * slots)),
    )
    sums = sums + swap(sums, 2)
    chip_scalar = jnp.reshape(chip, (1,)).astype(jnp.int32)
    cache_pieces = list(arrange(chip_scalar, cache_pool, scale_rows, sums))

    def handed(k):
        cache_pieces[k] = swap(cache_pieces[k], 2 * k)

    for bit in (1, 4, 8):
        sums = sums + swap(sums, bit)
    normed = (
        hidden * lax.rsqrt(sums[..., None] / D + EPSILON) * norm_gain.astype(jnp.float32)
    ).astype(jnp.bfloat16)
    normed = normed.reshape(rows, width)

    step_ids = jnp.arange(STEPS, dtype=jnp.int32)
    row_ids = jnp.arange(QR, dtype=jnp.int32)
    position = (
        request_length[None, :, None] + QR * step_ids[:, None, None] + row_ids[None, None, :]
    )
    freqs = ROPE_BASE ** (-(jnp.arange(HD // 2, dtype=jnp.float32) * 2.0 / HD))
    angles = position.reshape(rows, 1).astype(jnp.float32) * freqs
    cosine = jnp.concatenate([jnp.cos(angles)] * 2, 1)
    sine = jnp.concatenate([-jnp.sin(angles), jnp.sin(angles)], 1)

    def folded(part, b, landed, low, *after, cost=SHORT):
        return fold(bits[b], part, landed, low, cost, after)

    def finished(part, number, landed, *after):
        return finish(bits[0], part, landed, cosine, sine, PART_HEADS[number], after)

    for k in (1, 3, 4, 5, 6):
        handed(k)
    held_a, sent_a = project(bits[0], normed, qkv_weight, 0, cache_pieces[:1])
    core_a = swap(sent_a, 1)
    held_b, sent_b = project(
        bits[0], normed, qkv_weight, 1, [held_a, cache_pieces[1], cache_pieces[3]]
    )
    sent_b, cache_pieces[2], cache_pieces[7] = together(
        [sent_b, cache_pieces[2], cache_pieces[7]], cache_pieces[4:7]
    )
    core_b = swap(sent_b, 1)
    for k in (2, 7):
        handed(k)
    held_b, sent_b = folded(held_b, 2, core_b, 2, sent_b)
    line_b = swap(sent_b, 4)
    held_a, sent_a = folded(
        held_a, 1, core_a, 1, held_b, cache_pieces[2], cache_pieces[7], cost=LONG
    )
    line_a = swap(sent_a, 2)
    held_b, sent_b = folded(held_b, 1, line_b, 1, held_a)
    line_b = swap(sent_b, 2)
    held_a, sent_a = folded(held_a, 2, line_a, 1, held_b)
    line_a = swap(sent_a, 4)
    (cache_own,) = pack(cache_pieces, [tuple(range(KVH))], [held_a])
    cache_other = swap(cache_own, 1)
    held_a, sent_a = folded(held_a, 3, line_a, 1, cache_own)
    line_a = swap(sent_a, 8)
    held_b, sent_b = folded(held_b, 3, line_b, 1, held_a)
    line_b = swap(sent_b, 8)
    query_a, pair = finished(held_a, 0, line_a, held_b)
    (pair,) = together([pair], [line_b])
    pair_other = swap(pair, 1)
    (query_b,) = finished(held_b, 1, line_b, query_a)
    query_chunks = [query_a, query_b]
    cache_parts = (cache_own, cache_other)
    keys = jnp.where(core == 0, pair, pair_other)
    raw_values = jnp.where(core == 0, pair_other, pair)
    queries = jnp.concatenate(query_chunks, 1).reshape(STEPS, requests, QR, heads, HD)
    queries = jnp.transpose(queries, (1, 0, 2, 3, 4)).reshape(requests, STEPS * QR * heads, HD)

    def by_request(value):
        value = jnp.transpose(value.reshape(STEPS, requests, QR, HD), (1, 0, 2, 3))
        value = value.reshape(requests, STEPS * QR, HD)
        return jnp.pad(value, ((0, 0), (0, TILE - STEPS * QR), (0, 0)))

    slot_request, slot_rank, slot_length = slot_layout(request_length, block_table, slots, stripe)
    source = chip ^ jnp.arange(KVH, dtype=jnp.int32)
    sources = jnp.stack([source * 2 + core, source * 2 + 1 - core])
    offset = sources[:, :, None] * BLK + jnp.arange(BLK, dtype=jnp.int32)[None, None, :]
    token = slot_rank[:, None] * stripe + offset.reshape(1, stripe)
    cache_bias = jnp.where(token < slot_length[:, None], 0.0, NEG_FILL).astype(jnp.float32)
    scales = jnp.concatenate([part[:, slots * BLK, : 2 * slots] for part in cache_parts])
    scales = scales.astype(jnp.float32).reshape(2 * KVH, 2, slots)
    scales = jnp.repeat(jnp.transpose(scales, (1, 2, 0)), BLK, axis=2)
    order = jnp.arange(STEPS * QR * heads, dtype=jnp.int32) // heads
    key_order = jnp.arange(TILE, dtype=jnp.int32)
    new_bias = jnp.where(key_order[None, :] <= order[:, None], 0.0, NEG_FILL).astype(jnp.float32)
    attention = attend(
        slot_request,
        queries,
        by_request(keys),
        by_request(raw_values),
        *cache_parts,
        scales[0] * HD ** (-0.5),
        scales[1],
        cache_bias,
        new_bias,
    )
    attention = jnp.transpose(
        attention.reshape(requests, STEPS, QR, heads, HD), (1, 0, 2, 3, 4)
    ).reshape(rows, heads * HD)
    mixed = gather_and_mix(attention, out_weight, hidden_in.reshape(rows, width), device)
    return mixed.reshape(hidden_in.shape)


def solution(mesh):
    return jax.shard_map(
        local_pairs if mesh.shape["tensor"] == 2 * KVH else local_general,
        mesh=mesh,
        in_specs=(
            P(None, "groups", "tensor"),
            P("tensor"),
            P("tensor", None),
            P(None, "tensor"),
            P(("groups", "tensor"), None, None, None),
            P(("groups", "tensor"), None, None),
            P("groups"),
            P("groups", None),
        ),
        out_specs=P(None, "groups", "tensor"),
        check_vma=False,
    )
```

```python
import functools

import jax
import jax.numpy as jnp
from jax import lax
from jax.experimental import pallas as pl
from jax.experimental.pallas import tpu as pltpu
from jax.sharding import PartitionSpec as P

D = 16384
QH = 128
KVH = 8
HD = 128
QR = 6
STEPS = 2
BLK = 16
GQ = 16
GW = 2304


EPSILON = 1e-05
ROPE_BASE = 500000.0
NEG_FILL = -1e30


def rotate(values, positions):
    half = values.shape[-1] // 2
    freqs = ROPE_BASE ** (-(jnp.arange(half, dtype=jnp.float32) * 2.0 / values.shape[-1]))
    angles = positions.astype(jnp.float32)[..., None] * freqs
    cosine = jnp.cos(angles)
    sine = jnp.sin(angles)
    first = values[..., :half]
    second = values[..., half:]
    return jnp.concatenate([first * cosine - second * sine, second * cosine + first * sine], -1)


def request_layout(request_owner, request_length, block_table, owners, stripe):
    requests = request_owner.shape[0]
    most = block_table.shape[1]
    order = jnp.arange(requests, dtype=jnp.int32)
    stripes = (request_length + stripe - 1) // stripe
    before = (
        (request_owner[None, :] == request_owner[:, None]) & (order[None, :] < order[:, None])
    ).astype(jnp.int32)
    rank = jnp.sum(before, 1)
    offset = jnp.sum(before * stripes[None, :], 1)
    owner_ids = jnp.arange(owners, dtype=jnp.int32)
    mine = request_owner[None, :] == owner_ids[:, None]
    member = mine[:, :, None] & (
        rank[None, :, None] == jnp.arange(requests // owners, dtype=jnp.int32)[None, None, :]
    )
    owner_requests = jnp.sum(member.astype(jnp.int32) * order[None, :, None], 1)
    columns = jnp.arange(most, dtype=jnp.int32)
    within = columns[None, None, :] - offset[None, :, None]
    hit = (mine[:, :, None] & (within >= 0) & (within < stripes[None, :, None])).astype(jnp.int32)
    stripe_request = jnp.sum(hit * order[None, :, None], 1) - (1 - jnp.sum(hit, 1))
    stripe_rank = jnp.sum(hit * within, 1)
    pick = (within[..., None] == columns[None, None, None, :]).astype(jnp.int32)
    slots = jnp.sum(hit[..., None] * pick * block_table[None, :, None, :], (1, 3))
    return (owner_requests, stripe_request, stripe_rank, slots, rank, stripes)


def cache_partial(queries, keys, values, key_scale, value_scale, mask):
    scores = jnp.einsum("srgd,td->srgt", queries, keys, preferred_element_type=jnp.float32)
    scores = jnp.where(mask, scores * key_scale * HD ** (-0.5), NEG_FILL)
    best = jnp.max(scores, -1)
    expo = jnp.where(mask, jnp.exp(scores - best[..., None]), 0.0)
    total = jnp.sum(expo, -1)
    weights = (expo * value_scale).astype(jnp.bfloat16)
    summed = jnp.einsum("srgt,td->srgd", weights, values, preferred_element_type=jnp.float32)
    return (best, total, summed)


def local_general(
    hidden_in,
    norm_gain,
    qkv_weight,
    out_weight,
    cache_pool,
    cache_scale,
    request_length,
    block_table,
):
    devices = lax.axis_size("tensor")
    device = lax.axis_index("tensor")
    owners = devices // KVH
    stripe = devices * BLK
    requests = request_length.shape[0]
    request_owner = jnp.arange(requests, dtype=jnp.int32) % owners
    unit_rows = requests // owners * QR
    most = block_table.shape[1]
    local_width = hidden_in.shape[2]
    my_owner = device // KVH
    owner_requests, stripe_request, stripe_rank, slots, rank, stripes = request_layout(
        request_owner, request_length, block_table, owners, stripe
    )
    step_rows = jnp.arange(QR, dtype=jnp.int32)
    row_order = (owner_requests[:, :, None] * QR + step_rows[None, None, :]).reshape(
        owners * unit_rows
    )
    inverse = ((request_owner * unit_rows + rank * QR)[:, None] + step_rows[None, :]).reshape(
        requests * QR
    )
    row_request = jnp.repeat(owner_requests[my_owner], QR)
    row_length = request_length[row_request]
    row_step = jnp.arange(unit_rows, dtype=jnp.int32) % QR
    same_request = row_request[:, None] == row_request[None, :]
    gain = norm_gain.astype(jnp.float32)
    weight_grouped = qkv_weight.reshape(local_width, KVH, GW)
    sent = cache_pool[jnp.transpose(slots)].reshape(most, devices, BLK, 2 * HD)
    sent_scale = cache_scale[jnp.transpose(slots)].reshape(most, devices, 2)
    landed, landed_scale = (
        lax.all_to_all(sent, "tensor", split_axis=1, concat_axis=1, tiled=True),
        lax.all_to_all(sent_scale, "tensor", split_axis=1, concat_axis=1, tiled=True),
    )
    cache_data = landed.reshape(most * stripe, 2 * HD)
    token_scale = jnp.broadcast_to(
        landed_scale.astype(jnp.float32)[:, :, None, :], (most, devices, BLK, 2)
    ).reshape(most * stripe, 2)
    token = jnp.arange(most * stripe, dtype=jnp.int32)
    token_stripe = token // stripe
    token_request = stripe_request[my_owner][token_stripe]
    token_position = stripe_rank[my_owner][token_stripe] * stripe + token % stripe
    token_length = jnp.where(token_request >= 0, request_length[jnp.maximum(token_request, 0)], 0)
    cache_mask = (
        (token_request[None, :] == row_request[:, None]) & (token_position < token_length)[None, :]
    )[None, :, None, :]
    outputs = []
    keys_seen = []
    values_seen = []
    for step in range(STEPS):
        block = hidden_in[step : step + 1]
        project_count = block.shape[0]
        values = block.astype(jnp.float32)
        sums = lax.psum(jnp.sum(values * values, -1), "tensor")
        normed = (values * lax.rsqrt(sums[..., None] / D + EPSILON) * gain).astype(jnp.bfloat16)
        ordered = jnp.take(normed, row_order, axis=1).reshape(
            project_count, owners, unit_rows, local_width
        )
        term = jnp.einsum(
            "sojd,dhg->ohsjg", ordered, weight_grouped, preferred_element_type=jnp.float32
        )
        term = term.reshape(owners * KVH * project_count * unit_rows, GW)
        mine = lax.psum_scatter(term, "tensor", scatter_dimension=0, tiled=True)
        joined_block = mine.astype(jnp.bfloat16).reshape(project_count, unit_rows, GW)
        prepare_count = joined_block.shape[0]
        steps_here = step + jnp.arange(prepare_count, dtype=jnp.int32)
        position = row_length[None, :] + QR * steps_here[:, None] + row_step[None, :]
        prepare_queries = rotate(
            joined_block[..., : GQ * HD]
            .reshape(prepare_count, unit_rows, GQ, HD)
            .astype(jnp.float32),
            position[:, :, None],
        ).astype(jnp.bfloat16)
        keys = rotate(
            joined_block[..., GQ * HD : GQ * HD + HD].astype(jnp.float32), position
        ).astype(jnp.bfloat16)
        queries, keys, values = (prepare_queries, keys, joined_block[..., GQ * HD + HD :])
        keys_seen.append(keys)
        values_seen.append(values)
        keys_all = jnp.concatenate(keys_seen, 0)
        attend_count = queries.shape[0]
        cache_best, cache_total, cache_summed = cache_partial(
            queries,
            cache_data[:, :HD],
            cache_data[:, HD:],
            token_scale[:, 0],
            token_scale[:, 1],
            cache_mask,
        )
        news = jnp.einsum(
            "srgd,pjd->srgpj", queries, keys_all, preferred_element_type=jnp.float32
        ) * HD ** (-0.5)
        query_step = step + jnp.arange(attend_count, dtype=jnp.int32)[:, None, None, None]
        key_step = jnp.arange(keys_all.shape[0], dtype=jnp.int32)[None, None, :, None]
        allowed = (key_step < query_step) | (key_step == query_step) & (
            row_step[None, None, None, :] <= row_step[None, :, None, None]
        )
        allowed = (allowed & same_request[None, :, None, :])[:, :, None, :, :]
        news = jnp.where(allowed, news, NEG_FILL)
        best = jnp.maximum(cache_best, jnp.max(news, (3, 4)))
        factor = jnp.exp(cache_best - best)
        expo = jnp.where(allowed, jnp.exp(news - best[..., None, None]), 0.0)
        total = cache_total * factor + jnp.sum(expo, (3, 4))
        summed = cache_summed * factor[..., None] + jnp.einsum(
            "srgpj,pjd->srgd",
            expo.astype(jnp.bfloat16),
            jnp.concatenate(values_seen, 0),
            preferred_element_type=jnp.float32,
        )
        attention = (
            (summed / total[..., None])
            .astype(jnp.bfloat16)
            .reshape(attend_count, unit_rows, GQ * HD)
        )
        count = attention.shape[0]
        gathered = lax.all_gather(attention, "tensor", axis=2, tiled=True).reshape(
            count, unit_rows, owners, QH * HD
        )
        mixed = jnp.einsum(
            "sjof,fd->sojd", gathered, out_weight, preferred_element_type=jnp.float32
        )
        mixed = jnp.take(mixed.reshape(count, owners * unit_rows, local_width), inverse, axis=1)
        outputs.append(
            (hidden_in[step : step + count].astype(jnp.float32) + mixed).astype(jnp.bfloat16)
        )
    return jnp.concatenate(outputs, 0)


VMEM_LIMIT = 48 * 1024 * 1024
SHORT = pl.CostEstimate(flops=1, bytes_accessed=1, transcendentals=0)
LONG = pl.CostEstimate(flops=2 * 10**10, bytes_accessed=1, transcendentals=0)
LOW_BITS = 4
PACKED = 16 // LOW_BITS
LEVELS = 32600.0 * 2**LOW_BITS
POWER_STEPS = 8.0
TILE = 16
MESH_BITS = (1, 2, 4, 8)


def swap(value, bit):
    devices = lax.axis_size("tensor")
    return lax.ppermute(value, "tensor", [(i, i ^ bit) for i in range(devices)])


def no_work(*refs):
    del refs


def together(arrays, after):
    anywhere = pl.BlockSpec(memory_space=pl.ANY)
    return pl.pallas_call(
        no_work,
        in_specs=[anywhere] * (len(arrays) + len(after)),
        out_specs=[anywhere] * len(arrays),
        out_shape=[jax.ShapeDtypeStruct(a.shape, a.dtype) for a in arrays],
        input_output_aliases={i: i for i in range(len(arrays))},
        compiler_params=pltpu.CompilerParams(vmem_limit_bytes=VMEM_LIMIT),
        cost_estimate=SHORT,
        name="together",
    )(*arrays, *after)


def coded_rows(rows):
    return rows + rows // PACKED


def encode(block):
    top = jnp.max(jnp.abs(block), 0, keepdims=True)
    power = jnp.ceil(jnp.log2(jnp.maximum(top, 1e-30)) * POWER_STEPS)
    codes = jnp.round(block * (jnp.exp2(power * (-1.0 / POWER_STEPS)) * LEVELS)).astype(jnp.int32)
    low = codes & (2**LOW_BITS - 1)
    part = block.shape[0] // PACKED
    packed = low[:part]
    for i in range(1, PACKED):
        packed = packed + (low[i * part : (i + 1) * part] << (LOW_BITS * i))
    high = (codes >> LOW_BITS).astype(jnp.int16)
    return jnp.concatenate([high, (packed - 32768).astype(jnp.int16)], 0), power


def decode(codes, power):
    rows = codes.shape[0] * PACKED // (PACKED + 1)
    high = codes[:rows].astype(jnp.int32) << LOW_BITS
    packed = codes[rows:].astype(jnp.int32) + 32768
    low = jnp.concatenate(
        [(packed >> (LOW_BITS * i)) & (2**LOW_BITS - 1) for i in range(PACKED)], 0
    )
    scale = jnp.exp2(power * (1.0 / POWER_STEPS)) * (1.0 / LEVELS)
    return (high + low).astype(jnp.float32) * scale


def pick_row(rows, index):
    ids = lax.broadcasted_iota(jnp.int32, rows.shape, 0)
    return jnp.sum(jnp.where(ids == index, rows, 0.0), 0, keepdims=True)


def store_codes(sent, powers, block, index, steps):
    rows = coded_rows(block.shape[0])
    codes, power = encode(block)
    sent[pl.ds(pl.multiple_of(index * rows, TILE), rows), :] = codes

    powers[pl.ds(index, 1), :] = power

    @pl.when(index == steps - 1)
    def _():
        sent[pl.ds(steps * rows, TILE), :] = powers[...].astype(jnp.int32).astype(jnp.int16)


PART_HEADS = (3, 5)


def project_kernel(part, core, normed, weights, *refs):
    kept, sent, powers, slabs, arrived = refs[-5:]
    index = pl.program_id(0)
    half = kept.shape[2]
    heads = PART_HEADS[part] * HD
    first = sum(PART_HEADS[:part]) * HD

    def copies(group):
        found = []
        for side in range(2):
            owner = core[0] if side == 0 else 1 - core[0]
            spans = [(group * GW + owner * (GQ // 2 * HD) + first, 0, heads)]
            if half > heads:
                spans.append((group * GW + (GQ + owner) * HD, heads, HD))
            for number, (start, offset, size) in enumerate(spans):
                found.append(
                    pltpu.make_async_copy(
                        weights.at[:, pl.ds(pl.multiple_of(start, HD), size)],
                        slabs.at[group, :, pl.ds(side * half + offset, size)],
                        arrived.at[group, side, number],
                    )
                )
        return found

    @pl.when(index == 0)
    def _():
        for group in range(KVH):
            for copy in copies(group):
                copy.start()
        powers[...] = jnp.zeros_like(powers)

    for copy in copies(index):
        copy.wait()

    found = []
    rows = coded_rows(normed.shape[0])
    place = pl.ds(pl.multiple_of(index * rows, TILE), rows)
    for start in range(0, 2 * half, 2 * HD):
        stop = start + 2 * HD
        product = jnp.dot(
            normed[...], slabs[index, :, start:stop], preferred_element_type=jnp.float32
        )
        if start < half:
            kept[0, :, start : min(stop, half)] = product[:, : half - start]
        if stop > half:
            first = max(start, half)
            codes, power = encode(product[:, first - start :])
            sent[place, first - half : stop - half] = codes
            found.append(power)
    powers[pl.ds(index, 1), :] = jnp.concatenate(found, 1)

    @pl.when(index == KVH - 1)
    def _():
        sent[pl.ds(KVH * rows, TILE), :] = powers[...].astype(jnp.int32).astype(jnp.int16)


def project(core, normed, qkv_weight, part, after):
    rows, width = normed.shape
    columns = PART_HEADS[part] * HD + (HD if part == 0 else 0)
    sent_rows = KVH * coded_rows(rows) + TILE
    return pl.pallas_call(
        functools.partial(project_kernel, part),
        grid_spec=pltpu.PrefetchScalarGridSpec(
            num_scalar_prefetch=1,
            grid=(KVH,),
            in_specs=[pl.BlockSpec((rows, width), lambda t, c: (0, 0))]
            + [pl.BlockSpec(memory_space=pl.ANY)] * (1 + len(after)),
            out_specs=[
                pl.BlockSpec((1, rows, columns), lambda t, c: (t, 0, 0)),
                pl.BlockSpec((sent_rows, columns), lambda t, c: (0, 0)),
            ],
            scratch_shapes=[
                pltpu.VMEM((TILE, columns), jnp.float32),
                pltpu.VMEM((KVH, width, 2 * columns), jnp.bfloat16),
                pltpu.SemaphoreType.DMA((KVH, 2, 2)),
            ],
        ),
        out_shape=[
            pltpu.HBM((KVH, rows, columns), jnp.float32),
            jax.ShapeDtypeStruct((sent_rows, columns), jnp.int16),
        ],
        compiler_params=pltpu.CompilerParams(vmem_limit_bytes=VMEM_LIMIT),
        cost_estimate=SHORT,
        name="project",
    )(core, normed, qkv_weight, *after)


def fold_kernel(steps, low, bit, held, held_out, landed, landed_out, landed_powers, *refs):
    kept, sent, powers = refs[-3:]
    index = pl.program_id(0)
    rows_of_powers = landed_powers[...].astype(jnp.int32).astype(jnp.float32)
    first = index // low * (2 * low) + index % low

    def total(side, block, codes):
        power = pick_row(rows_of_powers, first + side * low)
        return block[0] + decode(codes[...], power)

    @pl.when(index == 0)
    def _():
        powers[...] = jnp.zeros_like(powers)

    kept[0] = total(bit[0], held, landed)
    store_codes(sent, powers, total(1 - bit[0], held_out, landed_out), index, steps)


def fold(bit, held, landed, low, cost, after):
    blocks, rows, columns = held.shape
    steps = blocks // 2
    coded = coded_rows(rows)

    def block(i, b, out):
        side = 1 - b[0] if out else b[0]
        return i // low * (2 * low) + side * low + i % low

    return pl.pallas_call(
        functools.partial(fold_kernel, steps, low),
        grid_spec=pltpu.PrefetchScalarGridSpec(
            num_scalar_prefetch=1,
            grid=(steps,),
            in_specs=[
                pl.BlockSpec((1, rows, columns), lambda i, b: (block(i, b, False), 0, 0)),
                pl.BlockSpec((1, rows, columns), lambda i, b: (block(i, b, True), 0, 0)),
                pl.BlockSpec((coded, columns), lambda i, b: (block(i, b, False), 0)),
                pl.BlockSpec((coded, columns), lambda i, b: (block(i, b, True), 0)),
                pl.BlockSpec((TILE, columns), lambda i, b: (blocks * coded // TILE, 0)),
            ]
            + [pl.BlockSpec(memory_space=pl.ANY)] * len(after),
            out_specs=[
                pl.BlockSpec((1, rows, columns), lambda i, b: (i, 0, 0)),
                pl.BlockSpec((steps * coded + TILE, columns), lambda i, b: (0, 0)),
            ],
            scratch_shapes=[pltpu.VMEM((TILE, columns), jnp.float32)],
        ),
        out_shape=[
            jax.ShapeDtypeStruct((steps, rows, columns), jnp.float32),
            jax.ShapeDtypeStruct((steps * coded + TILE, columns), jnp.int16),
        ],
        compiler_params=pltpu.CompilerParams(vmem_limit_bytes=VMEM_LIMIT),
        cost_estimate=cost,
        name="fold",
    )(bit, held, held, landed, landed, landed, *after)


def finish_kernel(heads, after_count, core, held, landed, cosine, sine, *refs):
    queries, *pair = refs[after_count:]
    coded = coded_rows(held.shape[1])
    power = landed[pl.ds(coded, TILE), :].astype(jnp.int32).astype(jnp.float32)[0:1]
    total = held[0] + decode(landed[pl.ds(0, coded), :], power)
    joined = total.astype(jnp.bfloat16)
    for head in range(joined.shape[1] // HD):
        raw = joined[:, head * HD : (head + 1) * HD].astype(jnp.float32)
        turned = raw * cosine[...] + pltpu.roll(raw, HD // 2, 1) * sine[...]
        if head < heads:
            queries[:, head * HD : (head + 1) * HD] = turned.astype(jnp.bfloat16)
        else:
            pair[0][...] = jnp.where(core[0] == 0, turned, raw).astype(jnp.bfloat16)


def finish(core, held, landed, cosine, sine, heads, after):
    _, rows, columns = held.shape
    whole = pl.BlockSpec(memory_space=pltpu.VMEM)
    shapes = [jax.ShapeDtypeStruct((rows, heads * HD), jnp.bfloat16)]
    if columns > heads * HD:
        shapes.append(jax.ShapeDtypeStruct((rows, HD), jnp.bfloat16))
    return pl.pallas_call(
        functools.partial(finish_kernel, heads, len(after)),
        in_specs=[pl.BlockSpec(memory_space=pltpu.SMEM)]
        + [whole] * 4
        + [pl.BlockSpec(memory_space=pl.ANY)] * len(after),
        out_specs=[whole] * len(shapes),
        out_shape=shapes,
        compiler_params=pltpu.CompilerParams(vmem_limit_bytes=VMEM_LIMIT),
        cost_estimate=LONG,
        name="finish",
    )(core, held, landed, cosine, sine, *after)


def mix_kernel(count, places, *refs):
    pieces = refs[:count]
    weights, start, mixed, total, wide, arrived = refs[count:]
    depth = wide.shape[1]
    columns = wide.shape[2] // 2
    flat = []
    for piece in pieces:
        flat += [piece] if len(piece.shape) == 2 else [piece.at[i] for i in range(piece.shape[0])]
    copies = [
        pltpu.make_async_copy(
            weights.at[pl.ds(pl.multiple_of(places[i] * depth, depth), depth), :],
            wide.at[i],
            arrived.at[i],
        )
        for i in range(len(flat))
    ]
    for copy in copies:
        copy.start()
    cuts = [0, 1, 2, 4, len(flat)]
    cuts = sorted(set(min(cut, len(flat)) for cut in cuts))
    for first, last in zip(cuts, cuts[1:]):
        for copy in copies[first:last]:
            copy.wait()
        for side in range(2):
            span = pl.ds(side * columns, columns)
            source = start if first == 0 else total
            value = source[:, span].astype(jnp.float32)
            for i in range(first, last):
                value = value + jnp.dot(
                    flat[i][...], wide[i, :, span], preferred_element_type=jnp.float32
                )
            target = mixed if last == len(flat) else total
            target[:, span] = value.astype(target.dtype)


def mix(places, pieces, out_weight, start, dtype):
    columns = out_weight.shape[1]
    rows, width = pieces[0].shape[-2:]
    count = sum(1 if len(p.shape) == 2 else p.shape[0] for p in pieces)
    whole = pl.BlockSpec(memory_space=pltpu.VMEM)
    return pl.pallas_call(
        functools.partial(mix_kernel, len(pieces)),
        in_specs=[pl.BlockSpec(memory_space=pltpu.SMEM)]
        + [whole] * len(pieces)
        + [pl.BlockSpec(memory_space=pl.ANY), whole],
        out_specs=whole,
        scratch_shapes=[
            pltpu.VMEM((rows, columns), jnp.float32),
            pltpu.VMEM((count, width, columns), jnp.bfloat16),
            pltpu.SemaphoreType.DMA((count,)),
        ],
        out_shape=jax.ShapeDtypeStruct((rows, columns), dtype),
        compiler_params=pltpu.CompilerParams(vmem_limit_bytes=VMEM_LIMIT),
        cost_estimate=SHORT,
        name="mix",
    )(places, *pieces, out_weight, start)


def pack_kernel(groups, count, *refs):
    flat = []
    for ref in refs[:count]:
        flat += [ref] if len(ref.shape) == 2 else [ref.at[i] for i in range(ref.shape[0])]
    for group, target in zip(groups, refs[-len(groups) :]):
        for place, index in enumerate(group):
            target[place] = flat[index][...]


def pack(pieces, groups, after):
    whole = pl.BlockSpec(memory_space=pltpu.VMEM)
    shape = pieces[0].shape[-2:]
    return pl.pallas_call(
        functools.partial(pack_kernel, groups, len(pieces)),
        in_specs=[whole] * len(pieces) + [pl.BlockSpec(memory_space=pl.ANY)] * len(after),
        out_specs=[whole] * len(groups),
        out_shape=[jax.ShapeDtypeStruct((len(g),) + shape, pieces[0].dtype) for g in groups],
        compiler_params=pltpu.CompilerParams(vmem_limit_bytes=VMEM_LIMIT),
        cost_estimate=SHORT,
        name="pack",
    )(*pieces, *after)


def gather_and_mix(attention, out_weight, start, device):
    def add(mixed, pieces, offsets, dtype=jnp.float32):
        places = jnp.stack([device ^ offset for offset in offsets])
        return mix(places, pieces, out_weight, mixed, dtype)

    near = swap(attention, 4)
    across = swap(attention, 2)
    far = swap(attention, 8)
    partner = swap(attention, 1)
    first, onward = pack([near, across, far], [(0, 1, 2), (0, 2)], [partner])
    (attention,) = together([attention], [onward])

    across_onward = swap(onward, 2)
    farthest = swap(attention, 12)
    first_partner = swap(first, 1)
    mixed = add(start, [attention, partner], (0, 1))
    mixed = add(mixed, [first, first_partner], (4, 2, 8, 5, 3, 9))
    (second,) = pack([across_onward, farthest], [(0, 1, 2)], [mixed])

    last = swap(farthest, 2)
    second_partner = swap(second, 1)
    mixed = add(mixed, [second, second_partner], (6, 10, 12, 7, 11, 13))
    (last,) = together([last], [mixed])

    last_partner = swap(last, 1)
    return add(mixed, [last, last_partner], (14, 15), jnp.bfloat16)


def attend_kernel(
    slot_request,
    queries,
    new_keys,
    new_values,
    own,
    other,
    key_scale,
    value_scale,
    cache_bias,
    new_bias,
    attention,
    slot_best,
    slot_total,
    slot_sum,
    best,
    total,
    summed,
):
    slots = slot_best.shape[0]
    requests, count, _ = queries.shape
    transposed = (((1,), (1,)), ((), ()))
    for request in range(requests):
        scores = (
            lax.dot_general(
                queries[request],
                new_keys[request],
                transposed,
                preferred_element_type=jnp.float32,
            )
            * HD ** (-0.5)
            + new_bias[...]
        )
        top = jnp.max(scores, -1, keepdims=True)
        expo = jnp.exp(scores - top)
        best[request] = jnp.broadcast_to(top, (count, HD))
        total[request] = jnp.broadcast_to(jnp.sum(expo, -1, keepdims=True), (count, HD))
        summed[request] = jnp.dot(
            expo.astype(jnp.bfloat16), new_values[request], preferred_element_type=jnp.float32
        )
    for slot in range(slots):
        request = slot_request[slot]
        query = queries[request]
        raw = [
            part[:, slot * BLK : (slot + 1) * BLK, :].reshape(KVH * BLK, 2 * HD)
            for part in (own, other)
        ]
        scores = jnp.concatenate(
            [
                lax.dot_general(
                    query, kv[:, :HD], transposed, preferred_element_type=jnp.float32
                )
                for kv in raw
            ],
            1,
        )
        scores = scores * key_scale[slot : slot + 1, :] + cache_bias[slot : slot + 1, :]
        top = jnp.max(scores, -1, keepdims=True)
        expo = jnp.exp(scores - top)
        weights = (expo * value_scale[slot : slot + 1, :]).astype(jnp.bfloat16)
        slot_best[slot] = jnp.broadcast_to(top, (count, HD))
        slot_total[slot] = jnp.broadcast_to(jnp.sum(expo, -1, keepdims=True), (count, HD))
        values = jnp.concatenate([kv[:, HD:] for kv in raw], 0)
        slot_sum[slot] = jnp.dot(weights, values, preferred_element_type=jnp.float32)
    for slot in range(slots):
        request = slot_request[slot]
        before = best[request]
        here = slot_best[slot]
        top = jnp.maximum(before, here)
        keep = jnp.exp(before - top)
        add = jnp.exp(here - top)
        best[request] = top
        total[request] = total[request] * keep + slot_total[slot] * add
        summed[request] = summed[request] * keep + slot_sum[slot] * add
    for request in range(requests):
        attention[request] = (summed[request] / total[request]).astype(jnp.bfloat16)


def attend(slot_request, *arrays):
    queries = arrays[0]
    slots = arrays[5].shape[0]
    requests, count, _ = queries.shape
    whole = pl.BlockSpec(memory_space=pltpu.VMEM)
    return pl.pallas_call(
        attend_kernel,
        in_specs=[pl.BlockSpec(memory_space=pltpu.SMEM)] + [whole] * len(arrays),
        out_specs=whole,
        out_shape=jax.ShapeDtypeStruct((requests, count, HD), jnp.bfloat16),
        scratch_shapes=[pltpu.VMEM((slots, count, HD), jnp.float32)] * 3
        + [pltpu.VMEM((requests, count, HD), jnp.float32)] * 3,
        compiler_params=pltpu.CompilerParams(vmem_limit_bytes=VMEM_LIMIT),
        cost_estimate=SHORT,
        name="attend",
    )(slot_request, *arrays)


def slot_layout(request_length, block_table, slots, stripe):
    requests, most = block_table.shape
    stripes = (request_length + stripe - 1) // stripe
    columns = jnp.arange(most, dtype=jnp.int32)
    held = columns[None, :] < stripes[:, None]
    hit = held[:, :, None] & (
        block_table[:, :, None] == jnp.arange(slots, dtype=jnp.int32)[None, None, :]
    )
    hit = hit.astype(jnp.int32)
    order = jnp.arange(requests, dtype=jnp.int32)
    request = jnp.sum(hit * order[:, None, None], (0, 1))
    rank = jnp.sum(hit * columns[None, :, None], (0, 1))
    length = jnp.sum(hit * request_length[:, None, None], (0, 1))
    return request, rank, length


def arrange_kernel(chip, pool, scales, after, *sent):
    slots = pool.shape[0]
    for k, target in enumerate(sent):
        head = chip[0] ^ k
        target[: slots * BLK, :] = pool[:, head].reshape(slots * BLK, 2 * HD)
        target[slots * BLK :, :] = scales[head]


def arrange(chip, cache_pool, scales, after):
    rows = cache_pool.shape[0] * BLK + TILE
    whole = pl.BlockSpec(memory_space=pltpu.VMEM)
    return pl.pallas_call(
        arrange_kernel,
        in_specs=[
            pl.BlockSpec(memory_space=pltpu.SMEM),
            whole,
            whole,
            pl.BlockSpec(memory_space=pl.ANY),
        ],
        out_specs=[whole] * KVH,
        out_shape=[jax.ShapeDtypeStruct((rows, 2 * HD), jnp.bfloat16)] * KVH,
        compiler_params=pltpu.CompilerParams(vmem_limit_bytes=VMEM_LIMIT),
        cost_estimate=SHORT,
        name="arrange",
    )(chip, cache_pool, scales, after)


def local_pairs(
    hidden_in,
    norm_gain,
    qkv_weight,
    out_weight,
    cache_pool,
    cache_scale,
    request_length,
    block_table,
):
    devices = lax.axis_size("tensor")
    device = lax.axis_index("tensor")
    core = device % 2
    chip = device // 2
    stripe = devices * BLK
    slots = cache_pool.shape[0]
    requests = request_length.shape[0]
    rows = STEPS * requests * QR
    width = hidden_in.shape[2]
    heads = GQ // 2

    hidden = hidden_in.astype(jnp.float32)
    sums = jnp.sum(hidden * hidden, -1)
    bits = [jnp.reshape((device >> b) & 1, (1,)).astype(jnp.int32) for b in range(4)]
    scale_rows = jnp.pad(
        jnp.transpose(cache_scale, (1, 2, 0)).reshape(KVH, 1, 2 * slots),
        ((0, 0), (0, TILE - 1), (0, 2 * HD - 2 * slots)),
    )
    sums = sums + swap(sums, 2)
    chip_scalar = jnp.reshape(chip, (1,)).astype(jnp.int32)
    cache_pieces = list(arrange(chip_scalar, cache_pool, scale_rows, sums))

    def handed(k):
        cache_pieces[k] = swap(cache_pieces[k], 2 * k)

    for bit in (1, 4, 8):
        sums = sums + swap(sums, bit)
    normed = (
        hidden * lax.rsqrt(sums[..., None] / D + EPSILON) * norm_gain.astype(jnp.float32)
    ).astype(jnp.bfloat16)
    normed = normed.reshape(rows, width)

    step_ids = jnp.arange(STEPS, dtype=jnp.int32)
    row_ids = jnp.arange(QR, dtype=jnp.int32)
    position = (
        request_length[None, :, None] + QR * step_ids[:, None, None] + row_ids[None, None, :]
    )
    freqs = ROPE_BASE ** (-(jnp.arange(HD // 2, dtype=jnp.float32) * 2.0 / HD))
    angles = position.reshape(rows, 1).astype(jnp.float32) * freqs
    cosine = jnp.concatenate([jnp.cos(angles)] * 2, 1)
    sine = jnp.concatenate([-jnp.sin(angles), jnp.sin(angles)], 1)

    def folded(part, b, landed, low, *after, cost=SHORT):
        return fold(bits[b], part, landed, low, cost, after)

    def finished(part, number, landed, *after):
        return finish(bits[0], part, landed, cosine, sine, PART_HEADS[number], after)

    for k in (1, 3, 4, 5, 6):
        handed(k)
    held_a, sent_a = project(bits[0], normed, qkv_weight, 0, cache_pieces[:1])
    core_a = swap(sent_a, 1)
    held_b, sent_b = project(
        bits[0], normed, qkv_weight, 1, [held_a, cache_pieces[1], cache_pieces[3]]
    )
    sent_b, cache_pieces[2], cache_pieces[7] = together(
        [sent_b, cache_pieces[2], cache_pieces[7]], cache_pieces[4:7]
    )
    core_b = swap(sent_b, 1)
    for k in (2, 7):
        handed(k)
    held_b, sent_b = folded(held_b, 2, core_b, 2, sent_b)
    line_b = swap(sent_b, 4)
    held_a, sent_a = folded(
        held_a, 1, core_a, 1, held_b, cache_pieces[2], cache_pieces[7], cost=LONG
    )
    line_a = swap(sent_a, 2)
    held_b, sent_b = folded(held_b, 1, line_b, 1, held_a)
    line_b = swap(sent_b, 2)
    held_a, sent_a = folded(held_a, 2, line_a, 1, held_b)
    line_a = swap(sent_a, 4)
    far_pieces = [pltpu.with_memory_space_constraint(p, pltpu.HBM) for p in cache_pieces]
    (cache_own,) = pack(far_pieces, [tuple(range(KVH))], [held_a])
    cache_other = swap(cache_own, 1)
    held_a, sent_a = folded(held_a, 3, line_a, 1, cache_own)
    line_a = swap(sent_a, 8)
    held_b, sent_b = folded(held_b, 3, line_b, 1, held_a)
    line_b = swap(sent_b, 8)
    query_a, pair = finished(held_a, 0, line_a, held_b)
    (pair,) = together([pair], [line_b])
    pair_other = swap(pair, 1)
    (query_b,) = finished(held_b, 1, line_b, query_a)
    query_chunks = [query_a, query_b]
    cache_parts = (cache_own, cache_other)
    keys = jnp.where(core == 0, pair, pair_other)
    raw_values = jnp.where(core == 0, pair_other, pair)
    queries = jnp.concatenate(query_chunks, 1).reshape(STEPS, requests, QR, heads, HD)
    queries = jnp.transpose(queries, (1, 0, 2, 3, 4)).reshape(requests, STEPS * QR * heads, HD)

    def by_request(value):
        value = jnp.transpose(value.reshape(STEPS, requests, QR, HD), (1, 0, 2, 3))
        value = value.reshape(requests, STEPS * QR, HD)
        return jnp.pad(value, ((0, 0), (0, TILE - STEPS * QR), (0, 0)))

    slot_request, slot_rank, slot_length = slot_layout(request_length, block_table, slots, stripe)
    source = chip ^ jnp.arange(KVH, dtype=jnp.int32)
    sources = jnp.stack([source * 2 + core, source * 2 + 1 - core])
    offset = sources[:, :, None] * BLK + jnp.arange(BLK, dtype=jnp.int32)[None, None, :]
    token = slot_rank[:, None] * stripe + offset.reshape(1, stripe)
    cache_bias = jnp.where(token < slot_length[:, None], 0.0, NEG_FILL).astype(jnp.float32)
    scales = jnp.concatenate([part[:, slots * BLK, : 2 * slots] for part in cache_parts])
    scales = scales.astype(jnp.float32).reshape(2 * KVH, 2, slots)
    scales = jnp.repeat(jnp.transpose(scales, (1, 2, 0)), BLK, axis=2)
    order = jnp.arange(STEPS * QR * heads, dtype=jnp.int32) // heads
    key_order = jnp.arange(TILE, dtype=jnp.int32)
    new_bias = jnp.where(key_order[None, :] <= order[:, None], 0.0, NEG_FILL).astype(jnp.float32)
    attention = attend(
        slot_request,
        queries,
        by_request(keys),
        by_request(raw_values),
        *cache_parts,
        scales[0] * HD ** (-0.5),
        scales[1],
        cache_bias,
        new_bias,
    )
    attention = jnp.transpose(
        attention.reshape(requests, STEPS, QR, heads, HD), (1, 0, 2, 3, 4)
    ).reshape(rows, heads * HD)
    mixed = gather_and_mix(attention, out_weight, hidden_in.reshape(rows, width), device)
    return mixed.reshape(hidden_in.shape)


def solution(mesh):
    return jax.shard_map(
        local_pairs if mesh.shape["tensor"] == 2 * KVH else local_general,
        mesh=mesh,
        in_specs=(
            P(None, "groups", "tensor"),
            P("tensor"),
            P("tensor", None),
            P(None, "tensor"),
            P(("groups", "tensor"), None, None, None),
            P(("groups", "tensor"), None, None),
            P("groups"),
            P("groups", None),
        ),
        out_specs=P(None, "groups", "tensor"),
        check_vma=False,
    )
```

```python
import functools

import jax
import jax.numpy as jnp
from jax import lax
from jax.experimental import pallas as pl
from jax.experimental.pallas import tpu as pltpu
from jax.sharding import PartitionSpec as P

D = 16384
QH = 128
KVH = 8
HD = 128
QR = 6
STEPS = 2
BLK = 16
GQ = 16
GW = 2304


EPSILON = 1e-05
ROPE_BASE = 500000.0
NEG_FILL = -1e30


def rotate(values, positions):
    half = values.shape[-1] // 2
    freqs = ROPE_BASE ** (-(jnp.arange(half, dtype=jnp.float32) * 2.0 / values.shape[-1]))
    angles = positions.astype(jnp.float32)[..., None] * freqs
    cosine = jnp.cos(angles)
    sine = jnp.sin(angles)
    first = values[..., :half]
    second = values[..., half:]
    return jnp.concatenate([first * cosine - second * sine, second * cosine + first * sine], -1)


def request_layout(request_owner, request_length, block_table, owners, stripe):
    requests = request_owner.shape[0]
    most = block_table.shape[1]
    order = jnp.arange(requests, dtype=jnp.int32)
    stripes = (request_length + stripe - 1) // stripe
    before = (
        (request_owner[None, :] == request_owner[:, None]) & (order[None, :] < order[:, None])
    ).astype(jnp.int32)
    rank = jnp.sum(before, 1)
    offset = jnp.sum(before * stripes[None, :], 1)
    owner_ids = jnp.arange(owners, dtype=jnp.int32)
    mine = request_owner[None, :] == owner_ids[:, None]
    member = mine[:, :, None] & (
        rank[None, :, None] == jnp.arange(requests // owners, dtype=jnp.int32)[None, None, :]
    )
    owner_requests = jnp.sum(member.astype(jnp.int32) * order[None, :, None], 1)
    columns = jnp.arange(most, dtype=jnp.int32)
    within = columns[None, None, :] - offset[None, :, None]
    hit = (mine[:, :, None] & (within >= 0) & (within < stripes[None, :, None])).astype(jnp.int32)
    stripe_request = jnp.sum(hit * order[None, :, None], 1) - (1 - jnp.sum(hit, 1))
    stripe_rank = jnp.sum(hit * within, 1)
    pick = (within[..., None] == columns[None, None, None, :]).astype(jnp.int32)
    slots = jnp.sum(hit[..., None] * pick * block_table[None, :, None, :], (1, 3))
    return (owner_requests, stripe_request, stripe_rank, slots, rank, stripes)


def cache_partial(queries, keys, values, key_scale, value_scale, mask):
    scores = jnp.einsum("srgd,td->srgt", queries, keys, preferred_element_type=jnp.float32)
    scores = jnp.where(mask, scores * key_scale * HD ** (-0.5), NEG_FILL)
    best = jnp.max(scores, -1)
    expo = jnp.where(mask, jnp.exp(scores - best[..., None]), 0.0)
    total = jnp.sum(expo, -1)
    weights = (expo * value_scale).astype(jnp.bfloat16)
    summed = jnp.einsum("srgt,td->srgd", weights, values, preferred_element_type=jnp.float32)
    return (best, total, summed)


def local_general(
    hidden_in,
    norm_gain,
    qkv_weight,
    out_weight,
    cache_pool,
    cache_scale,
    request_length,
    block_table,
):
    devices = lax.axis_size("tensor")
    device = lax.axis_index("tensor")
    owners = devices // KVH
    stripe = devices * BLK
    requests = request_length.shape[0]
    request_owner = jnp.arange(requests, dtype=jnp.int32) % owners
    unit_rows = requests // owners * QR
    most = block_table.shape[1]
    local_width = hidden_in.shape[2]
    my_owner = device // KVH
    owner_requests, stripe_request, stripe_rank, slots, rank, stripes = request_layout(
        request_owner, request_length, block_table, owners, stripe
    )
    step_rows = jnp.arange(QR, dtype=jnp.int32)
    row_order = (owner_requests[:, :, None] * QR + step_rows[None, None, :]).reshape(
        owners * unit_rows
    )
    inverse = ((request_owner * unit_rows + rank * QR)[:, None] + step_rows[None, :]).reshape(
        requests * QR
    )
    row_request = jnp.repeat(owner_requests[my_owner], QR)
    row_length = request_length[row_request]
    row_step = jnp.arange(unit_rows, dtype=jnp.int32) % QR
    same_request = row_request[:, None] == row_request[None, :]
    gain = norm_gain.astype(jnp.float32)
    weight_grouped = qkv_weight.reshape(local_width, KVH, GW)
    sent = cache_pool[jnp.transpose(slots)].reshape(most, devices, BLK, 2 * HD)
    sent_scale = cache_scale[jnp.transpose(slots)].reshape(most, devices, 2)
    landed, landed_scale = (
        lax.all_to_all(sent, "tensor", split_axis=1, concat_axis=1, tiled=True),
        lax.all_to_all(sent_scale, "tensor", split_axis=1, concat_axis=1, tiled=True),
    )
    cache_data = landed.reshape(most * stripe, 2 * HD)
    token_scale = jnp.broadcast_to(
        landed_scale.astype(jnp.float32)[:, :, None, :], (most, devices, BLK, 2)
    ).reshape(most * stripe, 2)
    token = jnp.arange(most * stripe, dtype=jnp.int32)
    token_stripe = token // stripe
    token_request = stripe_request[my_owner][token_stripe]
    token_position = stripe_rank[my_owner][token_stripe] * stripe + token % stripe
    token_length = jnp.where(token_request >= 0, request_length[jnp.maximum(token_request, 0)], 0)
    cache_mask = (
        (token_request[None, :] == row_request[:, None]) & (token_position < token_length)[None, :]
    )[None, :, None, :]
    outputs = []
    keys_seen = []
    values_seen = []
    for step in range(STEPS):
        block = hidden_in[step : step + 1]
        project_count = block.shape[0]
        values = block.astype(jnp.float32)
        sums = lax.psum(jnp.sum(values * values, -1), "tensor")
        normed = (values * lax.rsqrt(sums[..., None] / D + EPSILON) * gain).astype(jnp.bfloat16)
        ordered = jnp.take(normed, row_order, axis=1).reshape(
            project_count, owners, unit_rows, local_width
        )
        term = jnp.einsum(
            "sojd,dhg->ohsjg", ordered, weight_grouped, preferred_element_type=jnp.float32
        )
        term = term.reshape(owners * KVH * project_count * unit_rows, GW)
        mine = lax.psum_scatter(term, "tensor", scatter_dimension=0, tiled=True)
        joined_block = mine.astype(jnp.bfloat16).reshape(project_count, unit_rows, GW)
        prepare_count = joined_block.shape[0]
        steps_here = step + jnp.arange(prepare_count, dtype=jnp.int32)
        position = row_length[None, :] + QR * steps_here[:, None] + row_step[None, :]
        prepare_queries = rotate(
            joined_block[..., : GQ * HD]
            .reshape(prepare_count, unit_rows, GQ, HD)
            .astype(jnp.float32),
            position[:, :, None],
        ).astype(jnp.bfloat16)
        keys = rotate(
            joined_block[..., GQ * HD : GQ * HD + HD].astype(jnp.float32), position
        ).astype(jnp.bfloat16)
        queries, keys, values = (prepare_queries, keys, joined_block[..., GQ * HD + HD :])
        keys_seen.append(keys)
        values_seen.append(values)
        keys_all = jnp.concatenate(keys_seen, 0)
        attend_count = queries.shape[0]
        cache_best, cache_total, cache_summed = cache_partial(
            queries,
            cache_data[:, :HD],
            cache_data[:, HD:],
            token_scale[:, 0],
            token_scale[:, 1],
            cache_mask,
        )
        news = jnp.einsum(
            "srgd,pjd->srgpj", queries, keys_all, preferred_element_type=jnp.float32
        ) * HD ** (-0.5)
        query_step = step + jnp.arange(attend_count, dtype=jnp.int32)[:, None, None, None]
        key_step = jnp.arange(keys_all.shape[0], dtype=jnp.int32)[None, None, :, None]
        allowed = (key_step < query_step) | (key_step == query_step) & (
            row_step[None, None, None, :] <= row_step[None, :, None, None]
        )
        allowed = (allowed & same_request[None, :, None, :])[:, :, None, :, :]
        news = jnp.where(allowed, news, NEG_FILL)
        best = jnp.maximum(cache_best, jnp.max(news, (3, 4)))
        factor = jnp.exp(cache_best - best)
        expo = jnp.where(allowed, jnp.exp(news - best[..., None, None]), 0.0)
        total = cache_total * factor + jnp.sum(expo, (3, 4))
        summed = cache_summed * factor[..., None] + jnp.einsum(
            "srgpj,pjd->srgd",
            expo.astype(jnp.bfloat16),
            jnp.concatenate(values_seen, 0),
            preferred_element_type=jnp.float32,
        )
        attention = (
            (summed / total[..., None])
            .astype(jnp.bfloat16)
            .reshape(attend_count, unit_rows, GQ * HD)
        )
        count = attention.shape[0]
        gathered = lax.all_gather(attention, "tensor", axis=2, tiled=True).reshape(
            count, unit_rows, owners, QH * HD
        )
        mixed = jnp.einsum(
            "sjof,fd->sojd", gathered, out_weight, preferred_element_type=jnp.float32
        )
        mixed = jnp.take(mixed.reshape(count, owners * unit_rows, local_width), inverse, axis=1)
        outputs.append(
            (hidden_in[step : step + count].astype(jnp.float32) + mixed).astype(jnp.bfloat16)
        )
    return jnp.concatenate(outputs, 0)


VMEM_LIMIT = 48 * 1024 * 1024
SHORT = pl.CostEstimate(flops=1, bytes_accessed=1, transcendentals=0)
LONG = pl.CostEstimate(flops=2 * 10**10, bytes_accessed=1, transcendentals=0)
LOW_BITS = 4
PACKED = 16 // LOW_BITS
LEVELS = 32600.0 * 2**LOW_BITS
POWER_STEPS = 8.0
TILE = 16
MESH_BITS = (1, 2, 4, 8)


def swap(value, bit):
    devices = lax.axis_size("tensor")
    return lax.ppermute(value, "tensor", [(i, i ^ bit) for i in range(devices)])


def no_work(*refs):
    del refs


def together(arrays, after):
    anywhere = pl.BlockSpec(memory_space=pl.ANY)
    return pl.pallas_call(
        no_work,
        in_specs=[anywhere] * (len(arrays) + len(after)),
        out_specs=[anywhere] * len(arrays),
        out_shape=[jax.ShapeDtypeStruct(a.shape, a.dtype) for a in arrays],
        input_output_aliases={i: i for i in range(len(arrays))},
        compiler_params=pltpu.CompilerParams(vmem_limit_bytes=VMEM_LIMIT),
        cost_estimate=SHORT,
        name="together",
    )(*arrays, *after)


def coded_rows(rows):
    return rows + rows // PACKED


def encode(block):
    top = jnp.max(jnp.abs(block), 0, keepdims=True)
    power = jnp.ceil(jnp.log2(jnp.maximum(top, 1e-30)) * POWER_STEPS)
    codes = jnp.round(block * (jnp.exp2(power * (-1.0 / POWER_STEPS)) * LEVELS)).astype(jnp.int32)
    low = codes & (2**LOW_BITS - 1)
    part = block.shape[0] // PACKED
    packed = low[:part]
    for i in range(1, PACKED):
        packed = packed + (low[i * part : (i + 1) * part] << (LOW_BITS * i))
    high = (codes >> LOW_BITS).astype(jnp.int16)
    return jnp.concatenate([high, (packed - 32768).astype(jnp.int16)], 0), power


def decode(codes, power):
    rows = codes.shape[0] * PACKED // (PACKED + 1)
    high = codes[:rows].astype(jnp.int32) << LOW_BITS
    packed = codes[rows:].astype(jnp.int32) + 32768
    low = jnp.concatenate(
        [(packed >> (LOW_BITS * i)) & (2**LOW_BITS - 1) for i in range(PACKED)], 0
    )
    scale = jnp.exp2(power * (1.0 / POWER_STEPS)) * (1.0 / LEVELS)
    return (high + low).astype(jnp.float32) * scale


def pick_row(rows, index):
    ids = lax.broadcasted_iota(jnp.int32, rows.shape, 0)
    return jnp.sum(jnp.where(ids == index, rows, 0.0), 0, keepdims=True)


def store_codes(sent, powers, block, index, steps):
    rows = coded_rows(block.shape[0])
    codes, power = encode(block)
    sent[pl.ds(pl.multiple_of(index * rows, TILE), rows), :] = codes

    powers[pl.ds(index, 1), :] = power

    @pl.when(index == steps - 1)
    def _():
        sent[pl.ds(steps * rows, TILE), :] = powers[...].astype(jnp.int32).astype(jnp.int16)


PART_HEADS = (3, 5)


def project_kernel(part, core, normed, weights, *refs):
    kept, sent, powers, slabs, arrived = refs[-5:]
    index = pl.program_id(0)
    half = kept.shape[2]
    heads = PART_HEADS[part] * HD
    first = sum(PART_HEADS[:part]) * HD

    def copies(group):
        found = []
        for side in range(2):
            owner = core[0] if side == 0 else 1 - core[0]
            spans = [(group * GW + owner * (GQ // 2 * HD) + first, 0, heads)]
            if half > heads:
                spans.append((group * GW + (GQ + owner) * HD, heads, HD))
            for number, (start, offset, size) in enumerate(spans):
                found.append(
                    pltpu.make_async_copy(
                        weights.at[:, pl.ds(pl.multiple_of(start, HD), size)],
                        slabs.at[group, :, pl.ds(side * half + offset, size)],
                        arrived.at[group, side, number],
                    )
                )
        return found

    @pl.when(index == 0)
    def _():
        for group in range(KVH):
            for copy in copies(group):
                copy.start()
        powers[...] = jnp.zeros_like(powers)

    for copy in copies(index):
        copy.wait()

    found = []
    rows = coded_rows(normed.shape[0])
    place = pl.ds(pl.multiple_of(index * rows, TILE), rows)
    for start in range(0, 2 * half, 2 * HD):
        stop = start + 2 * HD
        product = jnp.dot(
            normed[...], slabs[index, :, start:stop], preferred_element_type=jnp.float32
        )
        if start < half:
            kept[0, :, start : min(stop, half)] = product[:, : half - start]
        if stop > half:
            first = max(start, half)
            codes, power = encode(product[:, first - start :])
            sent[place, first - half : stop - half] = codes
            found.append(power)
    powers[pl.ds(index, 1), :] = jnp.concatenate(found, 1)

    @pl.when(index == KVH - 1)
    def _():
        sent[pl.ds(KVH * rows, TILE), :] = powers[...].astype(jnp.int32).astype(jnp.int16)


def project(core, normed, qkv_weight, part, after):
    rows, width = normed.shape
    columns = PART_HEADS[part] * HD + (HD if part == 0 else 0)
    sent_rows = KVH * coded_rows(rows) + TILE
    return pl.pallas_call(
        functools.partial(project_kernel, part),
        grid_spec=pltpu.PrefetchScalarGridSpec(
            num_scalar_prefetch=1,
            grid=(KVH,),
            in_specs=[pl.BlockSpec((rows, width), lambda t, c: (0, 0))]
            + [pl.BlockSpec(memory_space=pl.ANY)] * (1 + len(after)),
            out_specs=[
                pl.BlockSpec((1, rows, columns), lambda t, c: (t, 0, 0)),
                pl.BlockSpec((sent_rows, columns), lambda t, c: (0, 0)),
            ],
            scratch_shapes=[
                pltpu.VMEM((TILE, columns), jnp.float32),
                pltpu.VMEM((KVH, width, 2 * columns), jnp.bfloat16),
                pltpu.SemaphoreType.DMA((KVH, 2, 2)),
            ],
        ),
        out_shape=[
            pltpu.HBM((KVH, rows, columns), jnp.float32),
            jax.ShapeDtypeStruct((sent_rows, columns), jnp.int16),
        ],
        compiler_params=pltpu.CompilerParams(vmem_limit_bytes=VMEM_LIMIT),
        cost_estimate=SHORT,
        name="project",
    )(core, normed, qkv_weight, *after)


def fold_kernel(steps, low, bit, held, held_out, landed, landed_out, landed_powers, *refs):
    kept, sent, powers = refs[-3:]
    index = pl.program_id(0)
    rows_of_powers = landed_powers[...].astype(jnp.int32).astype(jnp.float32)
    first = index // low * (2 * low) + index % low

    def total(side, block, codes):
        power = pick_row(rows_of_powers, first + side * low)
        return block[0] + decode(codes[...], power)

    @pl.when(index == 0)
    def _():
        powers[...] = jnp.zeros_like(powers)

    kept[0] = total(bit[0], held, landed)
    store_codes(sent, powers, total(1 - bit[0], held_out, landed_out), index, steps)


def fold(bit, held, landed, low, after):
    blocks, rows, columns = held.shape
    steps = blocks // 2
    coded = coded_rows(rows)

    def block(i, b, out):
        side = 1 - b[0] if out else b[0]
        return i // low * (2 * low) + side * low + i % low

    return pl.pallas_call(
        functools.partial(fold_kernel, steps, low),
        grid_spec=pltpu.PrefetchScalarGridSpec(
            num_scalar_prefetch=1,
            grid=(steps,),
            in_specs=[
                pl.BlockSpec((1, rows, columns), lambda i, b: (block(i, b, False), 0, 0)),
                pl.BlockSpec((1, rows, columns), lambda i, b: (block(i, b, True), 0, 0)),
                pl.BlockSpec((coded, columns), lambda i, b: (block(i, b, False), 0)),
                pl.BlockSpec((coded, columns), lambda i, b: (block(i, b, True), 0)),
                pl.BlockSpec((TILE, columns), lambda i, b: (blocks * coded // TILE, 0)),
            ]
            + [pl.BlockSpec(memory_space=pl.ANY)] * len(after),
            out_specs=[
                pl.BlockSpec((1, rows, columns), lambda i, b: (i, 0, 0)),
                pl.BlockSpec((steps * coded + TILE, columns), lambda i, b: (0, 0)),
            ],
            scratch_shapes=[pltpu.VMEM((TILE, columns), jnp.float32)],
        ),
        out_shape=[
            jax.ShapeDtypeStruct((steps, rows, columns), jnp.float32),
            jax.ShapeDtypeStruct((steps * coded + TILE, columns), jnp.int16),
        ],
        compiler_params=pltpu.CompilerParams(vmem_limit_bytes=VMEM_LIMIT),
        cost_estimate=SHORT,
        name="fold",
    )(bit, held, held, landed, landed, landed, *after)


def finish_kernel(heads, after_count, core, held, landed, cosine, sine, *refs):
    queries, *pair = refs[after_count:]
    coded = coded_rows(held.shape[1])
    power = landed[pl.ds(coded, TILE), :].astype(jnp.int32).astype(jnp.float32)[0:1]
    total = held[0] + decode(landed[pl.ds(0, coded), :], power)
    joined = total.astype(jnp.bfloat16)
    for head in range(joined.shape[1] // HD):
        raw = joined[:, head * HD : (head + 1) * HD].astype(jnp.float32)
        turned = raw * cosine[...] + pltpu.roll(raw, HD // 2, 1) * sine[...]
        if head < heads:
            queries[:, head * HD : (head + 1) * HD] = turned.astype(jnp.bfloat16)
        else:
            pair[0][...] = jnp.where(core[0] == 0, turned, raw).astype(jnp.bfloat16)


def finish(core, held, landed, cosine, sine, heads, after):
    _, rows, columns = held.shape
    whole = pl.BlockSpec(memory_space=pltpu.VMEM)
    shapes = [jax.ShapeDtypeStruct((rows, heads * HD), jnp.bfloat16)]
    if columns > heads * HD:
        shapes.append(jax.ShapeDtypeStruct((rows, HD), jnp.bfloat16))
    return pl.pallas_call(
        functools.partial(finish_kernel, heads, len(after)),
        in_specs=[pl.BlockSpec(memory_space=pltpu.SMEM)]
        + [whole] * 4
        + [pl.BlockSpec(memory_space=pl.ANY)] * len(after),
        out_specs=[whole] * len(shapes),
        out_shape=shapes,
        compiler_params=pltpu.CompilerParams(vmem_limit_bytes=VMEM_LIMIT),
        cost_estimate=LONG,
        name="finish",
    )(core, held, landed, cosine, sine, *after)


def mix_kernel(count, places, *refs):
    pieces = refs[:count]
    weights, start, mixed, total, wide, arrived = refs[count:]
    depth = wide.shape[1]
    columns = wide.shape[2] // 2
    flat = []
    for piece in pieces:
        flat += [piece] if len(piece.shape) == 2 else [piece.at[i] for i in range(piece.shape[0])]
    copies = [
        pltpu.make_async_copy(
            weights.at[pl.ds(pl.multiple_of(places[i] * depth, depth), depth), :],
            wide.at[i],
            arrived.at[i],
        )
        for i in range(len(flat))
    ]
    for copy in copies:
        copy.start()
    cuts = [0, 1, 2, 4, len(flat)]
    cuts = sorted(set(min(cut, len(flat)) for cut in cuts))
    for first, last in zip(cuts, cuts[1:]):
        for copy in copies[first:last]:
            copy.wait()
        for side in range(2):
            span = pl.ds(side * columns, columns)
            source = start if first == 0 else total
            value = source[:, span].astype(jnp.float32)
            for i in range(first, last):
                value = value + jnp.dot(
                    flat[i][...], wide[i, :, span], preferred_element_type=jnp.float32
                )
            target = mixed if last == len(flat) else total
            target[:, span] = value.astype(target.dtype)


def mix(places, pieces, out_weight, start, dtype):
    columns = out_weight.shape[1]
    rows, width = pieces[0].shape[-2:]
    count = sum(1 if len(p.shape) == 2 else p.shape[0] for p in pieces)
    whole = pl.BlockSpec(memory_space=pltpu.VMEM)
    return pl.pallas_call(
        functools.partial(mix_kernel, len(pieces)),
        in_specs=[pl.BlockSpec(memory_space=pltpu.SMEM)]
        + [whole] * len(pieces)
        + [pl.BlockSpec(memory_space=pl.ANY), whole],
        out_specs=whole,
        scratch_shapes=[
            pltpu.VMEM((rows, columns), jnp.float32),
            pltpu.VMEM((count, width, columns), jnp.bfloat16),
            pltpu.SemaphoreType.DMA((count,)),
        ],
        out_shape=jax.ShapeDtypeStruct((rows, columns), dtype),
        compiler_params=pltpu.CompilerParams(vmem_limit_bytes=VMEM_LIMIT),
        cost_estimate=SHORT,
        name="mix",
    )(places, *pieces, out_weight, start)


def pack_kernel(groups, count, *refs):
    flat = []
    for ref in refs[:count]:
        flat += [ref] if len(ref.shape) == 2 else [ref.at[i] for i in range(ref.shape[0])]
    for group, target in zip(groups, refs[-len(groups) :]):
        for place, index in enumerate(group):
            target[place] = flat[index][...]


def pack(pieces, groups, after):
    whole = pl.BlockSpec(memory_space=pltpu.VMEM)
    shape = pieces[0].shape[-2:]
    return pl.pallas_call(
        functools.partial(pack_kernel, groups, len(pieces)),
        in_specs=[whole] * len(pieces) + [pl.BlockSpec(memory_space=pl.ANY)] * len(after),
        out_specs=[whole] * len(groups),
        out_shape=[jax.ShapeDtypeStruct((len(g),) + shape, pieces[0].dtype) for g in groups],
        compiler_params=pltpu.CompilerParams(vmem_limit_bytes=VMEM_LIMIT),
        cost_estimate=SHORT,
        name="pack",
    )(*pieces, *after)


def gather_and_mix(attention, out_weight, start, device):
    def add(mixed, pieces, offsets, dtype=jnp.float32):
        places = jnp.stack([device ^ offset for offset in offsets])
        return mix(places, pieces, out_weight, mixed, dtype)

    near = swap(attention, 4)
    across = swap(attention, 2)
    far = swap(attention, 8)
    partner = swap(attention, 1)
    first, onward = pack([near, across, far], [(0, 1, 2), (0, 2)], [partner])
    (attention,) = together([attention], [onward])

    across_onward = swap(onward, 2)
    farthest = swap(attention, 12)
    first_partner = swap(first, 1)
    mixed = add(start, [attention, partner], (0, 1))
    mixed = add(mixed, [first, first_partner], (4, 2, 8, 5, 3, 9))
    (second,) = pack([across_onward, farthest], [(0, 1, 2)], [mixed])

    last = swap(farthest, 2)
    second_partner = swap(second, 1)
    mixed = add(mixed, [second, second_partner], (6, 10, 12, 7, 11, 13))
    (last,) = together([last], [mixed])

    last_partner = swap(last, 1)
    mixed = add(mixed, [last], (14,))
    return add(mixed, [last_partner], (15,), jnp.bfloat16)


def attend_kernel(
    slot_request,
    queries,
    new_keys,
    new_values,
    own,
    other,
    key_scale,
    value_scale,
    cache_bias,
    new_bias,
    attention,
    slot_best,
    slot_total,
    slot_sum,
    best,
    total,
    summed,
):
    slots = slot_best.shape[0]
    requests, count, _ = queries.shape
    transposed = (((1,), (1,)), ((), ()))
    for request in range(requests):
        scores = (
            lax.dot_general(
                queries[request],
                new_keys[request],
                transposed,
                preferred_element_type=jnp.float32,
            )
            * HD ** (-0.5)
            + new_bias[...]
        )
        top = jnp.max(scores, -1, keepdims=True)
        expo = jnp.exp(scores - top)
        best[request] = jnp.broadcast_to(top, (count, HD))
        total[request] = jnp.broadcast_to(jnp.sum(expo, -1, keepdims=True), (count, HD))
        summed[request] = jnp.dot(
            expo.astype(jnp.bfloat16), new_values[request], preferred_element_type=jnp.float32
        )
    for slot in range(slots):
        request = slot_request[slot]
        query = queries[request]
        raw = [
            part[:, slot * BLK : (slot + 1) * BLK, :].reshape(KVH * BLK, 2 * HD)
            for part in (own, other)
        ]
        scores = jnp.concatenate(
            [
                lax.dot_general(
                    query, kv[:, :HD], transposed, preferred_element_type=jnp.float32
                )
                for kv in raw
            ],
            1,
        )
        scores = scores * key_scale[slot : slot + 1, :] + cache_bias[slot : slot + 1, :]
        top = jnp.max(scores, -1, keepdims=True)
        expo = jnp.exp(scores - top)
        weights = (expo * value_scale[slot : slot + 1, :]).astype(jnp.bfloat16)
        slot_best[slot] = jnp.broadcast_to(top, (count, HD))
        slot_total[slot] = jnp.broadcast_to(jnp.sum(expo, -1, keepdims=True), (count, HD))
        values = jnp.concatenate([kv[:, HD:] for kv in raw], 0)
        slot_sum[slot] = jnp.dot(weights, values, preferred_element_type=jnp.float32)
    for slot in range(slots):
        request = slot_request[slot]
        before = best[request]
        here = slot_best[slot]
        top = jnp.maximum(before, here)
        keep = jnp.exp(before - top)
        add = jnp.exp(here - top)
        best[request] = top
        total[request] = total[request] * keep + slot_total[slot] * add
        summed[request] = summed[request] * keep + slot_sum[slot] * add
    for request in range(requests):
        attention[request] = (summed[request] / total[request]).astype(jnp.bfloat16)


def attend(slot_request, *arrays):
    queries = arrays[0]
    slots = arrays[5].shape[0]
    requests, count, _ = queries.shape
    whole = pl.BlockSpec(memory_space=pltpu.VMEM)
    return pl.pallas_call(
        attend_kernel,
        in_specs=[pl.BlockSpec(memory_space=pltpu.SMEM)] + [whole] * len(arrays),
        out_specs=whole,
        out_shape=jax.ShapeDtypeStruct((requests, count, HD), jnp.bfloat16),
        scratch_shapes=[pltpu.VMEM((slots, count, HD), jnp.float32)] * 3
        + [pltpu.VMEM((requests, count, HD), jnp.float32)] * 3,
        compiler_params=pltpu.CompilerParams(vmem_limit_bytes=VMEM_LIMIT),
        cost_estimate=SHORT,
        name="attend",
    )(slot_request, *arrays)


def slot_layout(request_length, block_table, slots, stripe):
    requests, most = block_table.shape
    stripes = (request_length + stripe - 1) // stripe
    columns = jnp.arange(most, dtype=jnp.int32)
    held = columns[None, :] < stripes[:, None]
    hit = held[:, :, None] & (
        block_table[:, :, None] == jnp.arange(slots, dtype=jnp.int32)[None, None, :]
    )
    hit = hit.astype(jnp.int32)
    order = jnp.arange(requests, dtype=jnp.int32)
    request = jnp.sum(hit * order[:, None, None], (0, 1))
    rank = jnp.sum(hit * columns[None, :, None], (0, 1))
    length = jnp.sum(hit * request_length[:, None, None], (0, 1))
    return request, rank, length


def arrange_kernel(chip, pool, scales, after, *sent):
    slots = pool.shape[0]
    for k, target in enumerate(sent):
        head = chip[0] ^ k
        target[: slots * BLK, :] = pool[:, head].reshape(slots * BLK, 2 * HD)
        target[slots * BLK :, :] = scales[head]


def arrange(chip, cache_pool, scales, after):
    rows = cache_pool.shape[0] * BLK + TILE
    whole = pl.BlockSpec(memory_space=pltpu.VMEM)
    return pl.pallas_call(
        arrange_kernel,
        in_specs=[
            pl.BlockSpec(memory_space=pltpu.SMEM),
            whole,
            whole,
            pl.BlockSpec(memory_space=pl.ANY),
        ],
        out_specs=[whole] * KVH,
        out_shape=[jax.ShapeDtypeStruct((rows, 2 * HD), jnp.bfloat16)] * KVH,
        compiler_params=pltpu.CompilerParams(vmem_limit_bytes=VMEM_LIMIT),
        cost_estimate=SHORT,
        name="arrange",
    )(chip, cache_pool, scales, after)


def local_pairs(
    hidden_in,
    norm_gain,
    qkv_weight,
    out_weight,
    cache_pool,
    cache_scale,
    request_length,
    block_table,
):
    devices = lax.axis_size("tensor")
    device = lax.axis_index("tensor")
    core = device % 2
    chip = device // 2
    stripe = devices * BLK
    slots = cache_pool.shape[0]
    requests = request_length.shape[0]
    rows = STEPS * requests * QR
    width = hidden_in.shape[2]
    heads = GQ // 2

    hidden = hidden_in.astype(jnp.float32)
    sums = jnp.sum(hidden * hidden, -1)
    bits = [jnp.reshape((device >> b) & 1, (1,)).astype(jnp.int32) for b in range(4)]
    scale_rows = jnp.pad(
        jnp.transpose(cache_scale, (1, 2, 0)).reshape(KVH, 1, 2 * slots),
        ((0, 0), (0, TILE - 1), (0, 2 * HD - 2 * slots)),
    )
    sums = sums + swap(sums, 2)
    chip_scalar = jnp.reshape(chip, (1,)).astype(jnp.int32)
    cache_pieces = list(arrange(chip_scalar, cache_pool, scale_rows, sums))

    def handed(k):
        cache_pieces[k] = swap(cache_pieces[k], 2 * k)

    for bit in (1, 4, 8):
        sums = sums + swap(sums, bit)
    normed = (
        hidden * lax.rsqrt(sums[..., None] / D + EPSILON) * norm_gain.astype(jnp.float32)
    ).astype(jnp.bfloat16)
    normed = normed.reshape(rows, width)

    step_ids = jnp.arange(STEPS, dtype=jnp.int32)
    row_ids = jnp.arange(QR, dtype=jnp.int32)
    position = (
        request_length[None, :, None] + QR * step_ids[:, None, None] + row_ids[None, None, :]
    )
    freqs = ROPE_BASE ** (-(jnp.arange(HD // 2, dtype=jnp.float32) * 2.0 / HD))
    angles = position.reshape(rows, 1).astype(jnp.float32) * freqs
    cosine = jnp.concatenate([jnp.cos(angles)] * 2, 1)
    sine = jnp.concatenate([-jnp.sin(angles), jnp.sin(angles)], 1)

    def folded(part, b, landed, low, *after):
        return fold(bits[b], part, landed, low, after)

    def finished(part, number, landed, *after):
        return finish(bits[0], part, landed, cosine, sine, PART_HEADS[number], after)

    for k in (1, 3, 4, 5, 6):
        handed(k)
    held_a, sent_a = project(bits[0], normed, qkv_weight, 0, cache_pieces[:1])
    core_a = swap(sent_a, 1)
    held_b, sent_b = project(
        bits[0], normed, qkv_weight, 1, [held_a, cache_pieces[1], cache_pieces[3]]
    )
    sent_b, cache_pieces[2], cache_pieces[7] = together(
        [sent_b, cache_pieces[2], cache_pieces[7]], cache_pieces[4:7]
    )
    core_b = swap(sent_b, 1)
    for k in (2, 7):
        handed(k)
    held_a, sent_a = folded(held_a, 1, core_a, 1, sent_b)
    line_a = swap(sent_a, 2)
    held_b, sent_b = folded(held_b, 2, core_b, 2, held_a, cache_pieces[2], cache_pieces[7])
    line_b = swap(sent_b, 4)
    held_a, sent_a = folded(held_a, 2, line_a, 1, held_b)
    line_a = swap(sent_a, 4)
    held_b, sent_b = folded(held_b, 1, line_b, 1, held_a)
    line_b = swap(sent_b, 2)
    (cache_own,) = pack(cache_pieces, [tuple(range(KVH))], [held_b])
    cache_other = swap(cache_own, 1)
    held_a, sent_a = folded(held_a, 3, line_a, 1, cache_own)
    line_a = swap(sent_a, 8)
    held_b, sent_b = folded(held_b, 3, line_b, 1, held_a)
    line_b = swap(sent_b, 8)
    query_a, pair = finished(held_a, 0, line_a, held_b)
    (pair,) = together([pair], [line_b])
    pair_other = swap(pair, 1)
    (query_b,) = finished(held_b, 1, line_b, query_a)
    query_chunks = [query_a, query_b]
    cache_parts = (cache_own, cache_other)
    keys = jnp.where(core == 0, pair, pair_other)
    raw_values = jnp.where(core == 0, pair_other, pair)
    queries = jnp.concatenate(query_chunks, 1).reshape(STEPS, requests, QR, heads, HD)
    queries = jnp.transpose(queries, (1, 0, 2, 3, 4)).reshape(requests, STEPS * QR * heads, HD)

    def by_request(value):
        value = jnp.transpose(value.reshape(STEPS, requests, QR, HD), (1, 0, 2, 3))
        value = value.reshape(requests, STEPS * QR, HD)
        return jnp.pad(value, ((0, 0), (0, TILE - STEPS * QR), (0, 0)))

    slot_request, slot_rank, slot_length = slot_layout(request_length, block_table, slots, stripe)
    source = chip ^ jnp.arange(KVH, dtype=jnp.int32)
    sources = jnp.stack([source * 2 + core, source * 2 + 1 - core])
    offset = sources[:, :, None] * BLK + jnp.arange(BLK, dtype=jnp.int32)[None, None, :]
    token = slot_rank[:, None] * stripe + offset.reshape(1, stripe)
    cache_bias = jnp.where(token < slot_length[:, None], 0.0, NEG_FILL).astype(jnp.float32)
    scales = jnp.concatenate([part[:, slots * BLK, : 2 * slots] for part in cache_parts])
    scales = scales.astype(jnp.float32).reshape(2 * KVH, 2, slots)
    scales = jnp.repeat(jnp.transpose(scales, (1, 2, 0)), BLK, axis=2)
    order = jnp.arange(STEPS * QR * heads, dtype=jnp.int32) // heads
    key_order = jnp.arange(TILE, dtype=jnp.int32)
    new_bias = jnp.where(key_order[None, :] <= order[:, None], 0.0, NEG_FILL).astype(jnp.float32)
    attention = attend(
        slot_request,
        queries,
        by_request(keys),
        by_request(raw_values),
        *cache_parts,
        scales[0] * HD ** (-0.5),
        scales[1],
        cache_bias,
        new_bias,
    )
    attention = jnp.transpose(
        attention.reshape(requests, STEPS, QR, heads, HD), (1, 0, 2, 3, 4)
    ).reshape(rows, heads * HD)
    mixed = gather_and_mix(attention, out_weight, hidden_in.reshape(rows, width), device)
    return mixed.reshape(hidden_in.shape)


def solution(mesh):
    return jax.shard_map(
        local_pairs if mesh.shape["tensor"] == 2 * KVH else local_general,
        mesh=mesh,
        in_specs=(
            P(None, "groups", "tensor"),
            P("tensor"),
            P("tensor", None),
            P(None, "tensor"),
            P(("groups", "tensor"), None, None, None),
            P(("groups", "tensor"), None, None),
            P("groups"),
            P("groups", None),
        ),
        out_specs=P(None, "groups", "tensor"),
        check_vma=False,
    )
```
